512 devices in a mesh: tm: 16 (over x, y), users: 8 (over z_lo), mp: 4 (over z_hi, core).
Axes of the slice: x: 4, y: 4, z: 16 (z_hi: 2, z_lo: 8; z = z_hi * 8 + z_lo), core: 2. Of those that a mesh axis runs over, the one named last changes fastest.
Arguments:
- history: bfloat16 [32, 4096, 512], P(('users', 'mp'), 'tm'), may hold values from -6 to 6
- ln_gain: float32 [512], replicated, may hold values from 0.1 to 1.9
- w_proj: bfloat16 [512, 2048], replicated, may hold values from -18 to 18
- w_out: bfloat16 [512, 512], replicated, may hold values from -0.25 to 0.25
- pool_query: bfloat16 [4, 512], replicated, may hold values from -0.25 to 0.25
- lengths: int32 [32], P(('users', 'mp')), may hold values from 256 to 4096, as said below
- slots: int32 [32], replicated, may hold values from 0 to 31, each once
- cand_ids: int32 [32, 1024], P('users', 'tm'), may hold values from 0 to 511
- item_table: bfloat16 [4096, 512], P('users'), may hold values from -6 to 6
- w_rank: bfloat16 [1024, 1024], P(None, 'mp'), may hold values from -0.1875 to 0.1875
- b_rank: float32 [1024], P('mp'), may hold values from -1 to 1
- w_score: float32 [1024], P('mp'), may hold values from -0.1875 to 0.1875
Outputs:
- layer_out: bfloat16 [32, 4096, 512], P(('users', 'mp'), 'tm')
- scores: float32 [32, 1024], P('users', 'tm')
The draws below stay inside these ranges and needn't reach their ends.
Inputs may be any that keep to these rules, and one draw needn't show every extreme that they name: `lengths`: at least one user has history length exactly 4096. `slots`: each user has its own ranker slot; slot s belongs to ranker owner s // 4.
All inputs are finite; a program needn't handle non-finite values.
Results may differ from the reference program's by a relative error of at most 0.015.
Values may be sent and summed in bfloat16 or wider, within the bound.
A program may use at most 128 MiB of HBM per device.

```python
import math
import jax
import jax.numpy as jnp
from jax import lax

D = 512
HEADS = 4
DH = 128
GROUPS = 4
HID = 1024
POOL = 512
LEN = 4096
USERS = 32
RU = 4
CAND = 1024
N_USERS = 8


def draw_lengths(key, part):
    key = jax.random.fold_in(key, 11)
    first, second = jax.random.split(key)
    values = jax.random.randint(first, (USERS,), max(1, LEN // 16), LEN + 1, dtype=jnp.int32)
    chosen = jax.random.randint(second, (), 0, USERS, dtype=jnp.int32)
    return jnp.where(jnp.arange(USERS, dtype=jnp.int32) == chosen, LEN, values).astype(jnp.int32)


def draw_w_proj(key, part):
    key = jax.random.fold_in(key, 23)
    first, second = jax.random.split(key)
    base = jnp.clip(jax.random.normal(first, (D, 4 * D), jnp.float32), -6.0, 6.0)
    spread = jnp.exp(jax.random.uniform(second, (4 * D,), jnp.float32, -0.6931472, 0.6931472))
    blocks = jnp.concatenate([jnp.full((D,), 1.0, jnp.float32), jnp.full((D,), 0.35, jnp.float32), jnp.full((D,), 12.0, jnp.float32), jnp.full((D,), 0.25, jnp.float32)])
    return (base * D ** (-0.5) * blocks[None, :] * spread[None, :]).astype(jnp.bfloat16)


def plant(result, key, smallest, high):
    dims = result.shape
    place = [jax.random.randint(jax.random.fold_in(key, axis), (), 0, dims[axis]) for axis in range(len(dims))]
    result = result.at[tuple(place)].set(smallest)
    longest = dims.index(max(dims))
    place[longest] = (place[longest] + 1) % dims[longest]
    return result.at[tuple(place)].set(high)


def levels(stream_key, extent, pieces, smallest, largest):
    loudness, own = 1.0, jax.random.fold_in(stream_key, 6)
    for dim, blocks in pieces:
        heights = jnp.exp(jax.random.uniform(jax.random.fold_in(own, dim), (blocks,), jnp.float32, smallest / len(pieces), largest / len(pieces)))
        loudness = loudness * jnp.repeat(heights, extent[dim] // blocks).reshape([-1 if axis == dim else 1 for axis in range(len(extent))])
    return loudness


def scatter_about(rng, dims, scale, limit, cuts=(), kind=jnp.bfloat16):
    entries = jax.random.normal(rng, dims, jnp.float32) * scale
    if len(cuts) > 0:
        entries = levels(rng, dims, cuts, -0.22, 0.18) * entries
    return jnp.clip(entries, min=-limit, max=limit).astype(kind)


def setup_inputs(seed: int = 0) -> dict:
    key_list = jax.random.split(jax.random.key(seed), 13)
    return {
        "history": scatter_about(key_list[0], (USERS, LEN, D), 1.0, 6.0, ((0, 32), (1, 16))),
        "ln_gain": jnp.clip(1.0 + 0.18 * jax.random.normal(key_list[1], (D,), jnp.float32), 0.1, 1.9),
        "w_proj": draw_w_proj(jax.random.fold_in(key_list[12], 71), 0),
        "w_out": scatter_about(key_list[3], (D, D), D ** -0.5, 0.25),
        "pool_query": scatter_about(key_list[4], (GROUPS, D), D ** -0.5, 0.25),
        "lengths": draw_lengths(jax.random.fold_in(key_list[12], 71), 0),
        "slots": jax.random.permutation(key_list[6], USERS).astype(jnp.int32),
        "cand_ids": plant(jax.random.randint(key_list[7], (USERS, CAND), 0, POOL), jax.random.fold_in(key_list[7], 1), 0, POOL - 1).astype(jnp.int32),
        "item_table": scatter_about(key_list[8], (N_USERS * POOL, D), 1.0, 6.0, ((0, 8),)),
        "w_rank": scatter_about(key_list[9], (2 * D, HID), (2 * D) ** -0.5, 0.1875, ((1, 4),)),
        "b_rank": jnp.clip(jax.random.uniform(key_list[10], (HID,), jnp.float32, -1.0, 1.0) * levels(key_list[10], (HID,), ((0, 4),), -0.4, 0.0), -1.0, 1.0),
        "w_score": scatter_about(key_list[11], (HID,), HID ** -0.5, 0.1875, ((0, 4),), jnp.float32),
    }


EPS = 1e-05

def layer_norm(values):
    mean = lax.optimization_barrier(jnp.mean(values, axis=-1, keepdims=True))
    centred = values - mean
    var = lax.optimization_barrier(jnp.mean(centred * centred, axis=-1, keepdims=True))
    return centred * lax.rsqrt(var + EPS)

def reference(history, ln_gain, w_proj, w_out, pool_query, lengths, slots, cand_ids, item_table, w_rank, b_rank, w_score):
    width = D
    block = math.gcd(LEN, 512)
    normed = (layer_norm(history.astype(jnp.float32)) * ln_gain).astype(jnp.bfloat16)
    proj = jax.nn.silu(jnp.dot(normed.reshape(-1, width), w_proj, preferred_element_type=jnp.float32))
    proj = proj.astype(jnp.bfloat16).reshape(USERS, LEN, 4 * width)

    def one_user(packed):
        proj_u, hist_u, length = packed
        gate_u = proj_u[:, :width].astype(jnp.float32)
        values = proj_u[:, width:2 * width].astype(jnp.float32).reshape(LEN, HEADS, DH)
        query = proj_u[:, 2 * width:3 * width].astype(jnp.float32).reshape(LEN, HEADS, DH)
        keys = proj_u[:, 3 * width:].astype(jnp.float32).reshape(LEN, HEADS, DH)
        parts = []
        for index in range(LEN // block):
            top = (index + 1) * block
            q_pos = index * block + jnp.arange(block, dtype=jnp.int32)
            k_pos = jnp.arange(top, dtype=jnp.int32)
            scores = jnp.einsum('ihe,jhe->hij', query[index * block:top], keys[:top], precision=lax.Precision.HIGHEST)
            keep = (k_pos[None, :] <= q_pos[:, None]) & (k_pos[None, :] < length)
            weights = jnp.where(keep[None], jax.nn.silu(scores * DH ** (-0.5)), 0.0).astype(jnp.bfloat16)
            mixed = jnp.einsum('hij,jhe->ihe', weights.astype(jnp.float32), values[:top], precision=lax.Precision.HIGHEST)
            parts.append(mixed.reshape(block, width))
        attended = jnp.concatenate(parts, axis=0)
        mixed = (layer_norm(attended) * gate_u).astype(jnp.bfloat16)
        out = hist_u.astype(jnp.float32) + jnp.dot(mixed, w_out, preferred_element_type=jnp.float32)
        layer_u = out.astype(jnp.bfloat16)
        live = jnp.arange(LEN, dtype=jnp.int32) < length
        pool_w = jnp.dot(layer_u, pool_query.T, preferred_element_type=jnp.float32)
        pool_w = jnp.where(live[:, None], jax.nn.silu(pool_w), 0.0).astype(jnp.bfloat16)
        sums = jnp.dot(pool_w.T, layer_u, preferred_element_type=jnp.float32)
        state = sums.astype(jnp.bfloat16)
        return (layer_u, state.reshape(GROUPS * width))
    layer_out, states = lax.map(one_user, (proj, history, lengths))
    placed = jnp.zeros_like(states).at[slots].set(states).reshape(USERS, GROUPS, width)
    interest = layer_norm(placed.astype(jnp.float32)).astype(jnp.bfloat16)
    owner = jnp.arange(USERS, dtype=jnp.int32) // RU
    rows = owner[:, None] * POOL + cand_ids
    cand = item_table[rows]
    attn = jax.nn.silu(jnp.einsum('scd,sgd->scg', cand.astype(jnp.float32), interest.astype(jnp.float32), precision=lax.Precision.HIGHEST) * width ** (-0.5))
    context = jnp.einsum('scg,sgd->scd', attn, interest.astype(jnp.float32), precision=lax.Precision.HIGHEST).astype(jnp.bfloat16)
    joined = jnp.concatenate([cand, context], axis=-1).reshape(-1, 2 * width)
    hidden = jax.nn.silu(jnp.dot(joined, w_rank, preferred_element_type=jnp.float32) + b_rank)
    scores = jnp.dot(hidden, w_score, precision=lax.Precision.HIGHEST).reshape(USERS, CAND)
    return (layer_out, scores)
```

```python
import jax
import jax.numpy as jnp
from jax import lax
from jax.experimental import pallas as pl
from jax.experimental.pallas import tpu as pltpu
from jax.sharding import PartitionSpec as P

HEADS = 4
SIDE = 4
EPS = 1e-05
MESH = pl.DeviceIdType.MESH
F32 = jnp.float32
BF16 = jnp.bfloat16
ROWS_BY_ROWS = (((1,), (1,)), ((), ()))


def layer_norm(values):
    mean = jnp.mean(values, axis=-1, keepdims=True)
    centred = values - mean
    var = jnp.mean(centred * centred, axis=-1, keepdims=True)
    return centred * lax.rsqrt(var + EPS)


def silu_of_twice(half):
    return half + half * jnp.tanh(half)


def dot_t(a, b, **kw):
    return lax.dot_general(a, b, ROWS_BY_ROWS, preferred_element_type=F32, **kw)


def kernel(
    lengths,
    history,
    ln_gain,
    w_proj,
    w_out,
    pool_query,
    slots,
    cand_ids,
    item_table,
    w_rank,
    b_rank,
    w_score,
    layer_out,
    scores,
    hist,
    wp,
    wo,
    table,
    wr,
    normed,
    gate,
    qkv,
    kv,
    qs,
    acc,
    back,
    att,
    result,
    cand,
    pre,
    part,
    parts,
    piece,
    pieces,
    chosen,
    interests,
    share,
    shares,
    load_sem,
    store_sem,
    kv_send,
    kv_recv,
    q_send,
    q_recv,
    pass_send,
    pass_recv,
    back_send,
    back_recv,
    sum_sem,
    state_sem,
    pick_sem,
    share_sem,
):
    events, width = hist.shape
    head_size = width // HEADS
    plane, line, ranks = parts.shape[0], pieces.shape[0], shares.shape[0]
    t = lax.axis_index("tm")
    owner = lax.axis_index("users")
    mp = lax.axis_index("mp")
    user = owner * ranks + mp
    x, y = lax.div(t, SIDE), lax.rem(t, SIDE)
    core = lax.rem(mp, 2)

    def even(v):
        return v + 1 - 2 * lax.rem(v, 2)

    def odd(v):
        return SIDE - 1 - v

    def swap(v):
        return even(v) + core * (odd(v) - even(v))

    def ring(v):
        return odd(v) + core * (even(v) - odd(v))

    def bit(v):
        first = lax.rem(lax.div(v + 1, 2), 2)
        return first + core * (lax.div(v, 2) - first)

    def head_of(a, b):
        return 2 * bit(a) + bit(b)

    def moved(a, b, rel, flip):
        first, second = lax.rem(rel, 2), lax.div(rel, 2)
        return a + first * (flip(a) - a), b + second * (flip(b) - b)

    def in_plane(a, b):
        return {"tm": a * SIDE + b}

    head = head_of(x, y)

    barrier = pltpu.get_barrier_semaphore()

    @pl.loop(1, plane)
    def _(k):
        pl.semaphore_signal(
            barrier, inc=1, device_id={"tm": lax.rem(t + k, plane)}, device_id_type=MESH
        )

    @pl.loop(1, line)
    def _(k):
        other = lax.rem(user + k, line)
        pl.semaphore_signal(
            barrier,
            inc=1,
            device_id={"users": lax.div(other, ranks), "mp": lax.rem(other, ranks)},
            device_id_type=MESH,
        )

    loads = [pltpu.make_async_copy(history.at[0], hist, load_sem.at[0])]
    for n, block in enumerate((3, 1, 2, 0)):
        cols = pl.ds(block * width, width)
        loads.append(pltpu.make_async_copy(w_proj.at[:, cols], wp.at[n], load_sem.at[n + 1]))
    loads.append(pltpu.make_async_copy(w_out, wo, load_sem.at[5]))
    loads.append(pltpu.make_async_copy(item_table, table, load_sem.at[6]))
    loads.append(pltpu.make_async_copy(w_rank, wr, load_sem.at[7]))
    for load in loads:
        load.start()

    first_pos = t * events
    length = lengths[0]
    pos = first_pos + lax.broadcasted_iota(jnp.int32, (events, 1), 0)
    live = pos < length
    loads[0].wait()
    normed[...] = (layer_norm(hist[...].astype(F32)) * ln_gain[...]).astype(BF16)

    def project(n):
        loads[n + 1].wait()
        half = 0.5 * jnp.dot(normed[...], wp[n], preferred_element_type=F32)
        return silu_of_twice(half)

    keys = project(0).astype(BF16)
    for h in range(HEADS):
        qkv[h, 0] = keys[:, h * head_size : (h + 1) * head_size]
    values = jnp.where(live, project(1), 0.0).astype(BF16)
    for h in range(HEADS):
        qkv[h, 1] = values[:, h * head_size : (h + 1) * head_size]

    pl.semaphore_wait(barrier, plane - 1 + line - 1)

    kv_copies, q_copies = [], []
    for rel in (3, 2, 1):
        a, b = moved(x, y, rel, swap)
        copy = pltpu.make_async_remote_copy(
            src_ref=qkv.at[head_of(a, b), pl.ds(0, 2)],
            dst_ref=kv.at[rel],
            send_sem=kv_send.at[rel],
            recv_sem=kv_recv.at[rel],
            device_id=in_plane(a, b),
            device_id_type=MESH,
        )
        copy.start()
        kv_copies.append(copy)

    query = project(2).astype(BF16)
    for h in range(HEADS):
        qkv[h, 2] = query[:, h * head_size : (h + 1) * head_size]
    for rel in (3, 2, 1):
        a, b = moved(x, y, rel, swap)
        copy = pltpu.make_async_remote_copy(
            src_ref=qkv.at[head_of(a, b), 2],
            dst_ref=qs.at[rel],
            send_sem=q_send.at[rel],
            recv_sem=q_recv.at[rel],
            device_id=in_plane(a, b),
            device_id_type=MESH,
        )
        copy.start()
        q_copies.append(copy)
    kv[0] = qkv[head, pl.ds(0, 2)]
    qs[0] = qkv[head, 2]

    def pass_on(s, p):
        a, b = moved(x, y, p, ring)
        return pltpu.make_async_remote_copy(
            src_ref=kv.at[s],
            dst_ref=kv.at[p * HEADS + s],
            send_sem=pass_send.at[s, p],
            recv_sem=pass_recv.at[s, p],
            device_id=in_plane(a, b),
            device_id_type=MESH,
        )

    for p in (3, 2, 1):
        pass_on(0, p).start()

    gate[...] = project(3).astype(BF16)
    acc[...] = jnp.zeros_like(acc)

    owned, count = cand_ids.shape
    pool = table.shape[0]
    loads[6].wait()
    loads[7].wait()
    eye = lax.broadcasted_iota(jnp.int32, (count, count), 0) == lax.broadcasted_iota(
        jnp.int32, (count, count), 1
    )
    item = lax.broadcasted_iota(jnp.int32, (count, pool), 1).astype(F32)
    ids = cand_ids[...].astype(F32)
    for r in range(owned):
        column = jnp.sum(jnp.where(eye, ids[r : r + 1, :], 0.0), axis=1, keepdims=True)
        onehot = jnp.where(item == column, 1.0, 0.0).astype(BF16)
        cand[pl.ds(r * count, count)] = jnp.dot(
            onehot, table[...], preferred_element_type=F32
        ).astype(BF16)
    pre[...] = jnp.dot(cand[...], wr[:width], preferred_element_type=F32) + b_rank[...]

    scale = 0.5 * head_size**-0.5

    def time_of(p, s):
        a, b = moved(x, y, p, ring)
        a, b = moved(a, b, s, swap)
        return a * SIDE + b

    def attend(chunk, when, diagonal):
        key, value = kv[chunk, 0], kv[chunk, 1]
        for pair in range(2):
            weights = []
            score = dot_t(qs[pl.ds(2 * pair, 2)].reshape(2 * events, head_size), key)
            for n in range(2):
                now = time_of(0, 2 * pair + n)
                half = score[n * events : (n + 1) * events]
                if diagonal:
                    behind = (
                        lax.broadcasted_iota(jnp.int32, half.shape, 0)
                        - lax.broadcasted_iota(jnp.int32, half.shape, 1)
                        + (now - when) * events
                    )
                    half = jnp.where(behind >= 0, half * scale, 0.0)
                else:
                    half = half * (scale * (now > when).astype(F32))
                weights.append(silu_of_twice(half).astype(BF16))
            weights = jnp.concatenate(weights, axis=0)
            rows = pl.ds(pair * 2 * events, 2 * events)
            acc[rows] += jnp.dot(weights, value, preferred_element_type=F32)

    for copy in q_copies:
        copy.wait_recv()

    @pl.loop(0, HEADS)
    def _(s):
        @pl.when(s > 0)
        def _():
            pltpu.make_async_copy(kv.at[s], kv.at[s], kv_recv.at[s]).wait()
            for p in (3, 2, 1):
                pass_on(s, p).start()

        attend(s, time_of(0, s), True)

    @pl.loop(0, HEADS * (HEADS - 1))
    def _(n):
        s = lax.div(n, HEADS - 1)
        p = 1 + n - s * (HEADS - 1)
        pass_on(s, p).wait_recv()
        attend(p * HEADS + s, time_of(p, s), False)

    back_copies = []
    for rel in (3, 2, 1):
        back[rel] = acc[pl.ds(rel * events, events)].astype(BF16)
        a, b = moved(x, y, rel, swap)
        copy = pltpu.make_async_remote_copy(
            src_ref=back.at[rel],
            dst_ref=att.at[head],
            send_sem=back_send.at[rel],
            recv_sem=back_recv.at[rel],
            device_id=in_plane(a, b),
            device_id_type=MESH,
        )
        copy.start()
        back_copies.append(copy)
    att[head] = acc[pl.ds(0, events)].astype(BF16)
    for copy in back_copies:
        copy.wait_recv()

    attended = jnp.concatenate([att[h] for h in range(HEADS)], axis=1).astype(F32)
    mixed = (layer_norm(attended) * gate[...].astype(F32)).astype(BF16)
    loads[5].wait()
    projected = jnp.dot(mixed, wo[...], preferred_element_type=F32)
    out = (hist[...].astype(F32) + projected).astype(BF16)
    result[...] = out
    store = pltpu.make_async_copy(result, layer_out.at[0], store_sem)
    store.start()
    groups = pool_query.shape[0]
    half = 0.5 * dot_t(pool_query[...], out)
    lane = first_pos + lax.broadcasted_iota(jnp.int32, half.shape, 1)
    pool_w = jnp.where(lane < length, silu_of_twice(half), 0.0).astype(BF16)
    sums = jnp.dot(pool_w, out, preferred_element_type=F32)

    split = width // part.shape[2]
    lanes = part.shape[2]
    for n in range(plane):
        g, c = divmod(n, split)
        part[n] = sums[g : g + 1, c * lanes : (c + 1) * lanes]

    def send_part(k):
        other = lax.rem(t + k, plane)
        return pltpu.make_async_remote_copy(
            src_ref=part.at[other],
            dst_ref=parts.at[t],
            send_sem=sum_sem.at[0],
            recv_sem=sum_sem.at[1],
            device_id={"tm": other},
            device_id_type=MESH,
        )

    def wait_for(buffer, many, sem):
        some = buffer.at[pl.ds(0, many)]
        pltpu.make_async_copy(some, some, sem).wait()

    @pl.loop(1, plane)
    def _(k):
        send_part(k).start()

    parts[t] = part[t]
    wait_for(parts, plane - 1, sum_sem.at[1])
    whole = jnp.sum(parts[...], axis=0).astype(BF16).astype(F32)
    piece[...] = whole
    pieces[user] = whole

    @pl.loop(1, line)
    def _(k):
        other = lax.rem(user + k, line)
        pltpu.make_async_remote_copy(
            src_ref=piece,
            dst_ref=pieces.at[user],
            send_sem=state_sem.at[0],
            recv_sem=state_sem.at[1],
            device_id={"users": lax.div(other, ranks), "mp": lax.rem(other, ranks)},
            device_id_type=MESH,
        ).start()

    wait_for(pieces, line - 1, state_sem.at[1])
    mine = owner * owned + lax.broadcasted_iota(jnp.int32, (owned, line), 0)
    picker = jnp.where(slots[...] == mine, 1.0, 0.0).astype(BF16)
    states = pieces[...].reshape(line, lanes).astype(BF16)
    own_states = jnp.dot(picker, states, preferred_element_type=F32)
    chosen[...] = own_states
    interests[t] = own_states

    @pl.loop(1, plane)
    def _(k):
        pltpu.make_async_remote_copy(
            src_ref=chosen,
            dst_ref=interests.at[t],
            send_sem=pick_sem.at[0],
            recv_sem=pick_sem.at[1],
            device_id={"tm": lax.rem(t + k, plane)},
            device_id_type=MESH,
        ).start()

    wait_for(interests, plane - 1, pick_sem.at[1])

    interest = jnp.concatenate(
        [
            layer_norm(
                jnp.concatenate([interests[g * split + c] for c in range(split)], axis=1)
            )
            for g in range(groups)
        ],
        axis=0,
    ).astype(BF16)
    half = (0.5 * width**-0.5) * dot_t(cand[...], interest)
    row = lax.div(lax.broadcasted_iota(jnp.int32, half.shape, 0), count)
    column = lax.rem(lax.broadcasted_iota(jnp.int32, half.shape, 1), owned)
    attn = jnp.where(row == column, silu_of_twice(half), 0.0)
    context = jnp.dot(
        attn,
        interest.astype(F32),
        precision=lax.Precision.HIGHEST,
        preferred_element_type=F32,
    ).astype(BF16)
    half = 0.5 * (pre[...] + jnp.dot(context, wr[width:], preferred_element_type=F32))
    hidden = silu_of_twice(half)
    own_share = dot_t(w_score[...], hidden, precision=lax.Precision.HIGHEST)
    share[...] = own_share
    shares[mp] = own_share
    for k in range(1, ranks):
        pltpu.make_async_remote_copy(
            src_ref=share,
            dst_ref=shares.at[mp],
            send_sem=share_sem.at[0],
            recv_sem=share_sem.at[1],
            device_id={"mp": lax.rem(mp + k, ranks)},
            device_id_type=MESH,
        ).start()
    wait_for(shares, ranks - 1, share_sem.at[1])
    total = jnp.sum(shares[...], axis=0)
    for r in range(owned):
        scores[r : r + 1, :] = total[:, r * count : (r + 1) * count]

    for copy in kv_copies + q_copies + back_copies:
        copy.wait_send()
    for s in range(HEADS):
        for p in (3, 2, 1):
            pass_on(s, p).wait_send()
    wait_for(parts, plane - 1, sum_sem.at[0])
    wait_for(pieces, line - 1, state_sem.at[0])
    wait_for(interests, plane - 1, pick_sem.at[0])
    wait_for(shares, ranks - 1, share_sem.at[0])
    store.wait()


def solution(mesh):
    plane, owners, ranks = mesh.shape["tm"], mesh.shape["users"], mesh.shape["mp"]
    line = owners * ranks

    def shards(
        history,
        ln_gain,
        w_proj,
        w_out,
        pool_query,
        lengths,
        slots,
        cand_ids,
        item_table,
        w_rank,
        b_rank,
        w_score,
    ):
        _, events, width = history.shape
        head_size = width // HEADS
        groups = pool_query.shape[0]
        owned, count = cand_ids.shape
        lanes = groups * width // plane
        cands = owned * count
        hidden = w_rank.shape[1]
        vmem = pl.BlockSpec(memory_space=pltpu.VMEM)
        smem = pl.BlockSpec(memory_space=pltpu.SMEM)
        hbm = pl.BlockSpec(memory_space=pl.ANY)
        dma = pltpu.SemaphoreType.DMA
        return pl.pallas_call(
            kernel,
            out_shape=(
                jax.ShapeDtypeStruct(history.shape, BF16),
                jax.ShapeDtypeStruct((owned, count), F32),
            ),
            in_specs=[smem, hbm, vmem, hbm, hbm, vmem, vmem, vmem, hbm, hbm, vmem, vmem],
            out_specs=(hbm, vmem),
            scratch_shapes=[
                pltpu.VMEM((events, width), BF16),
                pltpu.VMEM((4, width, width), BF16),
                pltpu.VMEM((width, width), BF16),
                pltpu.VMEM(item_table.shape, BF16),
                pltpu.VMEM(w_rank.shape, BF16),
                pltpu.VMEM((events, width), BF16),
                pltpu.VMEM((events, width), BF16),
                pltpu.VMEM((HEADS, 3, events, head_size), BF16),
                pltpu.VMEM((plane, 2, events, head_size), BF16),
                pltpu.VMEM((HEADS, events, head_size), BF16),
                pltpu.VMEM((HEADS * events, head_size), F32),
                pltpu.VMEM((HEADS, events, head_size), BF16),
                pltpu.VMEM((HEADS, events, head_size), BF16),
                pltpu.VMEM((events, width), BF16),
                pltpu.VMEM((cands, width), BF16),
                pltpu.VMEM((cands, hidden), F32),
                pltpu.VMEM((plane, 1, lanes), F32),
                pltpu.VMEM((plane, 1, lanes), F32),
                pltpu.VMEM((1, lanes), F32),
                pltpu.VMEM((line, 1, lanes), F32),
                pltpu.VMEM((owned, lanes), F32),
                pltpu.VMEM((plane, owned, lanes), F32),
                pltpu.VMEM((1, cands), F32),
                pltpu.VMEM((ranks, 1, cands), F32),
                dma((8,)),
                dma,
                dma((HEADS,)),
                dma((HEADS,)),
                dma((HEADS,)),
                dma((HEADS,)),
                dma((HEADS, HEADS)),
                dma((HEADS, HEADS)),
                dma((HEADS,)),
                dma((HEADS,)),
                dma((2,)),
                dma((2,)),
                dma((2,)),
                dma((2,)),
            ],
            compiler_params=pltpu.CompilerParams(
                collective_id=0, has_side_effects=True, vmem_limit_bytes=48 * 1024 * 1024
            ),
            cost_estimate=pl.CostEstimate(
                flops=4_000_000_000, bytes_accessed=6_000_000, transcendentals=5_000_000
            ),
        )(
            lengths,
            history,
            ln_gain.reshape(1, -1),
            w_proj,
            w_out,
            pool_query,
            slots.reshape(1, -1),
            cand_ids,
            item_table,
            w_rank,
            b_rank.reshape(1, -1),
            w_score.reshape(1, -1),
        )

    placed = (
        P(("users", "mp"), "tm", None),
        P(),
        P(),
        P(),
        P(),
        P(("users", "mp")),
        P(),
        P("users", "tm"),
        P("users", None),
        P(None, "mp"),
        P("mp"),
        P("mp"),
    )
    return jax.shard_map(
        shards,
        mesh=mesh,
        in_specs=placed,
        out_specs=(P(("users", "mp"), "tm", None), P("users", "tm")),
        check_vma=False,
    )
```

```python
import jax
import jax.numpy as jnp
from jax import lax
from jax.experimental import pallas as pl
from jax.experimental.pallas import tpu as pltpu
from jax.sharding import PartitionSpec as P

HEADS = 4
SIDE = 4
EPS = 1e-05
VMEM_BYTES = 64 * 1024 * 1024
MESH = pl.DeviceIdType.MESH
F32 = jnp.float32
BF16 = jnp.bfloat16
ROWS_BY_ROWS = (((1,), (1,)), ((), ()))


def layer_norm(values):
    mean = jnp.mean(values, axis=-1, keepdims=True)
    centred = values - mean
    var = jnp.mean(centred * centred, axis=-1, keepdims=True)
    return centred * lax.rsqrt(var + EPS)


def silu_of_twice(half):
    return half + half * jnp.tanh(half)


def dot_t(a, b, **kw):
    return lax.dot_general(a, b, ROWS_BY_ROWS, preferred_element_type=F32, **kw)


def wait_for(buffer, many, sem):
    some = buffer.at[pl.ds(0, many)]
    pltpu.make_async_copy(some, some, sem).wait()


def history_kernel(
    lengths,
    history,
    ln_gain_hbm,
    w_proj,
    w_out,
    pool_query_hbm,
    layer_out,
    piece,
    hist,
    ln_gain,
    wp,
    wo,
    pool_query,
    normed,
    gate,
    qkv,
    kv,
    qs,
    acc,
    back,
    att,
    result,
    part,
    parts,
    load_sem,
    store_sem,
    kv_send,
    kv_recv,
    q_send,
    q_recv,
    pass_send,
    pass_recv,
    back_send,
    back_recv,
    sum_sem,
):
    events, width = hist.shape
    head_size = width // HEADS
    plane = parts.shape[0]
    t = lax.axis_index("tm")
    mp = lax.axis_index("mp")
    x, y = lax.div(t, SIDE), lax.rem(t, SIDE)
    core = lax.rem(mp, 2)

    def even(v):
        return v + 1 - 2 * lax.rem(v, 2)

    def odd(v):
        return SIDE - 1 - v

    def swap(v):
        return even(v) + core * (odd(v) - even(v))

    def ring(v):
        return odd(v) + core * (even(v) - odd(v))

    def bit(v):
        first = lax.rem(lax.div(v + 1, 2), 2)
        return first + core * (lax.div(v, 2) - first)

    def head_of(a, b):
        return 2 * bit(a) + bit(b)

    def moved(a, b, rel, flip):
        first, second = lax.rem(rel, 2), lax.div(rel, 2)
        return a + first * (flip(a) - a), b + second * (flip(b) - b)

    def in_plane(a, b):
        return {"tm": a * SIDE + b}

    head = head_of(x, y)

    barrier = pltpu.get_barrier_semaphore()

    @pl.loop(1, plane)
    def _(k):
        pl.semaphore_signal(
            barrier, inc=1, device_id={"tm": lax.rem(t + k, plane)}, device_id_type=MESH
        )

    loads = [pltpu.make_async_copy(history.at[0], hist, load_sem.at[0])]
    for n, block in enumerate((3, 1, 2, 0)):
        cols = pl.ds(block * width, width)
        loads.append(pltpu.make_async_copy(w_proj.at[:, cols], wp.at[n], load_sem.at[n + 1]))
    loads.append(pltpu.make_async_copy(w_out, wo, load_sem.at[5]))
    loads.append(pltpu.make_async_copy(ln_gain_hbm, ln_gain, load_sem.at[6]))
    loads.append(pltpu.make_async_copy(pool_query_hbm, pool_query, load_sem.at[7]))
    for load in loads:
        load.start()

    first_pos = t * events
    length = lengths[0]
    pos = first_pos + lax.broadcasted_iota(jnp.int32, (events, 1), 0)
    live = pos < length
    loads[0].wait()
    loads[6].wait()
    normed[...] = (layer_norm(hist[...].astype(F32)) * ln_gain[...]).astype(BF16)

    def project(n):
        loads[n + 1].wait()
        half = 0.5 * jnp.dot(normed[...], wp[n], preferred_element_type=F32)
        return silu_of_twice(half)

    keys = project(0).astype(BF16)
    for h in range(HEADS):
        qkv[h, 0] = keys[:, h * head_size : (h + 1) * head_size]
    values = jnp.where(live, project(1), 0.0).astype(BF16)
    for h in range(HEADS):
        qkv[h, 1] = values[:, h * head_size : (h + 1) * head_size]

    pl.semaphore_wait(barrier, plane - 1)

    kv_copies, q_copies = [], []
    for rel in (3, 2, 1):
        a, b = moved(x, y, rel, swap)
        copy = pltpu.make_async_remote_copy(
            src_ref=qkv.at[head_of(a, b), pl.ds(0, 2)],
            dst_ref=kv.at[rel],
            send_sem=kv_send.at[rel],
            recv_sem=kv_recv.at[rel],
            device_id=in_plane(a, b),
            device_id_type=MESH,
        )
        copy.start()
        kv_copies.append(copy)

    query = project(2).astype(BF16)
    for h in range(HEADS):
        qkv[h, 2] = query[:, h * head_size : (h + 1) * head_size]
    for rel in (3, 2, 1):
        a, b = moved(x, y, rel, swap)
        copy = pltpu.make_async_remote_copy(
            src_ref=qkv.at[head_of(a, b), 2],
            dst_ref=qs.at[rel],
            send_sem=q_send.at[rel],
            recv_sem=q_recv.at[rel],
            device_id=in_plane(a, b),
            device_id_type=MESH,
        )
        copy.start()
        q_copies.append(copy)
    kv[0] = qkv[head, pl.ds(0, 2)]
    qs[0] = qkv[head, 2]

    def pass_on(s, p):
        a, b = moved(x, y, p, ring)
        return pltpu.make_async_remote_copy(
            src_ref=kv.at[s],
            dst_ref=kv.at[p * HEADS + s],
            send_sem=pass_send.at[s, p],
            recv_sem=pass_recv.at[s, p],
            device_id=in_plane(a, b),
            device_id_type=MESH,
        )

    for p in (3, 2, 1):
        pass_on(0, p).start()

    gate[...] = project(3).astype(BF16)
    acc[...] = jnp.zeros_like(acc)

    scale = 0.5 * head_size**-0.5

    def time_of(p, s):
        a, b = moved(x, y, p, ring)
        a, b = moved(a, b, s, swap)
        return a * SIDE + b

    def attend(chunk, when, diagonal):
        key, value = kv[chunk, 0], kv[chunk, 1]
        for pair in range(2):
            weights = []
            score = dot_t(qs[pl.ds(2 * pair, 2)].reshape(2 * events, head_size), key)
            for n in range(2):
                now = time_of(0, 2 * pair + n)
                half = score[n * events : (n + 1) * events]
                if diagonal:
                    behind = (
                        lax.broadcasted_iota(jnp.int32, half.shape, 0)
                        - lax.broadcasted_iota(jnp.int32, half.shape, 1)
                        + (now - when) * events
                    )
                    half = jnp.where(behind >= 0, half * scale, 0.0)
                else:
                    half = half * (scale * (now > when).astype(F32))
                weights.append(silu_of_twice(half).astype(BF16))
            weights = jnp.concatenate(weights, axis=0)
            rows = pl.ds(pair * 2 * events, 2 * events)
            acc[rows] += jnp.dot(weights, value, preferred_element_type=F32)

    for copy in q_copies:
        copy.wait_recv()

    @pl.loop(0, HEADS)
    def _(s):
        @pl.when(s > 0)
        def _():
            pltpu.make_async_copy(kv.at[s], kv.at[s], kv_recv.at[s]).wait()
            for p in (3, 2, 1):
                pass_on(s, p).start()

        attend(s, time_of(0, s), True)

    @pl.loop(0, HEADS * (HEADS - 1))
    def _(n):
        s = lax.div(n, HEADS - 1)
        p = 1 + n - s * (HEADS - 1)
        pass_on(s, p).wait_recv()
        attend(p * HEADS + s, time_of(p, s), False)

    back_copies = []
    for rel in (3, 2, 1):
        back[rel] = acc[pl.ds(rel * events, events)].astype(BF16)
        a, b = moved(x, y, rel, swap)
        copy = pltpu.make_async_remote_copy(
            src_ref=back.at[rel],
            dst_ref=att.at[head],
            send_sem=back_send.at[rel],
            recv_sem=back_recv.at[rel],
            device_id=in_plane(a, b),
            device_id_type=MESH,
        )
        copy.start()
        back_copies.append(copy)
    att[head] = acc[pl.ds(0, events)].astype(BF16)
    for copy in back_copies:
        copy.wait_recv()

    attended = jnp.concatenate([att[h] for h in range(HEADS)], axis=1).astype(F32)
    mixed = (layer_norm(attended) * gate[...].astype(F32)).astype(BF16)
    loads[5].wait()
    projected = jnp.dot(mixed, wo[...], preferred_element_type=F32)
    out = (hist[...].astype(F32) + projected).astype(BF16)
    result[...] = out
    store = pltpu.make_async_copy(result, layer_out.at[0], store_sem)
    store.start()
    loads[7].wait()
    half = 0.5 * dot_t(pool_query[...], out)
    lane = first_pos + lax.broadcasted_iota(jnp.int32, half.shape, 1)
    pool_w = jnp.where(lane < length, silu_of_twice(half), 0.0).astype(BF16)
    sums = jnp.dot(pool_w, out, preferred_element_type=F32)

    split = width // part.shape[2]
    lanes = part.shape[2]
    for n in range(plane):
        g, c = divmod(n, split)
        part[n] = sums[g : g + 1, c * lanes : (c + 1) * lanes]

    def send_part(k):
        other = lax.rem(t + k, plane)
        return pltpu.make_async_remote_copy(
            src_ref=part.at[other],
            dst_ref=parts.at[t],
            send_sem=sum_sem.at[0],
            recv_sem=sum_sem.at[1],
            device_id={"tm": other},
            device_id_type=MESH,
        )

    @pl.loop(1, plane)
    def _(k):
        send_part(k).start()

    parts[t] = part[t]
    wait_for(parts, plane - 1, sum_sem.at[1])
    whole = jnp.sum(parts[...], axis=0).astype(BF16).astype(F32)
    piece[...] = whole

    for copy in kv_copies + q_copies + back_copies:
        copy.wait_send()
    for s in range(HEADS):
        for p in (3, 2, 1):
            pass_on(s, p).wait_send()
    wait_for(parts, plane - 1, sum_sem.at[0])
    store.wait()


def ranker_kernel(
    piece,
    slots_hbm,
    cand_ids_hbm,
    item_table,
    w_rank,
    b_rank_hbm,
    w_score_hbm,
    scores,
    slots,
    cand_ids,
    table,
    wr,
    b_rank,
    w_score,
    cand,
    pre,
    pieces,
    chosen,
    interests,
    share,
    shares,
    load_sem,
    state_sem,
    pick_sem,
    share_sem,
):
    plane, line, ranks = interests.shape[0], pieces.shape[0], shares.shape[0]
    lanes, width = piece.shape[1], table.shape[1]
    split = width // lanes
    groups = plane // split
    t = lax.axis_index("tm")
    owner = lax.axis_index("users")
    mp = lax.axis_index("mp")
    user = owner * ranks + mp

    barrier = pltpu.get_barrier_semaphore()

    @pl.loop(1, line)
    def _(k):
        other = lax.rem(user + k, line)
        pl.semaphore_signal(
            barrier,
            inc=1,
            device_id={"users": lax.div(other, ranks), "mp": lax.rem(other, ranks)},
            device_id_type=MESH,
        )

    @pl.loop(1, plane)
    def _(k):
        pl.semaphore_signal(
            barrier, inc=1, device_id={"tm": lax.rem(t + k, plane)}, device_id_type=MESH
        )

    loads = [
        pltpu.make_async_copy(src, dst, load_sem.at[n])
        for n, (src, dst) in enumerate(
            (
                (cand_ids_hbm, cand_ids),
                (item_table, table),
                (w_rank, wr),
                (slots_hbm, slots),
                (b_rank_hbm, b_rank),
                (w_score_hbm, w_score),
            )
        )
    ]
    for load in loads:
        load.start()
    for load in loads:
        load.wait()

    owned, count = cand_ids.shape
    pool = table.shape[0]
    eye = lax.broadcasted_iota(jnp.int32, (count, count), 0) == lax.broadcasted_iota(
        jnp.int32, (count, count), 1
    )
    item = lax.broadcasted_iota(jnp.int32, (count, pool), 1).astype(F32)
    ids = cand_ids[...].astype(F32)
    for r in range(owned):
        column = jnp.sum(jnp.where(eye, ids[r : r + 1, :], 0.0), axis=1, keepdims=True)
        onehot = jnp.where(item == column, 1.0, 0.0).astype(BF16)
        cand[pl.ds(r * count, count)] = jnp.dot(
            onehot, table[...], preferred_element_type=F32
        ).astype(BF16)
    pre[...] = jnp.dot(cand[...], wr[:width], preferred_element_type=F32) + b_rank[...]

    pl.semaphore_wait(barrier, plane - 1 + line - 1)

    pieces[user] = piece[...]

    @pl.loop(1, line)
    def _(k):
        other = lax.rem(user + k, line)
        pltpu.make_async_remote_copy(
            src_ref=piece,
            dst_ref=pieces.at[user],
            send_sem=state_sem.at[0],
            recv_sem=state_sem.at[1],
            device_id={"users": lax.div(other, ranks), "mp": lax.rem(other, ranks)},
            device_id_type=MESH,
        ).start()

    wait_for(pieces, line - 1, state_sem.at[1])
    mine = owner * owned + lax.broadcasted_iota(jnp.int32, (owned, line), 0)
    picker = jnp.where(slots[...] == mine, 1.0, 0.0).astype(BF16)
    states = pieces[...].reshape(line, lanes).astype(BF16)
    own_states = jnp.dot(picker, states, preferred_element_type=F32)
    chosen[...] = own_states
    interests[t] = own_states

    @pl.loop(1, plane)
    def _(k):
        pltpu.make_async_remote_copy(
            src_ref=chosen,
            dst_ref=interests.at[t],
            send_sem=pick_sem.at[0],
            recv_sem=pick_sem.at[1],
            device_id={"tm": lax.rem(t + k, plane)},
            device_id_type=MESH,
        ).start()

    wait_for(interests, plane - 1, pick_sem.at[1])

    interest = jnp.concatenate(
        [
            layer_norm(
                jnp.concatenate([interests[g * split + c] for c in range(split)], axis=1)
            )
            for g in range(groups)
        ],
        axis=0,
    ).astype(BF16)
    half = (0.5 * width**-0.5) * dot_t(cand[...], interest)
    row = lax.div(lax.broadcasted_iota(jnp.int32, half.shape, 0), count)
    column = lax.rem(lax.broadcasted_iota(jnp.int32, half.shape, 1), owned)
    attn = jnp.where(row == column, silu_of_twice(half), 0.0)
    context = jnp.dot(
        attn,
        interest.astype(F32),
        precision=lax.Precision.HIGHEST,
        preferred_element_type=F32,
    ).astype(BF16)
    half = 0.5 * (pre[...] + jnp.dot(context, wr[width:], preferred_element_type=F32))
    hidden = silu_of_twice(half)
    own_share = dot_t(w_score[...], hidden, precision=lax.Precision.HIGHEST)
    share[...] = own_share
    shares[mp] = own_share
    for k in range(1, ranks):
        pltpu.make_async_remote_copy(
            src_ref=share,
            dst_ref=shares.at[mp],
            send_sem=share_sem.at[0],
            recv_sem=share_sem.at[1],
            device_id={"mp": lax.rem(mp + k, ranks)},
            device_id_type=MESH,
        ).start()
    wait_for(shares, ranks - 1, share_sem.at[1])
    total = jnp.sum(shares[...], axis=0)
    for r in range(owned):
        scores[r : r + 1, :] = total[:, r * count : (r + 1) * count]

    wait_for(pieces, line - 1, state_sem.at[0])
    wait_for(interests, plane - 1, pick_sem.at[0])
    wait_for(shares, ranks - 1, share_sem.at[0])


def solution(mesh):
    plane, owners, ranks = mesh.shape["tm"], mesh.shape["users"], mesh.shape["mp"]
    line = owners * ranks

    def shards(
        history,
        ln_gain,
        w_proj,
        w_out,
        pool_query,
        lengths,
        slots,
        cand_ids,
        item_table,
        w_rank,
        b_rank,
        w_score,
    ):
        _, events, width = history.shape
        head_size = width // HEADS
        groups = pool_query.shape[0]
        owned, count = cand_ids.shape
        lanes = groups * width // plane
        cands = owned * count
        hidden = w_rank.shape[1]
        vmem = pl.BlockSpec(memory_space=pltpu.VMEM)
        smem = pl.BlockSpec(memory_space=pltpu.SMEM)
        hbm = pl.BlockSpec(memory_space=pltpu.HBM)
        dma = pltpu.SemaphoreType.DMA
        layer_out, piece = pl.pallas_call(
            history_kernel,
            out_shape=(
                jax.ShapeDtypeStruct(history.shape, BF16),
                jax.ShapeDtypeStruct((1, lanes), F32),
            ),
            in_specs=[smem, hbm, hbm, hbm, hbm, hbm],
            out_specs=(hbm, vmem),
            scratch_shapes=[
                pltpu.VMEM((events, width), BF16),
                pltpu.VMEM((1, width), F32),
                pltpu.VMEM((4, width, width), BF16),
                pltpu.VMEM((width, width), BF16),
                pltpu.VMEM(pool_query.shape, BF16),
                pltpu.VMEM((events, width), BF16),
                pltpu.VMEM((events, width), BF16),
                pltpu.VMEM((HEADS, 3, events, head_size), BF16),
                pltpu.VMEM((plane, 2, events, head_size), BF16),
                pltpu.VMEM((HEADS, events, head_size), BF16),
                pltpu.VMEM((HEADS * events, head_size), F32),
                pltpu.VMEM((HEADS, events, head_size), BF16),
                pltpu.VMEM((HEADS, events, head_size), BF16),
                pltpu.VMEM((events, width), BF16),
                pltpu.VMEM((plane, 1, lanes), F32),
                pltpu.VMEM((plane, 1, lanes), F32),
                dma((8,)),
                dma,
                dma((HEADS,)),
                dma((HEADS,)),
                dma((HEADS,)),
                dma((HEADS,)),
                dma((HEADS, HEADS)),
                dma((HEADS, HEADS)),
                dma((HEADS,)),
                dma((HEADS,)),
                dma((2,)),
            ],
            compiler_params=pltpu.CompilerParams(
                collective_id=0, has_side_effects=True, vmem_limit_bytes=VMEM_BYTES
            ),
            name="history",
        )(lengths, history, ln_gain.reshape(1, -1), w_proj, w_out, pool_query)
        scores = pl.pallas_call(
            ranker_kernel,
            out_shape=jax.ShapeDtypeStruct((owned, count), F32),
            in_specs=[vmem, hbm, hbm, hbm, hbm, hbm, hbm],
            out_specs=vmem,
            scratch_shapes=[
                pltpu.VMEM((1, line), jnp.int32),
                pltpu.VMEM((owned, count), jnp.int32),
                pltpu.VMEM(item_table.shape, BF16),
                pltpu.VMEM(w_rank.shape, BF16),
                pltpu.VMEM((1, hidden), F32),
                pltpu.VMEM((1, hidden), F32),
                pltpu.VMEM((cands, width), BF16),
                pltpu.VMEM((cands, hidden), F32),
                pltpu.VMEM((line, 1, lanes), F32),
                pltpu.VMEM((owned, lanes), F32),
                pltpu.VMEM((plane, owned, lanes), F32),
                pltpu.VMEM((1, cands), F32),
                pltpu.VMEM((ranks, 1, cands), F32),
                dma((6,)),
                dma((2,)),
                dma((2,)),
                dma((2,)),
            ],
            compiler_params=pltpu.CompilerParams(
                collective_id=1, has_side_effects=True, vmem_limit_bytes=VMEM_BYTES
            ),
            name="ranker",
        )(
            piece,
            slots.reshape(1, -1),
            cand_ids,
            item_table,
            w_rank,
            b_rank.reshape(1, -1),
            w_score.reshape(1, -1),
        )
        return layer_out, scores

    placed = (
        P(("users", "mp"), "tm", None),
        P(),
        P(),
        P(),
        P(),
        P(("users", "mp")),
        P(),
        P("users", "tm"),
        P("users", None),
        P(None, "mp"),
        P("mp"),
        P("mp"),
    )
    return jax.shard_map(
        shards,
        mesh=mesh,
        in_specs=placed,
        out_specs=(P(("users", "mp"), "tm", None), P("users", "tm")),
        check_vma=False,
    )
```

```python
import jax
import jax.numpy as jnp
from jax import lax
from jax.experimental import pallas as pl
from jax.experimental.pallas import tpu as pltpu
from jax.sharding import PartitionSpec as P

HEADS = 4
SIDE = 4
EPS = 1e-05
VMEM_BYTES = 64 * 1024 * 1024
MESH = pl.DeviceIdType.MESH
STEPS = sorted(
    ((a, b) for a in range(SIDE) for b in range(SIDE) if a or b),
    key=lambda step: -sum(min(n, SIDE - n) for n in step),
)
F32 = jnp.float32
BF16 = jnp.bfloat16
ROWS_BY_ROWS = (((1,), (1,)), ((), ()))


def layer_norm(values):
    mean = jnp.mean(values, axis=-1, keepdims=True)
    centred = values - mean
    var = jnp.mean(centred * centred, axis=-1, keepdims=True)
    return centred * lax.rsqrt(var + EPS)


def silu_of_twice(half):
    return half + half * jnp.tanh(half)


def dot_t(a, b, **kw):
    return lax.dot_general(a, b, ROWS_BY_ROWS, preferred_element_type=F32, **kw)


def kernel(
    lengths,
    history,
    ln_gain_hbm,
    w_proj,
    w_out,
    pool_query_hbm,
    slots_hbm,
    cand_ids_hbm,
    item_table,
    w_rank,
    b_rank_hbm,
    w_score_hbm,
    layer_out,
    scores,
    hist,
    ln_gain,
    pool_query,
    slots,
    cand_ids,
    b_rank,
    w_score,
    wp,
    wo,
    table,
    wr,
    normed,
    gate,
    qkv,
    kv,
    qs,
    acc,
    back,
    att,
    cand,
    pre,
    part,
    parts,
    piece,
    pieces,
    chosen,
    interests,
    share,
    shares,
    load_sem,
    kv_send,
    kv_recv,
    q_send,
    q_recv,
    pass_send,
    pass_recv,
    half_send,
    half_recv,
    back_send,
    back_recv,
    sum_sem,
    state_sem,
    pick_sem,
    share_sem,
):
    events, width = hist.shape
    head_size = width // HEADS
    plane, line, ranks = parts.shape[0], pieces.shape[0], shares.shape[0]
    t = lax.axis_index("tm")
    owner = lax.axis_index("users")
    mp = lax.axis_index("mp")
    user = owner * ranks + mp
    x, y = lax.div(t, SIDE), lax.rem(t, SIDE)
    core = lax.rem(mp, 2)

    def even(v):
        return v + 1 - 2 * lax.rem(v, 2)

    def odd(v):
        return SIDE - 1 - v

    def swap(v):
        return even(v) + core * (odd(v) - even(v))

    def ring(v):
        return odd(v) + core * (even(v) - odd(v))

    def bit(v):
        first = lax.rem(lax.div(v + 1, 2), 2)
        return first + core * (lax.div(v, 2) - first)

    def head_of(a, b):
        return 2 * bit(a) + bit(b)

    def moved(a, b, rel, flip):
        first, second = lax.rem(rel, 2), lax.div(rel, 2)
        return a + first * (flip(a) - a), b + second * (flip(b) - b)

    def in_plane(a, b):
        return {"tm": a * SIDE + b}

    head = head_of(x, y)

    barrier = pltpu.get_barrier_semaphore()

    def plane_device(step):
        a, b = step
        return lax.rem(x + a, SIDE) * SIDE + lax.rem(y + b, SIDE)

    height = line // 2
    low = height // 2

    def line_device(k):
        j = lax.div(k, 2)
        far = lax.div(j + 1, 2)
        chip = low + far * (1 - 2 * lax.rem(j, 2)) + lax.div(mp, 2) * low + owner
        chip = lax.rem(chip, height)
        other = lax.rem(core + k + 1, 2)
        return {"users": lax.rem(chip, low), "mp": 2 * lax.div(chip, low) + other}

    @pl.loop(0, line - 1)
    def _(k):
        pl.semaphore_signal(barrier, inc=1, device_id=line_device(k), device_id_type=MESH)

    for step in STEPS:
        pl.semaphore_signal(
            barrier, inc=1, device_id={"tm": plane_device(step)}, device_id_type=MESH
        )

    loads = [pltpu.make_async_copy(history.at[0], hist, load_sem.at[0])]
    for n, block in enumerate((3, 1, 2, 0)):
        cols = pl.ds(block * width, width)
        loads.append(pltpu.make_async_copy(w_proj.at[:, cols], wp.at[n], load_sem.at[n + 1]))
    rest = (
        (ln_gain_hbm, ln_gain),
        (pool_query_hbm, pool_query),
        (slots_hbm, slots),
        (cand_ids_hbm, cand_ids),
        (b_rank_hbm, b_rank),
        (w_score_hbm, w_score),
        (w_out, wo),
        (item_table, table),
        (w_rank, wr),
    )
    for n, (src, dst) in enumerate(rest):
        loads.append(pltpu.make_async_copy(src, dst, load_sem.at[5 + n]))
    loads[0].start()
    loads[5].start()
    for load in loads[1:5] + loads[6:]:
        load.start()

    first_pos = t * events
    length = lengths[0]
    pos = first_pos + lax.broadcasted_iota(jnp.int32, (events, 1), 0)
    live = pos < length
    loads[0].wait()
    loads[5].wait()
    normed[...] = (layer_norm(hist[...].astype(F32)) * ln_gain[...]).astype(BF16)

    def project(n):
        loads[n + 1].wait()
        half = 0.5 * jnp.dot(normed[...], wp[n], preferred_element_type=F32)
        return silu_of_twice(half)

    keys = project(0).astype(BF16)
    for h in range(HEADS):
        qkv[h, 0] = keys[:, h * head_size : (h + 1) * head_size]
    values = jnp.where(live, project(1), 0.0).astype(BF16)
    for h in range(HEADS):
        qkv[h, 1] = values[:, h * head_size : (h + 1) * head_size]

    pl.semaphore_wait(barrier, plane - 1 + line - 1)

    kv_copies, q_copies = [], []
    for rel in (3, 2, 1):
        a, b = moved(x, y, rel, swap)
        copy = pltpu.make_async_remote_copy(
            src_ref=qkv.at[head_of(a, b), pl.ds(0, 2)],
            dst_ref=kv.at[rel],
            send_sem=kv_send.at[rel],
            recv_sem=kv_recv.at[rel],
            device_id=in_plane(a, b),
            device_id_type=MESH,
        )
        copy.start()
        kv_copies.append(copy)

    query = project(2).astype(BF16)
    for h in range(HEADS):
        qkv[h, 2] = query[:, h * head_size : (h + 1) * head_size]
    for rel in (3, 2, 1):
        a, b = moved(x, y, rel, swap)
        copy = pltpu.make_async_remote_copy(
            src_ref=qkv.at[head_of(a, b), 2],
            dst_ref=qs.at[rel],
            send_sem=q_send.at[rel],
            recv_sem=q_recv.at[rel],
            device_id=in_plane(a, b),
            device_id_type=MESH,
        )
        copy.start()
        q_copies.append(copy)
    kv[0] = qkv[head, pl.ds(0, 2)]
    qs[0] = qkv[head, 2]

    def pass_on(s, p):
        a, b = moved(x, y, p, ring)
        return pltpu.make_async_remote_copy(
            src_ref=kv.at[s],
            dst_ref=kv.at[p * HEADS + s],
            send_sem=pass_send.at[s, p],
            recv_sem=pass_recv.at[s, p],
            device_id=in_plane(a, b),
            device_id_type=MESH,
        )

    def pass_half(s, p):
        a, b = moved(x, y, 3 - p, ring)
        return pltpu.make_async_remote_copy(
            src_ref=kv.at[p * HEADS + s, p - 1],
            dst_ref=kv.at[3 * HEADS + s, p - 1],
            send_sem=half_send.at[s, p],
            recv_sem=half_recv.at[s, p],
            device_id=in_plane(a, b),
            device_id_type=MESH,
        )

    for p in (1, 2):
        pass_on(0, p).start()

    gate[...] = project(3).astype(BF16)
    acc[...] = jnp.zeros_like(acc)

    owned, count = cand_ids.shape
    pool = table.shape[0]
    for load in loads[6:]:
        load.wait()

    @pl.loop(0, owned)
    def _(r):
        @pl.when(r > 0)
        def _():
            pltpu.make_async_copy(kv.at[r], kv.at[r], kv_recv.at[r]).wait()
            for p in (1, 2):
                pass_on(r, p).start()

        eye = lax.broadcasted_iota(jnp.int32, (count, count), 0) == lax.broadcasted_iota(
            jnp.int32, (count, count), 1
        )
        item = lax.broadcasted_iota(jnp.int32, (count, pool), 1).astype(F32)
        ids = cand_ids[pl.ds(r, 1), :].astype(F32)
        column = jnp.sum(jnp.where(eye, ids, 0.0), axis=1, keepdims=True)
        onehot = jnp.where(item == column, 1.0, 0.0).astype(BF16)
        cand[pl.ds(r * count, count)] = jnp.dot(
            onehot, table[...], preferred_element_type=F32
        ).astype(BF16)

    pre[...] = jnp.dot(cand[...], wr[:width], preferred_element_type=F32) + b_rank[...]

    scale = 0.5 * head_size**-0.5

    def time_of(p, s):
        a, b = moved(x, y, p, ring)
        a, b = moved(a, b, s, swap)
        return a * SIDE + b

    def attend(chunk, when, diagonal):
        key, value = kv[chunk, 0], kv[chunk, 1]
        for pair in range(2):
            weights = []
            score = dot_t(qs[pl.ds(2 * pair, 2)].reshape(2 * events, head_size), key)
            for n in range(2):
                now = time_of(0, 2 * pair + n)
                half = score[n * events : (n + 1) * events]
                if diagonal:
                    behind = (
                        lax.broadcasted_iota(jnp.int32, half.shape, 0)
                        - lax.broadcasted_iota(jnp.int32, half.shape, 1)
                        + (now - when) * events
                    )
                    half = jnp.where(behind >= 0, half * scale, 0.0)
                else:
                    half = half * (scale * (now > when).astype(F32))
                weights.append(silu_of_twice(half).astype(BF16))
            weights = jnp.concatenate(weights, axis=0)
            rows = pl.ds(pair * 2 * events, 2 * events)
            acc[rows] += jnp.dot(weights, value, preferred_element_type=F32)

    for copy in q_copies:
        copy.wait_recv()

    @pl.loop(0, HEADS)
    def _(s):
        attend(s, time_of(0, s), True)

    @pl.loop(0, HEADS + 1)
    def _(s):
        @pl.when(s < HEADS)
        def _():
            @pl.loop(1, 3)
            def _(p):
                pass_on(s, p).wait_recv()
                pass_half(s, p).start()
                attend(p * HEADS + s, time_of(p, s), False)

        @pl.when(s > 0)
        def _():
            for p in (1, 2):
                pass_half(s - 1, p).wait_recv()
            attend(3 * HEADS + s - 1, time_of(3, s - 1), False)

    back_copies = []
    for rel in (3, 2, 1):
        back[rel] = acc[pl.ds(rel * events, events)].astype(BF16)
        a, b = moved(x, y, rel, swap)
        copy = pltpu.make_async_remote_copy(
            src_ref=back.at[rel],
            dst_ref=att.at[head],
            send_sem=back_send.at[rel],
            recv_sem=back_recv.at[rel],
            device_id=in_plane(a, b),
            device_id_type=MESH,
        )
        copy.start()
        back_copies.append(copy)
    att[head] = acc[pl.ds(0, events)].astype(BF16)
    for copy in back_copies:
        copy.wait_recv()

    attended = jnp.concatenate([att[h] for h in range(HEADS)], axis=1).astype(F32)
    mixed = (layer_norm(attended) * gate[...].astype(F32)).astype(BF16)
    projected = jnp.dot(mixed, wo[...], preferred_element_type=F32)
    out = (hist[...].astype(F32) + projected).astype(BF16)
    layer_out[0] = out
    groups = pool_query.shape[0]
    half = 0.5 * dot_t(pool_query[...], out)
    lane = first_pos + lax.broadcasted_iota(jnp.int32, half.shape, 1)
    pool_w = jnp.where(lane < length, silu_of_twice(half), 0.0).astype(BF16)
    sums = jnp.dot(pool_w, out, preferred_element_type=F32)

    split = width // part.shape[2]
    lanes = part.shape[2]
    for n in range(plane):
        g, c = divmod(n, split)
        part[n] = sums[g : g + 1, c * lanes : (c + 1) * lanes]

    def wait_for(buffer, many, sem):
        some = buffer.at[pl.ds(0, many)]
        pltpu.make_async_copy(some, some, sem).wait()

    for step in STEPS:
        other = plane_device(step)
        pltpu.make_async_remote_copy(
            src_ref=part.at[other],
            dst_ref=parts.at[t],
            send_sem=sum_sem.at[0],
            recv_sem=sum_sem.at[1],
            device_id={"tm": other},
            device_id_type=MESH,
        ).start()

    parts[t] = part[t]
    wait_for(parts, plane - 1, sum_sem.at[1])
    whole = jnp.sum(parts[...], axis=0).astype(BF16).astype(F32)
    piece[...] = whole
    pieces[user] = whole

    @pl.loop(0, line - 1)
    def _(k):
        pltpu.make_async_remote_copy(
            src_ref=piece,
            dst_ref=pieces.at[user],
            send_sem=state_sem.at[0],
            recv_sem=state_sem.at[1],
            device_id=line_device(k),
            device_id_type=MESH,
        ).start()

    wait_for(pieces, line - 1, state_sem.at[1])
    mine = owner * owned + lax.broadcasted_iota(jnp.int32, (owned, line), 0)
    picker = jnp.where(slots[...] == mine, 1.0, 0.0).astype(BF16)
    states = pieces[...].reshape(line, lanes).astype(BF16)
    own_states = jnp.dot(picker, states, preferred_element_type=F32)
    chosen[...] = own_states
    interests[t] = own_states

    for step in STEPS:
        pltpu.make_async_remote_copy(
            src_ref=chosen,
            dst_ref=interests.at[t],
            send_sem=pick_sem.at[0],
            recv_sem=pick_sem.at[1],
            device_id={"tm": plane_device(step)},
            device_id_type=MESH,
        ).start()

    wait_for(interests, plane - 1, pick_sem.at[1])

    interest = jnp.concatenate(
        [
            layer_norm(
                jnp.concatenate([interests[g * split + c] for c in range(split)], axis=1)
            )
            for g in range(groups)
        ],
        axis=0,
    ).astype(BF16)
    half = (0.5 * width**-0.5) * dot_t(cand[...], interest)
    row = lax.div(lax.broadcasted_iota(jnp.int32, half.shape, 0), count)
    column = lax.rem(lax.broadcasted_iota(jnp.int32, half.shape, 1), owned)
    attn = jnp.where(row == column, silu_of_twice(half), 0.0)
    context = jnp.dot(
        attn,
        interest.astype(F32),
        precision=lax.Precision.HIGHEST,
        preferred_element_type=F32,
    ).astype(BF16)
    half = 0.5 * (pre[...] + jnp.dot(context, wr[width:], preferred_element_type=F32))
    hidden = silu_of_twice(half)
    own_share = dot_t(w_score[...], hidden, precision=lax.Precision.HIGHEST)
    share[...] = own_share
    shares[mp] = own_share
    for k in range(1, ranks):
        pltpu.make_async_remote_copy(
            src_ref=share,
            dst_ref=shares.at[mp],
            send_sem=share_sem.at[0],
            recv_sem=share_sem.at[1],
            device_id={"mp": lax.rem(mp + k, ranks)},
            device_id_type=MESH,
        ).start()
    wait_for(shares, ranks - 1, share_sem.at[1])
    total = jnp.sum(shares[...], axis=0)
    for r in range(owned):
        scores[r : r + 1, :] = total[:, r * count : (r + 1) * count]

    for copy in kv_copies + q_copies + back_copies:
        copy.wait_send()
    for s in range(HEADS):
        for p in (1, 2):
            pass_on(s, p).wait_send()
            pass_half(s, p).wait_send()
    wait_for(parts, plane - 1, sum_sem.at[0])
    wait_for(pieces, line - 1, state_sem.at[0])
    wait_for(interests, plane - 1, pick_sem.at[0])
    wait_for(shares, ranks - 1, share_sem.at[0])


def solution(mesh):
    plane, owners, ranks = mesh.shape["tm"], mesh.shape["users"], mesh.shape["mp"]
    line = owners * ranks

    def shards(
        history,
        ln_gain,
        w_proj,
        w_out,
        pool_query,
        lengths,
        slots,
        cand_ids,
        item_table,
        w_rank,
        b_rank,
        w_score,
    ):
        _, events, width = history.shape
        head_size = width // HEADS
        groups = pool_query.shape[0]
        owned, count = cand_ids.shape
        lanes = groups * width // plane
        cands = owned * count
        hidden = w_rank.shape[1]
        vmem = pl.BlockSpec(memory_space=pltpu.VMEM)
        smem = pl.BlockSpec(memory_space=pltpu.SMEM)
        hbm = pl.BlockSpec(memory_space=pltpu.HBM)
        dma = pltpu.SemaphoreType.DMA
        return pl.pallas_call(
            kernel,
            out_shape=(
                jax.ShapeDtypeStruct(history.shape, BF16),
                jax.ShapeDtypeStruct((owned, count), F32),
            ),
            in_specs=[smem] + [hbm] * 11,
            out_specs=(vmem, vmem),
            scratch_shapes=[
                pltpu.VMEM((events, width), BF16),
                pltpu.VMEM((1, width), F32),
                pltpu.VMEM(pool_query.shape, BF16),
                pltpu.VMEM((1, line), jnp.int32),
                pltpu.VMEM((owned, count), jnp.int32),
                pltpu.VMEM((1, hidden), F32),
                pltpu.VMEM((1, hidden), F32),
                pltpu.VMEM((4, width, width), BF16),
                pltpu.VMEM((width, width), BF16),
                pltpu.VMEM(item_table.shape, BF16),
                pltpu.VMEM(w_rank.shape, BF16),
                pltpu.VMEM((events, width), BF16),
                pltpu.VMEM((events, width), BF16),
                pltpu.VMEM((HEADS, 3, events, head_size), BF16),
                pltpu.VMEM((plane, 2, events, head_size), BF16),
                pltpu.VMEM((HEADS, events, head_size), BF16),
                pltpu.VMEM((HEADS * events, head_size), F32),
                pltpu.VMEM((HEADS, events, head_size), BF16),
                pltpu.VMEM((HEADS, events, head_size), BF16),
                pltpu.VMEM((cands, width), BF16),
                pltpu.VMEM((cands, hidden), F32),
                pltpu.VMEM((plane, 1, lanes), F32),
                pltpu.VMEM((plane, 1, lanes), F32),
                pltpu.VMEM((1, lanes), F32),
                pltpu.VMEM((line, 1, lanes), F32),
                pltpu.VMEM((owned, lanes), F32),
                pltpu.VMEM((plane, owned, lanes), F32),
                pltpu.VMEM((1, cands), F32),
                pltpu.VMEM((ranks, 1, cands), F32),
                dma((14,)),
                dma((HEADS,)),
                dma((HEADS,)),
                dma((HEADS,)),
                dma((HEADS,)),
                dma((HEADS, HEADS)),
                dma((HEADS, HEADS)),
                dma((HEADS, HEADS)),
                dma((HEADS, HEADS)),
                dma((HEADS,)),
                dma((HEADS,)),
                dma((2,)),
                dma((2,)),
                dma((2,)),
                dma((2,)),
            ],
            compiler_params=pltpu.CompilerParams(
                collective_id=0, has_side_effects=True, vmem_limit_bytes=VMEM_BYTES
            ),
            cost_estimate=pl.CostEstimate(
                flops=4_000_000_000, bytes_accessed=6_000_000, transcendentals=5_000_000
            ),
        )(
            lengths,
            history,
            ln_gain.reshape(1, -1),
            w_proj,
            w_out,
            pool_query,
            slots.reshape(1, -1),
            cand_ids,
            item_table,
            w_rank,
            b_rank.reshape(1, -1),
            w_score.reshape(1, -1),
        )

    placed = (
        P(("users", "mp"), "tm", None),
        P(),
        P(),
        P(),
        P(),
        P(("users", "mp")),
        P(),
        P("users", "tm"),
        P("users", None),
        P(None, "mp"),
        P("mp"),
        P("mp"),
    )
    return jax.shard_map(
        shards,
        mesh=mesh,
        in_specs=placed,
        out_specs=(P(("users", "mp"), "tm", None), P("users", "tm")),
        check_vma=False,
    )
```

```python
import jax
import jax.numpy as jnp
from jax import lax
from jax.experimental import pallas as pl
from jax.experimental.pallas import tpu as pltpu
from jax.sharding import PartitionSpec as P

HEADS = 4
SIDE = 4
EPS = 1e-05
VMEM_BYTES = 64 * 1024 * 1024
MESH = pl.DeviceIdType.MESH
STEPS = sorted(
    ((a, b) for a in range(SIDE) for b in range(SIDE) if a or b),
    key=lambda step: -sum(min(n, SIDE - n) for n in step),
)
F32 = jnp.float32
BF16 = jnp.bfloat16
ROWS_BY_ROWS = (((1,), (1,)), ((), ()))


def layer_norm(values):
    mean = jnp.mean(values, axis=-1, keepdims=True)
    centred = values - mean
    var = jnp.mean(centred * centred, axis=-1, keepdims=True)
    return centred * lax.rsqrt(var + EPS)


def silu_of_twice(half):
    return half + half * jnp.tanh(half)


def dot_t(a, b, **kw):
    return lax.dot_general(a, b, ROWS_BY_ROWS, preferred_element_type=F32, **kw)


def kernel(
    lengths,
    history,
    ln_gain_hbm,
    w_proj,
    w_out,
    pool_query_hbm,
    slots_hbm,
    cand_ids_hbm,
    item_table,
    w_rank,
    b_rank_hbm,
    w_score_hbm,
    layer_out,
    scores,
    hist,
    ln_gain,
    pool_query,
    slots,
    cand_ids,
    b_rank,
    w_score,
    wp,
    wo,
    table,
    wr,
    normed,
    gate,
    qkv,
    kv,
    qs,
    acc,
    back,
    att,
    cand,
    pre,
    part,
    parts,
    piece,
    pieces,
    chosen,
    interests,
    share,
    shares,
    load_sem,
    kv_send,
    kv_recv,
    q_send,
    q_recv,
    pass_send,
    pass_recv,
    back_send,
    back_recv,
    sum_sem,
    state_sem,
    pick_sem,
    share_sem,
):
    events, width = hist.shape
    head_size = width // HEADS
    plane, line, ranks = parts.shape[0], pieces.shape[0], shares.shape[0]
    t = lax.axis_index("tm")
    owner = lax.axis_index("users")
    mp = lax.axis_index("mp")
    user = owner * ranks + mp
    x, y = lax.div(t, SIDE), lax.rem(t, SIDE)
    core = lax.rem(mp, 2)

    def even(v):
        return v + 1 - 2 * lax.rem(v, 2)

    def odd(v):
        return SIDE - 1 - v

    def swap_y(v):
        return even(v) + core * (odd(v) - even(v))

    def ring_y(v):
        return odd(v) + core * (even(v) - odd(v))

    swap = (odd, swap_y)
    ring = (even, ring_y)

    def head_of(a, b):
        first = lax.rem(lax.div(b + 1, 2), 2)
        return 2 * lax.div(a, 2) + first + core * (lax.div(b, 2) - first)

    def moved(a, b, rel, flip):
        first, second = lax.rem(rel, 2), lax.div(rel, 2)
        return a + second * (flip[0](a) - a), b + first * (flip[1](b) - b)

    def in_plane(a, b):
        return {"tm": a * SIDE + b}

    head = head_of(x, y)

    loads = [pltpu.make_async_copy(history.at[0], hist, load_sem.at[0])]
    for n, block in enumerate((3, 1, 2, 0)):
        cols = pl.ds(block * width, width)
        loads.append(pltpu.make_async_copy(w_proj.at[:, cols], wp.at[n], load_sem.at[n + 1]))
    rest = (
        (ln_gain_hbm, ln_gain),
        (pool_query_hbm, pool_query),
        (slots_hbm, slots),
        (cand_ids_hbm, cand_ids),
        (b_rank_hbm, b_rank),
        (w_score_hbm, w_score),
        (w_out, wo),
        (item_table, table),
        (w_rank, wr),
    )
    for n, (src, dst) in enumerate(rest):
        loads.append(pltpu.make_async_copy(src, dst, load_sem.at[5 + n]))
    loads[0].start()
    loads[5].start()
    for load in loads[1:5] + loads[6:]:
        load.start()

    barrier = pltpu.get_barrier_semaphore()

    def plane_device(step):
        a, b = step
        return lax.rem(x + a, SIDE) * SIDE + lax.rem(y + b, SIDE)

    height = line // 2
    low = height // 2

    def line_device(k):
        j = lax.div(k, 2)
        far = lax.div(j + 1, 2)
        chip = low + far * (1 - 2 * lax.rem(j, 2)) + lax.div(mp, 2) * low + owner
        chip = lax.rem(chip, height)
        other = lax.rem(core + k + 1, 2)
        return {"users": lax.rem(chip, low), "mp": 2 * lax.div(chip, low) + other}

    @pl.loop(0, line - 1)
    def _(k):
        pl.semaphore_signal(barrier, inc=1, device_id=line_device(k), device_id_type=MESH)

    for step in STEPS:
        pl.semaphore_signal(
            barrier, inc=1, device_id={"tm": plane_device(step)}, device_id_type=MESH
        )

    first_pos = t * events
    length = lengths[0]
    pos = first_pos + lax.broadcasted_iota(jnp.int32, (events, 1), 0)
    live = pos < length
    loads[0].wait()
    loads[5].wait()
    normed[...] = (layer_norm(hist[...].astype(F32)) * ln_gain[...]).astype(BF16)

    def project(n):
        loads[n + 1].wait()
        half = 0.5 * jnp.dot(normed[...], wp[n], preferred_element_type=F32)
        return silu_of_twice(half)

    keys = project(0)
    for h in range(HEADS):
        for n in range(0, events, head_size):
            square = keys[n : n + head_size, h * head_size : (h + 1) * head_size]
            qkv[h, 0, n : n + head_size] = square.T.astype(BF16)
    values = jnp.where(live, project(1), 0.0).astype(BF16)
    for h in range(HEADS):
        qkv[h, 1] = values[:, h * head_size : (h + 1) * head_size]

    pl.semaphore_wait(barrier, plane - 1 + line - 1)

    kv_copies, q_copies = [], []
    for rel in (3, 2, 1):
        a, b = moved(x, y, rel, swap)
        copy = pltpu.make_async_remote_copy(
            src_ref=qkv.at[head_of(a, b), pl.ds(0, 2)],
            dst_ref=kv.at[rel],
            send_sem=kv_send.at[rel],
            recv_sem=kv_recv.at[rel],
            device_id=in_plane(a, b),
            device_id_type=MESH,
        )
        copy.start()
        kv_copies.append(copy)

    query = project(2).astype(BF16)
    for h in range(HEADS):
        qkv[h, 2] = query[:, h * head_size : (h + 1) * head_size]
    for rel in (3, 2, 1):
        a, b = moved(x, y, rel, swap)
        copy = pltpu.make_async_remote_copy(
            src_ref=qkv.at[head_of(a, b), 2],
            dst_ref=qs.at[rel],
            send_sem=q_send.at[rel],
            recv_sem=q_recv.at[rel],
            device_id=in_plane(a, b),
            device_id_type=MESH,
        )
        copy.start()
        q_copies.append(copy)
    kv[0] = qkv[head, pl.ds(0, 2)]
    qs[0] = qkv[head, 2]

    def pass_on(s, p):
        a, b = moved(x, y, p, ring)
        return pltpu.make_async_remote_copy(
            src_ref=kv.at[s],
            dst_ref=kv.at[p * HEADS + s],
            send_sem=pass_send.at[s, p],
            recv_sem=pass_recv.at[s, p],
            device_id=in_plane(a, b),
            device_id_type=MESH,
        )

    def pass_third(s):
        a, b = moved(x, y, 1, ring)
        return pltpu.make_async_remote_copy(
            src_ref=kv.at[2 * HEADS + s],
            dst_ref=kv.at[3 * HEADS + s],
            send_sem=pass_send.at[s, 3],
            recv_sem=pass_recv.at[s, 3],
            device_id=in_plane(a, b),
            device_id_type=MESH,
        )

    for p in (2, 1):
        pass_on(0, p).start()

    gate[...] = project(3).astype(BF16)
    acc[...] = jnp.zeros_like(acc)

    owned, count = cand_ids.shape
    pool = table.shape[0]
    for load in loads[6:]:
        load.wait()

    @pl.loop(0, owned)
    def _(r):
        @pl.when(r > 0)
        def _():
            pltpu.make_async_copy(kv.at[r], kv.at[r], kv_recv.at[r]).wait()
            for p in (2, 1):
                pass_on(r, p).start()

        eye = lax.broadcasted_iota(jnp.int32, (count, count), 0) == lax.broadcasted_iota(
            jnp.int32, (count, count), 1
        )
        item = lax.broadcasted_iota(jnp.int32, (count, pool), 1).astype(F32)
        ids = cand_ids[pl.ds(r, 1), :].astype(F32)
        column = jnp.sum(jnp.where(eye, ids, 0.0), axis=1, keepdims=True)
        onehot = jnp.where(item == column, 1.0, 0.0).astype(BF16)
        cand[pl.ds(r * count, count)] = jnp.dot(
            onehot, table[...], preferred_element_type=F32
        ).astype(BF16)

    pre[...] = jnp.dot(cand[...], wr[:width], preferred_element_type=F32) + b_rank[...]

    scale = 0.5 * head_size**-0.5

    def time_of(p, s):
        a, b = moved(x, y, p, ring)
        a, b = moved(a, b, s, swap)
        return a * SIDE + b

    def attend(chunk, when, diagonal):
        key = jnp.concatenate(
            [kv[chunk, 0, pl.ds(n, head_size)] for n in range(0, events, head_size)], axis=1
        )
        value = kv[chunk, 1]
        for pair in range(2):
            nows = [time_of(0, 2 * pair + n) for n in range(2)]

            @pl.when(jnp.maximum(*nows) >= when)
            def _():
                weights = []
                score = jnp.dot(
                    qs[pl.ds(2 * pair, 2)].reshape(2 * events, head_size),
                    key,
                    preferred_element_type=F32,
                )
                for n, now in enumerate(nows):
                    half = score[n * events : (n + 1) * events]
                    if diagonal:
                        behind = (
                            lax.broadcasted_iota(jnp.int32, half.shape, 0)
                            - lax.broadcasted_iota(jnp.int32, half.shape, 1)
                            + (now - when) * events
                        )
                        half = jnp.where(behind >= 0, half * scale, 0.0)
                    else:
                        half = half * (scale * (now > when).astype(F32))
                    weights.append(silu_of_twice(half).astype(BF16))
                weights = jnp.concatenate(weights, axis=0)
                rows = pl.ds(pair * 2 * events, 2 * events)
                acc[rows] += jnp.dot(weights, value, preferred_element_type=F32)

    for copy in q_copies:
        copy.wait_recv()

    @pl.loop(0, HEADS)
    def _(s):
        attend(s, time_of(0, s), True)

    @pl.loop(0, 3 * HEADS + 3)
    def _(n):
        s = lax.div(n, 3)
        p = 2 - (n - 3 * s)
        s = s - lax.div(2 - p, 2)
        p = p + 3 * lax.div(2 - p, 2)

        @pl.when(jnp.logical_and(s >= 0, s < HEADS))
        def _():
            pltpu.make_async_copy(kv.at[0], kv.at[0], pass_recv.at[s, p]).wait()

            @pl.when(p == 2)
            def _():
                pass_third(s).start()

            attend(p * HEADS + s, time_of(p, s), False)

    back_copies = []
    for rel in (3, 2, 1):
        back[rel] = acc[pl.ds(rel * events, events)].astype(BF16)
        a, b = moved(x, y, rel, swap)
        copy = pltpu.make_async_remote_copy(
            src_ref=back.at[rel],
            dst_ref=att.at[head],
            send_sem=back_send.at[rel],
            recv_sem=back_recv.at[rel],
            device_id=in_plane(a, b),
            device_id_type=MESH,
        )
        copy.start()
        back_copies.append(copy)
    att[head] = acc[pl.ds(0, events)].astype(BF16)
    for copy in back_copies:
        copy.wait_recv()

    attended = jnp.concatenate([att[h] for h in range(HEADS)], axis=1).astype(F32)
    mixed = (layer_norm(attended) * gate[...].astype(F32)).astype(BF16)
    projected = jnp.dot(mixed, wo[...], preferred_element_type=F32)
    out = (hist[...].astype(F32) + projected).astype(BF16)
    layer_out[0] = out
    groups = pool_query.shape[0]
    half = 0.5 * dot_t(pool_query[...], out)
    lane = first_pos + lax.broadcasted_iota(jnp.int32, half.shape, 1)
    pool_w = jnp.where(lane < length, silu_of_twice(half), 0.0).astype(BF16)
    sums = jnp.dot(pool_w, out, preferred_element_type=F32)

    split = width // part.shape[2]
    lanes = part.shape[2]
    for n in range(plane):
        g, c = divmod(n, split)
        part[n] = sums[g : g + 1, c * lanes : (c + 1) * lanes]

    def wait_for(buffer, many, sem):
        some = buffer.at[pl.ds(0, many)]
        pltpu.make_async_copy(some, some, sem).wait()

    for step in STEPS:
        other = plane_device(step)
        pltpu.make_async_remote_copy(
            src_ref=part.at[other],
            dst_ref=parts.at[t],
            send_sem=sum_sem.at[0],
            recv_sem=sum_sem.at[1],
            device_id={"tm": other},
            device_id_type=MESH,
        ).start()

    parts[t] = part[t]
    wait_for(parts, plane - 1, sum_sem.at[1])
    whole = jnp.sum(parts[...], axis=0).astype(BF16).astype(F32)
    piece[...] = whole
    pieces[user] = whole

    @pl.loop(0, line - 1)
    def _(k):
        pltpu.make_async_remote_copy(
            src_ref=piece,
            dst_ref=pieces.at[user],
            send_sem=state_sem.at[0],
            recv_sem=state_sem.at[1],
            device_id=line_device(k),
            device_id_type=MESH,
        ).start()

    wait_for(pieces, line - 1, state_sem.at[1])
    mine = owner * owned + lax.broadcasted_iota(jnp.int32, (owned, line), 0)
    picker = jnp.where(slots[...] == mine, 1.0, 0.0).astype(BF16)
    states = pieces[...].reshape(line, lanes).astype(BF16)
    own_states = jnp.dot(picker, states, preferred_element_type=F32)
    chosen[...] = own_states
    interests[t] = own_states

    for step in STEPS:
        pltpu.make_async_remote_copy(
            src_ref=chosen,
            dst_ref=interests.at[t],
            send_sem=pick_sem.at[0],
            recv_sem=pick_sem.at[1],
            device_id={"tm": plane_device(step)},
            device_id_type=MESH,
        ).start()

    wait_for(interests, plane - 1, pick_sem.at[1])

    interest = jnp.concatenate(
        [
            layer_norm(
                jnp.concatenate([interests[g * split + c] for c in range(split)], axis=1)
            )
            for g in range(groups)
        ],
        axis=0,
    ).astype(BF16)
    half = (0.5 * width**-0.5) * dot_t(cand[...], interest)
    row = lax.div(lax.broadcasted_iota(jnp.int32, half.shape, 0), count)
    column = lax.rem(lax.broadcasted_iota(jnp.int32, half.shape, 1), owned)
    attn = jnp.where(row == column, silu_of_twice(half), 0.0)
    context = jnp.dot(
        attn,
        interest.astype(F32),
        precision=lax.Precision.HIGHEST,
        preferred_element_type=F32,
    ).astype(BF16)
    half = 0.5 * (pre[...] + jnp.dot(context, wr[width:], preferred_element_type=F32))
    hidden = silu_of_twice(half)
    own_share = dot_t(w_score[...], hidden, precision=lax.Precision.HIGHEST)
    share[...] = own_share
    shares[mp] = own_share
    for k in range(1, ranks):
        pltpu.make_async_remote_copy(
            src_ref=share,
            dst_ref=shares.at[mp],
            send_sem=share_sem.at[0],
            recv_sem=share_sem.at[1],
            device_id={"mp": lax.rem(mp + k, ranks)},
            device_id_type=MESH,
        ).start()
    wait_for(shares, ranks - 1, share_sem.at[1])
    total = jnp.sum(shares[...], axis=0)
    for r in range(owned):
        scores[r : r + 1, :] = total[:, r * count : (r + 1) * count]

    for copy in kv_copies + q_copies + back_copies:
        copy.wait_send()
    for s in range(HEADS):
        for p in (2, 1):
            pass_on(s, p).wait_send()
        pass_third(s).wait_send()
    wait_for(parts, plane - 1, sum_sem.at[0])
    wait_for(pieces, line - 1, state_sem.at[0])
    wait_for(interests, plane - 1, pick_sem.at[0])
    wait_for(shares, ranks - 1, share_sem.at[0])


def solution(mesh):
    plane, owners, ranks = mesh.shape["tm"], mesh.shape["users"], mesh.shape["mp"]
    line = owners * ranks

    def shards(
        history,
        ln_gain,
        w_proj,
        w_out,
        pool_query,
        lengths,
        slots,
        cand_ids,
        item_table,
        w_rank,
        b_rank,
        w_score,
    ):
        _, events, width = history.shape
        head_size = width // HEADS
        groups = pool_query.shape[0]
        owned, count = cand_ids.shape
        lanes = groups * width // plane
        cands = owned * count
        hidden = w_rank.shape[1]
        vmem = pl.BlockSpec(memory_space=pltpu.VMEM)
        smem = pl.BlockSpec(memory_space=pltpu.SMEM)
        hbm = pl.BlockSpec(memory_space=pltpu.HBM)
        dma = pltpu.SemaphoreType.DMA
        return pl.pallas_call(
            kernel,
            out_shape=(
                jax.ShapeDtypeStruct(history.shape, BF16),
                jax.ShapeDtypeStruct((owned, count), F32),
            ),
            in_specs=[smem] + [hbm] * 11,
            out_specs=(vmem, vmem),
            scratch_shapes=[
                pltpu.VMEM((events, width), BF16),
                pltpu.VMEM((1, width), F32),
                pltpu.VMEM(pool_query.shape, BF16),
                pltpu.VMEM((1, line), jnp.int32),
                pltpu.VMEM((owned, count), jnp.int32),
                pltpu.VMEM((1, hidden), F32),
                pltpu.VMEM((1, hidden), F32),
                pltpu.VMEM((4, width, width), BF16),
                pltpu.VMEM((width, width), BF16),
                pltpu.VMEM(item_table.shape, BF16),
                pltpu.VMEM(w_rank.shape, BF16),
                pltpu.VMEM((events, width), BF16),
                pltpu.VMEM((events, width), BF16),
                pltpu.VMEM((HEADS, 3, events, head_size), BF16),
                pltpu.VMEM((plane, 2, events, head_size), BF16),
                pltpu.VMEM((HEADS, events, head_size), BF16),
                pltpu.VMEM((HEADS * events, head_size), F32),
                pltpu.VMEM((HEADS, events, head_size), BF16),
                pltpu.VMEM((HEADS, events, head_size), BF16),
                pltpu.VMEM((cands, width), BF16),
                pltpu.VMEM((cands, hidden), F32),
                pltpu.VMEM((plane, 1, lanes), F32),
                pltpu.VMEM((plane, 1, lanes), F32),
                pltpu.VMEM((1, lanes), F32),
                pltpu.VMEM((line, 1, lanes), F32),
                pltpu.VMEM((owned, lanes), F32),
                pltpu.VMEM((plane, owned, lanes), F32),
                pltpu.VMEM((1, cands), F32),
                pltpu.VMEM((ranks, 1, cands), F32),
                dma((14,)),
                dma((HEADS,)),
                dma((HEADS,)),
                dma((HEADS,)),
                dma((HEADS,)),
                dma((HEADS, HEADS)),
                dma((HEADS, HEADS)),
                dma((HEADS,)),
                dma((HEADS,)),
                dma((2,)),
                dma((2,)),
                dma((2,)),
                dma((2,)),
            ],
            compiler_params=pltpu.CompilerParams(
                collective_id=0, has_side_effects=True, vmem_limit_bytes=VMEM_BYTES
            ),
            cost_estimate=pl.CostEstimate(
                flops=4_000_000_000, bytes_accessed=6_000_000, transcendentals=5_000_000
            ),
        )(
            lengths,
            history,
            ln_gain.reshape(1, -1),
            w_proj,
            w_out,
            pool_query,
            slots.reshape(1, -1),
            cand_ids,
            item_table,
            w_rank,
            b_rank.reshape(1, -1),
            w_score.reshape(1, -1),
        )

    placed = (
        P(("users", "mp"), "tm", None),
        P(),
        P(),
        P(),
        P(),
        P(("users", "mp")),
        P(),
        P("users", "tm"),
        P("users", None),
        P(None, "mp"),
        P("mp"),
        P("mp"),
    )
    return jax.shard_map(
        shards,
        mesh=mesh,
        in_specs=placed,
        out_specs=(P(("users", "mp"), "tm", None), P("users", "tm")),
        check_vma=False,
    )
```

```python
import jax
import jax.numpy as jnp
from jax import lax
from jax.experimental import pallas as pl
from jax.experimental.pallas import tpu as pltpu
from jax.sharding import PartitionSpec as P

HEADS = 4
SIDE = 4
EPS = 1e-05
PARTS = 4
VMEM_BYTES = 64 * 1024 * 1024
MESH = pl.DeviceIdType.MESH
STEPS = sorted(
    ((a, b) for a in range(SIDE) for b in range(SIDE) if a or b),
    key=lambda step: -sum(min(n, SIDE - n) for n in step),
)
F32 = jnp.float32
BF16 = jnp.bfloat16
ROWS_BY_ROWS = (((1,), (1,)), ((), ()))


def layer_norm(values):
    mean = jnp.mean(values, axis=-1, keepdims=True)
    centred = values - mean
    var = jnp.mean(centred * centred, axis=-1, keepdims=True)
    return centred * lax.rsqrt(var + EPS)


def silu_of_twice(half):
    return half + half * jnp.tanh(half)


def dot_t(a, b, **kw):
    return lax.dot_general(a, b, ROWS_BY_ROWS, preferred_element_type=F32, **kw)


def kernel(
    lengths,
    history,
    ln_gain_hbm,
    w_proj,
    w_out,
    pool_query_hbm,
    slots_hbm,
    cand_ids_hbm,
    item_table,
    w_rank,
    b_rank_hbm,
    w_score_hbm,
    layer_out,
    scores,
    hist,
    ln_gain,
    pool_query,
    slots,
    cand_ids,
    b_rank,
    w_score,
    wp,
    wo,
    table,
    wr,
    normed,
    gate,
    qkv,
    kv,
    qs,
    acc,
    back,
    att,
    cand,
    pre,
    part,
    parts,
    piece,
    pieces,
    chosen,
    interests,
    vectors,
    load_sem,
    kv_send,
    kv_recv,
    q_send,
    q_recv,
    pass_send,
    pass_recv,
    half_send,
    half_recv,
    back_send,
    back_recv,
    sum_sem,
    state_sem,
    pick_sem,
    over_send,
    chain_send,
    chain_recv,
    twin_send,
    twin_recv,
):
    events, width = hist.shape
    head_size = width // HEADS
    plane, line, ranks = parts.shape[0], pieces.shape[0], wr.shape[0]
    t = lax.axis_index("tm")
    owner = lax.axis_index("users")
    mp = lax.axis_index("mp")
    user = owner * ranks + mp
    x, y = lax.div(t, SIDE), lax.rem(t, SIDE)
    core = lax.rem(mp, 2)

    def even(v):
        return v + 1 - 2 * lax.rem(v, 2)

    def odd(v):
        return SIDE - 1 - v

    def swap(v):
        return even(v) + core * (odd(v) - even(v))

    def ring(v):
        return odd(v) + core * (even(v) - odd(v))

    def bit(v):
        first = lax.rem(lax.div(v + 1, 2), 2)
        return first + core * (lax.div(v, 2) - first)

    def head_of(a, b):
        return 2 * bit(a) + bit(b)

    def moved(a, b, rel, flip):
        first, second = lax.rem(rel, 2), lax.div(rel, 2)
        return a + first * (flip(a) - a), b + second * (flip(b) - b)

    def in_plane(a, b):
        return {"tm": a * SIDE + b}

    head = head_of(x, y)

    depth = wr.shape[1] // PARTS
    last = line // ranks - 1
    twin = mp + 1 - 2 * core
    across = lax.rem(mp + 2, ranks)
    near = jnp.minimum(owner, last - owner)
    step_on = jnp.where(owner < near + 1, 1, -1)
    ends_at = last // 2

    def weights_of(whose, k):
        rows = pl.ds(pl.multiple_of(k * depth, depth), depth)
        return wr.at[whose, rows]

    def send_weights(whose, k, to, sems):
        return pltpu.make_async_remote_copy(
            src_ref=weights_of(whose, k),
            dst_ref=weights_of(whose, k),
            send_sem=sems.at[k],
            recv_sem=chain_recv.at[k],
            device_id=to,
            device_id_type=MESH,
        )

    def send_vectors(whose, to, sems):
        return pltpu.make_async_remote_copy(
            src_ref=vectors.at[whose],
            dst_ref=vectors.at[whose],
            send_sem=sems.at[PARTS],
            recv_sem=chain_recv.at[PARTS],
            device_id=to,
            device_id_type=MESH,
        )

    over = {"users": last - owner, "mp": across}
    onward = {"users": owner + step_on}

    def relay(j):
        k = j - near

        @pl.when(jnp.logical_and(k >= 0, k < PARTS))
        def _():
            here = weights_of(across, k)
            pltpu.make_async_copy(here, here, chain_recv.at[k]).wait()

            @pl.when(near < ends_at)
            def _():
                send_weights(across, k, onward, chain_send).start()

            @pl.when(k == PARTS - 1)
            def _():
                here = vectors.at[across]
                pltpu.make_async_copy(here, here, chain_recv.at[PARTS]).wait()

                @pl.when(near < ends_at)
                def _():
                    send_vectors(across, onward, chain_send).start()

    def twin_copies(whose, n):
        return [
            pltpu.make_async_remote_copy(
                src_ref=ref.at[whose],
                dst_ref=ref.at[whose],
                send_sem=twin_send.at[n + m],
                recv_sem=twin_recv.at[n + m],
                device_id={"mp": twin},
                device_id_type=MESH,
            )
            for m, ref in enumerate((wr, vectors))
        ]

    loads = [pltpu.make_async_copy(history.at[0], hist, load_sem.at[0])]
    for n, block in enumerate((3, 1, 2, 0)):
        cols = pl.ds(block * width, width)
        loads.append(pltpu.make_async_copy(w_proj.at[:, cols], wp.at[n], load_sem.at[n + 1]))
    rest = (
        (ln_gain_hbm, ln_gain),
        (pool_query_hbm, pool_query),
        (slots_hbm, slots),
        (cand_ids_hbm, cand_ids),
        (b_rank_hbm, b_rank),
        (w_score_hbm, w_score),
        (w_out, wo),
        (item_table, table),
        (w_rank, wr.at[mp]),
    )
    for n, (src, dst) in enumerate(rest):
        loads.append(pltpu.make_async_copy(src, dst, load_sem.at[5 + n]))
    loads[0].start()
    loads[5].start()
    for load in loads[1:5] + loads[6:]:
        load.start()

    barrier = pltpu.get_barrier_semaphore()

    def plane_device(step):
        a, b = step
        return lax.rem(x + a, SIDE) * SIDE + lax.rem(y + b, SIDE)

    height = line // 2
    low = height // 2

    def line_device(k):
        j = lax.div(k, 2)
        far = lax.div(j + 1, 2)
        chip = low + far * (1 - 2 * lax.rem(j, 2)) + lax.div(mp, 2) * low + owner
        chip = lax.rem(chip, height)
        other = lax.rem(core + k + 1, 2)
        return {"users": lax.rem(chip, low), "mp": 2 * lax.div(chip, low) + other}

    @pl.loop(0, line - 1)
    def _(k):
        pl.semaphore_signal(barrier, inc=1, device_id=line_device(k), device_id_type=MESH)

    for step in STEPS:
        pl.semaphore_signal(
            barrier, inc=1, device_id={"tm": plane_device(step)}, device_id_type=MESH
        )

    first_pos = t * events
    length = lengths[0]
    pos = first_pos + lax.broadcasted_iota(jnp.int32, (events, 1), 0)
    live = pos < length
    loads[0].wait()
    loads[5].wait()
    normed[...] = (layer_norm(hist[...].astype(F32)) * ln_gain[...]).astype(BF16)

    def project(n):
        loads[n + 1].wait()
        half = 0.5 * jnp.dot(normed[...], wp[n], preferred_element_type=F32)
        return silu_of_twice(half)

    keys = project(0).astype(BF16)
    for h in range(HEADS):
        qkv[h, 0] = keys[:, h * head_size : (h + 1) * head_size]
    values = jnp.where(live, project(1), 0.0).astype(BF16)
    for h in range(HEADS):
        qkv[h, 1] = values[:, h * head_size : (h + 1) * head_size]

    pl.semaphore_wait(barrier, plane - 1 + line - 1)

    kv_copies, q_copies = [], []
    for rel in (3, 2, 1):
        a, b = moved(x, y, rel, swap)
        copy = pltpu.make_async_remote_copy(
            src_ref=qkv.at[head_of(a, b), pl.ds(0, 2)],
            dst_ref=kv.at[rel],
            send_sem=kv_send.at[rel],
            recv_sem=kv_recv.at[rel],
            device_id=in_plane(a, b),
            device_id_type=MESH,
        )
        copy.start()
        kv_copies.append(copy)

    query = project(2).astype(BF16)
    for h in range(HEADS):
        qkv[h, 2] = query[:, h * head_size : (h + 1) * head_size]
    for rel in (3, 2, 1):
        a, b = moved(x, y, rel, swap)
        copy = pltpu.make_async_remote_copy(
            src_ref=qkv.at[head_of(a, b), 2],
            dst_ref=qs.at[rel],
            send_sem=q_send.at[rel],
            recv_sem=q_recv.at[rel],
            device_id=in_plane(a, b),
            device_id_type=MESH,
        )
        copy.start()
        q_copies.append(copy)
    for load in loads[9:11] + loads[13:]:
        load.wait()
    vectors[mp, 0:1] = b_rank[...]
    vectors[mp, 1:2] = w_score[...]

    @pl.when(near == 0)
    def _():
        for k in range(PARTS):
            send_weights(mp, k, over, over_send).start()
        send_vectors(mp, over, over_send).start()

    for copy in twin_copies(mp, 0):
        copy.start()

    kv[0] = qkv[head, pl.ds(0, 2)]
    qs[0] = qkv[head, 2]

    def pass_on(s, p):
        a, b = moved(x, y, p, ring)
        return pltpu.make_async_remote_copy(
            src_ref=kv.at[s],
            dst_ref=kv.at[p * HEADS + s],
            send_sem=pass_send.at[s, p],
            recv_sem=pass_recv.at[s, p],
            device_id=in_plane(a, b),
            device_id_type=MESH,
        )

    def pass_half(s, p):
        a, b = moved(x, y, 3 - p, ring)
        return pltpu.make_async_remote_copy(
            src_ref=kv.at[p * HEADS + s, p - 1],
            dst_ref=kv.at[3 * HEADS + s, p - 1],
            send_sem=half_send.at[s, p],
            recv_sem=half_recv.at[s, p],
            device_id=in_plane(a, b),
            device_id_type=MESH,
        )

    for p in (1, 2):
        pass_on(0, p).start()

    gate[...] = project(3).astype(BF16)
    acc[...] = jnp.zeros_like(acc)

    owned, count = cand_ids.shape
    pool = table.shape[0]
    for load in loads[6:9] + loads[11:13]:
        load.wait()

    @pl.loop(0, owned)
    def _(r):
        @pl.when(r > 0)
        def _():
            pltpu.make_async_copy(kv.at[r], kv.at[r], kv_recv.at[r]).wait()
            for p in (1, 2):
                pass_on(r, p).start()

        eye = lax.broadcasted_iota(jnp.int32, (count, count), 0) == lax.broadcasted_iota(
            jnp.int32, (count, count), 1
        )
        item = lax.broadcasted_iota(jnp.int32, (count, pool), 1).astype(F32)
        ids = cand_ids[pl.ds(r, 1), :].astype(F32)
        column = jnp.sum(jnp.where(eye, ids, 0.0), axis=1, keepdims=True)
        onehot = jnp.where(item == column, 1.0, 0.0).astype(BF16)
        cand[pl.ds(r * count, count)] = jnp.dot(
            onehot, table[...], preferred_element_type=F32
        ).astype(BF16)

    scale = 0.5 * head_size**-0.5

    def time_of(p, s):
        a, b = moved(x, y, p, ring)
        a, b = moved(a, b, s, swap)
        return a * SIDE + b

    def attend(chunk, when, diagonal):
        key, value = kv[chunk, 0], kv[chunk, 1]
        for pair in range(2):
            weights = []
            score = dot_t(qs[pl.ds(2 * pair, 2)].reshape(2 * events, head_size), key)
            for n in range(2):
                now = time_of(0, 2 * pair + n)
                half = score[n * events : (n + 1) * events]
                if diagonal:
                    behind = (
                        lax.broadcasted_iota(jnp.int32, half.shape, 0)
                        - lax.broadcasted_iota(jnp.int32, half.shape, 1)
                        + (now - when) * events
                    )
                    half = jnp.where(behind >= 0, half * scale, 0.0)
                else:
                    half = half * (scale * (now > when).astype(F32))
                weights.append(silu_of_twice(half).astype(BF16))
            weights = jnp.concatenate(weights, axis=0)
            rows = pl.ds(pair * 2 * events, 2 * events)
            acc[rows] += jnp.dot(weights, value, preferred_element_type=F32)

    for copy in q_copies:
        copy.wait_recv()

    @pl.loop(0, HEADS)
    def _(s):
        attend(s, time_of(0, s), True)

    @pl.loop(0, HEADS + 1)
    def _(s):
        @pl.when(s > 0)
        def _():
            relay(s - 1)

        @pl.when(s < HEADS)
        def _():
            @pl.loop(1, 3)
            def _(p):
                pass_on(s, p).wait_recv()
                pass_half(s, p).start()
                attend(p * HEADS + s, time_of(p, s), False)

        @pl.when(s > 0)
        def _():
            for p in (1, 2):
                pass_half(s - 1, p).wait_recv()
            attend(3 * HEADS + s - 1, time_of(3, s - 1), False)

    back_copies = []
    for rel in (3, 2, 1):
        back[rel] = acc[pl.ds(rel * events, events)].astype(BF16)
        a, b = moved(x, y, rel, swap)
        copy = pltpu.make_async_remote_copy(
            src_ref=back.at[rel],
            dst_ref=att.at[head],
            send_sem=back_send.at[rel],
            recv_sem=back_recv.at[rel],
            device_id=in_plane(a, b),
            device_id_type=MESH,
        )
        copy.start()
        back_copies.append(copy)
    att[head] = acc[pl.ds(0, events)].astype(BF16)
    relay(HEADS)
    for copy in back_copies:
        copy.wait_recv()

    attended = jnp.concatenate([att[h] for h in range(HEADS)], axis=1).astype(F32)
    mixed = (layer_norm(attended) * gate[...].astype(F32)).astype(BF16)
    projected = jnp.dot(mixed, wo[...], preferred_element_type=F32)
    out = (hist[...].astype(F32) + projected).astype(BF16)
    layer_out[0] = out
    groups = pool_query.shape[0]
    half = 0.5 * dot_t(pool_query[...], out)
    lane = first_pos + lax.broadcasted_iota(jnp.int32, half.shape, 1)
    pool_w = jnp.where(lane < length, silu_of_twice(half), 0.0).astype(BF16)
    sums = jnp.dot(pool_w, out, preferred_element_type=F32)

    split = width // part.shape[2]
    lanes = part.shape[2]
    for n in range(plane):
        g, c = divmod(n, split)
        part[n] = sums[g : g + 1, c * lanes : (c + 1) * lanes]

    def wait_for(buffer, many, sem):
        some = buffer.at[pl.ds(0, many)]
        pltpu.make_async_copy(some, some, sem).wait()

    for step in STEPS:
        other = plane_device(step)
        pltpu.make_async_remote_copy(
            src_ref=part.at[other],
            dst_ref=parts.at[t],
            send_sem=sum_sem.at[0],
            recv_sem=sum_sem.at[1],
            device_id={"tm": other},
            device_id_type=MESH,
        ).start()

    parts[t] = part[t]
    relay(HEADS + 1)
    wait_for(parts, plane - 1, sum_sem.at[1])
    whole = jnp.sum(parts[...], axis=0).astype(BF16).astype(F32)
    piece[...] = whole
    pieces[user] = whole

    @pl.loop(0, line - 1)
    def _(k):
        pltpu.make_async_remote_copy(
            src_ref=piece,
            dst_ref=pieces.at[user],
            send_sem=state_sem.at[0],
            recv_sem=state_sem.at[1],
            device_id=line_device(k),
            device_id_type=MESH,
        ).start()

    relay(HEADS + 2)
    for copy in twin_copies(across, 2):
        copy.start()
    wait_for(pieces, line - 1, state_sem.at[1])
    mine = owner * owned + lax.broadcasted_iota(jnp.int32, (owned, line), 0)
    picker = jnp.where(slots[...] == mine, 1.0, 0.0).astype(BF16)
    states = pieces[...].reshape(line, lanes).astype(BF16)
    own_states = jnp.dot(picker, states, preferred_element_type=F32)
    chosen[...] = own_states
    interests[t] = own_states

    for step in STEPS:
        pltpu.make_async_remote_copy(
            src_ref=chosen,
            dst_ref=interests.at[t],
            send_sem=pick_sem.at[0],
            recv_sem=pick_sem.at[1],
            device_id={"tm": plane_device(step)},
            device_id_type=MESH,
        ).start()

    for n in range(2):
        for copy in twin_copies((mp, across)[n], 2 * n):
            copy.wait_recv()
    for m in range(ranks):
        pre[m] = (
            jnp.dot(cand[...], wr[m, :width], preferred_element_type=F32) + vectors[m, 0:1]
        )
    wait_for(interests, plane - 1, pick_sem.at[1])

    interest = jnp.concatenate(
        [
            layer_norm(
                jnp.concatenate([interests[g * split + c] for c in range(split)], axis=1)
            )
            for g in range(groups)
        ],
        axis=0,
    ).astype(BF16)
    half = (0.5 * width**-0.5) * dot_t(cand[...], interest)
    row = lax.div(lax.broadcasted_iota(jnp.int32, half.shape, 0), count)
    column = lax.rem(lax.broadcasted_iota(jnp.int32, half.shape, 1), owned)
    attn = jnp.where(row == column, silu_of_twice(half), 0.0)
    high = attn.astype(BF16)
    low = (attn - high.astype(F32)).astype(BF16)
    context = (
        jnp.dot(high, interest, preferred_element_type=F32)
        + jnp.dot(low, interest, preferred_element_type=F32)
    ).astype(BF16)
    terms = jnp.zeros_like(pre[0])
    for m in range(ranks):
        half = 0.5 * (pre[m] + jnp.dot(context, wr[m, width:], preferred_element_type=F32))
        terms += silu_of_twice(half) * vectors[m, 1:2]
    high = terms.astype(BF16)
    low = (terms - high.astype(F32)).astype(BF16)
    ones = jnp.ones((16, terms.shape[1]), BF16)
    total = dot_t(ones, high) + dot_t(ones, low)
    for r in range(owned):
        scores[r : r + 1, :] = total[0:1, r * count : (r + 1) * count]

    for copy in kv_copies + q_copies + back_copies:
        copy.wait_send()
    for s in range(HEADS):
        for p in (1, 2):
            pass_on(s, p).wait_send()
            pass_half(s, p).wait_send()
    wait_for(parts, plane - 1, sum_sem.at[0])
    wait_for(pieces, line - 1, state_sem.at[0])
    wait_for(interests, plane - 1, pick_sem.at[0])
    for n in range(2):
        for copy in twin_copies((mp, across)[n], 2 * n):
            copy.wait_send()

    @pl.when(near == 0)
    def _():
        for k in range(PARTS):
            send_weights(mp, k, over, over_send).wait_send()
        send_vectors(mp, over, over_send).wait_send()

    @pl.when(near < ends_at)
    def _():
        for k in range(PARTS):
            send_weights(across, k, onward, chain_send).wait_send()
        send_vectors(across, onward, chain_send).wait_send()


def solution(mesh):
    plane, owners, ranks = mesh.shape["tm"], mesh.shape["users"], mesh.shape["mp"]
    line = owners * ranks

    def shards(
        history,
        ln_gain,
        w_proj,
        w_out,
        pool_query,
        lengths,
        slots,
        cand_ids,
        item_table,
        w_rank,
        b_rank,
        w_score,
    ):
        _, events, width = history.shape
        head_size = width // HEADS
        groups = pool_query.shape[0]
        owned, count = cand_ids.shape
        lanes = groups * width // plane
        cands = owned * count
        hidden = w_rank.shape[1]
        vmem = pl.BlockSpec(memory_space=pltpu.VMEM)
        smem = pl.BlockSpec(memory_space=pltpu.SMEM)
        hbm = pl.BlockSpec(memory_space=pltpu.HBM)
        dma = pltpu.SemaphoreType.DMA
        return pl.pallas_call(
            kernel,
            out_shape=(
                jax.ShapeDtypeStruct(history.shape, BF16),
                jax.ShapeDtypeStruct((owned, count), F32),
            ),
            in_specs=[smem] + [hbm] * 11,
            out_specs=(vmem, vmem),
            scratch_shapes=[
                pltpu.VMEM((events, width), BF16),
                pltpu.VMEM((1, width), F32),
                pltpu.VMEM(pool_query.shape, BF16),
                pltpu.VMEM((1, line), jnp.int32),
                pltpu.VMEM((owned, count), jnp.int32),
                pltpu.VMEM((1, hidden), F32),
                pltpu.VMEM((1, hidden), F32),
                pltpu.VMEM((4, width, width), BF16),
                pltpu.VMEM((width, width), BF16),
                pltpu.VMEM(item_table.shape, BF16),
                pltpu.VMEM((ranks, *w_rank.shape), BF16),
                pltpu.VMEM((events, width), BF16),
                pltpu.VMEM((events, width), BF16),
                pltpu.VMEM((HEADS, 3, events, head_size), BF16),
                pltpu.VMEM((plane, 2, events, head_size), BF16),
                pltpu.VMEM((HEADS, events, head_size), BF16),
                pltpu.VMEM((HEADS * events, head_size), F32),
                pltpu.VMEM((HEADS, events, head_size), BF16),
                pltpu.VMEM((HEADS, events, head_size), BF16),
                pltpu.VMEM((cands, width), BF16),
                pltpu.VMEM((ranks, cands, hidden), F32),
                pltpu.VMEM((plane, 1, lanes), F32),
                pltpu.VMEM((plane, 1, lanes), F32),
                pltpu.VMEM((1, lanes), F32),
                pltpu.VMEM((line, 1, lanes), F32),
                pltpu.VMEM((owned, lanes), F32),
                pltpu.VMEM((plane, owned, lanes), F32),
                pltpu.VMEM((ranks, 2, hidden), F32),
                dma((14,)),
                dma((HEADS,)),
                dma((HEADS,)),
                dma((HEADS,)),
                dma((HEADS,)),
                dma((HEADS, HEADS)),
                dma((HEADS, HEADS)),
                dma((HEADS, HEADS)),
                dma((HEADS, HEADS)),
                dma((HEADS,)),
                dma((HEADS,)),
                dma((2,)),
                dma((2,)),
                dma((2,)),
                dma((PARTS + 1,)),
                dma((PARTS + 1,)),
                dma((PARTS + 1,)),
                dma((4,)),
                dma((4,)),
            ],
            compiler_params=pltpu.CompilerParams(
                collective_id=0, has_side_effects=True, vmem_limit_bytes=VMEM_BYTES
            ),
            cost_estimate=pl.CostEstimate(
                flops=4_000_000_000, bytes_accessed=6_000_000, transcendentals=5_000_000
            ),
        )(
            lengths,
            history,
            ln_gain.reshape(1, -1),
            w_proj,
            w_out,
            pool_query,
            slots.reshape(1, -1),
            cand_ids,
            item_table,
            w_rank,
            b_rank.reshape(1, -1),
            w_score.reshape(1, -1),
        )

    placed = (
        P(("users", "mp"), "tm", None),
        P(),
        P(),
        P(),
        P(),
        P(("users", "mp")),
        P(),
        P("users", "tm"),
        P("users", None),
        P(None, "mp"),
        P("mp"),
        P("mp"),
    )
    return jax.shard_map(
        shards,
        mesh=mesh,
        in_specs=placed,
        out_specs=(P(("users", "mp"), "tm", None), P("users", "tm")),
        check_vma=False,
    )
```

```python
import jax
import jax.numpy as jnp
from jax import lax
from jax.experimental import pallas as pl
from jax.experimental.pallas import tpu as pltpu
from jax.sharding import PartitionSpec as P

HEADS = 4
SIDE = 4
EPS = 1e-05
PARTS = 4
VMEM_BYTES = 64 * 1024 * 1024
MESH = pl.DeviceIdType.MESH
STEPS = sorted(
    ((a, b) for a in range(SIDE) for b in range(SIDE) if a or b),
    key=lambda step: -sum(min(n, SIDE - n) for n in step),
)
F32 = jnp.float32
BF16 = jnp.bfloat16
ROWS_BY_ROWS = (((1,), (1,)), ((), ()))


def layer_norm(values):
    mean = jnp.mean(values, axis=-1, keepdims=True)
    centred = values - mean
    var = jnp.mean(centred * centred, axis=-1, keepdims=True)
    return centred * lax.rsqrt(var + EPS)


def silu_of_twice(half):
    return half + half * jnp.tanh(half)


def dot_t(a, b, **kw):
    return lax.dot_general(a, b, ROWS_BY_ROWS, preferred_element_type=F32, **kw)


def kernel(
    lengths,
    history,
    ln_gain_hbm,
    w_proj,
    w_out,
    pool_query_hbm,
    slots_hbm,
    cand_ids_hbm,
    item_table,
    w_rank,
    b_rank_hbm,
    w_score_hbm,
    layer_out,
    scores,
    hist,
    ln_gain,
    pool_query,
    slots,
    cand_ids,
    b_rank,
    w_score,
    wp,
    wo,
    table,
    wr,
    normed,
    masks,
    qkv,
    kv,
    qs,
    acc,
    back,
    att,
    cand,
    pre,
    part,
    parts,
    piece,
    pieces,
    chosen,
    interests,
    vectors,
    own_sums,
    terms_of,
    load_sem,
    kv_send,
    kv_recv,
    q_send,
    q_recv,
    pass_send,
    pass_recv,
    half_send,
    half_recv,
    back_send,
    back_recv,
    sum_sem,
    state_sem,
    pick_sem,
    over_send,
    chain_send,
    chain_recv,
    twin_send,
    twin_recv,
):
    events, width = hist.shape
    head_size = width // HEADS
    plane, line, ranks = parts.shape[0], pieces.shape[0], wr.shape[0]
    t = lax.axis_index("tm")
    owner = lax.axis_index("users")
    mp = lax.axis_index("mp")
    user = owner * ranks + mp
    x, y = lax.div(t, SIDE), lax.rem(t, SIDE)
    core = lax.rem(mp, 2)

    def even(v):
        return v + 1 - 2 * lax.rem(v, 2)

    def odd(v):
        return SIDE - 1 - v

    def swap(v):
        return even(v) + core * (odd(v) - even(v))

    def ring(v):
        return odd(v) + core * (even(v) - odd(v))

    def bit(v):
        first = lax.rem(lax.div(v + 1, 2), 2)
        return first + core * (lax.div(v, 2) - first)

    def head_of(a, b):
        return 2 * bit(a) + bit(b)

    def moved(a, b, rel, flip):
        first, second = lax.rem(rel, 2), lax.div(rel, 2)
        return a + first * (flip(a) - a), b + second * (flip(b) - b)

    def in_plane(a, b):
        return {"tm": a * SIDE + b}

    head = head_of(x, y)

    depth = wr.shape[1] // PARTS
    last = line // ranks - 1
    twin = mp + 1 - 2 * core
    across = lax.rem(mp + 2, ranks)
    near = jnp.minimum(owner, last - owner)
    step_on = jnp.where(owner < near + 1, 1, -1)
    ends_at = last // 2

    def weights_of(whose, k):
        rows = pl.ds(pl.multiple_of(k * depth, depth), depth)
        return wr.at[whose, rows]

    def send_weights(whose, k, to, sems):
        return pltpu.make_async_remote_copy(
            src_ref=weights_of(whose, k),
            dst_ref=weights_of(whose, k),
            send_sem=sems.at[k],
            recv_sem=chain_recv.at[k],
            device_id=to,
            device_id_type=MESH,
        )

    def send_vectors(whose, to, sems):
        return pltpu.make_async_remote_copy(
            src_ref=vectors.at[whose],
            dst_ref=vectors.at[whose],
            send_sem=sems.at[PARTS],
            recv_sem=chain_recv.at[PARTS],
            device_id=to,
            device_id_type=MESH,
        )

    over = {"users": last - owner, "mp": across}
    onward = {"users": owner + step_on}

    def relay(j):
        k = j - near

        @pl.when(jnp.logical_and(k >= 0, k < PARTS))
        def _():
            here = weights_of(across, k)
            pltpu.make_async_copy(here, here, chain_recv.at[k]).wait()

            @pl.when(near < ends_at)
            def _():
                send_weights(across, k, onward, chain_send).start()

            @pl.when(k == PARTS - 1)
            def _():
                here = vectors.at[across]
                pltpu.make_async_copy(here, here, chain_recv.at[PARTS]).wait()

                @pl.when(near < ends_at)
                def _():
                    send_vectors(across, onward, chain_send).start()

    def twin_copies(whose, n):
        return [
            pltpu.make_async_remote_copy(
                src_ref=ref.at[whose],
                dst_ref=ref.at[whose],
                send_sem=twin_send.at[n + m],
                recv_sem=twin_recv.at[n + m],
                device_id={"mp": twin},
                device_id_type=MESH,
            )
            for m, ref in enumerate((wr, vectors))
        ]

    loads = [pltpu.make_async_copy(history.at[0], hist, load_sem.at[0])]
    for n, block in enumerate((3, 1, 2, 0)):
        cols = pl.ds(block * width, width)
        loads.append(pltpu.make_async_copy(w_proj.at[:, cols], wp.at[n], load_sem.at[n + 1]))
    rest = (
        (ln_gain_hbm, ln_gain),
        (pool_query_hbm, pool_query),
        (slots_hbm, slots),
        (cand_ids_hbm, cand_ids),
        (b_rank_hbm, b_rank),
        (w_score_hbm, w_score),
        (w_out, wo),
        (item_table, table),
        (w_rank, wr.at[mp]),
    )
    for n, (src, dst) in enumerate(rest):
        loads.append(pltpu.make_async_copy(src, dst, load_sem.at[5 + n]))
    loads[0].start()
    loads[5].start()
    for load in loads[1:5] + loads[6:]:
        load.start()

    barrier = pltpu.get_barrier_semaphore()

    def plane_device(step):
        a, b = step
        return lax.rem(x + a, SIDE) * SIDE + lax.rem(y + b, SIDE)

    height = line // 2
    low = height // 2

    def line_device(k):
        j = lax.div(k, 2)
        far = lax.div(j + 1, 2)
        chip = low + far * (1 - 2 * lax.rem(j, 2)) + lax.div(mp, 2) * low + owner
        chip = lax.rem(chip, height)
        other = lax.rem(core + k + 1, 2)
        return {"users": lax.rem(chip, low), "mp": 2 * lax.div(chip, low) + other}

    @pl.loop(0, line - 1)
    def _(k):
        pl.semaphore_signal(barrier, inc=1, device_id=line_device(k), device_id_type=MESH)

    for step in STEPS:
        pl.semaphore_signal(
            barrier, inc=1, device_id={"tm": plane_device(step)}, device_id_type=MESH
        )

    first_pos = t * events
    length = lengths[0]
    pos = first_pos + lax.broadcasted_iota(jnp.int32, (events, 1), 0)
    live = pos < length
    loads[0].wait()
    loads[5].wait()
    @pl.loop(0, 2)
    def _(n):
        rows = pl.ds(pl.multiple_of(n * events // 2, events // 2), events // 2)
        normed[rows] = (layer_norm(hist[rows].astype(F32)) * ln_gain[...]).astype(BF16)

    behind = lax.broadcasted_iota(jnp.int32, (events, events), 0) >= lax.broadcasted_iota(
        jnp.int32, (events, events), 1
    )
    scale = 0.5 * head_size**-0.5
    masks[0] = jnp.zeros((events, events), F32)
    masks[1] = jnp.where(behind, scale, 0.0)
    masks[2] = jnp.full((events, events), scale, F32)

    def kv_copy(rel):
        a, b = moved(x, y, rel, swap)
        return pltpu.make_async_remote_copy(
            src_ref=qkv.at[head_of(a, b), pl.ds(0, 2)],
            dst_ref=kv.at[rel],
            send_sem=kv_send.at[rel],
            recv_sem=kv_recv.at[rel],
            device_id=in_plane(a, b),
            device_id_type=MESH,
        )

    def q_copy(rel):
        a, b = moved(x, y, rel, swap)
        return pltpu.make_async_remote_copy(
            src_ref=qkv.at[head_of(a, b), 2],
            dst_ref=qs.at[rel],
            send_sem=q_send.at[rel],
            recv_sem=q_recv.at[rel],
            device_id=in_plane(a, b),
            device_id_type=MESH,
        )

    def pass_on(s, p):
        a, b = moved(x, y, p, ring)
        return pltpu.make_async_remote_copy(
            src_ref=kv.at[s],
            dst_ref=kv.at[p * HEADS + s],
            send_sem=pass_send.at[s, p],
            recv_sem=pass_recv.at[s, p],
            device_id=in_plane(a, b),
            device_id_type=MESH,
        )

    def pass_half(s, p):
        a, b = moved(x, y, 3 - p, ring)
        return pltpu.make_async_remote_copy(
            src_ref=kv.at[p * HEADS + s, p - 1],
            dst_ref=kv.at[3 * HEADS + s, p - 1],
            send_sem=half_send.at[s, p],
            recv_sem=half_recv.at[s, p],
            device_id=in_plane(a, b),
            device_id_type=MESH,
        )

    @pl.loop(0, 4)
    def _(n):
        pltpu.make_async_copy(wp.at[n], wp.at[n], load_sem.at[n + 1]).wait()
        half = 0.5 * jnp.dot(normed[...], wp[n], preferred_element_type=F32)
        made = jnp.where(jnp.logical_or(live, n != 1), silu_of_twice(half), 0.0).astype(BF16)
        for h in range(HEADS):
            qkv[h, n] = made[:, h * head_size : (h + 1) * head_size]

        @pl.when(n == 1)
        def _():
            pl.semaphore_wait(barrier, plane - 1 + line - 1)

            @pl.loop(1, HEADS)
            def _(k):
                kv_copy(HEADS - k).start()

        @pl.when(n == 2)
        def _():
            @pl.loop(1, HEADS)
            def _(k):
                q_copy(HEADS - k).start()

            kv[0] = qkv[head, pl.ds(0, 2)]
            qs[0] = qkv[head, 2]
            for p in (1, 2):
                pass_on(0, p).start()

    for load in loads[9:11] + loads[13:]:
        load.wait()
    vectors[mp, 0:1] = b_rank[...]
    vectors[mp, 1:2] = w_score[...]

    @pl.when(near == 0)
    def _():
        @pl.loop(0, PARTS)
        def _(k):
            send_weights(mp, k, over, over_send).start()

        send_vectors(mp, over, over_send).start()

    for copy in twin_copies(mp, 0):
        copy.start()

    acc[...] = jnp.zeros_like(acc)

    owned, count = cand_ids.shape
    pool = table.shape[0]
    for load in loads[6:9] + loads[11:13]:
        load.wait()

    @pl.loop(0, owned)
    def _(r):
        @pl.when(r > 0)
        def _():
            pltpu.make_async_copy(kv.at[r], kv.at[r], kv_recv.at[r]).wait()
            for p in (1, 2):
                pass_on(r, p).start()

        eye = lax.broadcasted_iota(jnp.int32, (count, count), 0) == lax.broadcasted_iota(
            jnp.int32, (count, count), 1
        )
        item = lax.broadcasted_iota(jnp.int32, (count, pool), 1).astype(F32)
        ids = cand_ids[pl.ds(r, 1), :].astype(F32)
        column = jnp.sum(jnp.where(eye, ids, 0.0), axis=1, keepdims=True)
        onehot = jnp.where(item == column, 1.0, 0.0).astype(BF16)
        cand[pl.ds(r * count, count)] = jnp.dot(
            onehot, table[...], preferred_element_type=F32
        ).astype(BF16)

    def time_of(p, s):
        a, b = moved(x, y, p, ring)
        a, b = moved(a, b, s, swap)
        return a * SIDE + b

    @pl.loop(1, HEADS)
    def _(rel):
        q_copy(rel).wait_recv()

    @pl.loop(0, HEADS + 3 * HEADS + 3)
    def _(n):
        turn = n - HEADS
        third = lax.div(turn, 3)
        which = turn - 3 * third
        p = jnp.where(n < HEADS, 0, which + 1)
        s = jnp.where(n < HEADS, n, third - lax.div(which, 2))

        @pl.when(jnp.logical_and(p == 1, s > 0))
        def _():
            relay(s - 1)

        @pl.when(jnp.logical_and(s >= 0, s < HEADS))
        def _():
            @pl.when(jnp.logical_or(p == 1, p == 2))
            def _():
                pass_on(s, p).wait_recv()
                pass_half(s, p).start()

            @pl.when(p == 3)
            def _():
                for q in (1, 2):
                    pass_half(s, q).wait_recv()

            chunk = p * HEADS + s
            when = time_of(p, s)

            @pl.loop(0, 2)
            def _(pair):
                score = dot_t(
                    qs[pl.ds(2 * pair, 2)].reshape(2 * events, head_size), kv[chunk, 0]
                )
                weights = []
                for m in range(2):
                    ahead = time_of(0, 2 * pair + m) - when
                    mask = masks[1 + jnp.clip(ahead, -1, 1)]
                    half = score[m * events : (m + 1) * events] * mask
                    weights.append(silu_of_twice(half).astype(BF16))
                weights = jnp.concatenate(weights, axis=0)
                rows = pl.ds(pl.multiple_of(pair * 2 * events, 2 * events), 2 * events)
                acc[rows] += jnp.dot(weights, kv[chunk, 1], preferred_element_type=F32)

    def back_copy(rel):
        a, b = moved(x, y, rel, swap)
        return pltpu.make_async_remote_copy(
            src_ref=back.at[rel],
            dst_ref=att.at[head],
            send_sem=back_send.at[rel],
            recv_sem=back_recv.at[rel],
            device_id=in_plane(a, b),
            device_id_type=MESH,
        )

    @pl.loop(1, HEADS)
    def _(k):
        rel = HEADS - k
        rows = pl.ds(pl.multiple_of(rel * events, events), events)
        back[rel] = acc[rows].astype(BF16)
        back_copy(rel).start()

    att[head] = acc[pl.ds(0, events)].astype(BF16)
    relay(HEADS)

    @pl.loop(1, HEADS)
    def _(rel):
        back_copy(rel).wait_recv()

    groups = pool_query.shape[0]
    block = events // 2
    own_sums[...] = jnp.zeros_like(own_sums)

    @pl.loop(0, 2)
    def _(n):
        rows = pl.ds(pl.multiple_of(n * block, block), block)
        attended = jnp.concatenate([att[h, rows] for h in range(HEADS)], axis=1).astype(F32)
        gate = jnp.concatenate([qkv[h, 3, rows] for h in range(HEADS)], axis=1).astype(F32)
        mixed = (layer_norm(attended) * gate).astype(BF16)
        projected = jnp.dot(mixed, wo[...], preferred_element_type=F32)
        out = (hist[rows].astype(F32) + projected).astype(BF16)
        layer_out[0, rows] = out
        half = 0.5 * dot_t(pool_query[...], out)
        lane = first_pos + n * block + lax.broadcasted_iota(jnp.int32, half.shape, 1)
        pool_w = jnp.where(lane < length, silu_of_twice(half), 0.0).astype(BF16)
        own_sums[...] += jnp.dot(pool_w, out, preferred_element_type=F32)

    sums = own_sums[...]

    split = width // part.shape[2]
    lanes = part.shape[2]
    for n in range(plane):
        g, c = divmod(n, split)
        part[n] = sums[g : g + 1, c * lanes : (c + 1) * lanes]

    def wait_for(buffer, many, sem):
        some = buffer.at[pl.ds(0, many)]
        pltpu.make_async_copy(some, some, sem).wait()

    for step in STEPS:
        other = plane_device(step)
        pltpu.make_async_remote_copy(
            src_ref=part.at[other],
            dst_ref=parts.at[t],
            send_sem=sum_sem.at[0],
            recv_sem=sum_sem.at[1],
            device_id={"tm": other},
            device_id_type=MESH,
        ).start()

    parts[t] = part[t]
    relay(HEADS + 1)
    wait_for(parts, plane - 1, sum_sem.at[1])
    whole = jnp.sum(parts[...], axis=0).astype(BF16).astype(F32)
    piece[...] = whole
    pieces[user] = whole

    @pl.loop(0, line - 1)
    def _(k):
        pltpu.make_async_remote_copy(
            src_ref=piece,
            dst_ref=pieces.at[user],
            send_sem=state_sem.at[0],
            recv_sem=state_sem.at[1],
            device_id=line_device(k),
            device_id_type=MESH,
        ).start()

    relay(HEADS + 2)
    for copy in twin_copies(across, 2):
        copy.start()
    wait_for(pieces, line - 1, state_sem.at[1])
    mine = owner * owned + lax.broadcasted_iota(jnp.int32, (owned, line), 0)
    picker = jnp.where(slots[...] == mine, 1.0, 0.0).astype(BF16)
    states = pieces[...].reshape(line, lanes).astype(BF16)
    own_states = jnp.dot(picker, states, preferred_element_type=F32)
    chosen[...] = own_states
    interests[t] = own_states

    for step in STEPS:
        pltpu.make_async_remote_copy(
            src_ref=chosen,
            dst_ref=interests.at[t],
            send_sem=pick_sem.at[0],
            recv_sem=pick_sem.at[1],
            device_id={"tm": plane_device(step)},
            device_id_type=MESH,
        ).start()

    for n in range(2):
        for copy in twin_copies((mp, across)[n], 2 * n):
            copy.wait_recv()

    @pl.loop(0, ranks)
    def _(m):
        pre[m] = (
            jnp.dot(cand[...], wr[m, pl.ds(0, width)], preferred_element_type=F32)
            + vectors[m, 0:1]
        )

    wait_for(interests, plane - 1, pick_sem.at[1])

    interest = jnp.concatenate(
        [
            layer_norm(
                jnp.concatenate([interests[g * split + c] for c in range(split)], axis=1)
            )
            for g in range(groups)
        ],
        axis=0,
    ).astype(BF16)
    half = (0.5 * width**-0.5) * dot_t(cand[...], interest)
    row = lax.div(lax.broadcasted_iota(jnp.int32, half.shape, 0), count)
    column = lax.rem(lax.broadcasted_iota(jnp.int32, half.shape, 1), owned)
    attn = jnp.where(row == column, silu_of_twice(half), 0.0)
    high = attn.astype(BF16)
    low = (attn - high.astype(F32)).astype(BF16)
    context = (
        jnp.dot(high, interest, preferred_element_type=F32)
        + jnp.dot(low, interest, preferred_element_type=F32)
    ).astype(BF16)
    cand[...] = context
    terms_of[...] = jnp.zeros_like(terms_of)

    @pl.loop(0, ranks)
    def _(m):
        more = jnp.dot(cand[...], wr[m, pl.ds(width, width)], preferred_element_type=F32)
        terms_of[...] += silu_of_twice(0.5 * (pre[m] + more)) * vectors[m, 1:2]

    terms = terms_of[...]
    high = terms.astype(BF16)
    low = (terms - high.astype(F32)).astype(BF16)
    ones = jnp.ones((16, terms.shape[1]), BF16)
    total = dot_t(ones, high) + dot_t(ones, low)
    for r in range(owned):
        scores[r : r + 1, :] = total[0:1, r * count : (r + 1) * count]

    for rel in range(1, HEADS):
        kv_copy(rel).wait_send()
        q_copy(rel).wait_send()
        back_copy(rel).wait_send()
    for s in range(HEADS):
        for p in (1, 2):
            pass_on(s, p).wait_send()
            pass_half(s, p).wait_send()
    wait_for(parts, plane - 1, sum_sem.at[0])
    wait_for(pieces, line - 1, state_sem.at[0])
    wait_for(interests, plane - 1, pick_sem.at[0])
    for n in range(2):
        for copy in twin_copies((mp, across)[n], 2 * n):
            copy.wait_send()

    @pl.when(near == 0)
    def _():
        for k in range(PARTS):
            send_weights(mp, k, over, over_send).wait_send()
        send_vectors(mp, over, over_send).wait_send()

    @pl.when(near < ends_at)
    def _():
        for k in range(PARTS):
            send_weights(across, k, onward, chain_send).wait_send()
        send_vectors(across, onward, chain_send).wait_send()


def solution(mesh):
    plane, owners, ranks = mesh.shape["tm"], mesh.shape["users"], mesh.shape["mp"]
    line = owners * ranks

    def shards(
        history,
        ln_gain,
        w_proj,
        w_out,
        pool_query,
        lengths,
        slots,
        cand_ids,
        item_table,
        w_rank,
        b_rank,
        w_score,
    ):
        _, events, width = history.shape
        head_size = width // HEADS
        groups = pool_query.shape[0]
        owned, count = cand_ids.shape
        lanes = groups * width // plane
        cands = owned * count
        hidden = w_rank.shape[1]
        vmem = pl.BlockSpec(memory_space=pltpu.VMEM)
        smem = pl.BlockSpec(memory_space=pltpu.SMEM)
        hbm = pl.BlockSpec(memory_space=pltpu.HBM)
        dma = pltpu.SemaphoreType.DMA
        return pl.pallas_call(
            kernel,
            out_shape=(
                jax.ShapeDtypeStruct(history.shape, BF16),
                jax.ShapeDtypeStruct((owned, count), F32),
            ),
            in_specs=[smem] + [hbm] * 11,
            out_specs=(vmem, vmem),
            scratch_shapes=[
                pltpu.VMEM((events, width), BF16),
                pltpu.VMEM((1, width), F32),
                pltpu.VMEM(pool_query.shape, BF16),
                pltpu.VMEM((1, line), jnp.int32),
                pltpu.VMEM((owned, count), jnp.int32),
                pltpu.VMEM((1, hidden), F32),
                pltpu.VMEM((1, hidden), F32),
                pltpu.VMEM((4, width, width), BF16),
                pltpu.VMEM((width, width), BF16),
                pltpu.VMEM(item_table.shape, BF16),
                pltpu.VMEM((ranks, *w_rank.shape), BF16),
                pltpu.VMEM((events, width), BF16),
                pltpu.VMEM((3, events, events), F32),
                pltpu.VMEM((HEADS, 4, events, head_size), BF16),
                pltpu.VMEM((plane, 2, events, head_size), BF16),
                pltpu.VMEM((HEADS, events, head_size), BF16),
                pltpu.VMEM((HEADS * events, head_size), F32),
                pltpu.VMEM((HEADS, events, head_size), BF16),
                pltpu.VMEM((HEADS, events, head_size), BF16),
                pltpu.VMEM((cands, width), BF16),
                pltpu.VMEM((ranks, cands, hidden), F32),
                pltpu.VMEM((plane, 1, lanes), F32),
                pltpu.VMEM((plane, 1, lanes), F32),
                pltpu.VMEM((1, lanes), F32),
                pltpu.VMEM((line, 1, lanes), F32),
                pltpu.VMEM((owned, lanes), F32),
                pltpu.VMEM((plane, owned, lanes), F32),
                pltpu.VMEM((ranks, 2, hidden), F32),
                pltpu.VMEM((groups, width), F32),
                pltpu.VMEM((cands, hidden), F32),
                dma((14,)),
                dma((HEADS,)),
                dma((HEADS,)),
                dma((HEADS,)),
                dma((HEADS,)),
                dma((HEADS, HEADS)),
                dma((HEADS, HEADS)),
                dma((HEADS, HEADS)),
                dma((HEADS, HEADS)),
                dma((HEADS,)),
                dma((HEADS,)),
                dma((2,)),
                dma((2,)),
                dma((2,)),
                dma((PARTS + 1,)),
                dma((PARTS + 1,)),
                dma((PARTS + 1,)),
                dma((4,)),
                dma((4,)),
            ],
            compiler_params=pltpu.CompilerParams(
                collective_id=0, has_side_effects=True, vmem_limit_bytes=VMEM_BYTES
            ),
            cost_estimate=pl.CostEstimate(
                flops=4_000_000_000, bytes_accessed=6_000_000, transcendentals=5_000_000
            ),
        )(
            lengths,
            history,
            ln_gain.reshape(1, -1),
            w_proj,
            w_out,
            pool_query,
            slots.reshape(1, -1),
            cand_ids,
            item_table,
            w_rank,
            b_rank.reshape(1, -1),
            w_score.reshape(1, -1),
        )

    placed = (
        P(("users", "mp"), "tm", None),
        P(),
        P(),
        P(),
        P(),
        P(("users", "mp")),
        P(),
        P("users", "tm"),
        P("users", None),
        P(None, "mp"),
        P("mp"),
        P("mp"),
    )
    return jax.shard_map(
        shards,
        mesh=mesh,
        in_specs=placed,
        out_specs=(P(("users", "mp"), "tm", None), P("users", "tm")),
        check_vma=False,
    )
```

```python
import jax
import jax.numpy as jnp
from jax import lax
from jax.experimental import pallas as pl
from jax.experimental.pallas import tpu as pltpu
from jax.sharding import PartitionSpec as P

HEADS = 4
SIDE = 4
EPS = 1e-05
PARTS = 4
VMEM_BYTES = 64 * 1024 * 1024
MESH = pl.DeviceIdType.MESH
F32 = jnp.float32
BF16 = jnp.bfloat16
ROWS_BY_ROWS = (((1,), (1,)), ((), ()))


def layer_norm(values):
    mean = jnp.mean(values, axis=-1, keepdims=True)
    centred = values - mean
    var = jnp.mean(centred * centred, axis=-1, keepdims=True)
    return centred * lax.rsqrt(var + EPS)


def silu_of_twice(half):
    return half + half * jnp.tanh(half)


def dot_t(a, b, **kw):
    return lax.dot_general(a, b, ROWS_BY_ROWS, preferred_element_type=F32, **kw)


def kernel(
    lengths,
    history,
    ln_gain_hbm,
    w_proj,
    w_out,
    pool_query_hbm,
    slots_hbm,
    cand_ids_hbm,
    item_table,
    w_rank,
    b_rank_hbm,
    w_score_hbm,
    layer_out,
    scores,
    hist,
    ln_gain,
    pool_query,
    slots,
    cand_ids,
    b_rank,
    w_score,
    wp,
    wo,
    table,
    wr,
    normed,
    gate,
    qkv,
    kv,
    qs,
    acc,
    back,
    att,
    cand,
    pre,
    part,
    parts,
    piece,
    columns,
    told,
    pieces,
    chosen,
    interests,
    vectors,
    load_sem,
    kv_send,
    kv_recv,
    q_send,
    q_recv,
    pass_send,
    pass_recv,
    half_send,
    half_recv,
    back_send,
    back_recv,
    sum_sem,
    whole_sem,
    state_sem,
    pick_sem,
    over_send,
    chain_send,
    chain_recv,
    twin_send,
    twin_recv,
):
    events, width = hist.shape
    head_size = width // HEADS
    line, ranks = pieces.shape[0], wr.shape[0]
    t = lax.axis_index("tm")
    owner = lax.axis_index("users")
    mp = lax.axis_index("mp")
    user = owner * ranks + mp
    x, y = lax.div(t, SIDE), lax.rem(t, SIDE)
    core = lax.rem(mp, 2)

    def even(v):
        return v + 1 - 2 * lax.rem(v, 2)

    def odd(v):
        return SIDE - 1 - v

    def swap(v):
        return even(v) + core * (odd(v) - even(v))

    def ring(v):
        return odd(v) + core * (even(v) - odd(v))

    def bit(v):
        first = lax.rem(lax.div(v + 1, 2), 2)
        return first + core * (lax.div(v, 2) - first)

    def head_of(a, b):
        return 2 * bit(a) + bit(b)

    def moved(a, b, rel, flip):
        first, second = lax.rem(rel, 2), lax.div(rel, 2)
        return a + first * (flip(a) - a), b + second * (flip(b) - b)

    def in_plane(a, b):
        return {"tm": a * SIDE + b}

    head = head_of(x, y)

    depth = wr.shape[1] // PARTS
    last = line // ranks - 1
    twin = mp + 1 - 2 * core
    across = lax.rem(mp + 2, ranks)
    near = jnp.minimum(owner, last - owner)
    step_on = jnp.where(owner < near + 1, 1, -1)
    ends_at = last // 2

    def weights_of(whose, k):
        rows = pl.ds(pl.multiple_of(k * depth, depth), depth)
        return wr.at[whose, rows]

    def send_weights(whose, k, to, sems):
        return pltpu.make_async_remote_copy(
            src_ref=weights_of(whose, k),
            dst_ref=weights_of(whose, k),
            send_sem=sems.at[k],
            recv_sem=chain_recv.at[k],
            device_id=to,
            device_id_type=MESH,
        )

    def send_vectors(whose, to, sems):
        return pltpu.make_async_remote_copy(
            src_ref=vectors.at[whose],
            dst_ref=vectors.at[whose],
            send_sem=sems.at[PARTS],
            recv_sem=chain_recv.at[PARTS],
            device_id=to,
            device_id_type=MESH,
        )

    over = {"users": last - owner, "mp": across}
    onward = {"users": owner + step_on}

    def relay(j):
        k = j - near

        @pl.when(jnp.logical_and(k >= 0, k < PARTS))
        def _():
            here = weights_of(across, k)
            pltpu.make_async_copy(here, here, chain_recv.at[k]).wait()

            @pl.when(near < ends_at)
            def _():
                send_weights(across, k, onward, chain_send).start()

            @pl.when(k == PARTS - 1)
            def _():
                here = vectors.at[across]
                pltpu.make_async_copy(here, here, chain_recv.at[PARTS]).wait()

                @pl.when(near < ends_at)
                def _():
                    send_vectors(across, onward, chain_send).start()

    def twin_copies(whose, n):
        return [
            pltpu.make_async_remote_copy(
                src_ref=ref.at[whose],
                dst_ref=ref.at[whose],
                send_sem=twin_send.at[n + m],
                recv_sem=twin_recv.at[n + m],
                device_id={"mp": twin},
                device_id_type=MESH,
            )
            for m, ref in enumerate((wr, vectors))
        ]

    loads = [pltpu.make_async_copy(history.at[0], hist, load_sem.at[0])]
    for n, block in enumerate((3, 1, 2, 0)):
        cols = pl.ds(block * width, width)
        loads.append(pltpu.make_async_copy(w_proj.at[:, cols], wp.at[n], load_sem.at[n + 1]))
    rest = (
        (ln_gain_hbm, ln_gain),
        (pool_query_hbm, pool_query),
        (slots_hbm, slots),
        (cand_ids_hbm, cand_ids),
        (b_rank_hbm, b_rank),
        (w_score_hbm, w_score),
        (w_out, wo),
        (item_table, table),
        (w_rank, wr.at[mp]),
    )
    for n, (src, dst) in enumerate(rest):
        loads.append(pltpu.make_async_copy(src, dst, load_sem.at[5 + n]))
    loads[0].start()
    loads[5].start()
    for load in loads[1:5] + loads[6:]:
        load.start()

    pieces[...] = jnp.zeros_like(pieces)

    barrier = pltpu.get_barrier_semaphore()
    height = line // 2
    low = height // 2
    level = lax.div(mp, 2) * low + owner

    def level_device(k):
        far = lax.div(k + 1, 2)
        chip = lax.rem(low + far * (1 - 2 * lax.rem(k, 2)) + level, height)
        return {"users": lax.rem(chip, low), "mp": 2 * lax.div(chip, low) + core}

    def along(a, b):
        return {"tm": lax.rem(x + a, SIDE) * SIDE + lax.rem(y + b, SIDE)}

    def along_y(b, other):
        return {"tm": x * SIDE + lax.rem(y + b, SIDE), "mp": mp + other * (1 - 2 * core)}

    greeted = [in_plane(*moved(x, y, 3, flip)) for flip in (swap, ring)]
    greeted += [along(a, 0) for a in range(1, SIDE)]
    greeted += [along_y(b, n) for b in range(SIDE) for n in range(2) if b or n]
    for device in greeted:
        pl.semaphore_signal(barrier, inc=1, device_id=device, device_id_type=MESH)

    @pl.loop(0, height - 1)
    def _(k):
        pl.semaphore_signal(barrier, inc=1, device_id=level_device(k), device_id_type=MESH)

    first_pos = t * events
    length = lengths[0]
    pos = first_pos + lax.broadcasted_iota(jnp.int32, (events, 1), 0)
    live = pos < length
    loads[0].wait()
    loads[5].wait()
    normed[...] = (layer_norm(hist[...].astype(F32)) * ln_gain[...]).astype(BF16)

    def project(n):
        loads[n + 1].wait()
        half = 0.5 * jnp.dot(normed[...], wp[n], preferred_element_type=F32)
        return silu_of_twice(half)

    keys = project(0).astype(BF16)
    for h in range(HEADS):
        qkv[h, 0] = keys[:, h * head_size : (h + 1) * head_size]
    values = jnp.where(live, project(1), 0.0).astype(BF16)
    for h in range(HEADS):
        qkv[h, 1] = values[:, h * head_size : (h + 1) * head_size]

    pl.semaphore_wait(barrier, len(greeted) + height - 1)

    kv_copies, q_copies = [], []
    for rel in (3, 2, 1):
        a, b = moved(x, y, rel, swap)
        copy = pltpu.make_async_remote_copy(
            src_ref=qkv.at[head_of(a, b), pl.ds(0, 2)],
            dst_ref=kv.at[rel],
            send_sem=kv_send.at[rel],
            recv_sem=kv_recv.at[rel],
            device_id=in_plane(a, b),
            device_id_type=MESH,
        )
        copy.start()
        kv_copies.append(copy)

    query = project(2).astype(BF16)
    for h in range(HEADS):
        qkv[h, 2] = query[:, h * head_size : (h + 1) * head_size]
    for rel in (3, 2, 1):
        a, b = moved(x, y, rel, swap)
        copy = pltpu.make_async_remote_copy(
            src_ref=qkv.at[head_of(a, b), 2],
            dst_ref=qs.at[rel],
            send_sem=q_send.at[rel],
            recv_sem=q_recv.at[rel],
            device_id=in_plane(a, b),
            device_id_type=MESH,
        )
        copy.start()
        q_copies.append(copy)
    for load in loads[9:11] + loads[13:]:
        load.wait()
    vectors[mp, 0:1] = b_rank[...]
    vectors[mp, 1:2] = w_score[...]

    @pl.when(near == 0)
    def _():
        for k in range(PARTS):
            send_weights(mp, k, over, over_send).start()
        send_vectors(mp, over, over_send).start()

    for copy in twin_copies(mp, 0):
        copy.start()

    kv[0] = qkv[head, pl.ds(0, 2)]
    qs[0] = qkv[head, 2]

    def pass_on(s, p):
        a, b = moved(x, y, p, ring)
        return pltpu.make_async_remote_copy(
            src_ref=kv.at[s],
            dst_ref=kv.at[p * HEADS + s],
            send_sem=pass_send.at[s, p],
            recv_sem=pass_recv.at[s, p],
            device_id=in_plane(a, b),
            device_id_type=MESH,
        )

    def pass_half(s, p):
        a, b = moved(x, y, 3 - p, ring)
        return pltpu.make_async_remote_copy(
            src_ref=kv.at[p * HEADS + s, p - 1],
            dst_ref=kv.at[3 * HEADS + s, p - 1],
            send_sem=half_send.at[s, p],
            recv_sem=half_recv.at[s, p],
            device_id=in_plane(a, b),
            device_id_type=MESH,
        )

    for p in (1, 2):
        pass_on(0, p).start()

    gate[...] = project(3).astype(BF16)
    acc[...] = jnp.zeros_like(acc)

    owned, count = cand_ids.shape
    pool = table.shape[0]
    for load in loads[6:9] + loads[11:13]:
        load.wait()

    @pl.loop(0, owned)
    def _(r):
        @pl.when(r > 0)
        def _():
            pltpu.make_async_copy(kv.at[r], kv.at[r], kv_recv.at[r]).wait()
            for p in (1, 2):
                pass_on(r, p).start()

        eye = lax.broadcasted_iota(jnp.int32, (count, count), 0) == lax.broadcasted_iota(
            jnp.int32, (count, count), 1
        )
        item = lax.broadcasted_iota(jnp.int32, (count, pool), 1).astype(F32)
        ids = cand_ids[pl.ds(r, 1), :].astype(F32)
        column = jnp.sum(jnp.where(eye, ids, 0.0), axis=1, keepdims=True)
        onehot = jnp.where(item == column, 1.0, 0.0).astype(BF16)
        cand[pl.ds(r * count, count)] = jnp.dot(
            onehot, table[...], preferred_element_type=F32
        ).astype(BF16)

    scale = 0.5 * head_size**-0.5

    def time_of(p, s):
        a, b = moved(x, y, p, ring)
        a, b = moved(a, b, s, swap)
        return a * SIDE + b

    def attend(chunk, when, diagonal):
        key, value = kv[chunk, 0], kv[chunk, 1]
        for pair in range(2):
            weights = []
            score = dot_t(qs[pl.ds(2 * pair, 2)].reshape(2 * events, head_size), key)
            for n in range(2):
                now = time_of(0, 2 * pair + n)
                half = score[n * events : (n + 1) * events]
                if diagonal:
                    behind = (
                        lax.broadcasted_iota(jnp.int32, half.shape, 0)
                        - lax.broadcasted_iota(jnp.int32, half.shape, 1)
                        + (now - when) * events
                    )
                    half = jnp.where(behind >= 0, half * scale, 0.0)
                else:
                    half = half * (scale * (now > when).astype(F32))
                weights.append(silu_of_twice(half).astype(BF16))
            weights = jnp.concatenate(weights, axis=0)
            rows = pl.ds(pair * 2 * events, 2 * events)
            acc[rows] += jnp.dot(weights, value, preferred_element_type=F32)

    for copy in q_copies:
        copy.wait_recv()

    @pl.loop(0, HEADS)
    def _(s):
        attend(s, time_of(0, s), True)

    @pl.loop(0, HEADS + 1)
    def _(s):
        @pl.when(s > 0)
        def _():
            relay(s - 1)

        @pl.when(s < HEADS)
        def _():
            @pl.loop(1, 3)
            def _(p):
                pass_on(s, p).wait_recv()
                pass_half(s, p).start()
                attend(p * HEADS + s, time_of(p, s), False)

        @pl.when(s > 0)
        def _():
            for p in (1, 2):
                pass_half(s - 1, p).wait_recv()
            attend(3 * HEADS + s - 1, time_of(3, s - 1), False)

    back_copies = []
    for rel in (3, 2, 1):
        back[rel] = acc[pl.ds(rel * events, events)].astype(BF16)
        a, b = moved(x, y, rel, swap)
        copy = pltpu.make_async_remote_copy(
            src_ref=back.at[rel],
            dst_ref=att.at[head],
            send_sem=back_send.at[rel],
            recv_sem=back_recv.at[rel],
            device_id=in_plane(a, b),
            device_id_type=MESH,
        )
        copy.start()
        back_copies.append(copy)
    att[head] = acc[pl.ds(0, events)].astype(BF16)
    relay(HEADS)
    for copy in back_copies:
        copy.wait_recv()

    attended = jnp.concatenate([att[h] for h in range(HEADS)], axis=1).astype(F32)
    mixed = (layer_norm(attended) * gate[...].astype(F32)).astype(BF16)
    projected = jnp.dot(mixed, wo[...], preferred_element_type=F32)
    out = (hist[...].astype(F32) + projected).astype(BF16)
    layer_out[0] = out
    groups = pool_query.shape[0]
    half = 0.5 * dot_t(pool_query[...], out)
    lane = first_pos + lax.broadcasted_iota(jnp.int32, half.shape, 1)
    pool_w = jnp.where(lane < length, silu_of_twice(half), 0.0).astype(BF16)
    sums = jnp.dot(pool_w, out, preferred_element_type=F32)

    for g in range(groups):
        part[g] = sums[g : g + 1]
    for b in (2, 1, 3):
        other = lax.rem(y + b, SIDE)
        pltpu.make_async_remote_copy(
            src_ref=part.at[other],
            dst_ref=parts.at[y],
            send_sem=sum_sem.at[0],
            recv_sem=sum_sem.at[1],
            device_id=along(0, b),
            device_id_type=MESH,
        ).start()

    def wait_for(buffer, many, sem):
        some = buffer.at[pl.ds(0, many)]
        pltpu.make_async_copy(some, some, sem).wait()

    parts[y] = part[y]
    relay(HEADS + 1)
    wait_for(parts, SIDE - 1, sum_sem.at[1])
    column = jnp.sum(parts[...], axis=0)
    piece[...] = column
    columns[x] = column
    for a in (2, 1, 3):
        pltpu.make_async_remote_copy(
            src_ref=piece,
            dst_ref=columns.at[x],
            send_sem=whole_sem.at[0],
            recv_sem=whole_sem.at[1],
            device_id=along(a, 0),
            device_id_type=MESH,
        ).start()
    wait_for(columns, SIDE - 1, whole_sem.at[1])
    state = jnp.sum(columns[...], axis=0).astype(BF16).astype(F32)

    own_interest = layer_norm(state).astype(BF16).astype(F32)
    told[...] = own_interest
    pieces[user] = own_interest

    @pl.loop(0, height - 1)
    def _(k):
        pltpu.make_async_remote_copy(
            src_ref=told,
            dst_ref=pieces.at[user],
            send_sem=state_sem.at[0],
            recv_sem=state_sem.at[1],
            device_id=level_device(k),
            device_id_type=MESH,
        ).start()

    relay(HEADS + 2)
    for copy in twin_copies(across, 2):
        copy.start()
    wait_for(pieces, height - 1, state_sem.at[1])
    mine = owner * owned + lax.broadcasted_iota(jnp.int32, (owned, line), 0)
    picker = jnp.where(slots[...] == mine, 1.0, 0.0).astype(BF16)
    known = pieces[...].reshape(line, width).astype(BF16)
    own_slots = jnp.dot(picker, known, preferred_element_type=F32)
    chosen[...] = own_slots
    interests[core * SIDE + y] = own_slots
    for b, n in ((2, 0), (2, 1), (1, 0), (3, 0), (1, 1), (3, 1), (0, 1)):
        pltpu.make_async_remote_copy(
            src_ref=chosen,
            dst_ref=interests.at[core * SIDE + y],
            send_sem=pick_sem.at[0],
            recv_sem=pick_sem.at[1],
            device_id=along_y(b, n),
            device_id_type=MESH,
        ).start()

    for n in range(2):
        for copy in twin_copies((mp, across)[n], 2 * n):
            copy.wait_recv()
    for m in range(ranks):
        pre[m] = (
            jnp.dot(cand[...], wr[m, :width], preferred_element_type=F32) + vectors[m, 0:1]
        )
    wait_for(interests, 2 * SIDE - 1, pick_sem.at[1])

    interest = jnp.concatenate(
        [interests[g] + interests[SIDE + g] for g in range(groups)], axis=0
    ).astype(BF16)
    half = (0.5 * width**-0.5) * dot_t(cand[...], interest)
    row = lax.div(lax.broadcasted_iota(jnp.int32, half.shape, 0), count)
    column = lax.rem(lax.broadcasted_iota(jnp.int32, half.shape, 1), owned)
    attn = jnp.where(row == column, silu_of_twice(half), 0.0)
    high = attn.astype(BF16)
    low = (attn - high.astype(F32)).astype(BF16)
    context = (
        jnp.dot(high, interest, preferred_element_type=F32)
        + jnp.dot(low, interest, preferred_element_type=F32)
    ).astype(BF16)
    terms = jnp.zeros_like(pre[0])
    for m in range(ranks):
        half = 0.5 * (pre[m] + jnp.dot(context, wr[m, width:], preferred_element_type=F32))
        terms += silu_of_twice(half) * vectors[m, 1:2]
    high = terms.astype(BF16)
    low = (terms - high.astype(F32)).astype(BF16)
    ones = jnp.ones((16, terms.shape[1]), BF16)
    total = dot_t(ones, high) + dot_t(ones, low)
    for r in range(owned):
        scores[r : r + 1, :] = total[0:1, r * count : (r + 1) * count]

    for copy in kv_copies + q_copies + back_copies:
        copy.wait_send()
    for s in range(HEADS):
        for p in (1, 2):
            pass_on(s, p).wait_send()
            pass_half(s, p).wait_send()
    wait_for(parts, SIDE - 1, sum_sem.at[0])
    wait_for(columns, SIDE - 1, whole_sem.at[0])
    wait_for(pieces, height - 1, state_sem.at[0])
    wait_for(interests, 2 * SIDE - 1, pick_sem.at[0])
    for n in range(2):
        for copy in twin_copies((mp, across)[n], 2 * n):
            copy.wait_send()

    @pl.when(near == 0)
    def _():
        for k in range(PARTS):
            send_weights(mp, k, over, over_send).wait_send()
        send_vectors(mp, over, over_send).wait_send()

    @pl.when(near < ends_at)
    def _():
        for k in range(PARTS):
            send_weights(across, k, onward, chain_send).wait_send()
        send_vectors(across, onward, chain_send).wait_send()


def solution(mesh):
    plane, owners, ranks = mesh.shape["tm"], mesh.shape["users"], mesh.shape["mp"]
    line = owners * ranks

    def shards(
        history,
        ln_gain,
        w_proj,
        w_out,
        pool_query,
        lengths,
        slots,
        cand_ids,
        item_table,
        w_rank,
        b_rank,
        w_score,
    ):
        _, events, width = history.shape
        head_size = width // HEADS
        groups = pool_query.shape[0]
        owned, count = cand_ids.shape
        cands = owned * count
        hidden = w_rank.shape[1]
        vmem = pl.BlockSpec(memory_space=pltpu.VMEM)
        smem = pl.BlockSpec(memory_space=pltpu.SMEM)
        hbm = pl.BlockSpec(memory_space=pltpu.HBM)
        dma = pltpu.SemaphoreType.DMA
        return pl.pallas_call(
            kernel,
            out_shape=(
                jax.ShapeDtypeStruct(history.shape, BF16),
                jax.ShapeDtypeStruct((owned, count), F32),
            ),
            in_specs=[smem] + [hbm] * 11,
            out_specs=(vmem, vmem),
            scratch_shapes=[
                pltpu.VMEM((events, width), BF16),
                pltpu.VMEM((1, width), F32),
                pltpu.VMEM(pool_query.shape, BF16),
                pltpu.VMEM((1, line), jnp.int32),
                pltpu.VMEM((owned, count), jnp.int32),
                pltpu.VMEM((1, hidden), F32),
                pltpu.VMEM((1, hidden), F32),
                pltpu.VMEM((4, width, width), BF16),
                pltpu.VMEM((width, width), BF16),
                pltpu.VMEM(item_table.shape, BF16),
                pltpu.VMEM((ranks, *w_rank.shape), BF16),
                pltpu.VMEM((events, width), BF16),
                pltpu.VMEM((events, width), BF16),
                pltpu.VMEM((HEADS, 3, events, head_size), BF16),
                pltpu.VMEM((plane, 2, events, head_size), BF16),
                pltpu.VMEM((HEADS, events, head_size), BF16),
                pltpu.VMEM((HEADS * events, head_size), F32),
                pltpu.VMEM((HEADS, events, head_size), BF16),
                pltpu.VMEM((HEADS, events, head_size), BF16),
                pltpu.VMEM((cands, width), BF16),
                pltpu.VMEM((ranks, cands, hidden), F32),
                pltpu.VMEM((SIDE, 1, width), F32),
                pltpu.VMEM((SIDE, 1, width), F32),
                pltpu.VMEM((1, width), F32),
                pltpu.VMEM((SIDE, 1, width), F32),
                pltpu.VMEM((1, width), F32),
                pltpu.VMEM((line, 1, width), F32),
                pltpu.VMEM((owned, width), F32),
                pltpu.VMEM((2 * SIDE, owned, width), F32),
                pltpu.VMEM((ranks, 2, hidden), F32),
                dma((14,)),
                dma((HEADS,)),
                dma((HEADS,)),
                dma((HEADS,)),
                dma((HEADS,)),
                dma((HEADS, HEADS)),
                dma((HEADS, HEADS)),
                dma((HEADS, HEADS)),
                dma((HEADS, HEADS)),
                dma((HEADS,)),
                dma((HEADS,)),
                dma((2,)),
                dma((2,)),
                dma((2,)),
                dma((2,)),
                dma((PARTS + 1,)),
                dma((PARTS + 1,)),
                dma((PARTS + 1,)),
                dma((4,)),
                dma((4,)),
            ],
            compiler_params=pltpu.CompilerParams(
                collective_id=0, has_side_effects=True, vmem_limit_bytes=VMEM_BYTES
            ),
            cost_estimate=pl.CostEstimate(
                flops=4_000_000_000, bytes_accessed=6_000_000, transcendentals=5_000_000
            ),
        )(
            lengths,
            history,
            ln_gain.reshape(1, -1),
            w_proj,
            w_out,
            pool_query,
            slots.reshape(1, -1),
            cand_ids,
            item_table,
            w_rank,
            b_rank.reshape(1, -1),
            w_score.reshape(1, -1),
        )

    placed = (
        P(("users", "mp"), "tm", None),
        P(),
        P(),
        P(),
        P(),
        P(("users", "mp")),
        P(),
        P("users", "tm"),
        P("users", None),
        P(None, "mp"),
        P("mp"),
        P("mp"),
    )
    return jax.shard_map(
        shards,
        mesh=mesh,
        in_specs=placed,
        out_specs=(P(("users", "mp"), "tm", None), P("users", "tm")),
        check_vma=False,
    )
```

```python
import jax
import jax.numpy as jnp
from jax import lax
from jax.experimental import pallas as pl
from jax.experimental.pallas import tpu as pltpu
from jax.sharding import PartitionSpec as P

HEADS = 4
SIDE = 4
EPS = 1e-05
PARTS = 4
VMEM_BYTES = 64 * 1024 * 1024
MESH = pl.DeviceIdType.MESH
STEPS = sorted(
    ((a, b) for a in range(SIDE) for b in range(SIDE) if a or b),
    key=lambda step: -sum(min(n, SIDE - n) for n in step),
)
F32 = jnp.float32
BF16 = jnp.bfloat16
ROWS_BY_ROWS = (((1,), (1,)), ((), ()))


def layer_norm(values):
    mean = jnp.mean(values, axis=-1, keepdims=True)
    centred = values - mean
    var = jnp.mean(centred * centred, axis=-1, keepdims=True)
    return centred * lax.rsqrt(var + EPS)


def silu_of_twice(half):
    return half + half * jnp.tanh(half)


def dot_t(a, b, **kw):
    return lax.dot_general(a, b, ROWS_BY_ROWS, preferred_element_type=F32, **kw)


def kernel(
    lengths,
    history,
    ln_gain_hbm,
    w_proj,
    w_out,
    pool_query_hbm,
    slots_hbm,
    cand_ids_hbm,
    item_table,
    w_rank,
    b_rank_hbm,
    w_score_hbm,
    layer_out,
    scores,
    hist,
    ln_gain,
    pool_query,
    slots,
    cand_ids,
    b_rank,
    w_score,
    wp,
    wo,
    table,
    wr,
    normed,
    gate,
    qkv,
    kv,
    qs,
    acc,
    back,
    att,
    given,
    taken,
    masks,
    cand,
    pre,
    part,
    parts,
    piece,
    pieces,
    chosen,
    interests,
    vectors,
    load_sem,
    kv_send,
    kv_recv,
    q_send,
    q_recv,
    pass_send,
    pass_recv,
    back_send,
    back_recv,
    sum_sem,
    state_sem,
    pick_sem,
    over_send,
    chain_send,
    chain_recv,
    twin_send,
    twin_recv,
):
    events, width = hist.shape
    head_size = width // HEADS
    plane, line, ranks = parts.shape[0], pieces.shape[0], wr.shape[0]
    t = lax.axis_index("tm")
    owner = lax.axis_index("users")
    mp = lax.axis_index("mp")
    user = owner * ranks + mp
    x, y = lax.div(t, SIDE), lax.rem(t, SIDE)
    core = lax.rem(mp, 2)

    def even(v):
        return v + 1 - 2 * lax.rem(v, 2)

    def odd(v):
        return SIDE - 1 - v

    def swap_y(v):
        return even(v) + core * (odd(v) - even(v))

    def ring_y(v):
        return odd(v) + core * (even(v) - odd(v))

    def head_of(a, b):
        first = lax.rem(lax.div(b + 1, 2), 2)
        return 2 * lax.div(a, 2) + first + core * (lax.div(b, 2) - first)

    def moved(a, b, rel):
        first, second = lax.rem(rel, 2), lax.div(rel, 2)
        return a + second * (odd(a) - a), b + first * (swap_y(b) - b)

    def in_plane(a, b):
        return {"tm": a * SIDE + b}

    head = head_of(x, y)

    depth = wr.shape[1] // PARTS
    last = line // ranks - 1
    twin = mp + 1 - 2 * core
    across = lax.rem(mp + 2, ranks)
    near = jnp.minimum(owner, last - owner)
    step_on = jnp.where(owner < near + 1, 1, -1)
    ends_at = last // 2

    def weights_of(whose, k):
        rows = pl.ds(pl.multiple_of(k * depth, depth), depth)
        return wr.at[whose, rows]

    def send_weights(whose, k, to, sems):
        return pltpu.make_async_remote_copy(
            src_ref=weights_of(whose, k),
            dst_ref=weights_of(whose, k),
            send_sem=sems.at[k],
            recv_sem=chain_recv.at[k],
            device_id=to,
            device_id_type=MESH,
        )

    def send_vectors(whose, to, sems):
        return pltpu.make_async_remote_copy(
            src_ref=vectors.at[whose],
            dst_ref=vectors.at[whose],
            send_sem=sems.at[PARTS],
            recv_sem=chain_recv.at[PARTS],
            device_id=to,
            device_id_type=MESH,
        )

    over = {"users": last - owner, "mp": across}
    onward = {"users": owner + step_on}

    def relay(j):
        k = j - near

        @pl.when(jnp.logical_and(k >= 0, k < PARTS))
        def _():
            here = weights_of(across, k)
            pltpu.make_async_copy(here, here, chain_recv.at[k]).wait()

            @pl.when(near < ends_at)
            def _():
                send_weights(across, k, onward, chain_send).start()

            @pl.when(k == PARTS - 1)
            def _():
                here = vectors.at[across]
                pltpu.make_async_copy(here, here, chain_recv.at[PARTS]).wait()

                @pl.when(near < ends_at)
                def _():
                    send_vectors(across, onward, chain_send).start()

    def twin_copies(whose, n):
        return [
            pltpu.make_async_remote_copy(
                src_ref=ref.at[whose],
                dst_ref=ref.at[whose],
                send_sem=twin_send.at[n + m],
                recv_sem=twin_recv.at[n + m],
                device_id={"mp": twin},
                device_id_type=MESH,
            )
            for m, ref in enumerate((wr, vectors))
        ]

    loads = [pltpu.make_async_copy(history.at[0], hist, load_sem.at[0])]
    for n, block in enumerate((3, 1, 2, 0)):
        cols = pl.ds(block * width, width)
        loads.append(pltpu.make_async_copy(w_proj.at[:, cols], wp.at[n], load_sem.at[n + 1]))
    rest = (
        (ln_gain_hbm, ln_gain),
        (pool_query_hbm, pool_query),
        (slots_hbm, slots),
        (cand_ids_hbm, cand_ids),
        (b_rank_hbm, b_rank),
        (w_score_hbm, w_score),
        (w_out, wo),
        (item_table, table),
        (w_rank, wr.at[mp]),
    )
    for n, (src, dst) in enumerate(rest):
        loads.append(pltpu.make_async_copy(src, dst, load_sem.at[5 + n]))
    loads[0].start()
    loads[5].start()
    for load in loads[1:5] + loads[6:]:
        load.start()

    barrier = pltpu.get_barrier_semaphore()

    def plane_device(step):
        a, b = step
        return lax.rem(x + a, SIDE) * SIDE + lax.rem(y + b, SIDE)

    height = line // 2
    low = height // 2

    def line_device(k):
        j = lax.div(k, 2)
        far = lax.div(j + 1, 2)
        chip = low + far * (1 - 2 * lax.rem(j, 2)) + lax.div(mp, 2) * low + owner
        chip = lax.rem(chip, height)
        other = lax.rem(core + k + 1, 2)
        return {"users": lax.rem(chip, low), "mp": 2 * lax.div(chip, low) + other}

    @pl.loop(0, line - 1)
    def _(k):
        pl.semaphore_signal(barrier, inc=1, device_id=line_device(k), device_id_type=MESH)

    for step in STEPS:
        pl.semaphore_signal(
            barrier, inc=1, device_id={"tm": plane_device(step)}, device_id_type=MESH
        )

    first_pos = t * events
    length = lengths[0]
    pos = first_pos + lax.broadcasted_iota(jnp.int32, (events, 1), 0)
    live = pos < length
    loads[0].wait()
    loads[5].wait()
    normed[...] = (layer_norm(hist[...].astype(F32)) * ln_gain[...]).astype(BF16)

    def project(n):
        loads[n + 1].wait()
        half = 0.5 * jnp.dot(normed[...], wp[n], preferred_element_type=F32)
        return silu_of_twice(half)

    keys = project(0).astype(BF16)
    for h in range(HEADS):
        qkv[h, 0] = keys[:, h * head_size : (h + 1) * head_size]
    values = jnp.where(live, project(1), 0.0).astype(BF16)
    for h in range(HEADS):
        qkv[h, 1] = values[:, h * head_size : (h + 1) * head_size]

    pl.semaphore_wait(barrier, plane - 1 + line - 1)

    kv_copies, q_copies = [], []
    for rel in (3, 2, 1):
        a, b = moved(x, y, rel)
        copy = pltpu.make_async_remote_copy(
            src_ref=qkv.at[head_of(a, b), pl.ds(0, 2)],
            dst_ref=kv.at[rel],
            send_sem=kv_send.at[rel],
            recv_sem=kv_recv.at[rel],
            device_id=in_plane(a, b),
            device_id_type=MESH,
        )
        copy.start()
        kv_copies.append(copy)

    query = (project(2) * (0.5 * head_size**-0.5)).astype(BF16)
    for h in range(HEADS):
        qkv[h, 2] = query[:, h * head_size : (h + 1) * head_size]
    for rel in (3, 2, 1):
        a, b = moved(x, y, rel)
        copy = pltpu.make_async_remote_copy(
            src_ref=qkv.at[head_of(a, b), 2],
            dst_ref=qs.at[rel],
            send_sem=q_send.at[rel],
            recv_sem=q_recv.at[rel],
            device_id=in_plane(a, b),
            device_id_type=MESH,
        )
        copy.start()
        q_copies.append(copy)
    for load in loads[9:11] + loads[13:]:
        load.wait()
    vectors[mp, 0:1] = b_rank[...]
    vectors[mp, 1:2] = w_score[...]

    @pl.when(near == 0)
    def _():
        for k in range(PARTS):
            send_weights(mp, k, over, over_send).start()
        send_vectors(mp, over, over_send).start()

    for copy in twin_copies(mp, 0):
        copy.start()

    kv[0] = qkv[head, pl.ds(0, 2)]
    qs[0] = qkv[head, 2]

    x_near, y_near = even(x), ring_y(y)

    def pass_kv(n):
        return pltpu.make_async_remote_copy(
            src_ref=kv.at[n],
            dst_ref=kv.at[HEADS + n],
            send_sem=pass_send.at[0, n],
            recv_sem=pass_recv.at[0, n],
            device_id=in_plane(x_near, y),
            device_id_type=MESH,
        )

    def pass_q(n):
        return pltpu.make_async_remote_copy(
            src_ref=qs.at[n],
            dst_ref=qs.at[HEADS + n],
            send_sem=pass_send.at[1, n],
            recv_sem=pass_recv.at[1, n],
            device_id=in_plane(x, y_near),
            device_id_type=MESH,
        )

    def give_sums(n):
        return pltpu.make_async_remote_copy(
            src_ref=given.at[n],
            dst_ref=taken.at[n],
            send_sem=pass_send.at[2, n],
            recv_sem=pass_recv.at[2, n],
            device_id=in_plane(x, y_near),
            device_id_type=MESH,
        )

    pass_q(0).start()
    pass_kv(0).start()

    gate[...] = project(3).astype(BF16)
    acc[...] = jnp.zeros_like(acc)

    owned, count = cand_ids.shape
    pool = table.shape[0]
    for load in loads[6:9] + loads[11:13]:
        load.wait()

    @pl.loop(0, owned)
    def _(r):
        @pl.when(r > 0)
        def _():
            pltpu.make_async_copy(kv.at[r], kv.at[r], kv_recv.at[r]).wait()
            pass_kv(r).start()

        eye = lax.broadcasted_iota(jnp.int32, (count, count), 0) == lax.broadcasted_iota(
            jnp.int32, (count, count), 1
        )
        item = lax.broadcasted_iota(jnp.int32, (count, pool), 1).astype(F32)
        ids = cand_ids[pl.ds(r, 1), :].astype(F32)
        column = jnp.sum(jnp.where(eye, ids, 0.0), axis=1, keepdims=True)
        onehot = jnp.where(item == column, 1.0, 0.0).astype(BF16)
        cand[pl.ds(r * count, count)] = jnp.dot(
            onehot, table[...], preferred_element_type=F32
        ).astype(BF16)

    pairs = 2 * events
    behind = lax.broadcasted_iota(jnp.int32, (events, events), 0) >= lax.broadcasted_iota(
        jnp.int32, (events, events), 1
    )
    masks[0] = jnp.zeros((events, events), F32)
    masks[1] = jnp.where(behind, 1.0, 0.0)
    masks[2] = jnp.ones((events, events), F32)

    def rows_of(which, pair):
        return pl.ds(pl.multiple_of((2 * which + pair) * pairs, pairs), pairs)

    def attend(q_set, q_pair, k_set, k_pair, masked):
        q_first, k_first = HEADS * q_set + 2 * q_pair, HEADS * k_set + 2 * k_pair
        query = qs[pl.ds(q_first, 2)].reshape(pairs, head_size)
        half = jnp.concatenate(
            [dot_t(query, kv[k_first + n, 0]) for n in range(2)], axis=1
        )
        if masked:
            q_y = y_near if q_set else y
            half = jnp.concatenate(
                [
                    jnp.concatenate(
                        [
                            half[a * events : (a + 1) * events, b * events : (b + 1) * events]
                            * masks[1 + jnp.clip(q_row - k_row, -1, 1)]
                            for b, k_row in enumerate((y, swap_y(y)))
                        ],
                        axis=1,
                    )
                    for a, q_row in enumerate((q_y, swap_y(q_y)))
                ],
                axis=0,
            )
        weights = silu_of_twice(half).astype(BF16)
        value = jnp.concatenate([kv[k_first + n, 1] for n in range(2)], axis=0)
        acc[rows_of(q_set, q_pair)] += jnp.dot(weights, value, preferred_element_type=F32)

    late = jnp.where(x < SIDE // 2, 1, 0)
    early = 1 - late
    outer = jnp.logical_or(x == 0, x == SIDE - 1)

    def attend_own(q_set):
        for pair in range(2):
            attend(q_set, pair, 0, pair, True)
        attend(q_set, late, 0, early, False)

    def attend_near(q_set):
        for n in range(2):
            q_pair = late if n else jnp.where(outer, late, early)
            k_pair = jnp.where(outer, n, jnp.where(x == 1, 0, 1))
            attend(q_set, q_pair, 1, k_pair, False)

    for n in range(1, HEADS):
        pltpu.make_async_copy(qs.at[n], qs.at[n], q_recv.at[n]).wait()
        pass_q(n).start()
    attend_own(0)
    relay(0)
    for n in range(HEADS):
        pass_q(n).wait_recv()
    attend_own(1)
    relay(1)
    for n in range(HEADS):
        pass_kv(n).wait_recv()
    attend_near(1)
    for n in range(HEADS):
        given[n] = acc[pl.ds((HEADS + n) * events, events)].astype(BF16)
        give_sums(n).start()
    relay(2)
    attend_near(0)
    relay(3)
    for n in range(HEADS):
        give_sums(n).wait_recv()

    back_copies = []
    for rel in (3, 2, 1):
        rows = pl.ds(rel * events, events)
        back[rel] = (acc[rows] + taken[rel].astype(F32)).astype(BF16)
        a, b = moved(x, y, rel)
        copy = pltpu.make_async_remote_copy(
            src_ref=back.at[rel],
            dst_ref=att.at[head],
            send_sem=back_send.at[rel],
            recv_sem=back_recv.at[rel],
            device_id=in_plane(a, b),
            device_id_type=MESH,
        )
        copy.start()
        back_copies.append(copy)
    att[head] = (acc[pl.ds(0, events)] + taken[0].astype(F32)).astype(BF16)
    relay(HEADS)
    for copy in back_copies:
        copy.wait_recv()

    attended = jnp.concatenate([att[h] for h in range(HEADS)], axis=1).astype(F32)
    mixed = (layer_norm(attended) * gate[...].astype(F32)).astype(BF16)
    projected = jnp.dot(mixed, wo[...], preferred_element_type=F32)
    out = (hist[...].astype(F32) + projected).astype(BF16)
    layer_out[0] = out
    groups = pool_query.shape[0]
    half = 0.5 * dot_t(pool_query[...], out)
    lane = first_pos + lax.broadcasted_iota(jnp.int32, half.shape, 1)
    pool_w = jnp.where(lane < length, silu_of_twice(half), 0.0).astype(BF16)
    sums = jnp.dot(pool_w, out, preferred_element_type=F32)

    split = width // part.shape[2]
    lanes = part.shape[2]
    for n in range(plane):
        g, c = divmod(n, split)
        part[n] = sums[g : g + 1, c * lanes : (c + 1) * lanes]

    def wait_for(buffer, many, sem):
        some = buffer.at[pl.ds(0, many)]
        pltpu.make_async_copy(some, some, sem).wait()

    for step in STEPS:
        other = plane_device(step)
        pltpu.make_async_remote_copy(
            src_ref=part.at[other],
            dst_ref=parts.at[t],
            send_sem=sum_sem.at[0],
            recv_sem=sum_sem.at[1],
            device_id={"tm": other},
            device_id_type=MESH,
        ).start()

    parts[t] = part[t]
    relay(HEADS + 1)
    wait_for(parts, plane - 1, sum_sem.at[1])
    whole = jnp.sum(parts[...], axis=0).astype(BF16).astype(F32)
    piece[...] = whole
    pieces[user] = whole

    @pl.loop(0, line - 1)
    def _(k):
        pltpu.make_async_remote_copy(
            src_ref=piece,
            dst_ref=pieces.at[user],
            send_sem=state_sem.at[0],
            recv_sem=state_sem.at[1],
            device_id=line_device(k),
            device_id_type=MESH,
        ).start()

    relay(HEADS + 2)
    for copy in twin_copies(across, 2):
        copy.start()
    wait_for(pieces, line - 1, state_sem.at[1])
    mine = owner * owned + lax.broadcasted_iota(jnp.int32, (owned, line), 0)
    picker = jnp.where(slots[...] == mine, 1.0, 0.0).astype(BF16)
    states = pieces[...].reshape(line, lanes).astype(BF16)
    own_states = jnp.dot(picker, states, preferred_element_type=F32)
    chosen[...] = own_states
    interests[t] = own_states

    for step in STEPS:
        pltpu.make_async_remote_copy(
            src_ref=chosen,
            dst_ref=interests.at[t],
            send_sem=pick_sem.at[0],
            recv_sem=pick_sem.at[1],
            device_id={"tm": plane_device(step)},
            device_id_type=MESH,
        ).start()

    for n in range(2):
        for copy in twin_copies((mp, across)[n], 2 * n):
            copy.wait_recv()
    for m in range(ranks):
        pre[m] = (
            jnp.dot(cand[...], wr[m, :width], preferred_element_type=F32) + vectors[m, 0:1]
        )
    wait_for(interests, plane - 1, pick_sem.at[1])

    interest = jnp.concatenate(
        [
            layer_norm(
                jnp.concatenate([interests[g * split + c] for c in range(split)], axis=1)
            )
            for g in range(groups)
        ],
        axis=0,
    ).astype(BF16)
    half = (0.5 * width**-0.5) * dot_t(cand[...], interest)
    row = lax.div(lax.broadcasted_iota(jnp.int32, half.shape, 0), count)
    column = lax.rem(lax.broadcasted_iota(jnp.int32, half.shape, 1), owned)
    attn = jnp.where(row == column, silu_of_twice(half), 0.0)
    high = attn.astype(BF16)
    low = (attn - high.astype(F32)).astype(BF16)
    context = (
        jnp.dot(high, interest, preferred_element_type=F32)
        + jnp.dot(low, interest, preferred_element_type=F32)
    ).astype(BF16)
    terms = jnp.zeros_like(pre[0])
    for m in range(ranks):
        half = 0.5 * (pre[m] + jnp.dot(context, wr[m, width:], preferred_element_type=F32))
        terms += silu_of_twice(half) * vectors[m, 1:2]
    high = terms.astype(BF16)
    low = (terms - high.astype(F32)).astype(BF16)
    ones = jnp.ones((16, terms.shape[1]), BF16)
    total = dot_t(ones, high) + dot_t(ones, low)
    for r in range(owned):
        scores[r : r + 1, :] = total[0:1, r * count : (r + 1) * count]

    for copy in kv_copies + q_copies + back_copies:
        copy.wait_send()
    for n in range(HEADS):
        pass_kv(n).wait_send()
        pass_q(n).wait_send()
        give_sums(n).wait_send()
    wait_for(parts, plane - 1, sum_sem.at[0])
    wait_for(pieces, line - 1, state_sem.at[0])
    wait_for(interests, plane - 1, pick_sem.at[0])
    for n in range(2):
        for copy in twin_copies((mp, across)[n], 2 * n):
            copy.wait_send()

    @pl.when(near == 0)
    def _():
        for k in range(PARTS):
            send_weights(mp, k, over, over_send).wait_send()
        send_vectors(mp, over, over_send).wait_send()

    @pl.when(near < ends_at)
    def _():
        for k in range(PARTS):
            send_weights(across, k, onward, chain_send).wait_send()
        send_vectors(across, onward, chain_send).wait_send()


def solution(mesh):
    plane, owners, ranks = mesh.shape["tm"], mesh.shape["users"], mesh.shape["mp"]
    line = owners * ranks

    def shards(
        history,
        ln_gain,
        w_proj,
        w_out,
        pool_query,
        lengths,
        slots,
        cand_ids,
        item_table,
        w_rank,
        b_rank,
        w_score,
    ):
        _, events, width = history.shape
        head_size = width // HEADS
        groups = pool_query.shape[0]
        owned, count = cand_ids.shape
        lanes = groups * width // plane
        cands = owned * count
        hidden = w_rank.shape[1]
        vmem = pl.BlockSpec(memory_space=pltpu.VMEM)
        smem = pl.BlockSpec(memory_space=pltpu.SMEM)
        hbm = pl.BlockSpec(memory_space=pltpu.HBM)
        dma = pltpu.SemaphoreType.DMA
        return pl.pallas_call(
            kernel,
            out_shape=(
                jax.ShapeDtypeStruct(history.shape, BF16),
                jax.ShapeDtypeStruct((owned, count), F32),
            ),
            in_specs=[smem] + [hbm] * 11,
            out_specs=(vmem, vmem),
            scratch_shapes=[
                pltpu.VMEM((events, width), BF16),
                pltpu.VMEM((1, width), F32),
                pltpu.VMEM(pool_query.shape, BF16),
                pltpu.VMEM((1, line), jnp.int32),
                pltpu.VMEM((owned, count), jnp.int32),
                pltpu.VMEM((1, hidden), F32),
                pltpu.VMEM((1, hidden), F32),
                pltpu.VMEM((4, width, width), BF16),
                pltpu.VMEM((width, width), BF16),
                pltpu.VMEM(item_table.shape, BF16),
                pltpu.VMEM((ranks, *w_rank.shape), BF16),
                pltpu.VMEM((events, width), BF16),
                pltpu.VMEM((events, width), BF16),
                pltpu.VMEM((HEADS, 3, events, head_size), BF16),
                pltpu.VMEM((2 * HEADS, 2, events, head_size), BF16),
                pltpu.VMEM((2 * HEADS, events, head_size), BF16),
                pltpu.VMEM((2 * HEADS * events, head_size), F32),
                pltpu.VMEM((HEADS, events, head_size), BF16),
                pltpu.VMEM((HEADS, events, head_size), BF16),
                pltpu.VMEM((HEADS, events, head_size), BF16),
                pltpu.VMEM((HEADS, events, head_size), BF16),
                pltpu.VMEM((3, events, events), F32),
                pltpu.VMEM((cands, width), BF16),
                pltpu.VMEM((ranks, cands, hidden), F32),
                pltpu.VMEM((plane, 1, lanes), F32),
                pltpu.VMEM((plane, 1, lanes), F32),
                pltpu.VMEM((1, lanes), F32),
                pltpu.VMEM((line, 1, lanes), F32),
                pltpu.VMEM((owned, lanes), F32),
                pltpu.VMEM((plane, owned, lanes), F32),
                pltpu.VMEM((ranks, 2, hidden), F32),
                dma((14,)),
                dma((HEADS,)),
                dma((HEADS,)),
                dma((HEADS,)),
                dma((HEADS,)),
                dma((3, HEADS)),
                dma((3, HEADS)),
                dma((HEADS,)),
                dma((HEADS,)),
                dma((2,)),
                dma((2,)),
                dma((2,)),
                dma((PARTS + 1,)),
                dma((PARTS + 1,)),
                dma((PARTS + 1,)),
                dma((4,)),
                dma((4,)),
            ],
            compiler_params=pltpu.CompilerParams(
                collective_id=0, has_side_effects=True, vmem_limit_bytes=VMEM_BYTES
            ),
            cost_estimate=pl.CostEstimate(
                flops=4_000_000_000, bytes_accessed=6_000_000, transcendentals=5_000_000
            ),
        )(
            lengths,
            history,
            ln_gain.reshape(1, -1),
            w_proj,
            w_out,
            pool_query,
            slots.reshape(1, -1),
            cand_ids,
            item_table,
            w_rank,
            b_rank.reshape(1, -1),
            w_score.reshape(1, -1),
        )

    placed = (
        P(("users", "mp"), "tm", None),
        P(),
        P(),
        P(),
        P(),
        P(("users", "mp")),
        P(),
        P("users", "tm"),
        P("users", None),
        P(None, "mp"),
        P("mp"),
        P("mp"),
    )
    return jax.shard_map(
        shards,
        mesh=mesh,
        in_specs=placed,
        out_specs=(P(("users", "mp"), "tm", None), P("users", "tm")),
        check_vma=False,
    )
```

```python
import jax
import jax.numpy as jnp
from jax import lax
from jax.experimental import pallas as pl
from jax.experimental.pallas import tpu as pltpu
from jax.sharding import PartitionSpec as P

HEADS = 4
SIDE = 4
EPS = 1e-05
VMEM_BYTES = 64 * 1024 * 1024
MESH = pl.DeviceIdType.MESH
STEPS = sorted(
    ((a, b) for a in range(SIDE) for b in range(SIDE) if a or b),
    key=lambda step: -sum(min(n, SIDE - n) for n in step),
)
F32 = jnp.float32
BF16 = jnp.bfloat16
ROWS_BY_ROWS = (((1,), (1,)), ((), ()))


def layer_norm(values):
    mean = jnp.mean(values, axis=-1, keepdims=True)
    centred = values - mean
    var = jnp.mean(centred * centred, axis=-1, keepdims=True)
    return centred * lax.rsqrt(var + EPS)


def silu_of_twice(half):
    return half + half * jnp.tanh(half)


def dot_t(a, b, **kw):
    return lax.dot_general(a, b, ROWS_BY_ROWS, preferred_element_type=F32, **kw)


def kernel(
    lengths,
    history,
    ln_gain_hbm,
    w_proj,
    w_out,
    pool_query_hbm,
    slots_hbm,
    cand_ids_hbm,
    item_table,
    w_rank,
    b_rank_hbm,
    w_score_hbm,
    layer_out,
    scores,
    hist,
    ln_gain,
    pool_query,
    slots,
    cand_ids,
    b_rank,
    w_score,
    wp,
    wo,
    table,
    wr,
    normed,
    gate,
    qkv,
    kv,
    qs,
    acc,
    back,
    att,
    given,
    taken,
    masks,
    cand,
    pre,
    part,
    parts,
    piece,
    pieces,
    chosen,
    interests,
    share,
    shares,
    load_sem,
    kv_send,
    kv_recv,
    q_send,
    q_recv,
    pass_send,
    pass_recv,
    back_send,
    back_recv,
    sum_sem,
    state_sem,
    pick_sem,
    share_sem,
):
    events, width = hist.shape
    head_size = width // HEADS
    plane, line, ranks = parts.shape[0], pieces.shape[0], shares.shape[0]
    t = lax.axis_index("tm")
    owner = lax.axis_index("users")
    mp = lax.axis_index("mp")
    user = owner * ranks + mp
    x, y = lax.div(t, SIDE), lax.rem(t, SIDE)
    core = lax.rem(mp, 2)

    def even(v):
        return v + 1 - 2 * lax.rem(v, 2)

    def odd(v):
        return SIDE - 1 - v

    def swap_y(v):
        return even(v) + core * (odd(v) - even(v))

    def ring_y(v):
        return odd(v) + core * (even(v) - odd(v))

    def head_of(a, b):
        first = lax.rem(lax.div(b + 1, 2), 2)
        return 2 * lax.div(a, 2) + first + core * (lax.div(b, 2) - first)

    def moved(a, b, rel):
        first, second = lax.rem(rel, 2), lax.div(rel, 2)
        return a + second * (odd(a) - a), b + first * (swap_y(b) - b)

    def in_plane(a, b):
        return {"tm": a * SIDE + b}

    head = head_of(x, y)

    loads = [pltpu.make_async_copy(history.at[0], hist, load_sem.at[0])]
    for n, block in enumerate((3, 1, 2, 0)):
        cols = pl.ds(block * width, width)
        loads.append(pltpu.make_async_copy(w_proj.at[:, cols], wp.at[n], load_sem.at[n + 1]))
    rest = (
        (ln_gain_hbm, ln_gain),
        (pool_query_hbm, pool_query),
        (slots_hbm, slots),
        (cand_ids_hbm, cand_ids),
        (b_rank_hbm, b_rank),
        (w_score_hbm, w_score),
        (w_out, wo),
        (item_table, table),
        (w_rank, wr),
    )
    for n, (src, dst) in enumerate(rest):
        loads.append(pltpu.make_async_copy(src, dst, load_sem.at[5 + n]))
    loads[0].start()
    loads[5].start()
    for load in loads[1:5] + loads[6:]:
        load.start()

    barrier = pltpu.get_barrier_semaphore()

    def plane_device(step):
        a, b = step
        return lax.rem(x + a, SIDE) * SIDE + lax.rem(y + b, SIDE)

    height = line // 2
    low = height // 2

    def line_device(k):
        j = lax.div(k, 2)
        far = lax.div(j + 1, 2)
        chip = low + far * (1 - 2 * lax.rem(j, 2)) + lax.div(mp, 2) * low + owner
        chip = lax.rem(chip, height)
        other = lax.rem(core + k + 1, 2)
        return {"users": lax.rem(chip, low), "mp": 2 * lax.div(chip, low) + other}

    @pl.loop(0, line - 1)
    def _(k):
        pl.semaphore_signal(barrier, inc=1, device_id=line_device(k), device_id_type=MESH)

    for step in STEPS:
        pl.semaphore_signal(
            barrier, inc=1, device_id={"tm": plane_device(step)}, device_id_type=MESH
        )

    first_pos = t * events
    length = lengths[0]
    pos = first_pos + lax.broadcasted_iota(jnp.int32, (events, 1), 0)
    live = pos < length
    loads[0].wait()
    loads[5].wait()
    normed[...] = (layer_norm(hist[...].astype(F32)) * ln_gain[...]).astype(BF16)

    def project(n):
        loads[n + 1].wait()
        half = 0.5 * jnp.dot(normed[...], wp[n], preferred_element_type=F32)
        return silu_of_twice(half)

    keys = project(0).astype(BF16)
    for h in range(HEADS):
        qkv[h, 0] = keys[:, h * head_size : (h + 1) * head_size]
    values = jnp.where(live, project(1), 0.0).astype(BF16)
    for h in range(HEADS):
        qkv[h, 1] = values[:, h * head_size : (h + 1) * head_size]

    pl.semaphore_wait(barrier, plane - 1 + line - 1)

    kv_copies, q_copies = [], []
    for rel in (3, 2, 1):
        a, b = moved(x, y, rel)
        copy = pltpu.make_async_remote_copy(
            src_ref=qkv.at[head_of(a, b), pl.ds(0, 2)],
            dst_ref=kv.at[rel],
            send_sem=kv_send.at[rel],
            recv_sem=kv_recv.at[rel],
            device_id=in_plane(a, b),
            device_id_type=MESH,
        )
        copy.start()
        kv_copies.append(copy)

    query = (project(2) * (0.5 * head_size**-0.5)).astype(BF16)
    for h in range(HEADS):
        qkv[h, 2] = query[:, h * head_size : (h + 1) * head_size]
    for rel in (3, 2, 1):
        a, b = moved(x, y, rel)
        copy = pltpu.make_async_remote_copy(
            src_ref=qkv.at[head_of(a, b), 2],
            dst_ref=qs.at[rel],
            send_sem=q_send.at[rel],
            recv_sem=q_recv.at[rel],
            device_id=in_plane(a, b),
            device_id_type=MESH,
        )
        copy.start()
        q_copies.append(copy)
    kv[0] = qkv[head, pl.ds(0, 2)]
    qs[0] = qkv[head, 2]

    x_near, y_near = even(x), ring_y(y)

    def pass_kv(n):
        return pltpu.make_async_remote_copy(
            src_ref=kv.at[n],
            dst_ref=kv.at[HEADS + n],
            send_sem=pass_send.at[0, n],
            recv_sem=pass_recv.at[0, n],
            device_id=in_plane(x_near, y),
            device_id_type=MESH,
        )

    def pass_q(n):
        return pltpu.make_async_remote_copy(
            src_ref=qs.at[n],
            dst_ref=qs.at[HEADS + n],
            send_sem=pass_send.at[1, n],
            recv_sem=pass_recv.at[1, n],
            device_id=in_plane(x, y_near),
            device_id_type=MESH,
        )

    def give_sums(n):
        return pltpu.make_async_remote_copy(
            src_ref=given.at[n],
            dst_ref=taken.at[n],
            send_sem=pass_send.at[2, n],
            recv_sem=pass_recv.at[2, n],
            device_id=in_plane(x, y_near),
            device_id_type=MESH,
        )

    pass_q(0).start()
    pass_kv(0).start()

    gate[...] = project(3).astype(BF16)
    acc[...] = jnp.zeros_like(acc)

    owned, count = cand_ids.shape
    pool = table.shape[0]
    for load in loads[6:]:
        load.wait()

    @pl.loop(0, owned)
    def _(r):
        @pl.when(r > 0)
        def _():
            pltpu.make_async_copy(kv.at[r], kv.at[r], kv_recv.at[r]).wait()
            pass_kv(r).start()

        eye = lax.broadcasted_iota(jnp.int32, (count, count), 0) == lax.broadcasted_iota(
            jnp.int32, (count, count), 1
        )
        item = lax.broadcasted_iota(jnp.int32, (count, pool), 1).astype(F32)
        ids = cand_ids[pl.ds(r, 1), :].astype(F32)
        column = jnp.sum(jnp.where(eye, ids, 0.0), axis=1, keepdims=True)
        onehot = jnp.where(item == column, 1.0, 0.0).astype(BF16)
        cand[pl.ds(r * count, count)] = jnp.dot(
            onehot, table[...], preferred_element_type=F32
        ).astype(BF16)

    pre[...] = jnp.dot(cand[...], wr[:width], preferred_element_type=F32) + b_rank[...]

    pairs = 2 * events
    behind = lax.broadcasted_iota(jnp.int32, (events, events), 0) >= lax.broadcasted_iota(
        jnp.int32, (events, events), 1
    )
    masks[0] = jnp.zeros((events, events), F32)
    masks[1] = jnp.where(behind, 1.0, 0.0)
    masks[2] = jnp.ones((events, events), F32)

    def rows_of(which, pair):
        return pl.ds(pl.multiple_of((2 * which + pair) * pairs, pairs), pairs)

    def attend(q_set, q_pair, k_set, k_pair, masked):
        q_first, k_first = HEADS * q_set + 2 * q_pair, HEADS * k_set + 2 * k_pair
        query = qs[pl.ds(q_first, 2)].reshape(pairs, head_size)
        half = jnp.concatenate(
            [dot_t(query, kv[k_first + n, 0]) for n in range(2)], axis=1
        )
        if masked:
            q_y = y_near if q_set else y
            half = jnp.concatenate(
                [
                    jnp.concatenate(
                        [
                            half[a * events : (a + 1) * events, b * events : (b + 1) * events]
                            * masks[1 + jnp.clip(q_row - k_row, -1, 1)]
                            for b, k_row in enumerate((y, swap_y(y)))
                        ],
                        axis=1,
                    )
                    for a, q_row in enumerate((q_y, swap_y(q_y)))
                ],
                axis=0,
            )
        weights = silu_of_twice(half).astype(BF16)
        value = jnp.concatenate([kv[k_first + n, 1] for n in range(2)], axis=0)
        acc[rows_of(q_set, q_pair)] += jnp.dot(weights, value, preferred_element_type=F32)

    late = jnp.where(x < SIDE // 2, 1, 0)
    early = 1 - late
    outer = jnp.logical_or(x == 0, x == SIDE - 1)

    def attend_own(q_set):
        for pair in range(2):
            attend(q_set, pair, 0, pair, True)
        attend(q_set, late, 0, early, False)

    def attend_near(q_set):
        for n in range(2):
            q_pair = late if n else jnp.where(outer, late, early)
            k_pair = jnp.where(outer, n, jnp.where(x == 1, 0, 1))
            attend(q_set, q_pair, 1, k_pair, False)

    for n in range(1, HEADS):
        pltpu.make_async_copy(qs.at[n], qs.at[n], q_recv.at[n]).wait()
        pass_q(n).start()
    attend_own(0)
    for n in range(HEADS):
        pass_q(n).wait_recv()
    attend_own(1)
    for n in range(HEADS):
        pass_kv(n).wait_recv()
    attend_near(1)
    for n in range(HEADS):
        given[n] = acc[pl.ds((HEADS + n) * events, events)].astype(BF16)
        give_sums(n).start()
    attend_near(0)
    for n in range(HEADS):
        give_sums(n).wait_recv()

    back_copies = []
    for rel in (3, 2, 1):
        rows = pl.ds(rel * events, events)
        back[rel] = (acc[rows] + taken[rel].astype(F32)).astype(BF16)
        a, b = moved(x, y, rel)
        copy = pltpu.make_async_remote_copy(
            src_ref=back.at[rel],
            dst_ref=att.at[head],
            send_sem=back_send.at[rel],
            recv_sem=back_recv.at[rel],
            device_id=in_plane(a, b),
            device_id_type=MESH,
        )
        copy.start()
        back_copies.append(copy)
    att[head] = (acc[pl.ds(0, events)] + taken[0].astype(F32)).astype(BF16)
    for copy in back_copies:
        copy.wait_recv()

    attended = jnp.concatenate([att[h] for h in range(HEADS)], axis=1).astype(F32)
    mixed = (layer_norm(attended) * gate[...].astype(F32)).astype(BF16)
    projected = jnp.dot(mixed, wo[...], preferred_element_type=F32)
    out = (hist[...].astype(F32) + projected).astype(BF16)
    layer_out[0] = out
    groups = pool_query.shape[0]
    half = 0.5 * dot_t(pool_query[...], out)
    lane = first_pos + lax.broadcasted_iota(jnp.int32, half.shape, 1)
    pool_w = jnp.where(lane < length, silu_of_twice(half), 0.0).astype(BF16)
    sums = jnp.dot(pool_w, out, preferred_element_type=F32)

    split = width // part.shape[2]
    lanes = part.shape[2]
    for n in range(plane):
        g, c = divmod(n, split)
        part[n] = sums[g : g + 1, c * lanes : (c + 1) * lanes]

    def wait_for(buffer, many, sem):
        some = buffer.at[pl.ds(0, many)]
        pltpu.make_async_copy(some, some, sem).wait()

    for step in STEPS:
        other = plane_device(step)
        pltpu.make_async_remote_copy(
            src_ref=part.at[other],
            dst_ref=parts.at[t],
            send_sem=sum_sem.at[0],
            recv_sem=sum_sem.at[1],
            device_id={"tm": other},
            device_id_type=MESH,
        ).start()

    parts[t] = part[t]
    wait_for(parts, plane - 1, sum_sem.at[1])
    whole = jnp.sum(parts[...], axis=0).astype(BF16).astype(F32)
    piece[...] = whole
    pieces[user] = whole

    @pl.loop(0, line - 1)
    def _(k):
        pltpu.make_async_remote_copy(
            src_ref=piece,
            dst_ref=pieces.at[user],
            send_sem=state_sem.at[0],
            recv_sem=state_sem.at[1],
            device_id=line_device(k),
            device_id_type=MESH,
        ).start()

    wait_for(pieces, line - 1, state_sem.at[1])
    mine = owner * owned + lax.broadcasted_iota(jnp.int32, (owned, line), 0)
    picker = jnp.where(slots[...] == mine, 1.0, 0.0).astype(BF16)
    states = pieces[...].reshape(line, lanes).astype(BF16)
    own_states = jnp.dot(picker, states, preferred_element_type=F32)
    chosen[...] = own_states
    interests[t] = own_states

    for step in STEPS:
        pltpu.make_async_remote_copy(
            src_ref=chosen,
            dst_ref=interests.at[t],
            send_sem=pick_sem.at[0],
            recv_sem=pick_sem.at[1],
            device_id={"tm": plane_device(step)},
            device_id_type=MESH,
        ).start()

    wait_for(interests, plane - 1, pick_sem.at[1])

    interest = jnp.concatenate(
        [
            layer_norm(
                jnp.concatenate([interests[g * split + c] for c in range(split)], axis=1)
            )
            for g in range(groups)
        ],
        axis=0,
    ).astype(BF16)
    half = (0.5 * width**-0.5) * dot_t(cand[...], interest)
    row = lax.div(lax.broadcasted_iota(jnp.int32, half.shape, 0), count)
    column = lax.rem(lax.broadcasted_iota(jnp.int32, half.shape, 1), owned)
    attn = jnp.where(row == column, silu_of_twice(half), 0.0)
    high = attn.astype(BF16)
    low = (attn - high.astype(F32)).astype(BF16)
    context = (
        jnp.dot(high, interest, preferred_element_type=F32)
        + jnp.dot(low, interest, preferred_element_type=F32)
    ).astype(BF16)
    half = 0.5 * (pre[...] + jnp.dot(context, wr[width:], preferred_element_type=F32))
    terms = silu_of_twice(half) * w_score[...]
    high = terms.astype(BF16)
    low = (terms - high.astype(F32)).astype(BF16)
    ones = jnp.ones((16, terms.shape[1]), BF16)
    own_share = (dot_t(ones, high) + dot_t(ones, low))[0:1]
    share[...] = own_share
    shares[mp] = own_share
    for k in (2, 3 - 2 * core, 1 + 2 * core):
        pltpu.make_async_remote_copy(
            src_ref=share,
            dst_ref=shares.at[mp],
            send_sem=share_sem.at[0],
            recv_sem=share_sem.at[1],
            device_id={"mp": lax.rem(mp + k, ranks)},
            device_id_type=MESH,
        ).start()
    wait_for(shares, ranks - 1, share_sem.at[1])
    total = jnp.sum(shares[...], axis=0)
    for r in range(owned):
        scores[r : r + 1, :] = total[0:1, r * count : (r + 1) * count]

    for copy in kv_copies + q_copies + back_copies:
        copy.wait_send()
    for n in range(HEADS):
        pass_kv(n).wait_send()
        pass_q(n).wait_send()
        give_sums(n).wait_send()
    wait_for(parts, plane - 1, sum_sem.at[0])
    wait_for(pieces, line - 1, state_sem.at[0])
    wait_for(interests, plane - 1, pick_sem.at[0])
    wait_for(shares, ranks - 1, share_sem.at[0])


def solution(mesh):
    plane, owners, ranks = mesh.shape["tm"], mesh.shape["users"], mesh.shape["mp"]
    line = owners * ranks

    def shards(
        history,
        ln_gain,
        w_proj,
        w_out,
        pool_query,
        lengths,
        slots,
        cand_ids,
        item_table,
        w_rank,
        b_rank,
        w_score,
    ):
        _, events, width = history.shape
        head_size = width // HEADS
        groups = pool_query.shape[0]
        owned, count = cand_ids.shape
        lanes = groups * width // plane
        cands = owned * count
        hidden = w_rank.shape[1]
        vmem = pl.BlockSpec(memory_space=pltpu.VMEM)
        smem = pl.BlockSpec(memory_space=pltpu.SMEM)
        hbm = pl.BlockSpec(memory_space=pltpu.HBM)
        dma = pltpu.SemaphoreType.DMA
        return pl.pallas_call(
            kernel,
            out_shape=(
                jax.ShapeDtypeStruct(history.shape, BF16),
                jax.ShapeDtypeStruct((owned, count), F32),
            ),
            in_specs=[smem] + [hbm] * 11,
            out_specs=(vmem, vmem),
            scratch_shapes=[
                pltpu.VMEM((events, width), BF16),
                pltpu.VMEM((1, width), F32),
                pltpu.VMEM(pool_query.shape, BF16),
                pltpu.VMEM((1, line), jnp.int32),
                pltpu.VMEM((owned, count), jnp.int32),
                pltpu.VMEM((1, hidden), F32),
                pltpu.VMEM((1, hidden), F32),
                pltpu.VMEM((4, width, width), BF16),
                pltpu.VMEM((width, width), BF16),
                pltpu.VMEM(item_table.shape, BF16),
                pltpu.VMEM(w_rank.shape, BF16),
                pltpu.VMEM((events, width), BF16),
                pltpu.VMEM((events, width), BF16),
                pltpu.VMEM((HEADS, 3, events, head_size), BF16),
                pltpu.VMEM((2 * HEADS, 2, events, head_size), BF16),
                pltpu.VMEM((2 * HEADS, events, head_size), BF16),
                pltpu.VMEM((2 * HEADS * events, head_size), F32),
                pltpu.VMEM((HEADS, events, head_size), BF16),
                pltpu.VMEM((HEADS, events, head_size), BF16),
                pltpu.VMEM((HEADS, events, head_size), BF16),
                pltpu.VMEM((HEADS, events, head_size), BF16),
                pltpu.VMEM((3, events, events), F32),
                pltpu.VMEM((cands, width), BF16),
                pltpu.VMEM((cands, hidden), F32),
                pltpu.VMEM((plane, 1, lanes), F32),
                pltpu.VMEM((plane, 1, lanes), F32),
                pltpu.VMEM((1, lanes), F32),
                pltpu.VMEM((line, 1, lanes), F32),
                pltpu.VMEM((owned, lanes), F32),
                pltpu.VMEM((plane, owned, lanes), F32),
                pltpu.VMEM((1, cands), F32),
                pltpu.VMEM((ranks, 1, cands), F32),
                dma((14,)),
                dma((HEADS,)),
                dma((HEADS,)),
                dma((HEADS,)),
                dma((HEADS,)),
                dma((3, HEADS)),
                dma((3, HEADS)),
                dma((HEADS,)),
                dma((HEADS,)),
                dma((2,)),
                dma((2,)),
                dma((2,)),
                dma((2,)),
            ],
            compiler_params=pltpu.CompilerParams(
                collective_id=0, has_side_effects=True, vmem_limit_bytes=VMEM_BYTES
            ),
            cost_estimate=pl.CostEstimate(
                flops=4_000_000_000, bytes_accessed=6_000_000, transcendentals=5_000_000
            ),
        )(
            lengths,
            history,
            ln_gain.reshape(1, -1),
            w_proj,
            w_out,
            pool_query,
            slots.reshape(1, -1),
            cand_ids,
            item_table,
            w_rank,
            b_rank.reshape(1, -1),
            w_score.reshape(1, -1),
        )

    placed = (
        P(("users", "mp"), "tm", None),
        P(),
        P(),
        P(),
        P(),
        P(("users", "mp")),
        P(),
        P("users", "tm"),
        P("users", None),
        P(None, "mp"),
        P("mp"),
        P("mp"),
    )
    return jax.shard_map(
        shards,
        mesh=mesh,
        in_specs=placed,
        out_specs=(P(("users", "mp"), "tm", None), P("users", "tm")),
        check_vma=False,
    )
```

```python
import jax
import jax.numpy as jnp
from jax import lax
from jax.experimental import pallas as pl
from jax.experimental.pallas import tpu as pltpu
from jax.sharding import PartitionSpec as P

HEADS = 4
SIDE = 4
EPS = 1e-05
PARTS = 8
VMEM_BYTES = 64 * 1024 * 1024
MESH = pl.DeviceIdType.MESH
STEPS = sorted(
    ((a, b) for a in range(SIDE) for b in range(SIDE) if a or b),
    key=lambda step: -sum(min(n, SIDE - n) for n in step),
)
F32 = jnp.float32
BF16 = jnp.bfloat16
ROWS_BY_ROWS = (((1,), (1,)), ((), ()))


def layer_norm(values):
    mean = jnp.mean(values, axis=-1, keepdims=True)
    centred = values - mean
    var = jnp.mean(centred * centred, axis=-1, keepdims=True)
    return centred * lax.rsqrt(var + EPS)


def silu_of_twice(half):
    return half + half * jnp.tanh(half)


def dot_t(a, b, **kw):
    return lax.dot_general(a, b, ROWS_BY_ROWS, preferred_element_type=F32, **kw)


def kernel(
    lengths,
    history,
    ln_gain_hbm,
    w_proj,
    w_out,
    pool_query_hbm,
    slots_hbm,
    cand_ids_hbm,
    item_table,
    w_rank,
    b_rank_hbm,
    w_score_hbm,
    layer_out,
    scores,
    hist,
    ln_gain,
    pool_query,
    slots,
    cand_ids,
    b_rank,
    w_score,
    wp,
    wo,
    table,
    wr,
    normed,
    gate,
    qkv,
    kv,
    qs,
    acc,
    back,
    att,
    masks,
    cand,
    pre,
    part,
    parts,
    piece,
    pieces,
    chosen,
    interests,
    vectors,
    load_sem,
    kv_send,
    kv_recv,
    q_send,
    q_recv,
    pass_send,
    pass_recv,
    back_send,
    back_recv,
    sum_sem,
    state_sem,
    pick_sem,
    over_send,
    chain_send,
    chain_recv,
    twin_send,
    twin_recv,
):
    events, width = hist.shape
    head_size = width // HEADS
    plane, line, ranks = parts.shape[0], pieces.shape[0], wr.shape[0]
    t = lax.axis_index("tm")
    owner = lax.axis_index("users")
    mp = lax.axis_index("mp")
    user = owner * ranks + mp
    x, y = lax.div(t, SIDE), lax.rem(t, SIDE)
    core = lax.rem(mp, 2)

    def even(v):
        return v + 1 - 2 * lax.rem(v, 2)

    def odd(v):
        return SIDE - 1 - v

    def swap_y(v):
        return even(v) + core * (odd(v) - even(v))

    def ring_y(v):
        return odd(v) + core * (even(v) - odd(v))

    def head_of(a, b):
        first = lax.rem(lax.div(b + 1, 2), 2)
        return 2 * lax.div(a, 2) + first + core * (lax.div(b, 2) - first)

    def moved(a, b, rel):
        first, second = lax.rem(rel, 2), lax.div(rel, 2)
        return a + second * (odd(a) - a), b + first * (swap_y(b) - b)

    def in_plane(a, b):
        return {"tm": a * SIDE + b}

    head = head_of(x, y)

    depth = wr.shape[1] // PARTS
    last = line // ranks - 1
    twin = mp + 1 - 2 * core
    across = lax.rem(mp + 2, ranks)
    near = jnp.minimum(owner, last - owner)
    step_on = jnp.where(owner < near + 1, 1, -1)
    ends_at = last // 2

    def weights_of(whose, k):
        rows = pl.ds(pl.multiple_of(k * depth, depth), depth)
        return wr.at[whose, rows]

    def send_weights(whose, k, to, sems):
        return pltpu.make_async_remote_copy(
            src_ref=weights_of(whose, k),
            dst_ref=weights_of(whose, k),
            send_sem=sems.at[k],
            recv_sem=chain_recv.at[k],
            device_id=to,
            device_id_type=MESH,
        )

    def send_vectors(whose, to, sems):
        return pltpu.make_async_remote_copy(
            src_ref=vectors.at[whose],
            dst_ref=vectors.at[whose],
            send_sem=sems.at[PARTS],
            recv_sem=chain_recv.at[PARTS],
            device_id=to,
            device_id_type=MESH,
        )

    over = {"users": last - owner, "mp": across}
    onward = {"users": owner + step_on}

    def relay(j):
        k = j - near

        @pl.when(jnp.logical_and(k >= 0, k < PARTS))
        def _():
            here = weights_of(across, k)
            pltpu.make_async_copy(here, here, chain_recv.at[k]).wait()

            @pl.when(near < ends_at)
            def _():
                send_weights(across, k, onward, chain_send).start()

            @pl.when(k == PARTS - 1)
            def _():
                here = vectors.at[across]
                pltpu.make_async_copy(here, here, chain_recv.at[PARTS]).wait()

                @pl.when(near < ends_at)
                def _():
                    send_vectors(across, onward, chain_send).start()

    def twin_copy(whose, n, sem):
        half = wr.shape[1] // 2
        ref = vectors.at[whose] if n == 2 else wr.at[whose, pl.ds(n * half, half)]
        return pltpu.make_async_remote_copy(
            src_ref=ref,
            dst_ref=ref,
            send_sem=twin_send.at[sem + n],
            recv_sem=twin_recv.at[sem + n],
            device_id={"mp": twin},
            device_id_type=MESH,
        )

    loads = [pltpu.make_async_copy(history.at[0], hist, load_sem.at[0])]
    for n, block in enumerate((3, 1, 2, 0)):
        cols = pl.ds(block * width, width)
        loads.append(pltpu.make_async_copy(w_proj.at[:, cols], wp.at[n], load_sem.at[n + 1]))
    rest = (
        (ln_gain_hbm, ln_gain),
        (pool_query_hbm, pool_query),
        (slots_hbm, slots),
        (cand_ids_hbm, cand_ids),
        (b_rank_hbm, b_rank),
        (w_score_hbm, w_score),
        (w_out, wo),
        (item_table, table),
        (w_rank, wr.at[mp]),
    )
    for n, (src, dst) in enumerate(rest):
        loads.append(pltpu.make_async_copy(src, dst, load_sem.at[5 + n]))
    loads[0].start()
    loads[5].start()
    for load in loads[1:5] + loads[6:]:
        load.start()

    barrier = pltpu.get_barrier_semaphore()

    def plane_device(step):
        a, b = step
        return lax.rem(x + a, SIDE) * SIDE + lax.rem(y + b, SIDE)

    height = line // 2
    low = height // 2

    def line_device(k):
        j = lax.div(k, 2)
        far = lax.div(j + 1, 2)
        chip = low + far * (1 - 2 * lax.rem(j, 2)) + lax.div(mp, 2) * low + owner
        chip = lax.rem(chip, height)
        other = lax.rem(core + k + 1, 2)
        return {"users": lax.rem(chip, low), "mp": 2 * lax.div(chip, low) + other}

    @pl.loop(0, line - 1)
    def _(k):
        pl.semaphore_signal(barrier, inc=1, device_id=line_device(k), device_id_type=MESH)

    for step in STEPS:
        pl.semaphore_signal(
            barrier, inc=1, device_id={"tm": plane_device(step)}, device_id_type=MESH
        )

    first_pos = t * events
    length = lengths[0]
    pos = first_pos + lax.broadcasted_iota(jnp.int32, (events, 1), 0)
    live = pos < length
    loads[0].wait()
    loads[5].wait()
    normed[...] = (layer_norm(hist[...].astype(F32)) * ln_gain[...]).astype(BF16)

    def project(n):
        loads[n + 1].wait()
        half = 0.5 * jnp.dot(normed[...], wp[n], preferred_element_type=F32)
        return silu_of_twice(half)

    keys = project(0).astype(BF16)
    for h in range(HEADS):
        qkv[h, 0] = keys[:, h * head_size : (h + 1) * head_size]
    values = jnp.where(live, project(1), 0.0).astype(BF16)
    for h in range(HEADS):
        qkv[h, 1] = values[:, h * head_size : (h + 1) * head_size]

    pl.semaphore_wait(barrier, plane - 1 + line - 1)

    kv_copies, q_copies = [], []
    for rel in (3, 2, 1):
        a, b = moved(x, y, rel)
        copy = pltpu.make_async_remote_copy(
            src_ref=qkv.at[head_of(a, b), pl.ds(0, 2)],
            dst_ref=kv.at[rel],
            send_sem=kv_send.at[rel],
            recv_sem=kv_recv.at[rel],
            device_id=in_plane(a, b),
            device_id_type=MESH,
        )
        copy.start()
        kv_copies.append(copy)

    query = (project(2) * (0.5 * head_size**-0.5)).astype(BF16)
    for h in range(HEADS):
        qkv[h, 2] = query[:, h * head_size : (h + 1) * head_size]
    for rel in (3, 2, 1):
        a, b = moved(x, y, rel)
        copy = pltpu.make_async_remote_copy(
            src_ref=qkv.at[head_of(a, b), 2],
            dst_ref=qs.at[rel],
            send_sem=q_send.at[rel],
            recv_sem=q_recv.at[rel],
            device_id=in_plane(a, b),
            device_id_type=MESH,
        )
        copy.start()
        q_copies.append(copy)
    for load in loads[9:11] + loads[13:]:
        load.wait()
    vectors[mp, 0:1] = b_rank[...]
    vectors[mp, 1:2] = w_score[...]

    @pl.when(near == 0)
    def _():
        for k in range(PARTS):
            send_weights(mp, k, over, over_send).start()
        send_vectors(mp, over, over_send).start()

    for n in range(3):
        twin_copy(mp, n, 0).start()

    kv[0] = qkv[head, pl.ds(0, 2)]
    qs[0] = qkv[head, 2]

    x_near, y_near = even(x), ring_y(y)

    def pass_kv(n):
        return pltpu.make_async_remote_copy(
            src_ref=kv.at[n],
            dst_ref=kv.at[HEADS + n],
            send_sem=pass_send.at[0, n],
            recv_sem=pass_recv.at[0, n],
            device_id=in_plane(x_near, y),
            device_id_type=MESH,
        )

    def pass_q(n):
        return pltpu.make_async_remote_copy(
            src_ref=qs.at[n],
            dst_ref=qs.at[HEADS + n],
            send_sem=pass_send.at[1, n],
            recv_sem=pass_recv.at[1, n],
            device_id=in_plane(x, y_near),
            device_id_type=MESH,
        )

    def back_copy(n, which):
        a, b = moved(x, y_near if which else y, n)
        return pltpu.make_async_remote_copy(
            src_ref=back.at[which, n],
            dst_ref=att.at[which, head],
            send_sem=back_send.at[which, n],
            recv_sem=back_recv.at[which, n],
            device_id=in_plane(a, b),
            device_id_type=MESH,
        )

    pass_q(0).start()
    pass_kv(0).start()

    gate[...] = project(3).astype(BF16)
    acc[...] = jnp.zeros_like(acc)

    owned, count = cand_ids.shape
    pool = table.shape[0]
    for load in loads[6:9] + loads[11:13]:
        load.wait()

    @pl.loop(0, owned)
    def _(r):
        @pl.when(r > 0)
        def _():
            pltpu.make_async_copy(kv.at[r], kv.at[r], kv_recv.at[r]).wait()
            pass_kv(r).start()

        eye = lax.broadcasted_iota(jnp.int32, (count, count), 0) == lax.broadcasted_iota(
            jnp.int32, (count, count), 1
        )
        item = lax.broadcasted_iota(jnp.int32, (count, pool), 1).astype(F32)
        ids = cand_ids[pl.ds(r, 1), :].astype(F32)
        column = jnp.sum(jnp.where(eye, ids, 0.0), axis=1, keepdims=True)
        onehot = jnp.where(item == column, 1.0, 0.0).astype(BF16)
        cand[pl.ds(r * count, count)] = jnp.dot(
            onehot, table[...], preferred_element_type=F32
        ).astype(BF16)

    pairs = 2 * events
    behind = lax.broadcasted_iota(jnp.int32, (events, events), 0) >= lax.broadcasted_iota(
        jnp.int32, (events, events), 1
    )
    masks[0] = jnp.zeros((events, events), F32)
    masks[1] = jnp.where(behind, 1.0, 0.0)
    masks[2] = jnp.ones((events, events), F32)

    def rows_of(which, pair):
        return pl.ds(pl.multiple_of((2 * which + pair) * pairs, pairs), pairs)

    def attend(q_set, q_pair, k_set, k_pair, masked):
        q_first, k_first = HEADS * q_set + 2 * q_pair, HEADS * k_set + 2 * k_pair
        query = qs[pl.ds(q_first, 2)].reshape(pairs, head_size)
        half = jnp.concatenate(
            [dot_t(query, kv[k_first + n, 0]) for n in range(2)], axis=1
        )
        if masked:
            q_y = y_near if q_set else y
            half = jnp.concatenate(
                [
                    jnp.concatenate(
                        [
                            half[a * events : (a + 1) * events, b * events : (b + 1) * events]
                            * masks[1 + jnp.clip(q_row - k_row, -1, 1)]
                            for b, k_row in enumerate((y, swap_y(y)))
                        ],
                        axis=1,
                    )
                    for a, q_row in enumerate((q_y, swap_y(q_y)))
                ],
                axis=0,
            )
        weights = silu_of_twice(half).astype(BF16)
        value = jnp.concatenate([kv[k_first + n, 1] for n in range(2)], axis=0)
        acc[rows_of(q_set, q_pair)] += jnp.dot(weights, value, preferred_element_type=F32)

    late = jnp.where(x < SIDE // 2, 1, 0)
    early = 1 - late
    outer = jnp.logical_or(x == 0, x == SIDE - 1)

    def attend_own(q_set):
        for pair in range(2):
            attend(q_set, pair, 0, pair, True)
        attend(q_set, late, 0, early, False)

    def attend_near(q_set, n):
        q_pair = late if n else jnp.where(outer, late, early)
        k_pair = jnp.where(outer, n, jnp.where(x == 1, 0, 1))
        attend(q_set, q_pair, 1, k_pair, False)

    for n in range(1, HEADS):
        pltpu.make_async_copy(qs.at[n], qs.at[n], q_recv.at[n]).wait()
        pass_q(n).start()
    attend_own(0)
    relay(0)
    for n in range(HEADS):
        pass_q(n).wait_recv()
    attend(1, 0, 0, 0, True)
    relay(1)
    attend(1, 1, 0, 1, True)
    relay(2)
    attend(1, late, 0, early, False)
    relay(3)
    for n in range(HEADS):
        pass_kv(n).wait_recv()
    attend_near(1, 0)
    attend_near(1, 1)
    for n in (3, 2, 1, 0):
        back[1, n] = acc[pl.ds((HEADS + n) * events, events)].astype(BF16)
        back_copy(n, 1).start()
    relay(4)
    attend_near(0, 0)
    relay(5)
    attend_near(0, 1)

    for n in (3, 2, 1):
        back[0, n] = acc[pl.ds(n * events, events)].astype(BF16)
        back_copy(n, 0).start()
    att[0, head] = acc[pl.ds(0, events)].astype(BF16)
    relay(6)
    relay(7)
    twin_copy(across, 0, 3).start()
    for n in range(HEADS):
        back_copy(n, 1).wait_recv()
    for n in range(1, HEADS):
        back_copy(n, 0).wait_recv()
    relay(8)

    attended = jnp.concatenate(
        [att[0, h].astype(F32) + att[1, h].astype(F32) for h in range(HEADS)], axis=1
    )
    mixed = (layer_norm(attended) * gate[...].astype(F32)).astype(BF16)
    projected = jnp.dot(mixed, wo[...], preferred_element_type=F32)
    out = (hist[...].astype(F32) + projected).astype(BF16)
    layer_out[0] = out
    groups = pool_query.shape[0]
    half = 0.5 * dot_t(pool_query[...], out)
    lane = first_pos + lax.broadcasted_iota(jnp.int32, half.shape, 1)
    pool_w = jnp.where(lane < length, silu_of_twice(half), 0.0).astype(BF16)
    sums = jnp.dot(pool_w, out, preferred_element_type=F32)

    split = width // part.shape[2]
    lanes = part.shape[2]
    for n in range(plane):
        g, c = divmod(n, split)
        part[n] = sums[g : g + 1, c * lanes : (c + 1) * lanes]

    def wait_for(buffer, many, sem):
        some = buffer.at[pl.ds(0, many)]
        pltpu.make_async_copy(some, some, sem).wait()

    for step in STEPS:
        other = plane_device(step)
        pltpu.make_async_remote_copy(
            src_ref=part.at[other],
            dst_ref=parts.at[t],
            send_sem=sum_sem.at[0],
            recv_sem=sum_sem.at[1],
            device_id={"tm": other},
            device_id_type=MESH,
        ).start()

    parts[t] = part[t]
    relay(9)
    wait_for(parts, plane - 1, sum_sem.at[1])
    whole = jnp.sum(parts[...], axis=0).astype(BF16).astype(F32)
    piece[...] = whole
    pieces[user] = whole

    @pl.loop(0, line - 1)
    def _(k):
        pltpu.make_async_remote_copy(
            src_ref=piece,
            dst_ref=pieces.at[user],
            send_sem=state_sem.at[0],
            recv_sem=state_sem.at[1],
            device_id=line_device(k),
            device_id_type=MESH,
        ).start()

    relay(10)
    twin_copy(across, 1, 3).start()
    twin_copy(across, 2, 3).start()
    wait_for(pieces, line - 1, state_sem.at[1])
    mine = owner * owned + lax.broadcasted_iota(jnp.int32, (owned, line), 0)
    picker = jnp.where(slots[...] == mine, 1.0, 0.0).astype(BF16)
    states = pieces[...].reshape(line, lanes).astype(BF16)
    own_states = jnp.dot(picker, states, preferred_element_type=F32)
    chosen[...] = own_states
    interests[t] = own_states

    for step in STEPS:
        pltpu.make_async_remote_copy(
            src_ref=chosen,
            dst_ref=interests.at[t],
            send_sem=pick_sem.at[0],
            recv_sem=pick_sem.at[1],
            device_id={"tm": plane_device(step)},
            device_id_type=MESH,
        ).start()

    for n in range(3):
        twin_copy(mp, n, 0).wait_recv()
        twin_copy(across, n, 3).wait_recv()
    for m in range(ranks):
        pre[m] = (
            jnp.dot(cand[...], wr[m, :width], preferred_element_type=F32) + vectors[m, 0:1]
        )
    wait_for(interests, plane - 1, pick_sem.at[1])

    interest = jnp.concatenate(
        [
            layer_norm(
                jnp.concatenate([interests[g * split + c] for c in range(split)], axis=1)
            )
            for g in range(groups)
        ],
        axis=0,
    ).astype(BF16)
    half = (0.5 * width**-0.5) * dot_t(cand[...], interest)
    row = lax.div(lax.broadcasted_iota(jnp.int32, half.shape, 0), count)
    column = lax.rem(lax.broadcasted_iota(jnp.int32, half.shape, 1), owned)
    attn = jnp.where(row == column, silu_of_twice(half), 0.0)
    high = attn.astype(BF16)
    low = (attn - high.astype(F32)).astype(BF16)
    context = (
        jnp.dot(high, interest, preferred_element_type=F32)
        + jnp.dot(low, interest, preferred_element_type=F32)
    ).astype(BF16)
    terms = jnp.zeros_like(pre[0])
    for m in range(ranks):
        half = 0.5 * (pre[m] + jnp.dot(context, wr[m, width:], preferred_element_type=F32))
        terms += silu_of_twice(half) * vectors[m, 1:2]
    high = terms.astype(BF16)
    low = (terms - high.astype(F32)).astype(BF16)
    ones = jnp.ones((16, terms.shape[1]), BF16)
    total = dot_t(ones, high) + dot_t(ones, low)
    for r in range(owned):
        scores[r : r + 1, :] = total[0:1, r * count : (r + 1) * count]

    for copy in kv_copies + q_copies:
        copy.wait_send()
    for n in range(HEADS):
        pass_kv(n).wait_send()
        pass_q(n).wait_send()
        back_copy(n, 1).wait_send()
    for n in range(1, HEADS):
        back_copy(n, 0).wait_send()
    wait_for(parts, plane - 1, sum_sem.at[0])
    wait_for(pieces, line - 1, state_sem.at[0])
    wait_for(interests, plane - 1, pick_sem.at[0])
    for n in range(3):
        twin_copy(mp, n, 0).wait_send()
        twin_copy(across, n, 3).wait_send()

    @pl.when(near == 0)
    def _():
        for k in range(PARTS):
            send_weights(mp, k, over, over_send).wait_send()
        send_vectors(mp, over, over_send).wait_send()

    @pl.when(near < ends_at)
    def _():
        for k in range(PARTS):
            send_weights(across, k, onward, chain_send).wait_send()
        send_vectors(across, onward, chain_send).wait_send()


def solution(mesh):
    plane, owners, ranks = mesh.shape["tm"], mesh.shape["users"], mesh.shape["mp"]
    line = owners * ranks

    def shards(
        history,
        ln_gain,
        w_proj,
        w_out,
        pool_query,
        lengths,
        slots,
        cand_ids,
        item_table,
        w_rank,
        b_rank,
        w_score,
    ):
        _, events, width = history.shape
        head_size = width // HEADS
        groups = pool_query.shape[0]
        owned, count = cand_ids.shape
        lanes = groups * width // plane
        cands = owned * count
        hidden = w_rank.shape[1]
        vmem = pl.BlockSpec(memory_space=pltpu.VMEM)
        smem = pl.BlockSpec(memory_space=pltpu.SMEM)
        hbm = pl.BlockSpec(memory_space=pltpu.HBM)
        dma = pltpu.SemaphoreType.DMA
        return pl.pallas_call(
            kernel,
            out_shape=(
                jax.ShapeDtypeStruct(history.shape, BF16),
                jax.ShapeDtypeStruct((owned, count), F32),
            ),
            in_specs=[smem] + [hbm] * 11,
            out_specs=(vmem, vmem),
            scratch_shapes=[
                pltpu.VMEM((events, width), BF16),
                pltpu.VMEM((1, width), F32),
                pltpu.VMEM(pool_query.shape, BF16),
                pltpu.VMEM((1, line), jnp.int32),
                pltpu.VMEM((owned, count), jnp.int32),
                pltpu.VMEM((1, hidden), F32),
                pltpu.VMEM((1, hidden), F32),
                pltpu.VMEM((4, width, width), BF16),
                pltpu.VMEM((width, width), BF16),
                pltpu.VMEM(item_table.shape, BF16),
                pltpu.VMEM((ranks, *w_rank.shape), BF16),
                pltpu.VMEM((events, width), BF16),
                pltpu.VMEM((events, width), BF16),
                pltpu.VMEM((HEADS, 3, events, head_size), BF16),
                pltpu.VMEM((2 * HEADS, 2, events, head_size), BF16),
                pltpu.VMEM((2 * HEADS, events, head_size), BF16),
                pltpu.VMEM((2 * HEADS * events, head_size), F32),
                pltpu.VMEM((2, HEADS, events, head_size), BF16),
                pltpu.VMEM((2, HEADS, events, head_size), BF16),
                pltpu.VMEM((3, events, events), F32),
                pltpu.VMEM((cands, width), BF16),
                pltpu.VMEM((ranks, cands, hidden), F32),
                pltpu.VMEM((plane, 1, lanes), F32),
                pltpu.VMEM((plane, 1, lanes), F32),
                pltpu.VMEM((1, lanes), F32),
                pltpu.VMEM((line, 1, lanes), F32),
                pltpu.VMEM((owned, lanes), F32),
                pltpu.VMEM((plane, owned, lanes), F32),
                pltpu.VMEM((ranks, 2, hidden), F32),
                dma((14,)),
                dma((HEADS,)),
                dma((HEADS,)),
                dma((HEADS,)),
                dma((HEADS,)),
                dma((2, HEADS)),
                dma((2, HEADS)),
                dma((2, HEADS)),
                dma((2, HEADS)),
                dma((2,)),
                dma((2,)),
                dma((2,)),
                dma((PARTS + 1,)),
                dma((PARTS + 1,)),
                dma((PARTS + 1,)),
                dma((6,)),
                dma((6,)),
            ],
            compiler_params=pltpu.CompilerParams(
                collective_id=0, has_side_effects=True, vmem_limit_bytes=VMEM_BYTES
            ),
            cost_estimate=pl.CostEstimate(
                flops=4_000_000_000, bytes_accessed=6_000_000, transcendentals=5_000_000
            ),
        )(
            lengths,
            history,
            ln_gain.reshape(1, -1),
            w_proj,
            w_out,
            pool_query,
            slots.reshape(1, -1),
            cand_ids,
            item_table,
            w_rank,
            b_rank.reshape(1, -1),
            w_score.reshape(1, -1),
        )

    placed = (
        P(("users", "mp"), "tm", None),
        P(),
        P(),
        P(),
        P(),
        P(("users", "mp")),
        P(),
        P("users", "tm"),
        P("users", None),
        P(None, "mp"),
        P("mp"),
        P("mp"),
    )
    return jax.shard_map(
        shards,
        mesh=mesh,
        in_specs=placed,
        out_specs=(P(("users", "mp"), "tm", None), P("users", "tm")),
        check_vma=False,
    )
```

```python
import jax
import jax.numpy as jnp
from jax import lax
from jax.experimental import pallas as pl
from jax.experimental.pallas import tpu as pltpu
from jax.sharding import PartitionSpec as P

HEADS = 4
SIDE = 4
EPS = 1e-05
PARTS = 4
VMEM_BYTES = 64 * 1024 * 1024
MESH = pl.DeviceIdType.MESH
STEPS = sorted(
    ((a, b) for a in range(SIDE) for b in range(SIDE) if a or b),
    key=lambda step: -sum(min(n, SIDE - n) for n in step),
)
F32 = jnp.float32
BF16 = jnp.bfloat16
ROWS_BY_ROWS = (((1,), (1,)), ((), ()))


def layer_norm(values):
    mean = jnp.mean(values, axis=-1, keepdims=True)
    centred = values - mean
    var = jnp.mean(centred * centred, axis=-1, keepdims=True)
    return centred * lax.rsqrt(var + EPS)


def silu_of_twice(half):
    return half + half * jnp.tanh(half)


def dot_t(a, b, **kw):
    return lax.dot_general(a, b, ROWS_BY_ROWS, preferred_element_type=F32, **kw)


def kernel(
    lengths,
    history,
    ln_gain_hbm,
    w_proj,
    w_out,
    pool_query_hbm,
    slots_hbm,
    cand_ids_hbm,
    item_table,
    w_rank,
    b_rank_hbm,
    w_score_hbm,
    layer_out,
    scores,
    hist,
    ln_gain,
    pool_query,
    slots,
    cand_ids,
    b_rank,
    w_score,
    wp,
    wo,
    table,
    wr,
    normed,
    gate,
    qkv,
    kv,
    qs,
    acc,
    back,
    att,
    cand,
    pre,
    part,
    parts,
    piece,
    pieces,
    chosen,
    interests,
    vectors,
    share,
    shares,
    load_sem,
    kv_send,
    kv_recv,
    q_send,
    q_recv,
    pass_send,
    pass_recv,
    half_send,
    half_recv,
    back_send,
    back_recv,
    sum_sem,
    state_sem,
    pick_sem,
    over_send,
    chain_send,
    chain_recv,
    twin_sem,
):
    events, width = hist.shape
    head_size = width // HEADS
    plane, line, ranks = parts.shape[0], pieces.shape[0], wr.shape[0]
    t = lax.axis_index("tm")
    owner = lax.axis_index("users")
    mp = lax.axis_index("mp")
    user = owner * ranks + mp
    x, y = lax.div(t, SIDE), lax.rem(t, SIDE)
    core = lax.rem(mp, 2)

    def even(v):
        return v + 1 - 2 * lax.rem(v, 2)

    def odd(v):
        return SIDE - 1 - v

    def swap(v):
        return even(v) + core * (odd(v) - even(v))

    def ring(v):
        return odd(v) + core * (even(v) - odd(v))

    def bit(v):
        first = lax.rem(lax.div(v + 1, 2), 2)
        return first + core * (lax.div(v, 2) - first)

    def head_of(a, b):
        return 2 * bit(a) + bit(b)

    def moved(a, b, rel, flip):
        first, second = lax.rem(rel, 2), lax.div(rel, 2)
        return a + first * (flip(a) - a), b + second * (flip(b) - b)

    def in_plane(a, b):
        return {"tm": a * SIDE + b}

    head = head_of(x, y)

    depth = wr.shape[1] // PARTS
    last = line // ranks - 1
    twin = mp + 1 - 2 * core
    across = lax.rem(mp + 2, ranks)
    near = jnp.minimum(owner, last - owner)
    step_on = jnp.where(owner < near + 1, 1, -1)
    ends_at = last // 2

    def weights_of(whose, k):
        rows = pl.ds(pl.multiple_of(k * depth, depth), depth)
        return wr.at[whose, rows]

    def send_weights(whose, k, to, sems):
        return pltpu.make_async_remote_copy(
            src_ref=weights_of(whose, k),
            dst_ref=weights_of(whose, k),
            send_sem=sems.at[k],
            recv_sem=chain_recv.at[k],
            device_id=to,
            device_id_type=MESH,
        )

    def send_vectors(whose, to, sems):
        return pltpu.make_async_remote_copy(
            src_ref=vectors.at[whose],
            dst_ref=vectors.at[whose],
            send_sem=sems.at[PARTS],
            recv_sem=chain_recv.at[PARTS],
            device_id=to,
            device_id_type=MESH,
        )

    over = {"users": last - owner, "mp": across}
    onward = {"users": owner + step_on}

    def relay(j):
        k = j - near

        @pl.when(jnp.logical_and(k >= 0, k < PARTS))
        def _():
            here = weights_of(across, k)
            pltpu.make_async_copy(here, here, chain_recv.at[k]).wait()

            @pl.when(near < ends_at)
            def _():
                send_weights(across, k, onward, chain_send).start()

            @pl.when(k == PARTS - 1)
            def _():
                here = vectors.at[across]
                pltpu.make_async_copy(here, here, chain_recv.at[PARTS]).wait()

                @pl.when(near < ends_at)
                def _():
                    send_vectors(across, onward, chain_send).start()

    loads = [pltpu.make_async_copy(history.at[0], hist, load_sem.at[0])]
    for n, block in enumerate((3, 1, 2, 0)):
        cols = pl.ds(block * width, width)
        loads.append(pltpu.make_async_copy(w_proj.at[:, cols], wp.at[n], load_sem.at[n + 1]))
    rest = (
        (ln_gain_hbm, ln_gain),
        (pool_query_hbm, pool_query),
        (slots_hbm, slots),
        (cand_ids_hbm, cand_ids),
        (b_rank_hbm, b_rank),
        (w_score_hbm, w_score),
        (w_out, wo),
        (item_table, table),
        (w_rank, wr.at[mp]),
    )
    for n, (src, dst) in enumerate(rest):
        loads.append(pltpu.make_async_copy(src, dst, load_sem.at[5 + n]))
    loads[0].start()
    loads[5].start()
    for load in loads[1:5] + loads[6:]:
        load.start()

    barrier = pltpu.get_barrier_semaphore()

    def plane_device(step):
        a, b = step
        return lax.rem(x + a, SIDE) * SIDE + lax.rem(y + b, SIDE)

    height = line // 2
    low = height // 2

    def line_device(k):
        j = lax.div(k, 2)
        far = lax.div(j + 1, 2)
        chip = low + far * (1 - 2 * lax.rem(j, 2)) + lax.div(mp, 2) * low + owner
        chip = lax.rem(chip, height)
        other = lax.rem(core + k + 1, 2)
        return {"users": lax.rem(chip, low), "mp": 2 * lax.div(chip, low) + other}

    @pl.loop(0, line - 1)
    def _(k):
        pl.semaphore_signal(barrier, inc=1, device_id=line_device(k), device_id_type=MESH)

    for step in STEPS:
        pl.semaphore_signal(
            barrier, inc=1, device_id={"tm": plane_device(step)}, device_id_type=MESH
        )

    first_pos = t * events
    length = lengths[0]
    pos = first_pos + lax.broadcasted_iota(jnp.int32, (events, 1), 0)
    live = pos < length
    loads[0].wait()
    loads[5].wait()
    normed[...] = (layer_norm(hist[...].astype(F32)) * ln_gain[...]).astype(BF16)

    def project(n):
        loads[n + 1].wait()
        half = 0.5 * jnp.dot(normed[...], wp[n], preferred_element_type=F32)
        return silu_of_twice(half)

    keys = project(0).astype(BF16)
    for h in range(HEADS):
        qkv[h, 0] = keys[:, h * head_size : (h + 1) * head_size]
    values = jnp.where(live, project(1), 0.0).astype(BF16)
    for h in range(HEADS):
        qkv[h, 1] = values[:, h * head_size : (h + 1) * head_size]

    pl.semaphore_wait(barrier, plane - 1 + line - 1)

    kv_copies, q_copies = [], []
    for rel in (3, 2, 1):
        a, b = moved(x, y, rel, swap)
        copy = pltpu.make_async_remote_copy(
            src_ref=qkv.at[head_of(a, b), pl.ds(0, 2)],
            dst_ref=kv.at[rel],
            send_sem=kv_send.at[rel],
            recv_sem=kv_recv.at[rel],
            device_id=in_plane(a, b),
            device_id_type=MESH,
        )
        copy.start()
        kv_copies.append(copy)

    query = project(2).astype(BF16)
    for h in range(HEADS):
        qkv[h, 2] = query[:, h * head_size : (h + 1) * head_size]
    for rel in (3, 2, 1):
        a, b = moved(x, y, rel, swap)
        copy = pltpu.make_async_remote_copy(
            src_ref=qkv.at[head_of(a, b), 2],
            dst_ref=qs.at[rel],
            send_sem=q_send.at[rel],
            recv_sem=q_recv.at[rel],
            device_id=in_plane(a, b),
            device_id_type=MESH,
        )
        copy.start()
        q_copies.append(copy)
    for load in loads[9:11] + loads[13:]:
        load.wait()
    vectors[mp, 0:1] = b_rank[...]
    vectors[mp, 1:2] = w_score[...]

    @pl.when(near == 0)
    def _():
        for k in range(PARTS):
            send_weights(mp, k, over, over_send).start()
        send_vectors(mp, over, over_send).start()

    kv[0] = qkv[head, pl.ds(0, 2)]
    qs[0] = qkv[head, 2]

    def pass_on(s, p):
        a, b = moved(x, y, p, ring)
        return pltpu.make_async_remote_copy(
            src_ref=kv.at[s],
            dst_ref=kv.at[p * HEADS + s],
            send_sem=pass_send.at[s, p],
            recv_sem=pass_recv.at[s, p],
            device_id=in_plane(a, b),
            device_id_type=MESH,
        )

    def pass_half(s, p):
        a, b = moved(x, y, 3 - p, ring)
        return pltpu.make_async_remote_copy(
            src_ref=kv.at[p * HEADS + s, p - 1],
            dst_ref=kv.at[3 * HEADS + s, p - 1],
            send_sem=half_send.at[s, p],
            recv_sem=half_recv.at[s, p],
            device_id=in_plane(a, b),
            device_id_type=MESH,
        )

    for p in (1, 2):
        pass_on(0, p).start()

    gate[...] = project(3).astype(BF16)
    acc[...] = jnp.zeros_like(acc)

    owned, count = cand_ids.shape
    pool = table.shape[0]
    for load in loads[6:9] + loads[11:13]:
        load.wait()

    @pl.loop(0, owned)
    def _(r):
        @pl.when(r > 0)
        def _():
            pltpu.make_async_copy(kv.at[r], kv.at[r], kv_recv.at[r]).wait()
            for p in (1, 2):
                pass_on(r, p).start()

        eye = lax.broadcasted_iota(jnp.int32, (count, count), 0) == lax.broadcasted_iota(
            jnp.int32, (count, count), 1
        )
        item = lax.broadcasted_iota(jnp.int32, (count, pool), 1).astype(F32)
        ids = cand_ids[pl.ds(r, 1), :].astype(F32)
        column = jnp.sum(jnp.where(eye, ids, 0.0), axis=1, keepdims=True)
        onehot = jnp.where(item == column, 1.0, 0.0).astype(BF16)
        cand[pl.ds(r * count, count)] = jnp.dot(
            onehot, table[...], preferred_element_type=F32
        ).astype(BF16)

    scale = 0.5 * head_size**-0.5

    def time_of(p, s):
        a, b = moved(x, y, p, ring)
        a, b = moved(a, b, s, swap)
        return a * SIDE + b

    def attend(chunk, when, diagonal):
        key, value = kv[chunk, 0], kv[chunk, 1]
        for pair in range(2):
            weights = []
            score = dot_t(qs[pl.ds(2 * pair, 2)].reshape(2 * events, head_size), key)
            for n in range(2):
                now = time_of(0, 2 * pair + n)
                half = score[n * events : (n + 1) * events]
                if diagonal:
                    behind = (
                        lax.broadcasted_iota(jnp.int32, half.shape, 0)
                        - lax.broadcasted_iota(jnp.int32, half.shape, 1)
                        + (now - when) * events
                    )
                    half = jnp.where(behind >= 0, half * scale, 0.0)
                else:
                    half = half * (scale * (now > when).astype(F32))
                weights.append(silu_of_twice(half).astype(BF16))
            weights = jnp.concatenate(weights, axis=0)
            rows = pl.ds(pair * 2 * events, 2 * events)
            acc[rows] += jnp.dot(weights, value, preferred_element_type=F32)

    for copy in q_copies:
        copy.wait_recv()

    @pl.loop(0, HEADS)
    def _(s):
        attend(s, time_of(0, s), True)

    @pl.loop(0, HEADS + 1)
    def _(s):
        @pl.when(jnp.logical_or(s == 2, s == HEADS))
        def _():
            relay(lax.div(s, 2) - 1)

        @pl.when(s < HEADS)
        def _():
            @pl.loop(1, 3)
            def _(p):
                pass_on(s, p).wait_recv()
                pass_half(s, p).start()
                attend(p * HEADS + s, time_of(p, s), False)

        @pl.when(s > 0)
        def _():
            for p in (1, 2):
                pass_half(s - 1, p).wait_recv()
            attend(3 * HEADS + s - 1, time_of(3, s - 1), False)

    back_copies = []
    for rel in (3, 2, 1):
        back[rel] = acc[pl.ds(rel * events, events)].astype(BF16)
        a, b = moved(x, y, rel, swap)
        copy = pltpu.make_async_remote_copy(
            src_ref=back.at[rel],
            dst_ref=att.at[head],
            send_sem=back_send.at[rel],
            recv_sem=back_recv.at[rel],
            device_id=in_plane(a, b),
            device_id_type=MESH,
        )
        copy.start()
        back_copies.append(copy)
    att[head] = acc[pl.ds(0, events)].astype(BF16)
    relay(2)
    for copy in back_copies:
        copy.wait_recv()
    relay(3)

    attended = jnp.concatenate([att[h] for h in range(HEADS)], axis=1).astype(F32)
    mixed = (layer_norm(attended) * gate[...].astype(F32)).astype(BF16)
    projected = jnp.dot(mixed, wo[...], preferred_element_type=F32)
    out = (hist[...].astype(F32) + projected).astype(BF16)
    layer_out[0] = out
    groups = pool_query.shape[0]
    half = 0.5 * dot_t(pool_query[...], out)
    lane = first_pos + lax.broadcasted_iota(jnp.int32, half.shape, 1)
    pool_w = jnp.where(lane < length, silu_of_twice(half), 0.0).astype(BF16)
    sums = jnp.dot(pool_w, out, preferred_element_type=F32)

    split = width // part.shape[2]
    lanes = part.shape[2]
    for n in range(plane):
        g, c = divmod(n, split)
        part[n] = sums[g : g + 1, c * lanes : (c + 1) * lanes]

    def wait_for(buffer, many, sem):
        some = buffer.at[pl.ds(0, many)]
        pltpu.make_async_copy(some, some, sem).wait()

    for step in STEPS:
        other = plane_device(step)
        pltpu.make_async_remote_copy(
            src_ref=part.at[other],
            dst_ref=parts.at[t],
            send_sem=sum_sem.at[0],
            recv_sem=sum_sem.at[1],
            device_id={"tm": other},
            device_id_type=MESH,
        ).start()

    parts[t] = part[t]
    relay(4)
    wait_for(parts, plane - 1, sum_sem.at[1])
    whole = jnp.sum(parts[...], axis=0).astype(BF16).astype(F32)
    piece[...] = whole
    pieces[user] = whole

    @pl.loop(0, line - 1)
    def _(k):
        pltpu.make_async_remote_copy(
            src_ref=piece,
            dst_ref=pieces.at[user],
            send_sem=state_sem.at[0],
            recv_sem=state_sem.at[1],
            device_id=line_device(k),
            device_id_type=MESH,
        ).start()

    relay(5)
    own_half = lax.div(mp, 2)
    pre[own_half] = jnp.dot(cand[...], wr[mp, :width], preferred_element_type=F32)
    wait_for(pieces, line - 1, state_sem.at[1])
    mine = owner * owned + lax.broadcasted_iota(jnp.int32, (owned, line), 0)
    picker = jnp.where(slots[...] == mine, 1.0, 0.0).astype(BF16)
    states = pieces[...].reshape(line, lanes).astype(BF16)
    own_states = jnp.dot(picker, states, preferred_element_type=F32)
    chosen[...] = own_states
    interests[t] = own_states

    for step in STEPS:
        pltpu.make_async_remote_copy(
            src_ref=chosen,
            dst_ref=interests.at[t],
            send_sem=pick_sem.at[0],
            recv_sem=pick_sem.at[1],
            device_id={"tm": plane_device(step)},
            device_id_type=MESH,
        ).start()

    relay(6)
    pre[1 - own_half] = jnp.dot(cand[...], wr[across, :width], preferred_element_type=F32)
    wait_for(interests, plane - 1, pick_sem.at[1])

    interest = jnp.concatenate(
        [
            layer_norm(
                jnp.concatenate([interests[g * split + c] for c in range(split)], axis=1)
            )
            for g in range(groups)
        ],
        axis=0,
    ).astype(BF16)
    half = (0.5 * width**-0.5) * dot_t(cand[...], interest)
    row = lax.div(lax.broadcasted_iota(jnp.int32, half.shape, 0), count)
    column = lax.rem(lax.broadcasted_iota(jnp.int32, half.shape, 1), owned)
    attn = jnp.where(row == column, silu_of_twice(half), 0.0)
    high = attn.astype(BF16)
    low = (attn - high.astype(F32)).astype(BF16)
    context = (
        jnp.dot(high, interest, preferred_element_type=F32)
        + jnp.dot(low, interest, preferred_element_type=F32)
    ).astype(BF16)
    terms = jnp.zeros_like(pre[0])
    for n in range(2):
        block = core + 2 * n
        more = jnp.dot(context, wr[block, width:], preferred_element_type=F32)
        half = 0.5 * (pre[n] + vectors[block, 0:1] + more)
        terms += silu_of_twice(half) * vectors[block, 1:2]
    high = terms.astype(BF16)
    low = (terms - high.astype(F32)).astype(BF16)
    ones = jnp.ones((16, terms.shape[1]), BF16)
    own_share = (dot_t(ones, high) + dot_t(ones, low))[0:1]
    share[...] = own_share
    shares[core] = own_share
    exchange = pltpu.make_async_remote_copy(
        src_ref=share,
        dst_ref=shares.at[core],
        send_sem=twin_sem.at[0],
        recv_sem=twin_sem.at[1],
        device_id={"mp": twin},
        device_id_type=MESH,
    )
    exchange.start()
    exchange.wait_recv()
    total = jnp.sum(shares[...], axis=0)
    for r in range(owned):
        scores[r : r + 1, :] = total[0:1, r * count : (r + 1) * count]

    for copy in kv_copies + q_copies + back_copies:
        copy.wait_send()
    for s in range(HEADS):
        for p in (1, 2):
            pass_on(s, p).wait_send()
            pass_half(s, p).wait_send()
    wait_for(parts, plane - 1, sum_sem.at[0])
    wait_for(pieces, line - 1, state_sem.at[0])
    wait_for(interests, plane - 1, pick_sem.at[0])
    exchange.wait_send()

    @pl.when(near == 0)
    def _():
        for k in range(PARTS):
            send_weights(mp, k, over, over_send).wait_send()
        send_vectors(mp, over, over_send).wait_send()

    @pl.when(near < ends_at)
    def _():
        for k in range(PARTS):
            send_weights(across, k, onward, chain_send).wait_send()
        send_vectors(across, onward, chain_send).wait_send()


def solution(mesh):
    plane, owners, ranks = mesh.shape["tm"], mesh.shape["users"], mesh.shape["mp"]
    line = owners * ranks

    def shards(
        history,
        ln_gain,
        w_proj,
        w_out,
        pool_query,
        lengths,
        slots,
        cand_ids,
        item_table,
        w_rank,
        b_rank,
        w_score,
    ):
        _, events, width = history.shape
        head_size = width // HEADS
        groups = pool_query.shape[0]
        owned, count = cand_ids.shape
        lanes = groups * width // plane
        cands = owned * count
        hidden = w_rank.shape[1]
        vmem = pl.BlockSpec(memory_space=pltpu.VMEM)
        smem = pl.BlockSpec(memory_space=pltpu.SMEM)
        hbm = pl.BlockSpec(memory_space=pltpu.HBM)
        dma = pltpu.SemaphoreType.DMA
        return pl.pallas_call(
            kernel,
            out_shape=(
                jax.ShapeDtypeStruct(history.shape, BF16),
                jax.ShapeDtypeStruct((owned, count), F32),
            ),
            in_specs=[smem] + [hbm] * 11,
            out_specs=(vmem, vmem),
            scratch_shapes=[
                pltpu.VMEM((events, width), BF16),
                pltpu.VMEM((1, width), F32),
                pltpu.VMEM(pool_query.shape, BF16),
                pltpu.VMEM((1, line), jnp.int32),
                pltpu.VMEM((owned, count), jnp.int32),
                pltpu.VMEM((1, hidden), F32),
                pltpu.VMEM((1, hidden), F32),
                pltpu.VMEM((4, width, width), BF16),
                pltpu.VMEM((width, width), BF16),
                pltpu.VMEM(item_table.shape, BF16),
                pltpu.VMEM((ranks, *w_rank.shape), BF16),
                pltpu.VMEM((events, width), BF16),
                pltpu.VMEM((events, width), BF16),
                pltpu.VMEM((HEADS, 3, events, head_size), BF16),
                pltpu.VMEM((plane, 2, events, head_size), BF16),
                pltpu.VMEM((HEADS, events, head_size), BF16),
                pltpu.VMEM((HEADS * events, head_size), F32),
                pltpu.VMEM((HEADS, events, head_size), BF16),
                pltpu.VMEM((HEADS, events, head_size), BF16),
                pltpu.VMEM((cands, width), BF16),
                pltpu.VMEM((2, cands, hidden), F32),
                pltpu.VMEM((plane, 1, lanes), F32),
                pltpu.VMEM((plane, 1, lanes), F32),
                pltpu.VMEM((1, lanes), F32),
                pltpu.VMEM((line, 1, lanes), F32),
                pltpu.VMEM((owned, lanes), F32),
                pltpu.VMEM((plane, owned, lanes), F32),
                pltpu.VMEM((ranks, 2, hidden), F32),
                pltpu.VMEM((1, cands), F32),
                pltpu.VMEM((2, 1, cands), F32),
                dma((14,)),
                dma((HEADS,)),
                dma((HEADS,)),
                dma((HEADS,)),
                dma((HEADS,)),
                dma((HEADS, HEADS)),
                dma((HEADS, HEADS)),
                dma((HEADS, HEADS)),
                dma((HEADS, HEADS)),
                dma((HEADS,)),
                dma((HEADS,)),
                dma((2,)),
                dma((2,)),
                dma((2,)),
                dma((PARTS + 1,)),
                dma((PARTS + 1,)),
                dma((PARTS + 1,)),
                dma((2,)),
            ],
            compiler_params=pltpu.CompilerParams(
                collective_id=0, has_side_effects=True, vmem_limit_bytes=VMEM_BYTES
            ),
            cost_estimate=pl.CostEstimate(
                flops=4_000_000_000, bytes_accessed=6_000_000, transcendentals=5_000_000
            ),
        )(
            lengths,
            history,
            ln_gain.reshape(1, -1),
            w_proj,
            w_out,
            pool_query,
            slots.reshape(1, -1),
            cand_ids,
            item_table,
            w_rank,
            b_rank.reshape(1, -1),
            w_score.reshape(1, -1),
        )

    placed = (
        P(("users", "mp"), "tm", None),
        P(),
        P(),
        P(),
        P(),
        P(("users", "mp")),
        P(),
        P("users", "tm"),
        P("users", None),
        P(None, "mp"),
        P("mp"),
        P("mp"),
    )
    return jax.shard_map(
        shards,
        mesh=mesh,
        in_specs=placed,
        out_specs=(P(("users", "mp"), "tm", None), P("users", "tm")),
        check_vma=False,
    )
```

```python
import jax
import jax.numpy as jnp
from jax import lax
from jax.experimental import pallas as pl
from jax.experimental.pallas import tpu as pltpu
from jax.sharding import PartitionSpec as P

HEADS = 4
SIDE = 4
EPS = 1e-05
PARTS = 4
VMEM_BYTES = 64 * 1024 * 1024
MESH = pl.DeviceIdType.MESH
STEPS = sorted(
    ((a, b) for a in range(SIDE) for b in range(SIDE) if a or b),
    key=lambda step: -sum(min(n, SIDE - n) for n in step),
)
F32 = jnp.float32
BF16 = jnp.bfloat16
ROWS_BY_ROWS = (((1,), (1,)), ((), ()))


def layer_norm(values):
    mean = jnp.mean(values, axis=-1, keepdims=True)
    centred = values - mean
    var = jnp.mean(centred * centred, axis=-1, keepdims=True)
    return centred * lax.rsqrt(var + EPS)


def silu_of_twice(half):
    return half + half * jnp.tanh(half)


def dot_t(a, b, **kw):
    return lax.dot_general(a, b, ROWS_BY_ROWS, preferred_element_type=F32, **kw)


def kernel(
    lengths,
    history,
    ln_gain_hbm,
    w_proj,
    w_out,
    pool_query_hbm,
    slots_hbm,
    cand_ids_hbm,
    item_table,
    w_rank,
    b_rank_hbm,
    w_score_hbm,
    layer_out,
    scores,
    hist,
    ln_gain,
    pool_query,
    slots,
    cand_ids,
    b_rank,
    w_score,
    wp,
    wo,
    table,
    wr,
    normed,
    gate,
    qkv,
    kv,
    qs,
    acc,
    back,
    att,
    masks,
    cand,
    pre,
    part,
    parts,
    piece,
    pieces,
    chosen,
    interests,
    vectors,
    share,
    shares,
    load_sem,
    kv_send,
    kv_recv,
    q_send,
    q_recv,
    pass_send,
    pass_recv,
    back_send,
    back_recv,
    sum_sem,
    state_sem,
    pick_sem,
    over_send,
    chain_send,
    chain_recv,
    twin_sem,
):
    events, width = hist.shape
    head_size = width // HEADS
    plane, line, ranks = parts.shape[0], pieces.shape[0], wr.shape[0]
    t = lax.axis_index("tm")
    owner = lax.axis_index("users")
    mp = lax.axis_index("mp")
    user = owner * ranks + mp
    x, y = lax.div(t, SIDE), lax.rem(t, SIDE)
    core = lax.rem(mp, 2)

    def even(v):
        return v + 1 - 2 * lax.rem(v, 2)

    def odd(v):
        return SIDE - 1 - v

    def swap_y(v):
        return even(v) + core * (odd(v) - even(v))

    def ring_y(v):
        return odd(v) + core * (even(v) - odd(v))

    def head_of(a, b):
        first = lax.rem(lax.div(b + 1, 2), 2)
        return 2 * lax.div(a, 2) + first + core * (lax.div(b, 2) - first)

    def moved(a, b, rel):
        first, second = lax.rem(rel, 2), lax.div(rel, 2)
        return a + second * (odd(a) - a), b + first * (swap_y(b) - b)

    def in_plane(a, b):
        return {"tm": a * SIDE + b}

    head = head_of(x, y)

    depth = wr.shape[1] // PARTS
    last = line // ranks - 1
    twin = mp + 1 - 2 * core
    across = lax.rem(mp + 2, ranks)
    near = jnp.minimum(owner, last - owner)
    step_on = jnp.where(owner < near + 1, 1, -1)
    ends_at = last // 2

    def weights_of(whose, k):
        rows = pl.ds(pl.multiple_of(k * depth, depth), depth)
        return wr.at[whose, rows]

    def send_weights(whose, k, to, sems):
        return pltpu.make_async_remote_copy(
            src_ref=weights_of(whose, k),
            dst_ref=weights_of(whose, k),
            send_sem=sems.at[k],
            recv_sem=chain_recv.at[k],
            device_id=to,
            device_id_type=MESH,
        )

    def send_vectors(whose, to, sems):
        return pltpu.make_async_remote_copy(
            src_ref=vectors.at[whose],
            dst_ref=vectors.at[whose],
            send_sem=sems.at[PARTS],
            recv_sem=chain_recv.at[PARTS],
            device_id=to,
            device_id_type=MESH,
        )

    over = {"users": last - owner, "mp": across}
    onward = {"users": owner + step_on}

    def relay(j):
        k = j - near

        @pl.when(jnp.logical_and(k >= 0, k < PARTS))
        def _():
            here = weights_of(across, k)
            pltpu.make_async_copy(here, here, chain_recv.at[k]).wait()

            @pl.when(near < ends_at)
            def _():
                send_weights(across, k, onward, chain_send).start()

            @pl.when(k == PARTS - 1)
            def _():
                here = vectors.at[across]
                pltpu.make_async_copy(here, here, chain_recv.at[PARTS]).wait()

                @pl.when(near < ends_at)
                def _():
                    send_vectors(across, onward, chain_send).start()

    loads = [pltpu.make_async_copy(history.at[0], hist, load_sem.at[0])]
    for n, block in enumerate((3, 1, 2, 0)):
        cols = pl.ds(block * width, width)
        loads.append(pltpu.make_async_copy(w_proj.at[:, cols], wp.at[n], load_sem.at[n + 1]))
    rest = (
        (ln_gain_hbm, ln_gain),
        (pool_query_hbm, pool_query),
        (slots_hbm, slots),
        (cand_ids_hbm, cand_ids),
        (b_rank_hbm, b_rank),
        (w_score_hbm, w_score),
        (w_out, wo),
        (item_table, table),
        (w_rank, wr.at[mp]),
    )
    for n, (src, dst) in enumerate(rest):
        loads.append(pltpu.make_async_copy(src, dst, load_sem.at[5 + n]))
    loads[0].start()
    loads[5].start()
    for load in loads[1:5] + loads[6:]:
        load.start()

    barrier = pltpu.get_barrier_semaphore()

    def plane_device(step):
        a, b = step
        return lax.rem(x + a, SIDE) * SIDE + lax.rem(y + b, SIDE)

    height = line // 2
    low = height // 2

    def line_device(k):
        j = lax.div(k, 2)
        far = lax.div(j + 1, 2)
        chip = low + far * (1 - 2 * lax.rem(j, 2)) + lax.div(mp, 2) * low + owner
        chip = lax.rem(chip, height)
        other = lax.rem(core + k + 1, 2)
        return {"users": lax.rem(chip, low), "mp": 2 * lax.div(chip, low) + other}

    @pl.loop(0, line - 1)
    def _(k):
        pl.semaphore_signal(barrier, inc=1, device_id=line_device(k), device_id_type=MESH)

    for step in STEPS:
        pl.semaphore_signal(
            barrier, inc=1, device_id={"tm": plane_device(step)}, device_id_type=MESH
        )

    first_pos = t * events
    length = lengths[0]
    pos = first_pos + lax.broadcasted_iota(jnp.int32, (events, 1), 0)
    live = pos < length
    loads[0].wait()
    loads[5].wait()
    normed[...] = (layer_norm(hist[...].astype(F32)) * ln_gain[...]).astype(BF16)

    def project(n):
        loads[n + 1].wait()
        half = 0.5 * jnp.dot(normed[...], wp[n], preferred_element_type=F32)
        return silu_of_twice(half)

    keys = project(0).astype(BF16)
    for h in range(HEADS):
        qkv[h, 0] = keys[:, h * head_size : (h + 1) * head_size]
    values = jnp.where(live, project(1), 0.0).astype(BF16)
    for h in range(HEADS):
        qkv[h, 1] = values[:, h * head_size : (h + 1) * head_size]

    pl.semaphore_wait(barrier, plane - 1 + line - 1)

    kv_copies, q_copies = [], []
    for rel in (3, 2, 1):
        a, b = moved(x, y, rel)
        copy = pltpu.make_async_remote_copy(
            src_ref=qkv.at[head_of(a, b), pl.ds(0, 2)],
            dst_ref=kv.at[rel],
            send_sem=kv_send.at[rel],
            recv_sem=kv_recv.at[rel],
            device_id=in_plane(a, b),
            device_id_type=MESH,
        )
        copy.start()
        kv_copies.append(copy)

    query = (project(2) * (0.5 * head_size**-0.5)).astype(BF16)
    for h in range(HEADS):
        qkv[h, 2] = query[:, h * head_size : (h + 1) * head_size]
    for rel in (3, 2, 1):
        a, b = moved(x, y, rel)
        copy = pltpu.make_async_remote_copy(
            src_ref=qkv.at[head_of(a, b), 2],
            dst_ref=qs.at[rel],
            send_sem=q_send.at[rel],
            recv_sem=q_recv.at[rel],
            device_id=in_plane(a, b),
            device_id_type=MESH,
        )
        copy.start()
        q_copies.append(copy)
    for load in loads[9:11] + loads[13:]:
        load.wait()
    vectors[mp, 0:1] = b_rank[...]
    vectors[mp, 1:2] = w_score[...]

    @pl.when(near == 0)
    def _():
        for k in range(PARTS):
            send_weights(mp, k, over, over_send).start()
        send_vectors(mp, over, over_send).start()

    kv[0] = qkv[head, pl.ds(0, 2)]
    qs[0] = qkv[head, 2]

    x_near, y_near = even(x), ring_y(y)

    def pass_kv(n):
        return pltpu.make_async_remote_copy(
            src_ref=kv.at[n],
            dst_ref=kv.at[HEADS + n],
            send_sem=pass_send.at[0, n],
            recv_sem=pass_recv.at[0, n],
            device_id=in_plane(x_near, y),
            device_id_type=MESH,
        )

    def pass_q(n):
        return pltpu.make_async_remote_copy(
            src_ref=qs.at[n],
            dst_ref=qs.at[HEADS + n],
            send_sem=pass_send.at[1, n],
            recv_sem=pass_recv.at[1, n],
            device_id=in_plane(x, y_near),
            device_id_type=MESH,
        )

    def back_copy(n, which):
        a, b = moved(x, y_near if which else y, n)
        return pltpu.make_async_remote_copy(
            src_ref=back.at[which, n],
            dst_ref=att.at[which, head],
            send_sem=back_send.at[which, n],
            recv_sem=back_recv.at[which, n],
            device_id=in_plane(a, b),
            device_id_type=MESH,
        )

    pass_q(0).start()
    pass_kv(0).start()

    gate[...] = project(3).astype(BF16)
    acc[...] = jnp.zeros_like(acc)

    owned, count = cand_ids.shape
    pool = table.shape[0]
    for load in loads[6:9] + loads[11:13]:
        load.wait()

    @pl.loop(0, owned)
    def _(r):
        @pl.when(r > 0)
        def _():
            pltpu.make_async_copy(kv.at[r], kv.at[r], kv_recv.at[r]).wait()
            pass_kv(r).start()

        eye = lax.broadcasted_iota(jnp.int32, (count, count), 0) == lax.broadcasted_iota(
            jnp.int32, (count, count), 1
        )
        item = lax.broadcasted_iota(jnp.int32, (count, pool), 1).astype(F32)
        ids = cand_ids[pl.ds(r, 1), :].astype(F32)
        column = jnp.sum(jnp.where(eye, ids, 0.0), axis=1, keepdims=True)
        onehot = jnp.where(item == column, 1.0, 0.0).astype(BF16)
        cand[pl.ds(r * count, count)] = jnp.dot(
            onehot, table[...], preferred_element_type=F32
        ).astype(BF16)

    pairs = 2 * events
    behind = lax.broadcasted_iota(jnp.int32, (events, events), 0) >= lax.broadcasted_iota(
        jnp.int32, (events, events), 1
    )
    masks[0] = jnp.zeros((events, events), F32)
    masks[1] = jnp.where(behind, 1.0, 0.0)
    masks[2] = jnp.ones((events, events), F32)

    def rows_of(which, pair):
        return pl.ds(pl.multiple_of((2 * which + pair) * pairs, pairs), pairs)

    def attend(q_set, q_pair, k_set, k_pair, masked):
        q_first, k_first = HEADS * q_set + 2 * q_pair, HEADS * k_set + 2 * k_pair
        query = qs[pl.ds(q_first, 2)].reshape(pairs, head_size)
        half = jnp.concatenate(
            [dot_t(query, kv[k_first + n, 0]) for n in range(2)], axis=1
        )
        if masked:
            q_y = y_near if q_set else y
            half = jnp.concatenate(
                [
                    jnp.concatenate(
                        [
                            half[a * events : (a + 1) * events, b * events : (b + 1) * events]
                            * masks[1 + jnp.clip(q_row - k_row, -1, 1)]
                            for b, k_row in enumerate((y, swap_y(y)))
                        ],
                        axis=1,
                    )
                    for a, q_row in enumerate((q_y, swap_y(q_y)))
                ],
                axis=0,
            )
        weights = silu_of_twice(half).astype(BF16)
        value = jnp.concatenate([kv[k_first + n, 1] for n in range(2)], axis=0)
        acc[rows_of(q_set, q_pair)] += jnp.dot(weights, value, preferred_element_type=F32)

    late = jnp.where(x < SIDE // 2, 1, 0)
    early = 1 - late
    outer = jnp.logical_or(x == 0, x == SIDE - 1)

    def attend_own(q_set):
        for pair in range(2):
            attend(q_set, pair, 0, pair, True)
        attend(q_set, late, 0, early, False)

    def attend_near(q_set, n):
        q_pair = late if n else jnp.where(outer, late, early)
        k_pair = jnp.where(outer, n, jnp.where(x == 1, 0, 1))
        attend(q_set, q_pair, 1, k_pair, False)

    for n in range(1, HEADS):
        pltpu.make_async_copy(qs.at[n], qs.at[n], q_recv.at[n]).wait()
        pass_q(n).start()
    attend_own(0)
    for n in range(HEADS):
        pass_q(n).wait_recv()
    attend(1, 0, 0, 0, True)
    attend(1, 1, 0, 1, True)
    relay(0)
    attend(1, late, 0, early, False)
    for n in range(HEADS):
        pass_kv(n).wait_recv()
    attend_near(1, 0)
    attend_near(1, 1)
    for n in (3, 2, 1, 0):
        back[1, n] = acc[pl.ds((HEADS + n) * events, events)].astype(BF16)
        back_copy(n, 1).start()
    relay(1)
    attend_near(0, 0)
    attend_near(0, 1)

    for n in (3, 2, 1):
        back[0, n] = acc[pl.ds(n * events, events)].astype(BF16)
        back_copy(n, 0).start()
    att[0, head] = acc[pl.ds(0, events)].astype(BF16)
    relay(2)
    for n in range(HEADS):
        back_copy(n, 1).wait_recv()
    for n in range(1, HEADS):
        back_copy(n, 0).wait_recv()
    relay(3)

    attended = jnp.concatenate(
        [att[0, h].astype(F32) + att[1, h].astype(F32) for h in range(HEADS)], axis=1
    )
    mixed = (layer_norm(attended) * gate[...].astype(F32)).astype(BF16)
    projected = jnp.dot(mixed, wo[...], preferred_element_type=F32)
    out = (hist[...].astype(F32) + projected).astype(BF16)
    layer_out[0] = out
    groups = pool_query.shape[0]
    half = 0.5 * dot_t(pool_query[...], out)
    lane = first_pos + lax.broadcasted_iota(jnp.int32, half.shape, 1)
    pool_w = jnp.where(lane < length, silu_of_twice(half), 0.0).astype(BF16)
    sums = jnp.dot(pool_w, out, preferred_element_type=F32)

    split = width // part.shape[2]
    lanes = part.shape[2]
    for n in range(plane):
        g, c = divmod(n, split)
        part[n] = sums[g : g + 1, c * lanes : (c + 1) * lanes]

    def wait_for(buffer, many, sem):
        some = buffer.at[pl.ds(0, many)]
        pltpu.make_async_copy(some, some, sem).wait()

    for step in STEPS:
        other = plane_device(step)
        pltpu.make_async_remote_copy(
            src_ref=part.at[other],
            dst_ref=parts.at[t],
            send_sem=sum_sem.at[0],
            recv_sem=sum_sem.at[1],
            device_id={"tm": other},
            device_id_type=MESH,
        ).start()

    parts[t] = part[t]
    relay(4)
    wait_for(parts, plane - 1, sum_sem.at[1])
    whole = jnp.sum(parts[...], axis=0).astype(BF16).astype(F32)
    piece[...] = whole
    pieces[user] = whole

    @pl.loop(0, line - 1)
    def _(k):
        pltpu.make_async_remote_copy(
            src_ref=piece,
            dst_ref=pieces.at[user],
            send_sem=state_sem.at[0],
            recv_sem=state_sem.at[1],
            device_id=line_device(k),
            device_id_type=MESH,
        ).start()

    relay(5)
    own_half = lax.div(mp, 2)
    pre[own_half] = jnp.dot(cand[...], wr[mp, :width], preferred_element_type=F32)
    wait_for(pieces, line - 1, state_sem.at[1])
    mine = owner * owned + lax.broadcasted_iota(jnp.int32, (owned, line), 0)
    picker = jnp.where(slots[...] == mine, 1.0, 0.0).astype(BF16)
    states = pieces[...].reshape(line, lanes).astype(BF16)
    own_states = jnp.dot(picker, states, preferred_element_type=F32)
    chosen[...] = own_states
    interests[t] = own_states

    for step in STEPS:
        pltpu.make_async_remote_copy(
            src_ref=chosen,
            dst_ref=interests.at[t],
            send_sem=pick_sem.at[0],
            recv_sem=pick_sem.at[1],
            device_id={"tm": plane_device(step)},
            device_id_type=MESH,
        ).start()

    relay(6)
    pre[1 - own_half] = jnp.dot(cand[...], wr[across, :width], preferred_element_type=F32)
    wait_for(interests, plane - 1, pick_sem.at[1])

    interest = jnp.concatenate(
        [
            layer_norm(
                jnp.concatenate([interests[g * split + c] for c in range(split)], axis=1)
            )
            for g in range(groups)
        ],
        axis=0,
    ).astype(BF16)
    half = (0.5 * width**-0.5) * dot_t(cand[...], interest)
    row = lax.div(lax.broadcasted_iota(jnp.int32, half.shape, 0), count)
    column = lax.rem(lax.broadcasted_iota(jnp.int32, half.shape, 1), owned)
    attn = jnp.where(row == column, silu_of_twice(half), 0.0)
    high = attn.astype(BF16)
    low = (attn - high.astype(F32)).astype(BF16)
    factors = jnp.concatenate([high, low, high], axis=1)
    terms = jnp.zeros_like(pre[0])
    for n in range(2):
        block = core + 2 * n
        mixed_in = jnp.dot(interest, wr[block, width:], preferred_element_type=F32)
        large = mixed_in.astype(BF16)
        small = (mixed_in - large.astype(F32)).astype(BF16)
        more = jnp.dot(
            factors, jnp.concatenate([large, large, small], axis=0), preferred_element_type=F32
        )
        half = 0.5 * (pre[n] + vectors[block, 0:1] + more)
        terms += silu_of_twice(half) * vectors[block, 1:2]
    high = terms.astype(BF16)
    low = (terms - high.astype(F32)).astype(BF16)
    ones = jnp.ones((16, terms.shape[1]), BF16)
    own_share = (dot_t(ones, high) + dot_t(ones, low))[0:1]
    share[...] = own_share
    shares[core] = own_share
    exchange = pltpu.make_async_remote_copy(
        src_ref=share,
        dst_ref=shares.at[core],
        send_sem=twin_sem.at[0],
        recv_sem=twin_sem.at[1],
        device_id={"mp": twin},
        device_id_type=MESH,
    )
    exchange.start()
    exchange.wait_recv()
    total = jnp.sum(shares[...], axis=0)
    for r in range(owned):
        scores[r : r + 1, :] = total[0:1, r * count : (r + 1) * count]

    for copy in kv_copies + q_copies:
        copy.wait_send()
    for n in range(HEADS):
        pass_kv(n).wait_send()
        pass_q(n).wait_send()
        back_copy(n, 1).wait_send()
    for n in range(1, HEADS):
        back_copy(n, 0).wait_send()
    wait_for(parts, plane - 1, sum_sem.at[0])
    wait_for(pieces, line - 1, state_sem.at[0])
    wait_for(interests, plane - 1, pick_sem.at[0])
    exchange.wait_send()

    @pl.when(near == 0)
    def _():
        for k in range(PARTS):
            send_weights(mp, k, over, over_send).wait_send()
        send_vectors(mp, over, over_send).wait_send()

    @pl.when(near < ends_at)
    def _():
        for k in range(PARTS):
            send_weights(across, k, onward, chain_send).wait_send()
        send_vectors(across, onward, chain_send).wait_send()


def solution(mesh):
    plane, owners, ranks = mesh.shape["tm"], mesh.shape["users"], mesh.shape["mp"]
    line = owners * ranks

    def shards(
        history,
        ln_gain,
        w_proj,
        w_out,
        pool_query,
        lengths,
        slots,
        cand_ids,
        item_table,
        w_rank,
        b_rank,
        w_score,
    ):
        _, events, width = history.shape
        head_size = width // HEADS
        groups = pool_query.shape[0]
        owned, count = cand_ids.shape
        lanes = groups * width // plane
        cands = owned * count
        hidden = w_rank.shape[1]
        vmem = pl.BlockSpec(memory_space=pltpu.VMEM)
        smem = pl.BlockSpec(memory_space=pltpu.SMEM)
        hbm = pl.BlockSpec(memory_space=pltpu.HBM)
        dma = pltpu.SemaphoreType.DMA
        return pl.pallas_call(
            kernel,
            out_shape=(
                jax.ShapeDtypeStruct(history.shape, BF16),
                jax.ShapeDtypeStruct((owned, count), F32),
            ),
            in_specs=[smem] + [hbm] * 11,
            out_specs=(vmem, vmem),
            scratch_shapes=[
                pltpu.VMEM((events, width), BF16),
                pltpu.VMEM((1, width), F32),
                pltpu.VMEM(pool_query.shape, BF16),
                pltpu.VMEM((1, line), jnp.int32),
                pltpu.VMEM((owned, count), jnp.int32),
                pltpu.VMEM((1, hidden), F32),
                pltpu.VMEM((1, hidden), F32),
                pltpu.VMEM((4, width, width), BF16),
                pltpu.VMEM((width, width), BF16),
                pltpu.VMEM(item_table.shape, BF16),
                pltpu.VMEM((ranks, *w_rank.shape), BF16),
                pltpu.VMEM((events, width), BF16),
                pltpu.VMEM((events, width), BF16),
                pltpu.VMEM((HEADS, 3, events, head_size), BF16),
                pltpu.VMEM((2 * HEADS, 2, events, head_size), BF16),
                pltpu.VMEM((2 * HEADS, events, head_size), BF16),
                pltpu.VMEM((2 * HEADS * events, head_size), F32),
                pltpu.VMEM((2, HEADS, events, head_size), BF16),
                pltpu.VMEM((2, HEADS, events, head_size), BF16),
                pltpu.VMEM((3, events, events), F32),
                pltpu.VMEM((cands, width), BF16),
                pltpu.VMEM((2, cands, hidden), F32),
                pltpu.VMEM((plane, 1, lanes), F32),
                pltpu.VMEM((plane, 1, lanes), F32),
                pltpu.VMEM((1, lanes), F32),
                pltpu.VMEM((line, 1, lanes), F32),
                pltpu.VMEM((owned, lanes), F32),
                pltpu.VMEM((plane, owned, lanes), F32),
                pltpu.VMEM((ranks, 2, hidden), F32),
                pltpu.VMEM((1, cands), F32),
                pltpu.VMEM((2, 1, cands), F32),
                dma((14,)),
                dma((HEADS,)),
                dma((HEADS,)),
                dma((HEADS,)),
                dma((HEADS,)),
                dma((2, HEADS)),
                dma((2, HEADS)),
                dma((2, HEADS)),
                dma((2, HEADS)),
                dma((2,)),
                dma((2,)),
                dma((2,)),
                dma((PARTS + 1,)),
                dma((PARTS + 1,)),
                dma((PARTS + 1,)),
                dma((2,)),
            ],
            compiler_params=pltpu.CompilerParams(
                collective_id=0, has_side_effects=True, vmem_limit_bytes=VMEM_BYTES
            ),
            cost_estimate=pl.CostEstimate(
                flops=4_000_000_000, bytes_accessed=6_000_000, transcendentals=5_000_000
            ),
        )(
            lengths,
            history,
            ln_gain.reshape(1, -1),
            w_proj,
            w_out,
            pool_query,
            slots.reshape(1, -1),
            cand_ids,
            item_table,
            w_rank,
            b_rank.reshape(1, -1),
            w_score.reshape(1, -1),
        )

    placed = (
        P(("users", "mp"), "tm", None),
        P(),
        P(),
        P(),
        P(),
        P(("users", "mp")),
        P(),
        P("users", "tm"),
        P("users", None),
        P(None, "mp"),
        P("mp"),
        P("mp"),
    )
    return jax.shard_map(
        shards,
        mesh=mesh,
        in_specs=placed,
        out_specs=(P(("users", "mp"), "tm", None), P("users", "tm")),
        check_vma=False,
    )
```

```python
import jax
import jax.numpy as jnp
from jax import lax
from jax.experimental import pallas as pl
from jax.experimental.pallas import tpu as pltpu
from jax.sharding import PartitionSpec as P

HEADS = 4
SIDE = 4
EPS = 1e-05
PARTS = 4
VMEM_BYTES = 64 * 1024 * 1024
MESH = pl.DeviceIdType.MESH
STEPS = sorted(
    ((a, b) for a in range(SIDE) for b in range(SIDE) if a or b),
    key=lambda step: -sum(min(n, SIDE - n) for n in step),
)
F32 = jnp.float32
BF16 = jnp.bfloat16
ROWS_BY_ROWS = (((1,), (1,)), ((), ()))


def layer_norm(values):
    mean = jnp.mean(values, axis=-1, keepdims=True)
    centred = values - mean
    var = jnp.mean(centred * centred, axis=-1, keepdims=True)
    return centred * lax.rsqrt(var + EPS)


def silu_of_twice(half):
    return half + half * jnp.tanh(half)


def dot_t(a, b, **kw):
    return lax.dot_general(a, b, ROWS_BY_ROWS, preferred_element_type=F32, **kw)


def kernel(
    lengths,
    history,
    ln_gain_hbm,
    w_proj,
    w_out,
    pool_query_hbm,
    slots_hbm,
    cand_ids_hbm,
    item_table,
    w_rank,
    b_rank_hbm,
    w_score_hbm,
    layer_out,
    scores,
    hist,
    ln_gain,
    pool_query,
    slots,
    cand_ids,
    b_rank,
    w_score,
    wp,
    wo,
    table,
    wr,
    normed,
    gate,
    qkv,
    kv,
    qs,
    acc,
    back,
    att,
    masks,
    cand,
    pre,
    part,
    parts,
    told,
    pieces,
    chosen,
    interests,
    vectors,
    share,
    shares,
    load_sem,
    kv_send,
    kv_recv,
    q_send,
    q_recv,
    pass_send,
    pass_recv,
    back_send,
    back_recv,
    sum_sem,
    state_sem,
    pick_sem,
    over_send,
    chain_send,
    chain_recv,
    twin_sem,
):
    events, width = hist.shape
    head_size = width // HEADS
    plane, line, ranks = parts.shape[0], pieces.shape[0], wr.shape[0]
    t = lax.axis_index("tm")
    owner = lax.axis_index("users")
    mp = lax.axis_index("mp")
    user = owner * ranks + mp
    x, y = lax.div(t, SIDE), lax.rem(t, SIDE)
    core = lax.rem(mp, 2)

    def even(v):
        return v + 1 - 2 * lax.rem(v, 2)

    def odd(v):
        return SIDE - 1 - v

    def swap_y(v):
        return even(v) + core * (odd(v) - even(v))

    def ring_y(v):
        return odd(v) + core * (even(v) - odd(v))

    def head_of(a, b):
        first = lax.rem(lax.div(b + 1, 2), 2)
        return 2 * lax.div(a, 2) + first + core * (lax.div(b, 2) - first)

    def moved(a, b, rel):
        first, second = lax.rem(rel, 2), lax.div(rel, 2)
        return a + second * (odd(a) - a), b + first * (swap_y(b) - b)

    def in_plane(a, b):
        return {"tm": a * SIDE + b}

    head = head_of(x, y)

    depth = wr.shape[1] // PARTS
    last = line // ranks - 1
    twin = mp + 1 - 2 * core
    across = lax.rem(mp + 2, ranks)
    near = jnp.minimum(owner, last - owner)
    step_on = jnp.where(owner < near + 1, 1, -1)
    ends_at = last // 2

    def weights_of(whose, k):
        rows = pl.ds(pl.multiple_of(k * depth, depth), depth)
        return wr.at[whose, rows]

    def send_weights(whose, k, to, sems):
        return pltpu.make_async_remote_copy(
            src_ref=weights_of(whose, k),
            dst_ref=weights_of(whose, k),
            send_sem=sems.at[k],
            recv_sem=chain_recv.at[k],
            device_id=to,
            device_id_type=MESH,
        )

    def send_vectors(whose, to, sems):
        return pltpu.make_async_remote_copy(
            src_ref=vectors.at[whose],
            dst_ref=vectors.at[whose],
            send_sem=sems.at[PARTS],
            recv_sem=chain_recv.at[PARTS],
            device_id=to,
            device_id_type=MESH,
        )

    over = {"users": last - owner, "mp": across}
    onward = {"users": owner + step_on}

    def relay(j):
        k = j - near

        @pl.when(jnp.logical_and(k >= 0, k < PARTS))
        def _():
            here = weights_of(across, k)
            pltpu.make_async_copy(here, here, chain_recv.at[k]).wait()

            @pl.when(near < ends_at)
            def _():
                send_weights(across, k, onward, chain_send).start()

            @pl.when(k == PARTS - 1)
            def _():
                here = vectors.at[across]
                pltpu.make_async_copy(here, here, chain_recv.at[PARTS]).wait()

                @pl.when(near < ends_at)
                def _():
                    send_vectors(across, onward, chain_send).start()

    loads = [pltpu.make_async_copy(history.at[0], hist, load_sem.at[0])]
    for n, block in enumerate((3, 1, 2, 0)):
        cols = pl.ds(block * width, width)
        loads.append(pltpu.make_async_copy(w_proj.at[:, cols], wp.at[n], load_sem.at[n + 1]))
    rest = (
        (ln_gain_hbm, ln_gain),
        (pool_query_hbm, pool_query),
        (slots_hbm, slots),
        (cand_ids_hbm, cand_ids),
        (b_rank_hbm, b_rank),
        (w_score_hbm, w_score),
        (w_out, wo),
        (item_table, table),
        (w_rank, wr.at[mp]),
    )
    for n, (src, dst) in enumerate(rest):
        loads.append(pltpu.make_async_copy(src, dst, load_sem.at[5 + n]))
    loads[0].start()
    loads[5].start()
    for load in loads[1:5] + loads[6:]:
        load.start()

    pieces[...] = jnp.zeros_like(pieces)

    barrier = pltpu.get_barrier_semaphore()
    height = line // 2
    low = height // 2
    level = lax.div(mp, 2) * low + owner

    def level_device(k):
        far = lax.div(k + 1, 2)
        chip = lax.rem(low + far * (1 - 2 * lax.rem(k, 2)) + level, height)
        return {"users": lax.rem(chip, low), "mp": 2 * lax.div(chip, low) + core}

    def along(a, b):
        return {"tm": lax.rem(x + a, SIDE) * SIDE + lax.rem(y + b, SIDE)}

    def along_y(b, other):
        return {"tm": x * SIDE + lax.rem(y + b, SIDE), "mp": mp + other * (1 - 2 * core)}

    greeted = [along(a, b) for a, b in STEPS] + [along_y(b, 1) for b in range(SIDE)]
    for device in greeted:
        pl.semaphore_signal(barrier, inc=1, device_id=device, device_id_type=MESH)

    @pl.loop(0, height - 1)
    def _(k):
        pl.semaphore_signal(barrier, inc=1, device_id=level_device(k), device_id_type=MESH)

    first_pos = t * events
    length = lengths[0]
    pos = first_pos + lax.broadcasted_iota(jnp.int32, (events, 1), 0)
    live = pos < length
    loads[0].wait()
    loads[5].wait()
    normed[...] = (layer_norm(hist[...].astype(F32)) * ln_gain[...]).astype(BF16)

    def project(n):
        loads[n + 1].wait()
        half = 0.5 * jnp.dot(normed[...], wp[n], preferred_element_type=F32)
        return silu_of_twice(half)

    keys = project(0).astype(BF16)
    for h in range(HEADS):
        qkv[h, 0] = keys[:, h * head_size : (h + 1) * head_size]
    values = jnp.where(live, project(1), 0.0).astype(BF16)
    for h in range(HEADS):
        qkv[h, 1] = values[:, h * head_size : (h + 1) * head_size]

    pl.semaphore_wait(barrier, len(greeted) + height - 1)

    kv_copies, q_copies = [], []
    for rel in (3, 2, 1):
        a, b = moved(x, y, rel)
        copy = pltpu.make_async_remote_copy(
            src_ref=qkv.at[head_of(a, b), pl.ds(0, 2)],
            dst_ref=kv.at[rel],
            send_sem=kv_send.at[rel],
            recv_sem=kv_recv.at[rel],
            device_id=in_plane(a, b),
            device_id_type=MESH,
        )
        copy.start()
        kv_copies.append(copy)

    query = (project(2) * (0.5 * head_size**-0.5)).astype(BF16)
    for h in range(HEADS):
        qkv[h, 2] = query[:, h * head_size : (h + 1) * head_size]
    for rel in (3, 2, 1):
        a, b = moved(x, y, rel)
        copy = pltpu.make_async_remote_copy(
            src_ref=qkv.at[head_of(a, b), 2],
            dst_ref=qs.at[rel],
            send_sem=q_send.at[rel],
            recv_sem=q_recv.at[rel],
            device_id=in_plane(a, b),
            device_id_type=MESH,
        )
        copy.start()
        q_copies.append(copy)
    for load in loads[9:11] + loads[13:]:
        load.wait()
    vectors[mp, 0:1] = b_rank[...]
    vectors[mp, 1:2] = w_score[...]

    @pl.when(near == 0)
    def _():
        for k in range(PARTS):
            send_weights(mp, k, over, over_send).start()
        send_vectors(mp, over, over_send).start()

    kv[0] = qkv[head, pl.ds(0, 2)]
    qs[0] = qkv[head, 2]

    x_near, y_near = even(x), ring_y(y)

    def pass_kv(n):
        return pltpu.make_async_remote_copy(
            src_ref=kv.at[n],
            dst_ref=kv.at[HEADS + n],
            send_sem=pass_send.at[0, n],
            recv_sem=pass_recv.at[0, n],
            device_id=in_plane(x_near, y),
            device_id_type=MESH,
        )

    def pass_q(n):
        return pltpu.make_async_remote_copy(
            src_ref=qs.at[n],
            dst_ref=qs.at[HEADS + n],
            send_sem=pass_send.at[1, n],
            recv_sem=pass_recv.at[1, n],
            device_id=in_plane(x, y_near),
            device_id_type=MESH,
        )

    def back_copy(n, which):
        a, b = moved(x, y_near if which else y, n)
        return pltpu.make_async_remote_copy(
            src_ref=back.at[which, n],
            dst_ref=att.at[which, head],
            send_sem=back_send.at[which, n],
            recv_sem=back_recv.at[which, n],
            device_id=in_plane(a, b),
            device_id_type=MESH,
        )

    pass_q(0).start()
    pass_kv(0).start()

    gate[...] = project(3).astype(BF16)
    acc[...] = jnp.zeros_like(acc)

    owned, count = cand_ids.shape
    pool = table.shape[0]
    for load in loads[6:9] + loads[11:13]:
        load.wait()

    @pl.loop(0, owned)
    def _(r):
        @pl.when(r > 0)
        def _():
            pltpu.make_async_copy(kv.at[r], kv.at[r], kv_recv.at[r]).wait()
            pass_kv(r).start()

        eye = lax.broadcasted_iota(jnp.int32, (count, count), 0) == lax.broadcasted_iota(
            jnp.int32, (count, count), 1
        )
        item = lax.broadcasted_iota(jnp.int32, (count, pool), 1).astype(F32)
        ids = cand_ids[pl.ds(r, 1), :].astype(F32)
        column = jnp.sum(jnp.where(eye, ids, 0.0), axis=1, keepdims=True)
        onehot = jnp.where(item == column, 1.0, 0.0).astype(BF16)
        cand[pl.ds(r * count, count)] = jnp.dot(
            onehot, table[...], preferred_element_type=F32
        ).astype(BF16)

    pairs = 2 * events
    behind = lax.broadcasted_iota(jnp.int32, (events, events), 0) >= lax.broadcasted_iota(
        jnp.int32, (events, events), 1
    )
    masks[0] = jnp.zeros((events, events), F32)
    masks[1] = jnp.where(behind, 1.0, 0.0)
    masks[2] = jnp.ones((events, events), F32)

    def rows_of(which, pair):
        return pl.ds(pl.multiple_of((2 * which + pair) * pairs, pairs), pairs)

    def attend(q_set, q_pair, k_set, k_pair, masked):
        q_first, k_first = HEADS * q_set + 2 * q_pair, HEADS * k_set + 2 * k_pair
        query = qs[pl.ds(q_first, 2)].reshape(pairs, head_size)
        half = jnp.concatenate(
            [dot_t(query, kv[k_first + n, 0]) for n in range(2)], axis=1
        )
        if masked:
            q_y = y_near if q_set else y
            half = jnp.concatenate(
                [
                    jnp.concatenate(
                        [
                            half[a * events : (a + 1) * events, b * events : (b + 1) * events]
                            * masks[1 + jnp.clip(q_row - k_row, -1, 1)]
                            for b, k_row in enumerate((y, swap_y(y)))
                        ],
                        axis=1,
                    )
                    for a, q_row in enumerate((q_y, swap_y(q_y)))
                ],
                axis=0,
            )
        weights = silu_of_twice(half).astype(BF16)
        value = jnp.concatenate([kv[k_first + n, 1] for n in range(2)], axis=0)
        acc[rows_of(q_set, q_pair)] += jnp.dot(weights, value, preferred_element_type=F32)

    late = jnp.where(x < SIDE // 2, 1, 0)
    early = 1 - late
    outer = jnp.logical_or(x == 0, x == SIDE - 1)

    def attend_own(q_set):
        for pair in range(2):
            attend(q_set, pair, 0, pair, True)
        attend(q_set, late, 0, early, False)

    def attend_near(q_set, n):
        q_pair = late if n else jnp.where(outer, late, early)
        k_pair = jnp.where(outer, n, jnp.where(x == 1, 0, 1))
        attend(q_set, q_pair, 1, k_pair, False)

    for n in range(1, HEADS):
        pltpu.make_async_copy(qs.at[n], qs.at[n], q_recv.at[n]).wait()
        pass_q(n).start()
    attend_own(0)
    for n in range(HEADS):
        pass_q(n).wait_recv()
    attend(1, 0, 0, 0, True)
    attend(1, 1, 0, 1, True)
    relay(0)
    attend(1, late, 0, early, False)
    for n in range(HEADS):
        pass_kv(n).wait_recv()
    attend_near(1, 0)
    attend_near(1, 1)
    for n in (3, 2, 1, 0):
        back[1, n] = acc[pl.ds((HEADS + n) * events, events)].astype(BF16)
        back_copy(n, 1).start()
    relay(1)
    attend_near(0, 0)
    attend_near(0, 1)

    for n in (3, 2, 1):
        back[0, n] = acc[pl.ds(n * events, events)].astype(BF16)
        back_copy(n, 0).start()
    att[0, head] = acc[pl.ds(0, events)].astype(BF16)
    relay(2)
    for n in range(HEADS):
        back_copy(n, 1).wait_recv()
    for n in range(1, HEADS):
        back_copy(n, 0).wait_recv()
    relay(3)

    attended = jnp.concatenate(
        [att[0, h].astype(F32) + att[1, h].astype(F32) for h in range(HEADS)], axis=1
    )
    mixed = (layer_norm(attended) * gate[...].astype(F32)).astype(BF16)
    projected = jnp.dot(mixed, wo[...], preferred_element_type=F32)
    out = (hist[...].astype(F32) + projected).astype(BF16)
    layer_out[0] = out
    groups = pool_query.shape[0]
    half = 0.5 * dot_t(pool_query[...], out)
    lane = first_pos + lax.broadcasted_iota(jnp.int32, half.shape, 1)
    pool_w = jnp.where(lane < length, silu_of_twice(half), 0.0).astype(BF16)
    sums = jnp.dot(pool_w, out, preferred_element_type=F32)

    for g in range(groups):
        part[g] = sums[g : g + 1]
    for a, b in STEPS:
        pltpu.make_async_remote_copy(
            src_ref=part.at[lax.rem(y + b, SIDE)],
            dst_ref=parts.at[t],
            send_sem=sum_sem.at[0],
            recv_sem=sum_sem.at[1],
            device_id=along(a, b),
            device_id_type=MESH,
        ).start()

    def wait_for(buffer, many, sem):
        some = buffer.at[pl.ds(0, many)]
        pltpu.make_async_copy(some, some, sem).wait()

    parts[t] = part[y]
    relay(4)
    wait_for(parts, plane - 1, sum_sem.at[1])
    state = jnp.sum(parts[...], axis=0).astype(BF16).astype(F32)

    own_interest = layer_norm(state).astype(BF16).astype(F32)
    told[...] = own_interest
    pieces[user] = own_interest

    @pl.loop(0, height - 1)
    def _(k):
        pltpu.make_async_remote_copy(
            src_ref=told,
            dst_ref=pieces.at[user],
            send_sem=state_sem.at[0],
            recv_sem=state_sem.at[1],
            device_id=level_device(k),
            device_id_type=MESH,
        ).start()

    relay(5)
    own_half = lax.div(mp, 2)
    pre[own_half] = jnp.dot(cand[...], wr[mp, :width], preferred_element_type=F32)
    wait_for(pieces, height - 1, state_sem.at[1])
    mine = owner * owned + lax.broadcasted_iota(jnp.int32, (owned, line), 0)
    picker = jnp.where(slots[...] == mine, 1.0, 0.0).astype(BF16)
    known = pieces[...].reshape(line, width).astype(BF16)
    own_slots = jnp.dot(picker, known, preferred_element_type=F32)
    chosen[...] = own_slots
    interests[core * SIDE + y] = own_slots
    for b, n in ((2, 0), (2, 1), (1, 0), (3, 0), (1, 1), (3, 1), (0, 1)):
        pltpu.make_async_remote_copy(
            src_ref=chosen,
            dst_ref=interests.at[core * SIDE + y],
            send_sem=pick_sem.at[0],
            recv_sem=pick_sem.at[1],
            device_id=along_y(b, n),
            device_id_type=MESH,
        ).start()

    relay(6)
    pre[1 - own_half] = jnp.dot(cand[...], wr[across, :width], preferred_element_type=F32)
    wait_for(interests, 2 * SIDE - 1, pick_sem.at[1])

    interest = jnp.concatenate(
        [interests[g] + interests[SIDE + g] for g in range(groups)], axis=0
    ).astype(BF16)
    half = (0.5 * width**-0.5) * dot_t(cand[...], interest)
    row = lax.div(lax.broadcasted_iota(jnp.int32, half.shape, 0), count)
    column = lax.rem(lax.broadcasted_iota(jnp.int32, half.shape, 1), owned)
    attn = jnp.where(row == column, silu_of_twice(half), 0.0)
    high = attn.astype(BF16)
    low = (attn - high.astype(F32)).astype(BF16)
    factors = jnp.concatenate([high, low, high], axis=1)
    terms = jnp.zeros_like(pre[0])
    for n in range(2):
        block = core + 2 * n
        mixed_in = jnp.dot(interest, wr[block, width:], preferred_element_type=F32)
        large = mixed_in.astype(BF16)
        small = (mixed_in - large.astype(F32)).astype(BF16)
        more = jnp.dot(
            factors, jnp.concatenate([large, large, small], axis=0), preferred_element_type=F32
        )
        half = 0.5 * (pre[n] + vectors[block, 0:1] + more)
        terms += silu_of_twice(half) * vectors[block, 1:2]
    high = terms.astype(BF16)
    low = (terms - high.astype(F32)).astype(BF16)
    ones = jnp.ones((16, terms.shape[1]), BF16)
    own_share = (dot_t(ones, high) + dot_t(ones, low))[0:1]
    share[...] = own_share
    shares[core] = own_share
    exchange = pltpu.make_async_remote_copy(
        src_ref=share,
        dst_ref=shares.at[core],
        send_sem=twin_sem.at[0],
        recv_sem=twin_sem.at[1],
        device_id={"mp": twin},
        device_id_type=MESH,
    )
    exchange.start()
    exchange.wait_recv()
    total = jnp.sum(shares[...], axis=0)
    for r in range(owned):
        scores[r : r + 1, :] = total[0:1, r * count : (r + 1) * count]

    for copy in kv_copies + q_copies:
        copy.wait_send()
    for n in range(HEADS):
        pass_kv(n).wait_send()
        pass_q(n).wait_send()
        back_copy(n, 1).wait_send()
    for n in range(1, HEADS):
        back_copy(n, 0).wait_send()
    wait_for(parts, plane - 1, sum_sem.at[0])
    wait_for(pieces, height - 1, state_sem.at[0])
    wait_for(interests, 2 * SIDE - 1, pick_sem.at[0])
    exchange.wait_send()

    @pl.when(near == 0)
    def _():
        for k in range(PARTS):
            send_weights(mp, k, over, over_send).wait_send()
        send_vectors(mp, over, over_send).wait_send()

    @pl.when(near < ends_at)
    def _():
        for k in range(PARTS):
            send_weights(across, k, onward, chain_send).wait_send()
        send_vectors(across, onward, chain_send).wait_send()


def solution(mesh):
    plane, owners, ranks = mesh.shape["tm"], mesh.shape["users"], mesh.shape["mp"]
    line = owners * ranks

    def shards(
        history,
        ln_gain,
        w_proj,
        w_out,
        pool_query,
        lengths,
        slots,
        cand_ids,
        item_table,
        w_rank,
        b_rank,
        w_score,
    ):
        _, events, width = history.shape
        head_size = width // HEADS
        groups = pool_query.shape[0]
        owned, count = cand_ids.shape
        cands = owned * count
        hidden = w_rank.shape[1]
        vmem = pl.BlockSpec(memory_space=pltpu.VMEM)
        smem = pl.BlockSpec(memory_space=pltpu.SMEM)
        hbm = pl.BlockSpec(memory_space=pltpu.HBM)
        dma = pltpu.SemaphoreType.DMA
        return pl.pallas_call(
            kernel,
            out_shape=(
                jax.ShapeDtypeStruct(history.shape, BF16),
                jax.ShapeDtypeStruct((owned, count), F32),
            ),
            in_specs=[smem] + [hbm] * 11,
            out_specs=(vmem, vmem),
            scratch_shapes=[
                pltpu.VMEM((events, width), BF16),
                pltpu.VMEM((1, width), F32),
                pltpu.VMEM(pool_query.shape, BF16),
                pltpu.VMEM((1, line), jnp.int32),
                pltpu.VMEM((owned, count), jnp.int32),
                pltpu.VMEM((1, hidden), F32),
                pltpu.VMEM((1, hidden), F32),
                pltpu.VMEM((4, width, width), BF16),
                pltpu.VMEM((width, width), BF16),
                pltpu.VMEM(item_table.shape, BF16),
                pltpu.VMEM((ranks, *w_rank.shape), BF16),
                pltpu.VMEM((events, width), BF16),
                pltpu.VMEM((events, width), BF16),
                pltpu.VMEM((HEADS, 3, events, head_size), BF16),
                pltpu.VMEM((2 * HEADS, 2, events, head_size), BF16),
                pltpu.VMEM((2 * HEADS, events, head_size), BF16),
                pltpu.VMEM((2 * HEADS * events, head_size), F32),
                pltpu.VMEM((2, HEADS, events, head_size), BF16),
                pltpu.VMEM((2, HEADS, events, head_size), BF16),
                pltpu.VMEM((3, events, events), F32),
                pltpu.VMEM((cands, width), BF16),
                pltpu.VMEM((2, cands, hidden), F32),
                pltpu.VMEM((groups, 1, width), F32),
                pltpu.VMEM((plane, 1, width), F32),
                pltpu.VMEM((1, width), F32),
                pltpu.VMEM((line, 1, width), F32),
                pltpu.VMEM((owned, width), F32),
                pltpu.VMEM((2 * SIDE, owned, width), F32),
                pltpu.VMEM((ranks, 2, hidden), F32),
                pltpu.VMEM((1, cands), F32),
                pltpu.VMEM((2, 1, cands), F32),
                dma((14,)),
                dma((HEADS,)),
                dma((HEADS,)),
                dma((HEADS,)),
                dma((HEADS,)),
                dma((2, HEADS)),
                dma((2, HEADS)),
                dma((2, HEADS)),
                dma((2, HEADS)),
                dma((2,)),
                dma((2,)),
                dma((2,)),
                dma((PARTS + 1,)),
                dma((PARTS + 1,)),
                dma((PARTS + 1,)),
                dma((2,)),
            ],
            compiler_params=pltpu.CompilerParams(
                collective_id=0, has_side_effects=True, vmem_limit_bytes=VMEM_BYTES
            ),
            cost_estimate=pl.CostEstimate(
                flops=4_000_000_000, bytes_accessed=6_000_000, transcendentals=5_000_000
            ),
        )(
            lengths,
            history,
            ln_gain.reshape(1, -1),
            w_proj,
            w_out,
            pool_query,
            slots.reshape(1, -1),
            cand_ids,
            item_table,
            w_rank,
            b_rank.reshape(1, -1),
            w_score.reshape(1, -1),
        )

    placed = (
        P(("users", "mp"), "tm", None),
        P(),
        P(),
        P(),
        P(),
        P(("users", "mp")),
        P(),
        P("users", "tm"),
        P("users", None),
        P(None, "mp"),
        P("mp"),
        P("mp"),
    )
    return jax.shard_map(
        shards,
        mesh=mesh,
        in_specs=placed,
        out_specs=(P(("users", "mp"), "tm", None), P("users", "tm")),
        check_vma=False,
    )
```

```python
import jax
import jax.numpy as jnp
from jax import lax
from jax.experimental import pallas as pl
from jax.experimental.pallas import tpu as pltpu
from jax.sharding import PartitionSpec as P

HEADS = 4
SIDE = 4
EPS = 1e-05
PARTS = 4
VMEM_BYTES = 64 * 1024 * 1024
MESH = pl.DeviceIdType.MESH
STEPS = sorted(
    ((a, b) for a in range(SIDE) for b in range(SIDE) if a or b),
    key=lambda step: -sum(min(n, SIDE - n) for n in step),
)
F32 = jnp.float32
BF16 = jnp.bfloat16
ROWS_BY_ROWS = (((1,), (1,)), ((), ()))


def layer_norm(values):
    mean = jnp.mean(values, axis=-1, keepdims=True)
    centred = values - mean
    var = jnp.mean(centred * centred, axis=-1, keepdims=True)
    return centred * lax.rsqrt(var + EPS)


def silu_of_twice(half):
    return half + half * jnp.tanh(half)


def dot_t(a, b, **kw):
    return lax.dot_general(a, b, ROWS_BY_ROWS, preferred_element_type=F32, **kw)


def kernel(
    lengths,
    history,
    ln_gain_hbm,
    w_proj,
    w_out,
    pool_query_hbm,
    slots_hbm,
    cand_ids_hbm,
    item_table,
    w_rank,
    b_rank_hbm,
    w_score_hbm,
    layer_out,
    scores,
    hist,
    ln_gain,
    pool_query,
    slots,
    cand_ids,
    b_rank,
    w_score,
    wp,
    wo,
    table,
    wr,
    normed,
    gate,
    qkv,
    kv,
    qs,
    acc,
    back,
    att,
    masks,
    cand,
    pre,
    part,
    parts,
    told,
    pieces,
    chosen,
    interests,
    vectors,
    share,
    shares,
    load_sem,
    kv_send,
    kv_recv,
    q_send,
    q_recv,
    pass_send,
    pass_recv,
    back_send,
    back_recv,
    sum_sem,
    state_sem,
    pick_sem,
    over_send,
    chain_send,
    chain_recv,
    twin_sem,
):
    events, width = hist.shape
    head_size = width // HEADS
    plane, line, ranks = parts.shape[0], pieces.shape[0], wr.shape[0]
    t = lax.axis_index("tm")
    owner = lax.axis_index("users")
    mp = lax.axis_index("mp")
    user = owner * ranks + mp
    x, y = lax.div(t, SIDE), lax.rem(t, SIDE)
    core = lax.rem(mp, 2)

    def even(v):
        return v + 1 - 2 * lax.rem(v, 2)

    def odd(v):
        return SIDE - 1 - v

    def swap_y(v):
        return even(v) + core * (odd(v) - even(v))

    def ring_y(v):
        return odd(v) + core * (even(v) - odd(v))

    def head_of(a, b):
        first = lax.rem(lax.div(b + 1, 2), 2)
        return 2 * lax.div(a, 2) + first + core * (lax.div(b, 2) - first)

    def moved(a, b, rel):
        first, second = lax.rem(rel, 2), lax.div(rel, 2)
        return a + second * (odd(a) - a), b + first * (swap_y(b) - b)

    def in_plane(a, b):
        return {"tm": a * SIDE + b}

    head = head_of(x, y)

    depth = wr.shape[1] // PARTS
    last = line // ranks - 1
    twin = mp + 1 - 2 * core
    across = lax.rem(mp + 2, ranks)
    near = jnp.minimum(owner, last - owner)
    step_on = jnp.where(owner < near + 1, 1, -1)
    ends_at = last // 2

    def weights_of(whose, k):
        rows = pl.ds(pl.multiple_of(k * depth, depth), depth)
        return wr.at[whose, rows]

    def send_weights(whose, k, to, sems):
        return pltpu.make_async_remote_copy(
            src_ref=weights_of(whose, k),
            dst_ref=weights_of(whose, k),
            send_sem=sems.at[k],
            recv_sem=chain_recv.at[k],
            device_id=to,
            device_id_type=MESH,
        )

    def send_vectors(whose, to, sems):
        return pltpu.make_async_remote_copy(
            src_ref=vectors.at[whose],
            dst_ref=vectors.at[whose],
            send_sem=sems.at[PARTS],
            recv_sem=chain_recv.at[PARTS],
            device_id=to,
            device_id_type=MESH,
        )

    over = {"users": last - owner, "mp": across}
    onward = {"users": owner + step_on}

    def relay(j):
        k = j - near

        @pl.when(jnp.logical_and(k >= 0, k < PARTS))
        def _():
            here = weights_of(across, k)
            pltpu.make_async_copy(here, here, chain_recv.at[k]).wait()

            @pl.when(near < ends_at)
            def _():
                send_weights(across, k, onward, chain_send).start()

            @pl.when(k == PARTS - 1)
            def _():
                here = vectors.at[across]
                pltpu.make_async_copy(here, here, chain_recv.at[PARTS]).wait()

                @pl.when(near < ends_at)
                def _():
                    send_vectors(across, onward, chain_send).start()

    loads = [pltpu.make_async_copy(history.at[0], hist, load_sem.at[0])]
    for n, block in enumerate((3, 1, 2, 0)):
        cols = pl.ds(block * width, width)
        loads.append(pltpu.make_async_copy(w_proj.at[:, cols], wp.at[n], load_sem.at[n + 1]))
    rest = (
        (ln_gain_hbm, ln_gain),
        (pool_query_hbm, pool_query),
        (slots_hbm, slots),
        (cand_ids_hbm, cand_ids),
        (b_rank_hbm, b_rank),
        (w_score_hbm, w_score),
        (w_out, wo),
        (item_table, table),
        (w_rank, wr.at[mp]),
    )
    for n, (src, dst) in enumerate(rest):
        loads.append(pltpu.make_async_copy(src, dst, load_sem.at[5 + n]))
    loads[0].start()
    loads[5].start()
    for load in loads[1:5] + loads[6:]:
        load.start()

    pieces[...] = jnp.zeros_like(pieces)

    barrier = pltpu.get_barrier_semaphore()
    height = line // 2
    low = height // 2
    level = lax.div(mp, 2) * low + owner

    levels = []
    for k in range(height - 1):
        chip = lax.rem(level + low + (k + 1) // 2 * (1 - 2 * (k % 2)), height)
        levels.append({"users": lax.rem(chip, low), "mp": 2 * lax.div(chip, low) + core})

    def along(a, b):
        return {"tm": lax.rem(x + a, SIDE) * SIDE + lax.rem(y + b, SIDE)}

    def along_y(b, other):
        return {"tm": x * SIDE + lax.rem(y + b, SIDE), "mp": mp + other * (1 - 2 * core)}

    greeted = [along(a, b) for a, b in STEPS] + [along_y(b, 1) for b in range(SIDE)]
    greeted = levels + greeted
    for device in greeted:
        pl.semaphore_signal(barrier, inc=1, device_id=device, device_id_type=MESH)

    first_pos = t * events
    length = lengths[0]
    pos = first_pos + lax.broadcasted_iota(jnp.int32, (events, 1), 0)
    live = pos < length
    loads[0].wait()
    loads[5].wait()
    normed[...] = (layer_norm(hist[...].astype(F32)) * ln_gain[...]).astype(BF16)

    def project(n):
        loads[n + 1].wait()
        half = 0.5 * jnp.dot(normed[...], wp[n], preferred_element_type=F32)
        return silu_of_twice(half)

    keys = project(0).astype(BF16)
    for h in range(HEADS):
        qkv[h, 0] = keys[:, h * head_size : (h + 1) * head_size]
    values = jnp.where(live, project(1), 0.0).astype(BF16)
    for h in range(HEADS):
        qkv[h, 1] = values[:, h * head_size : (h + 1) * head_size]

    pl.semaphore_wait(barrier, len(greeted))

    kv_copies, q_copies = [], []
    for rel in (3, 2, 1):
        a, b = moved(x, y, rel)
        copy = pltpu.make_async_remote_copy(
            src_ref=qkv.at[head_of(a, b), pl.ds(0, 2)],
            dst_ref=kv.at[rel],
            send_sem=kv_send.at[rel],
            recv_sem=kv_recv.at[rel],
            device_id=in_plane(a, b),
            device_id_type=MESH,
        )
        copy.start()
        kv_copies.append(copy)

    query = (project(2) * (0.5 * head_size**-0.5)).astype(BF16)
    for h in range(HEADS):
        qkv[h, 2] = query[:, h * head_size : (h + 1) * head_size]
    for rel in (3, 2, 1):
        a, b = moved(x, y, rel)
        copy = pltpu.make_async_remote_copy(
            src_ref=qkv.at[head_of(a, b), 2],
            dst_ref=qs.at[rel],
            send_sem=q_send.at[rel],
            recv_sem=q_recv.at[rel],
            device_id=in_plane(a, b),
            device_id_type=MESH,
        )
        copy.start()
        q_copies.append(copy)
    for load in loads[9:11] + loads[13:]:
        load.wait()
    vectors[mp, 0:1] = b_rank[...]
    vectors[mp, 1:2] = w_score[...]

    @pl.when(near == 0)
    def _():
        for k in range(PARTS):
            send_weights(mp, k, over, over_send).start()
        send_vectors(mp, over, over_send).start()

    kv[0] = qkv[head, pl.ds(0, 2)]
    qs[0] = qkv[head, 2]

    x_near, y_near = even(x), ring_y(y)

    def pass_kv(n):
        return pltpu.make_async_remote_copy(
            src_ref=kv.at[n],
            dst_ref=kv.at[HEADS + n],
            send_sem=pass_send.at[0, n],
            recv_sem=pass_recv.at[0, n],
            device_id=in_plane(x_near, y),
            device_id_type=MESH,
        )

    def pass_q(n):
        return pltpu.make_async_remote_copy(
            src_ref=qs.at[n],
            dst_ref=qs.at[HEADS + n],
            send_sem=pass_send.at[1, n],
            recv_sem=pass_recv.at[1, n],
            device_id=in_plane(x, y_near),
            device_id_type=MESH,
        )

    def back_copy(n, which):
        a, b = moved(x, y_near if which else y, n)
        return pltpu.make_async_remote_copy(
            src_ref=back.at[which, n],
            dst_ref=att.at[which, head],
            send_sem=back_send.at[which, n],
            recv_sem=back_recv.at[which, n],
            device_id=in_plane(a, b),
            device_id_type=MESH,
        )

    pass_q(0).start()
    pass_kv(0).start()

    gate[...] = project(3).astype(BF16)
    acc[...] = jnp.zeros_like(acc)

    owned, count = cand_ids.shape
    pool = table.shape[0]
    for load in loads[6:9] + loads[11:13]:
        load.wait()

    @pl.loop(0, owned)
    def _(r):
        @pl.when(r > 0)
        def _():
            pltpu.make_async_copy(kv.at[r], kv.at[r], kv_recv.at[r]).wait()
            pass_kv(r).start()

        eye = lax.broadcasted_iota(jnp.int32, (count, count), 0) == lax.broadcasted_iota(
            jnp.int32, (count, count), 1
        )
        item = lax.broadcasted_iota(jnp.int32, (count, pool), 1).astype(F32)
        ids = cand_ids[pl.ds(r, 1), :].astype(F32)
        column = jnp.sum(jnp.where(eye, ids, 0.0), axis=1, keepdims=True)
        onehot = jnp.where(item == column, 1.0, 0.0).astype(BF16)
        cand[pl.ds(r * count, count)] = jnp.dot(
            onehot, table[...], preferred_element_type=F32
        ).astype(BF16)

    pairs = 2 * events
    behind = lax.broadcasted_iota(jnp.int32, (events, events), 0) >= lax.broadcasted_iota(
        jnp.int32, (events, events), 1
    )
    masks[0] = jnp.zeros((events, events), F32)
    masks[1] = jnp.where(behind, 1.0, 0.0)
    masks[2] = jnp.ones((events, events), F32)

    def rows_of(which, pair):
        return pl.ds(pl.multiple_of((2 * which + pair) * pairs, pairs), pairs)

    def attend(q_set, q_pair, k_set, k_pair, masked):
        q_first, k_first = HEADS * q_set + 2 * q_pair, HEADS * k_set + 2 * k_pair
        query = qs[pl.ds(q_first, 2)].reshape(pairs, head_size)
        half = jnp.concatenate(
            [dot_t(query, kv[k_first + n, 0]) for n in range(2)], axis=1
        )
        if masked:
            q_y = y_near if q_set else y
            half = jnp.concatenate(
                [
                    jnp.concatenate(
                        [
                            half[a * events : (a + 1) * events, b * events : (b + 1) * events]
                            * masks[1 + jnp.clip(q_row - k_row, -1, 1)]
                            for b, k_row in enumerate((y, swap_y(y)))
                        ],
                        axis=1,
                    )
                    for a, q_row in enumerate((q_y, swap_y(q_y)))
                ],
                axis=0,
            )
        weights = silu_of_twice(half).astype(BF16)
        value = jnp.concatenate([kv[k_first + n, 1] for n in range(2)], axis=0)
        acc[rows_of(q_set, q_pair)] += jnp.dot(weights, value, preferred_element_type=F32)

    late = jnp.where(x < SIDE // 2, 1, 0)
    early = 1 - late
    outer = jnp.logical_or(x == 0, x == SIDE - 1)

    def attend_own(q_set):
        for pair in range(2):
            attend(q_set, pair, 0, pair, True)
        attend(q_set, late, 0, early, False)

    def attend_near(q_set, n):
        q_pair = late if n else jnp.where(outer, late, early)
        k_pair = jnp.where(outer, n, jnp.where(x == 1, 0, 1))
        attend(q_set, q_pair, 1, k_pair, False)

    for n in range(1, HEADS):
        pltpu.make_async_copy(qs.at[n], qs.at[n], q_recv.at[n]).wait()
        pass_q(n).start()
    attend_own(0)
    for n in range(HEADS):
        pass_q(n).wait_recv()
    attend(1, 0, 0, 0, True)
    attend(1, 1, 0, 1, True)
    relay(0)
    attend(1, late, 0, early, False)
    for n in range(HEADS):
        pass_kv(n).wait_recv()
    attend_near(1, 0)
    attend_near(1, 1)
    for n in (3, 2, 1, 0):
        back[1, n] = acc[pl.ds((HEADS + n) * events, events)].astype(BF16)
        back_copy(n, 1).start()
    relay(1)
    attend_near(0, 0)
    attend_near(0, 1)

    for n in (3, 2, 1):
        back[0, n] = acc[pl.ds(n * events, events)].astype(BF16)
        back_copy(n, 0).start()
    att[0, head] = acc[pl.ds(0, events)].astype(BF16)
    relay(2)
    for n in range(HEADS):
        back_copy(n, 1).wait_recv()
    for n in range(1, HEADS):
        back_copy(n, 0).wait_recv()
    relay(3)

    attended = jnp.concatenate(
        [att[0, h].astype(F32) + att[1, h].astype(F32) for h in range(HEADS)], axis=1
    )
    mixed = (layer_norm(attended) * gate[...].astype(F32)).astype(BF16)
    projected = jnp.dot(mixed, wo[...], preferred_element_type=F32)
    out = (hist[...].astype(F32) + projected).astype(BF16)
    layer_out[0] = out
    groups = pool_query.shape[0]
    half = 0.5 * dot_t(pool_query[...], out)
    lane = first_pos + lax.broadcasted_iota(jnp.int32, half.shape, 1)
    pool_w = jnp.where(lane < length, silu_of_twice(half), 0.0).astype(BF16)
    sums = jnp.dot(pool_w, out, preferred_element_type=F32)

    for g in range(groups):
        part[g] = sums[g : g + 1]
    for a, b in STEPS:
        pltpu.make_async_remote_copy(
            src_ref=part.at[lax.rem(y + b, SIDE)],
            dst_ref=parts.at[t],
            send_sem=sum_sem.at[0],
            recv_sem=sum_sem.at[1],
            device_id=along(a, b),
            device_id_type=MESH,
        ).start()

    def wait_for(buffer, many, sem):
        some = buffer.at[pl.ds(0, many)]
        pltpu.make_async_copy(some, some, sem).wait()

    parts[t] = part[y]
    relay(4)
    wait_for(parts, plane - 1, sum_sem.at[1])
    state = jnp.sum(parts[...], axis=0).astype(BF16).astype(F32)

    own_interest = layer_norm(state).astype(BF16).astype(F32)
    told[...] = own_interest
    pieces[user] = own_interest

    for device in levels:
        pltpu.make_async_remote_copy(
            src_ref=told,
            dst_ref=pieces.at[user],
            send_sem=state_sem.at[0],
            recv_sem=state_sem.at[1],
            device_id=device,
            device_id_type=MESH,
        ).start()

    relay(5)
    own_half = lax.div(mp, 2)
    pre[own_half] = jnp.dot(cand[...], wr[mp, :width], preferred_element_type=F32)
    wait_for(pieces, height - 1, state_sem.at[1])
    mine = owner * owned + lax.broadcasted_iota(jnp.int32, (owned, line), 0)
    picker = jnp.where(slots[...] == mine, 1.0, 0.0).astype(BF16)
    known = pieces[...].reshape(line, width).astype(BF16)
    own_slots = jnp.dot(picker, known, preferred_element_type=F32)
    chosen[...] = own_slots
    interests[core * SIDE + y] = own_slots
    for b, n in ((2, 0), (2, 1), (1, 0), (3, 0), (1, 1), (3, 1), (0, 1)):
        pltpu.make_async_remote_copy(
            src_ref=chosen,
            dst_ref=interests.at[core * SIDE + y],
            send_sem=pick_sem.at[0],
            recv_sem=pick_sem.at[1],
            device_id=along_y(b, n),
            device_id_type=MESH,
        ).start()

    relay(6)
    pre[1 - own_half] = jnp.dot(cand[...], wr[across, :width], preferred_element_type=F32)
    wait_for(interests, 2 * SIDE - 1, pick_sem.at[1])

    interest = jnp.concatenate(
        [interests[g] + interests[SIDE + g] for g in range(groups)], axis=0
    ).astype(BF16)
    half = (0.5 * width**-0.5) * dot_t(cand[...], interest)
    row = lax.div(lax.broadcasted_iota(jnp.int32, half.shape, 0), count)
    column = lax.rem(lax.broadcasted_iota(jnp.int32, half.shape, 1), owned)
    attn = jnp.where(row == column, silu_of_twice(half), 0.0)
    high = attn.astype(BF16)
    low = (attn - high.astype(F32)).astype(BF16)
    factors = jnp.concatenate([high, low, high], axis=1)
    terms = jnp.zeros_like(pre[0])
    for n in range(2):
        block = core + 2 * n
        mixed_in = jnp.dot(interest, wr[block, width:], preferred_element_type=F32)
        large = mixed_in.astype(BF16)
        small = (mixed_in - large.astype(F32)).astype(BF16)
        more = jnp.dot(
            factors, jnp.concatenate([large, large, small], axis=0), preferred_element_type=F32
        )
        half = 0.5 * (pre[n] + vectors[block, 0:1] + more)
        terms += silu_of_twice(half) * vectors[block, 1:2]
    high = terms.astype(BF16)
    low = (terms - high.astype(F32)).astype(BF16)
    ones = jnp.ones((16, terms.shape[1]), BF16)
    own_share = (dot_t(ones, high) + dot_t(ones, low))[0:1]
    share[...] = own_share
    shares[core] = own_share
    exchange = pltpu.make_async_remote_copy(
        src_ref=share,
        dst_ref=shares.at[core],
        send_sem=twin_sem.at[0],
        recv_sem=twin_sem.at[1],
        device_id={"mp": twin},
        device_id_type=MESH,
    )
    exchange.start()
    exchange.wait_recv()
    total = jnp.sum(shares[...], axis=0)
    for r in range(owned):
        scores[r : r + 1, :] = total[0:1, r * count : (r + 1) * count]

    for copy in kv_copies + q_copies:
        copy.wait_send()
    for n in range(HEADS):
        pass_kv(n).wait_send()
        pass_q(n).wait_send()
        back_copy(n, 1).wait_send()
    for n in range(1, HEADS):
        back_copy(n, 0).wait_send()
    wait_for(parts, plane - 1, sum_sem.at[0])
    wait_for(pieces, height - 1, state_sem.at[0])
    wait_for(interests, 2 * SIDE - 1, pick_sem.at[0])
    exchange.wait_send()

    @pl.when(near == 0)
    def _():
        for k in range(PARTS):
            send_weights(mp, k, over, over_send).wait_send()
        send_vectors(mp, over, over_send).wait_send()

    @pl.when(near < ends_at)
    def _():
        for k in range(PARTS):
            send_weights(across, k, onward, chain_send).wait_send()
        send_vectors(across, onward, chain_send).wait_send()


def solution(mesh):
    plane, owners, ranks = mesh.shape["tm"], mesh.shape["users"], mesh.shape["mp"]
    line = owners * ranks

    def shards(
        history,
        ln_gain,
        w_proj,
        w_out,
        pool_query,
        lengths,
        slots,
        cand_ids,
        item_table,
        w_rank,
        b_rank,
        w_score,
    ):
        _, events, width = history.shape
        head_size = width // HEADS
        groups = pool_query.shape[0]
        owned, count = cand_ids.shape
        cands = owned * count
        hidden = w_rank.shape[1]
        vmem = pl.BlockSpec(memory_space=pltpu.VMEM)
        smem = pl.BlockSpec(memory_space=pltpu.SMEM)
        hbm = pl.BlockSpec(memory_space=pltpu.HBM)
        dma = pltpu.SemaphoreType.DMA
        return pl.pallas_call(
            kernel,
            out_shape=(
                jax.ShapeDtypeStruct(history.shape, BF16),
                jax.ShapeDtypeStruct((owned, count), F32),
            ),
            in_specs=[smem] + [hbm] * 11,
            out_specs=(vmem, vmem),
            scratch_shapes=[
                pltpu.VMEM((events, width), BF16),
                pltpu.VMEM((1, width), F32),
                pltpu.VMEM(pool_query.shape, BF16),
                pltpu.VMEM((1, line), jnp.int32),
                pltpu.VMEM((owned, count), jnp.int32),
                pltpu.VMEM((1, hidden), F32),
                pltpu.VMEM((1, hidden), F32),
                pltpu.VMEM((4, width, width), BF16),
                pltpu.VMEM((width, width), BF16),
                pltpu.VMEM(item_table.shape, BF16),
                pltpu.VMEM((ranks, *w_rank.shape), BF16),
                pltpu.VMEM((events, width), BF16),
                pltpu.VMEM((events, width), BF16),
                pltpu.VMEM((HEADS, 3, events, head_size), BF16),
                pltpu.VMEM((2 * HEADS, 2, events, head_size), BF16),
                pltpu.VMEM((2 * HEADS, events, head_size), BF16),
                pltpu.VMEM((2 * HEADS * events, head_size), F32),
                pltpu.VMEM((2, HEADS, events, head_size), BF16),
                pltpu.VMEM((2, HEADS, events, head_size), BF16),
                pltpu.VMEM((3, events, events), F32),
                pltpu.VMEM((cands, width), BF16),
                pltpu.VMEM((2, cands, hidden), F32),
                pltpu.VMEM((groups, 1, width), F32),
                pltpu.VMEM((plane, 1, width), F32),
                pltpu.VMEM((1, width), F32),
                pltpu.VMEM((line, 1, width), F32),
                pltpu.VMEM((owned, width), F32),
                pltpu.VMEM((2 * SIDE, owned, width), F32),
                pltpu.VMEM((ranks, 2, hidden), F32),
                pltpu.VMEM((1, cands), F32),
                pltpu.VMEM((2, 1, cands), F32),
                dma((14,)),
                dma((HEADS,)),
                dma((HEADS,)),
                dma((HEADS,)),
                dma((HEADS,)),
                dma((2, HEADS)),
                dma((2, HEADS)),
                dma((2, HEADS)),
                dma((2, HEADS)),
                dma((2,)),
                dma((2,)),
                dma((2,)),
                dma((PARTS + 1,)),
                dma((PARTS + 1,)),
                dma((PARTS + 1,)),
                dma((2,)),
            ],
            compiler_params=pltpu.CompilerParams(
                collective_id=0, has_side_effects=True, vmem_limit_bytes=VMEM_BYTES
            ),
            cost_estimate=pl.CostEstimate(
                flops=4_000_000_000, bytes_accessed=6_000_000, transcendentals=5_000_000
            ),
        )(
            lengths,
            history,
            ln_gain.reshape(1, -1),
            w_proj,
            w_out,
            pool_query,
            slots.reshape(1, -1),
            cand_ids,
            item_table,
            w_rank,
            b_rank.reshape(1, -1),
            w_score.reshape(1, -1),
        )

    placed = (
        P(("users", "mp"), "tm", None),
        P(),
        P(),
        P(),
        P(),
        P(("users", "mp")),
        P(),
        P("users", "tm"),
        P("users", None),
        P(None, "mp"),
        P("mp"),
        P("mp"),
    )
    return jax.shard_map(
        shards,
        mesh=mesh,
        in_specs=placed,
        out_specs=(P(("users", "mp"), "tm", None), P("users", "tm")),
        check_vma=False,
    )
```

```python
import jax
import jax.numpy as jnp
from jax import lax
from jax.experimental import pallas as pl
from jax.experimental.pallas import tpu as pltpu
from jax.sharding import PartitionSpec as P

HEADS = 4
SIDE = 4
EPS = 1e-05
PARTS = 4
VMEM_BYTES = 64 * 1024 * 1024
MESH = pl.DeviceIdType.MESH
STEPS = sorted(
    ((a, b) for a in range(SIDE) for b in range(SIDE) if a or b),
    key=lambda step: -sum(min(n, SIDE - n) for n in step),
)
F32 = jnp.float32
BF16 = jnp.bfloat16
ROWS_BY_ROWS = (((1,), (1,)), ((), ()))


def layer_norm(values):
    mean = jnp.mean(values, axis=-1, keepdims=True)
    centred = values - mean
    var = jnp.mean(centred * centred, axis=-1, keepdims=True)
    return centred * lax.rsqrt(var + EPS)


def silu_of_twice(half):
    return half + half * jnp.tanh(half)


def dot_t(a, b, **kw):
    return lax.dot_general(a, b, ROWS_BY_ROWS, preferred_element_type=F32, **kw)


def kernel(
    lengths,
    history,
    ln_gain_hbm,
    w_proj,
    w_out,
    pool_query_hbm,
    slots_hbm,
    cand_ids_hbm,
    item_table,
    w_rank,
    b_rank_hbm,
    w_score_hbm,
    layer_out,
    scores,
    hist,
    ln_gain,
    pool_query,
    slots,
    cand_ids,
    b_rank,
    w_score,
    wp,
    wo,
    table,
    wr,
    normed,
    gate,
    qkv,
    kv,
    qs,
    acc,
    back,
    att,
    masks,
    cand,
    pre,
    part,
    parts,
    told,
    pieces,
    chosen,
    interests,
    vectors,
    share,
    shares,
    load_sem,
    kv_send,
    kv_recv,
    q_send,
    q_recv,
    pass_send,
    pass_recv,
    back_send,
    back_recv,
    sum_sem,
    state_sem,
    pick_sem,
    over_send,
    chain_send,
    chain_recv,
    twin_sem,
):
    events, width = hist.shape
    head_size = width // HEADS
    plane, line, ranks = parts.shape[0], pieces.shape[0], wr.shape[0]
    t = lax.axis_index("tm")
    owner = lax.axis_index("users")
    mp = lax.axis_index("mp")
    user = owner * ranks + mp
    x, y = lax.div(t, SIDE), lax.rem(t, SIDE)
    core = lax.rem(mp, 2)

    def even(v):
        return v + 1 - 2 * lax.rem(v, 2)

    def odd(v):
        return SIDE - 1 - v

    def swap_y(v):
        return even(v) + core * (odd(v) - even(v))

    def ring_y(v):
        return odd(v) + core * (even(v) - odd(v))

    def head_of(a, b):
        first = lax.rem(lax.div(b + 1, 2), 2)
        return 2 * lax.div(a, 2) + first + core * (lax.div(b, 2) - first)

    def moved(a, b, rel):
        first, second = lax.rem(rel, 2), lax.div(rel, 2)
        return a + second * (odd(a) - a), b + first * (swap_y(b) - b)

    def in_plane(a, b):
        return {"tm": a * SIDE + b}

    head = head_of(x, y)

    depth = wr.shape[1] // PARTS
    last = line // ranks - 1
    twin = mp + 1 - 2 * core
    across = lax.rem(mp + 2, ranks)
    near = jnp.minimum(owner, last - owner)
    step_on = jnp.where(owner < near + 1, 1, -1)
    ends_at = last // 2

    def weights_of(whose, k):
        rows = pl.ds(pl.multiple_of(k * depth, depth), depth)
        return wr.at[whose, rows]

    def send_weights(whose, k, to, sems):
        return pltpu.make_async_remote_copy(
            src_ref=weights_of(whose, k),
            dst_ref=weights_of(whose, k),
            send_sem=sems.at[k],
            recv_sem=chain_recv.at[k],
            device_id=to,
            device_id_type=MESH,
        )

    def send_vectors(whose, to, sems):
        return pltpu.make_async_remote_copy(
            src_ref=vectors.at[whose],
            dst_ref=vectors.at[whose],
            send_sem=sems.at[PARTS],
            recv_sem=chain_recv.at[PARTS],
            device_id=to,
            device_id_type=MESH,
        )

    over = {"users": last - owner, "mp": across}
    onward = {"users": owner + step_on}

    def relay(j):
        k = j - near

        @pl.when(jnp.logical_and(k >= 0, k < PARTS))
        def _():
            here = weights_of(across, k)
            pltpu.make_async_copy(here, here, chain_recv.at[k]).wait()

            @pl.when(near < ends_at)
            def _():
                send_weights(across, k, onward, chain_send).start()

            @pl.when(k == PARTS - 1)
            def _():
                here = vectors.at[across]
                pltpu.make_async_copy(here, here, chain_recv.at[PARTS]).wait()

                @pl.when(near < ends_at)
                def _():
                    send_vectors(across, onward, chain_send).start()

    loads = [pltpu.make_async_copy(history.at[0], hist, load_sem.at[0])]
    for n, block in enumerate((3, 1, 2, 0)):
        cols = pl.ds(block * width, width)
        loads.append(pltpu.make_async_copy(w_proj.at[:, cols], wp.at[n], load_sem.at[n + 1]))
    rest = (
        (ln_gain_hbm, ln_gain),
        (pool_query_hbm, pool_query),
        (slots_hbm, slots),
        (cand_ids_hbm, cand_ids),
        (b_rank_hbm, b_rank),
        (w_score_hbm, w_score),
        (w_out, wo),
        (item_table, table),
        (w_rank, wr.at[mp]),
    )
    for n, (src, dst) in enumerate(rest):
        loads.append(pltpu.make_async_copy(src, dst, load_sem.at[5 + n]))
    loads[0].start()
    loads[5].start()
    for load in loads[1:5] + loads[6:]:
        load.start()

    pieces[...] = jnp.zeros_like(pieces)

    barrier = pltpu.get_barrier_semaphore()
    height = line // 2
    low = height // 2
    level = lax.div(mp, 2) * low + owner

    levels = []
    for k in range(height - 1):
        chip = lax.rem(level + low + (k + 1) // 2 * (1 - 2 * (k % 2)), height)
        levels.append({"users": lax.rem(chip, low), "mp": 2 * lax.div(chip, low) + core})

    def along(a, b):
        return {"tm": lax.rem(x + a, SIDE) * SIDE + lax.rem(y + b, SIDE)}

    def along_y(b, other):
        return {"tm": x * SIDE + lax.rem(y + b, SIDE), "mp": mp + other * (1 - 2 * core)}

    greeted = [along(a, b) for a, b in STEPS] + [along_y(b, 1) for b in range(SIDE)]
    greeted = levels + greeted
    for device in greeted:
        pl.semaphore_signal(barrier, inc=1, device_id=device, device_id_type=MESH)

    first_pos = t * events
    length = lengths[0]
    pos = first_pos + lax.broadcasted_iota(jnp.int32, (events, 1), 0)
    live = pos < length
    loads[0].wait()
    loads[5].wait()
    normed[...] = (layer_norm(hist[...].astype(F32)) * ln_gain[...]).astype(BF16)

    def project(n):
        loads[n + 1].wait()
        half = 0.5 * jnp.dot(normed[...], wp[n], preferred_element_type=F32)
        return silu_of_twice(half)

    keys = project(0).astype(BF16)
    for h in range(HEADS):
        qkv[h, 0] = keys[:, h * head_size : (h + 1) * head_size]
    values = jnp.where(live, project(1), 0.0).astype(BF16)
    for h in range(HEADS):
        qkv[h, 1] = values[:, h * head_size : (h + 1) * head_size]

    pl.semaphore_wait(barrier, len(greeted))

    kv_copies, q_copies = [], []
    for rel in (3, 2, 1):
        a, b = moved(x, y, rel)
        for n in range(2):
            copy = pltpu.make_async_remote_copy(
                src_ref=qkv.at[head_of(a, b), n],
                dst_ref=kv.at[rel, n],
                send_sem=kv_send.at[rel, n],
                recv_sem=kv_recv.at[rel, n],
                device_id=in_plane(a, b),
                device_id_type=MESH,
            )
            copy.start()
            kv_copies.append(copy)

    query = (project(2) * (0.5 * head_size**-0.5)).astype(BF16)
    for h in range(HEADS):
        qkv[h, 2] = query[:, h * head_size : (h + 1) * head_size]
    for rel in (3, 2, 1):
        a, b = moved(x, y, rel)
        copy = pltpu.make_async_remote_copy(
            src_ref=qkv.at[head_of(a, b), 2],
            dst_ref=qs.at[rel],
            send_sem=q_send.at[rel],
            recv_sem=q_recv.at[rel],
            device_id=in_plane(a, b),
            device_id_type=MESH,
        )
        copy.start()
        q_copies.append(copy)
    for load in loads[9:11] + loads[13:]:
        load.wait()
    vectors[mp, 0:1] = b_rank[...]
    vectors[mp, 1:2] = w_score[...]

    @pl.when(near == 0)
    def _():
        for k in range(PARTS):
            send_weights(mp, k, over, over_send).start()
        send_vectors(mp, over, over_send).start()

    kv[0] = qkv[head, pl.ds(0, 2)]
    qs[0] = qkv[head, 2]

    x_near, y_near = even(x), ring_y(y)

    def pass_kv(n, m):
        return pltpu.make_async_remote_copy(
            src_ref=kv.at[n, m],
            dst_ref=kv.at[HEADS + n, m],
            send_sem=pass_send.at[m, n],
            recv_sem=pass_recv.at[m, n],
            device_id=in_plane(x_near, y),
            device_id_type=MESH,
        )

    def pass_q(n):
        return pltpu.make_async_remote_copy(
            src_ref=qs.at[n],
            dst_ref=qs.at[HEADS + n],
            send_sem=pass_send.at[2, n],
            recv_sem=pass_recv.at[2, n],
            device_id=in_plane(x, y_near),
            device_id_type=MESH,
        )

    def back_copy(n, which):
        a, b = moved(x, y_near if which else y, n)
        return pltpu.make_async_remote_copy(
            src_ref=back.at[which, n],
            dst_ref=att.at[which, head],
            send_sem=back_send.at[which, n],
            recv_sem=back_recv.at[which, n],
            device_id=in_plane(a, b),
            device_id_type=MESH,
        )

    pass_q(0).start()
    for m in range(2):
        pass_kv(0, m).start()

    gate[...] = project(3).astype(BF16)
    acc[...] = jnp.zeros_like(acc)

    owned, count = cand_ids.shape
    pool = table.shape[0]
    for load in loads[6:9] + loads[11:13]:
        load.wait()

    @pl.loop(0, owned)
    def _(r):
        @pl.when(r > 0)
        def _():
            for m in range(2):
                pltpu.make_async_copy(kv.at[r, m], kv.at[r, m], kv_recv.at[r, m]).wait()
                pass_kv(r, m).start()

        eye = lax.broadcasted_iota(jnp.int32, (count, count), 0) == lax.broadcasted_iota(
            jnp.int32, (count, count), 1
        )
        item = lax.broadcasted_iota(jnp.int32, (count, pool), 1).astype(F32)
        ids = cand_ids[pl.ds(r, 1), :].astype(F32)
        column = jnp.sum(jnp.where(eye, ids, 0.0), axis=1, keepdims=True)
        onehot = jnp.where(item == column, 1.0, 0.0).astype(BF16)
        cand[pl.ds(r * count, count)] = jnp.dot(
            onehot, table[...], preferred_element_type=F32
        ).astype(BF16)

    pairs = 2 * events
    behind = lax.broadcasted_iota(jnp.int32, (events, events), 0) >= lax.broadcasted_iota(
        jnp.int32, (events, events), 1
    )
    masks[0] = jnp.zeros((events, events), F32)
    masks[1] = jnp.where(behind, 1.0, 0.0)
    masks[2] = jnp.ones((events, events), F32)

    def rows_of(which, pair):
        return pl.ds(pl.multiple_of((2 * which + pair) * pairs, pairs), pairs)

    def attend(q_set, q_pair, k_set, k_pair, masked):
        q_first, k_first = HEADS * q_set + 2 * q_pair, HEADS * k_set + 2 * k_pair
        query = qs[pl.ds(q_first, 2)].reshape(pairs, head_size)
        half = jnp.concatenate(
            [dot_t(query, kv[k_first + n, 0]) for n in range(2)], axis=1
        )
        if masked:
            q_y = y_near if q_set else y
            half = jnp.concatenate(
                [
                    jnp.concatenate(
                        [
                            half[a * events : (a + 1) * events, b * events : (b + 1) * events]
                            * masks[1 + jnp.clip(q_row - k_row, -1, 1)]
                            for b, k_row in enumerate((y, swap_y(y)))
                        ],
                        axis=1,
                    )
                    for a, q_row in enumerate((q_y, swap_y(q_y)))
                ],
                axis=0,
            )
        weights = silu_of_twice(half).astype(BF16)
        value = jnp.concatenate([kv[k_first + n, 1] for n in range(2)], axis=0)
        acc[rows_of(q_set, q_pair)] += jnp.dot(weights, value, preferred_element_type=F32)

    late = jnp.where(x < SIDE // 2, 1, 0)
    early = 1 - late
    outer = jnp.logical_or(x == 0, x == SIDE - 1)

    def attend_own(q_set):
        for pair in range(2):
            attend(q_set, pair, 0, pair, True)
        attend(q_set, late, 0, early, False)

    def attend_near(q_set, n):
        q_pair = late if n else jnp.where(outer, late, early)
        k_pair = jnp.where(outer, n, jnp.where(x == 1, 0, 1))
        attend(q_set, q_pair, 1, k_pair, False)

    for n in range(1, HEADS):
        pltpu.make_async_copy(qs.at[n], qs.at[n], q_recv.at[n]).wait()
        pass_q(n).start()
    attend_own(0)
    for n in range(HEADS):
        pass_q(n).wait_recv()
    attend(1, 0, 0, 0, True)
    attend(1, 1, 0, 1, True)
    relay(0)
    attend(1, late, 0, early, False)
    for n in range(HEADS):
        for m in range(2):
            pass_kv(n, m).wait_recv()
    def send_back(which, pair):
        for m in (1, 0):
            n = 2 * pair + m
            rows = pl.ds(pl.multiple_of((HEADS * which + n) * events, events), events)
            summed = acc[rows].astype(BF16)
            away = n >= 1 - which

            @pl.when(away)
            def _():
                back[which, n] = summed
                back_copy(n, which).start()

            @pl.when(jnp.logical_not(away))
            def _():
                att[which, head] = summed

    attend_near(1, 0)
    send_back(1, early)
    attend_near(1, 1)
    send_back(1, late)
    relay(1)
    attend_near(0, 0)
    send_back(0, early)
    attend_near(0, 1)
    send_back(0, late)
    relay(2)
    for n in range(HEADS):
        back_copy(n, 1).wait_recv()
    for n in range(1, HEADS):
        back_copy(n, 0).wait_recv()
    relay(3)

    attended = jnp.concatenate(
        [att[0, h].astype(F32) + att[1, h].astype(F32) for h in range(HEADS)], axis=1
    )
    mixed = (layer_norm(attended) * gate[...].astype(F32)).astype(BF16)
    projected = jnp.dot(mixed, wo[...], preferred_element_type=F32)
    out = (hist[...].astype(F32) + projected).astype(BF16)
    layer_out[0] = out
    groups = pool_query.shape[0]
    half = 0.5 * dot_t(pool_query[...], out)
    lane = first_pos + lax.broadcasted_iota(jnp.int32, half.shape, 1)
    pool_w = jnp.where(lane < length, silu_of_twice(half), 0.0).astype(BF16)
    sums = jnp.dot(pool_w, out, preferred_element_type=F32)

    for g in range(groups):
        part[g] = sums[g : g + 1]
    for a, b in STEPS:
        pltpu.make_async_remote_copy(
            src_ref=part.at[lax.rem(y + b, SIDE)],
            dst_ref=parts.at[t],
            send_sem=sum_sem.at[0],
            recv_sem=sum_sem.at[1],
            device_id=along(a, b),
            device_id_type=MESH,
        ).start()

    def wait_for(buffer, many, sem):
        some = buffer.at[pl.ds(0, many)]
        pltpu.make_async_copy(some, some, sem).wait()

    parts[t] = part[y]
    relay(4)
    wait_for(parts, plane - 1, sum_sem.at[1])
    state = jnp.sum(parts[...], axis=0).astype(BF16).astype(F32)

    own_interest = layer_norm(state).astype(BF16).astype(F32)
    told[...] = own_interest
    pieces[user] = own_interest

    for device in levels:
        pltpu.make_async_remote_copy(
            src_ref=told,
            dst_ref=pieces.at[user],
            send_sem=state_sem.at[0],
            recv_sem=state_sem.at[1],
            device_id=device,
            device_id_type=MESH,
        ).start()

    relay(5)
    own_half = lax.div(mp, 2)
    pre[own_half] = jnp.dot(cand[...], wr[mp, :width], preferred_element_type=F32)
    wait_for(pieces, height - 1, state_sem.at[1])
    mine = owner * owned + lax.broadcasted_iota(jnp.int32, (owned, line), 0)
    picker = jnp.where(slots[...] == mine, 1.0, 0.0).astype(BF16)
    known = pieces[...].reshape(line, width).astype(BF16)
    own_slots = jnp.dot(picker, known, preferred_element_type=F32)
    chosen[...] = own_slots
    interests[core * SIDE + y] = own_slots
    for b, n in ((2, 0), (2, 1), (1, 0), (3, 0), (1, 1), (3, 1), (0, 1)):
        pltpu.make_async_remote_copy(
            src_ref=chosen,
            dst_ref=interests.at[core * SIDE + y],
            send_sem=pick_sem.at[0],
            recv_sem=pick_sem.at[1],
            device_id=along_y(b, n),
            device_id_type=MESH,
        ).start()

    relay(6)
    pre[1 - own_half] = jnp.dot(cand[...], wr[across, :width], preferred_element_type=F32)
    wait_for(interests, 2 * SIDE - 1, pick_sem.at[1])

    interest = jnp.concatenate(
        [interests[g] + interests[SIDE + g] for g in range(groups)], axis=0
    ).astype(BF16)
    half = (0.5 * width**-0.5) * dot_t(cand[...], interest)
    row = lax.div(lax.broadcasted_iota(jnp.int32, half.shape, 0), count)
    column = lax.rem(lax.broadcasted_iota(jnp.int32, half.shape, 1), owned)
    attn = jnp.where(row == column, silu_of_twice(half), 0.0)
    high = attn.astype(BF16)
    low = (attn - high.astype(F32)).astype(BF16)
    factors = jnp.concatenate([high, low, high], axis=1)
    terms = jnp.zeros_like(pre[0])
    for n in range(2):
        block = core + 2 * n
        mixed_in = jnp.dot(interest, wr[block, width:], preferred_element_type=F32)
        large = mixed_in.astype(BF16)
        small = (mixed_in - large.astype(F32)).astype(BF16)
        more = jnp.dot(
            factors, jnp.concatenate([large, large, small], axis=0), preferred_element_type=F32
        )
        half = 0.5 * (pre[n] + vectors[block, 0:1] + more)
        terms += silu_of_twice(half) * vectors[block, 1:2]
    high = terms.astype(BF16)
    low = (terms - high.astype(F32)).astype(BF16)
    ones = jnp.ones((16, terms.shape[1]), BF16)
    own_share = (dot_t(ones, high) + dot_t(ones, low))[0:1]
    share[...] = own_share
    shares[core] = own_share
    exchange = pltpu.make_async_remote_copy(
        src_ref=share,
        dst_ref=shares.at[core],
        send_sem=twin_sem.at[0],
        recv_sem=twin_sem.at[1],
        device_id={"mp": twin},
        device_id_type=MESH,
    )
    exchange.start()
    exchange.wait_recv()
    total = jnp.sum(shares[...], axis=0)
    for r in range(owned):
        scores[r : r + 1, :] = total[0:1, r * count : (r + 1) * count]

    for copy in kv_copies + q_copies:
        copy.wait_send()
    for n in range(HEADS):
        for m in range(2):
            pass_kv(n, m).wait_send()
        pass_q(n).wait_send()
        back_copy(n, 1).wait_send()
    for n in range(1, HEADS):
        back_copy(n, 0).wait_send()
    wait_for(parts, plane - 1, sum_sem.at[0])
    wait_for(pieces, height - 1, state_sem.at[0])
    wait_for(interests, 2 * SIDE - 1, pick_sem.at[0])
    exchange.wait_send()

    @pl.when(near == 0)
    def _():
        for k in range(PARTS):
            send_weights(mp, k, over, over_send).wait_send()
        send_vectors(mp, over, over_send).wait_send()

    @pl.when(near < ends_at)
    def _():
        for k in range(PARTS):
            send_weights(across, k, onward, chain_send).wait_send()
        send_vectors(across, onward, chain_send).wait_send()


def solution(mesh):
    plane, owners, ranks = mesh.shape["tm"], mesh.shape["users"], mesh.shape["mp"]
    line = owners * ranks

    def shards(
        history,
        ln_gain,
        w_proj,
        w_out,
        pool_query,
        lengths,
        slots,
        cand_ids,
        item_table,
        w_rank,
        b_rank,
        w_score,
    ):
        _, events, width = history.shape
        head_size = width // HEADS
        groups = pool_query.shape[0]
        owned, count = cand_ids.shape
        cands = owned * count
        hidden = w_rank.shape[1]
        vmem = pl.BlockSpec(memory_space=pltpu.VMEM)
        smem = pl.BlockSpec(memory_space=pltpu.SMEM)
        hbm = pl.BlockSpec(memory_space=pltpu.HBM)
        dma = pltpu.SemaphoreType.DMA
        return pl.pallas_call(
            kernel,
            out_shape=(
                jax.ShapeDtypeStruct(history.shape, BF16),
                jax.ShapeDtypeStruct((owned, count), F32),
            ),
            in_specs=[smem] + [hbm] * 11,
            out_specs=(vmem, vmem),
            scratch_shapes=[
                pltpu.VMEM((events, width), BF16),
                pltpu.VMEM((1, width), F32),
                pltpu.VMEM(pool_query.shape, BF16),
                pltpu.VMEM((1, line), jnp.int32),
                pltpu.VMEM((owned, count), jnp.int32),
                pltpu.VMEM((1, hidden), F32),
                pltpu.VMEM((1, hidden), F32),
                pltpu.VMEM((4, width, width), BF16),
                pltpu.VMEM((width, width), BF16),
                pltpu.VMEM(item_table.shape, BF16),
                pltpu.VMEM((ranks, *w_rank.shape), BF16),
                pltpu.VMEM((events, width), BF16),
                pltpu.VMEM((events, width), BF16),
                pltpu.VMEM((HEADS, 3, events, head_size), BF16),
                pltpu.VMEM((2 * HEADS, 2, events, head_size), BF16),
                pltpu.VMEM((2 * HEADS, events, head_size), BF16),
                pltpu.VMEM((2 * HEADS * events, head_size), F32),
                pltpu.VMEM((2, HEADS, events, head_size), BF16),
                pltpu.VMEM((2, HEADS, events, head_size), BF16),
                pltpu.VMEM((3, events, events), F32),
                pltpu.VMEM((cands, width), BF16),
                pltpu.VMEM((2, cands, hidden), F32),
                pltpu.VMEM((groups, 1, width), F32),
                pltpu.VMEM((plane, 1, width), F32),
                pltpu.VMEM((1, width), F32),
                pltpu.VMEM((line, 1, width), F32),
                pltpu.VMEM((owned, width), F32),
                pltpu.VMEM((2 * SIDE, owned, width), F32),
                pltpu.VMEM((ranks, 2, hidden), F32),
                pltpu.VMEM((1, cands), F32),
                pltpu.VMEM((2, 1, cands), F32),
                dma((14,)),
                dma((HEADS, 2)),
                dma((HEADS, 2)),
                dma((HEADS,)),
                dma((HEADS,)),
                dma((3, HEADS)),
                dma((3, HEADS)),
                dma((2, HEADS)),
                dma((2, HEADS)),
                dma((2,)),
                dma((2,)),
                dma((2,)),
                dma((PARTS + 1,)),
                dma((PARTS + 1,)),
                dma((PARTS + 1,)),
                dma((2,)),
            ],
            compiler_params=pltpu.CompilerParams(
                collective_id=0, has_side_effects=True, vmem_limit_bytes=VMEM_BYTES
            ),
            cost_estimate=pl.CostEstimate(
                flops=4_000_000_000, bytes_accessed=6_000_000, transcendentals=5_000_000
            ),
        )(
            lengths,
            history,
            ln_gain.reshape(1, -1),
            w_proj,
            w_out,
            pool_query,
            slots.reshape(1, -1),
            cand_ids,
            item_table,
            w_rank,
            b_rank.reshape(1, -1),
            w_score.reshape(1, -1),
        )

    placed = (
        P(("users", "mp"), "tm", None),
        P(),
        P(),
        P(),
        P(),
        P(("users", "mp")),
        P(),
        P("users", "tm"),
        P("users", None),
        P(None, "mp"),
        P("mp"),
        P("mp"),
    )
    return jax.shard_map(
        shards,
        mesh=mesh,
        in_specs=placed,
        out_specs=(P(("users", "mp"), "tm", None), P("users", "tm")),
        check_vma=False,
    )
```

```python
import jax
import jax.numpy as jnp
from jax import lax
from jax.experimental import pallas as pl
from jax.experimental.pallas import tpu as pltpu
from jax.sharding import PartitionSpec as P

HEADS = 4
SIDE = 4
EPS = 1e-05
VMEM_BYTES = 64 * 1024 * 1024
MESH = pl.DeviceIdType.MESH
STEPS = sorted(
    ((a, b) for a in range(SIDE) for b in range(SIDE) if a or b),
    key=lambda step: -sum(min(n, SIDE - n) for n in step),
)
F32 = jnp.float32
BF16 = jnp.bfloat16
ROWS_BY_ROWS = (((1,), (1,)), ((), ()))


def layer_norm(values):
    mean = jnp.mean(values, axis=-1, keepdims=True)
    centred = values - mean
    var = jnp.mean(centred * centred, axis=-1, keepdims=True)
    return centred * lax.rsqrt(var + EPS)


def silu_of_twice(half):
    return half + half * jnp.tanh(half)


def dot_t(a, b, **kw):
    return lax.dot_general(a, b, ROWS_BY_ROWS, preferred_element_type=F32, **kw)


def kernel(
    lengths,
    history,
    ln_gain_hbm,
    w_proj,
    w_out,
    pool_query_hbm,
    slots_hbm,
    cand_ids_hbm,
    item_table,
    w_rank,
    b_rank_hbm,
    w_score_hbm,
    layer_out,
    scores,
    hist,
    ln_gain,
    pool_query,
    slots,
    cand_ids,
    b_rank,
    w_score,
    wp,
    wo,
    table,
    wr,
    normed,
    gate,
    qkv,
    kv,
    qs,
    acc,
    back,
    att,
    masks,
    cand,
    pre,
    part,
    parts,
    told,
    pieces,
    chosen,
    interests,
    vectors,
    share,
    shares,
    load_sem,
    kv_send,
    kv_recv,
    q_send,
    q_recv,
    pass_send,
    pass_recv,
    back_send,
    back_recv,
    sum_sem,
    state_sem,
    pick_sem,
    over_send,
    chain_send,
    chain_recv,
    spread_sem,
    twin_sem,
):
    events, width = hist.shape
    head_size = width // HEADS
    plane, line, ranks = parts.shape[0], pieces.shape[0], wr.shape[0]
    t = lax.axis_index("tm")
    owner = lax.axis_index("users")
    mp = lax.axis_index("mp")
    user = owner * ranks + mp
    x, y = lax.div(t, SIDE), lax.rem(t, SIDE)
    core = lax.rem(mp, 2)

    def even(v):
        return v + 1 - 2 * lax.rem(v, 2)

    def odd(v):
        return SIDE - 1 - v

    def swap_y(v):
        return even(v) + core * (odd(v) - even(v))

    def ring_y(v):
        return odd(v) + core * (even(v) - odd(v))

    def head_of(a, b):
        first = lax.rem(lax.div(b + 1, 2), 2)
        return 2 * lax.div(a, 2) + first + core * (lax.div(b, 2) - first)

    def moved(a, b, rel):
        first, second = lax.rem(rel, 2), lax.div(rel, 2)
        return a + second * (odd(a) - a), b + first * (swap_y(b) - b)

    def in_plane(a, b):
        return {"tm": a * SIDE + b}

    head = head_of(x, y)

    depth = wr.shape[1] // SIDE
    last = line // ranks - 1
    twin = mp + 1 - 2 * core
    across = lax.rem(mp + 2, ranks)
    near = jnp.minimum(owner, last - owner)
    step_on = jnp.where(owner < near + 1, 1, -1)
    ends_at = last // 2

    def weights_of(whose):
        return wr.at[whose, pl.ds(pl.multiple_of(y * depth, depth), depth)]

    def chain_copies(whose, to, sems):
        return [
            pltpu.make_async_remote_copy(
                src_ref=ref,
                dst_ref=ref,
                send_sem=sems.at[n],
                recv_sem=chain_recv.at[n],
                device_id=to,
                device_id_type=MESH,
            )
            for n, ref in enumerate((weights_of(whose), vectors.at[whose]))
        ]

    over = {"users": last - owner, "mp": across}
    onward = {"users": owner + step_on}

    def relay(j):
        @pl.when(near == j)
        def _():
            for copy in chain_copies(across, onward, chain_send):
                copy.wait_recv()
                if j < ends_at:
                    copy.start()

    loads = [pltpu.make_async_copy(history.at[0], hist, load_sem.at[0])]
    for n, block in enumerate((3, 1, 2, 0)):
        cols = pl.ds(block * width, width)
        loads.append(pltpu.make_async_copy(w_proj.at[:, cols], wp.at[n], load_sem.at[n + 1]))
    rest = (
        (ln_gain_hbm, ln_gain),
        (pool_query_hbm, pool_query),
        (slots_hbm, slots),
        (cand_ids_hbm, cand_ids),
        (b_rank_hbm, b_rank),
        (w_score_hbm, w_score),
        (w_out, wo),
        (item_table, table),
        (w_rank, wr.at[mp]),
    )
    for n, (src, dst) in enumerate(rest):
        loads.append(pltpu.make_async_copy(src, dst, load_sem.at[5 + n]))
    loads[0].start()
    loads[5].start()
    for load in loads[1:5] + loads[6:]:
        load.start()

    pieces[...] = jnp.zeros_like(pieces)

    barrier = pltpu.get_barrier_semaphore()
    height = line // 2
    low = height // 2
    level = lax.div(mp, 2) * low + owner

    levels = []
    for k in range(height - 1):
        chip = lax.rem(level + low + (k + 1) // 2 * (1 - 2 * (k % 2)), height)
        levels.append({"users": lax.rem(chip, low), "mp": 2 * lax.div(chip, low) + core})

    def along(a, b):
        return {"tm": lax.rem(x + a, SIDE) * SIDE + lax.rem(y + b, SIDE)}

    def along_y(b, other):
        return {"tm": x * SIDE + lax.rem(y + b, SIDE), "mp": mp + other * (1 - 2 * core)}

    greeted = [along(a, b) for a, b in STEPS] + [along_y(b, 1) for b in range(SIDE)]
    greeted = levels + greeted
    for device in greeted:
        pl.semaphore_signal(barrier, inc=1, device_id=device, device_id_type=MESH)

    first_pos = t * events
    length = lengths[0]
    pos = first_pos + lax.broadcasted_iota(jnp.int32, (events, 1), 0)
    live = pos < length
    loads[0].wait()
    loads[5].wait()
    normed[...] = (layer_norm(hist[...].astype(F32)) * ln_gain[...]).astype(BF16)

    def project(n):
        loads[n + 1].wait()
        half = 0.5 * jnp.dot(normed[...], wp[n], preferred_element_type=F32)
        return silu_of_twice(half)

    keys = project(0).astype(BF16)
    for h in range(HEADS):
        qkv[h, 0] = keys[:, h * head_size : (h + 1) * head_size]
    values = jnp.where(live, project(1), 0.0).astype(BF16)
    for h in range(HEADS):
        qkv[h, 1] = values[:, h * head_size : (h + 1) * head_size]

    pl.semaphore_wait(barrier, len(greeted))

    kv_copies, q_copies = [], []
    for rel in (3, 2, 1):
        a, b = moved(x, y, rel)
        for n in range(2):
            copy = pltpu.make_async_remote_copy(
                src_ref=qkv.at[head_of(a, b), n],
                dst_ref=kv.at[rel, n],
                send_sem=kv_send.at[rel, n],
                recv_sem=kv_recv.at[rel, n],
                device_id=in_plane(a, b),
                device_id_type=MESH,
            )
            copy.start()
            kv_copies.append(copy)

    query = (project(2) * (0.5 * head_size**-0.5)).astype(BF16)
    for h in range(HEADS):
        qkv[h, 2] = query[:, h * head_size : (h + 1) * head_size]
    for rel in (3, 2, 1):
        a, b = moved(x, y, rel)
        copy = pltpu.make_async_remote_copy(
            src_ref=qkv.at[head_of(a, b), 2],
            dst_ref=qs.at[rel],
            send_sem=q_send.at[rel],
            recv_sem=q_recv.at[rel],
            device_id=in_plane(a, b),
            device_id_type=MESH,
        )
        copy.start()
        q_copies.append(copy)
    for load in loads[9:11] + loads[13:]:
        load.wait()
    vectors[mp, 0:1] = b_rank[...]
    vectors[mp, 1:2] = w_score[...]

    @pl.when(near == 0)
    def _():
        for copy in chain_copies(mp, over, over_send):
            copy.start()

    kv[0] = qkv[head, pl.ds(0, 2)]
    qs[0] = qkv[head, 2]

    x_near, y_near = even(x), ring_y(y)

    def pass_kv(n, m):
        return pltpu.make_async_remote_copy(
            src_ref=kv.at[n, m],
            dst_ref=kv.at[HEADS + n, m],
            send_sem=pass_send.at[m, n],
            recv_sem=pass_recv.at[m, n],
            device_id=in_plane(x_near, y),
            device_id_type=MESH,
        )

    def pass_q(n):
        return pltpu.make_async_remote_copy(
            src_ref=qs.at[n],
            dst_ref=qs.at[HEADS + n],
            send_sem=pass_send.at[2, n],
            recv_sem=pass_recv.at[2, n],
            device_id=in_plane(x, y_near),
            device_id_type=MESH,
        )

    def back_copy(n, which):
        a, b = moved(x, y_near if which else y, n)
        return pltpu.make_async_remote_copy(
            src_ref=back.at[which, n],
            dst_ref=att.at[which, head],
            send_sem=back_send.at[which, n],
            recv_sem=back_recv.at[which, n],
            device_id=in_plane(a, b),
            device_id_type=MESH,
        )

    pass_q(0).start()
    for m in range(2):
        pass_kv(0, m).start()

    gate[...] = project(3).astype(BF16)
    acc[...] = jnp.zeros_like(acc)

    owned, count = cand_ids.shape
    pool = table.shape[0]
    for load in loads[6:9] + loads[11:13]:
        load.wait()

    @pl.loop(0, owned)
    def _(r):
        @pl.when(r > 0)
        def _():
            for m in range(2):
                pltpu.make_async_copy(kv.at[r, m], kv.at[r, m], kv_recv.at[r, m]).wait()
                pass_kv(r, m).start()

        eye = lax.broadcasted_iota(jnp.int32, (count, count), 0) == lax.broadcasted_iota(
            jnp.int32, (count, count), 1
        )
        item = lax.broadcasted_iota(jnp.int32, (count, pool), 1).astype(F32)
        ids = cand_ids[pl.ds(r, 1), :].astype(F32)
        column = jnp.sum(jnp.where(eye, ids, 0.0), axis=1, keepdims=True)
        onehot = jnp.where(item == column, 1.0, 0.0).astype(BF16)
        cand[pl.ds(r * count, count)] = jnp.dot(
            onehot, table[...], preferred_element_type=F32
        ).astype(BF16)

    pairs = 2 * events
    behind = lax.broadcasted_iota(jnp.int32, (events, events), 0) >= lax.broadcasted_iota(
        jnp.int32, (events, events), 1
    )
    masks[0] = jnp.zeros((events, events), F32)
    masks[1] = jnp.where(behind, 1.0, 0.0)
    masks[2] = jnp.ones((events, events), F32)

    def rows_of(which, pair):
        return pl.ds(pl.multiple_of((2 * which + pair) * pairs, pairs), pairs)

    def attend(q_set, q_pair, k_set, k_pair, masked):
        q_first, k_first = HEADS * q_set + 2 * q_pair, HEADS * k_set + 2 * k_pair
        query = qs[pl.ds(q_first, 2)].reshape(pairs, head_size)
        half = jnp.concatenate(
            [dot_t(query, kv[k_first + n, 0]) for n in range(2)], axis=1
        )
        if masked:
            q_y = y_near if q_set else y
            half = jnp.concatenate(
                [
                    jnp.concatenate(
                        [
                            half[a * events : (a + 1) * events, b * events : (b + 1) * events]
                            * masks[1 + jnp.clip(q_row - k_row, -1, 1)]
                            for b, k_row in enumerate((y, swap_y(y)))
                        ],
                        axis=1,
                    )
                    for a, q_row in enumerate((q_y, swap_y(q_y)))
                ],
                axis=0,
            )
        weights = silu_of_twice(half).astype(BF16)
        value = jnp.concatenate([kv[k_first + n, 1] for n in range(2)], axis=0)
        acc[rows_of(q_set, q_pair)] += jnp.dot(weights, value, preferred_element_type=F32)

    late = jnp.where(x < SIDE // 2, 1, 0)
    early = 1 - late
    outer = jnp.logical_or(x == 0, x == SIDE - 1)

    def attend_own(q_set):
        for pair in range(2):
            attend(q_set, pair, 0, pair, True)
        attend(q_set, late, 0, early, False)

    def attend_near(q_set, n):
        q_pair = late if n else jnp.where(outer, late, early)
        k_pair = jnp.where(outer, n, jnp.where(x == 1, 0, 1))
        attend(q_set, q_pair, 1, k_pair, False)

    for n in range(1, HEADS):
        pltpu.make_async_copy(qs.at[n], qs.at[n], q_recv.at[n]).wait()
        pass_q(n).start()
    relay(0)
    attend_own(0)
    for n in range(HEADS):
        pass_q(n).wait_recv()
    attend(1, 0, 0, 0, True)
    attend(1, 1, 0, 1, True)
    attend(1, late, 0, early, False)
    relay(1)
    for n in range(HEADS):
        for m in range(2):
            pass_kv(n, m).wait_recv()
    def send_back(which, pair):
        for m in (1, 0):
            n = 2 * pair + m
            rows = pl.ds(pl.multiple_of((HEADS * which + n) * events, events), events)
            summed = acc[rows].astype(BF16)
            away = n >= 1 - which

            @pl.when(away)
            def _():
                back[which, n] = summed
                back_copy(n, which).start()

            @pl.when(jnp.logical_not(away))
            def _():
                att[which, head] = summed

    attend_near(1, 0)
    send_back(1, early)
    attend_near(1, 1)
    send_back(1, late)
    relay(2)
    attend_near(0, 0)
    send_back(0, early)
    attend_near(0, 1)
    send_back(0, late)
    relay(3)
    quarter = weights_of(across)
    for b in (2, 1, 3):
        pltpu.make_async_remote_copy(
            src_ref=quarter,
            dst_ref=quarter,
            send_sem=spread_sem.at[0],
            recv_sem=spread_sem.at[1],
            device_id=along(0, b),
            device_id_type=MESH,
        ).start()
    others = wr.at[across, pl.ds(0, (SIDE - 1) * depth)]
    for n in range(HEADS):
        back_copy(n, 1).wait_recv()
    for n in range(1, HEADS):
        back_copy(n, 0).wait_recv()

    own_half = lax.div(mp, 2)
    attended = jnp.concatenate(
        [att[0, h].astype(F32) + att[1, h].astype(F32) for h in range(HEADS)], axis=1
    )
    mixed = (layer_norm(attended) * gate[...].astype(F32)).astype(BF16)
    projected = jnp.dot(mixed, wo[...], preferred_element_type=F32)
    out = (hist[...].astype(F32) + projected).astype(BF16)
    layer_out[0] = out
    groups = pool_query.shape[0]
    half = 0.5 * dot_t(pool_query[...], out)
    lane = first_pos + lax.broadcasted_iota(jnp.int32, half.shape, 1)
    pool_w = jnp.where(lane < length, silu_of_twice(half), 0.0).astype(BF16)
    sums = jnp.dot(pool_w, out, preferred_element_type=F32)

    for g in range(groups):
        part[g] = sums[g : g + 1]
    for a, b in STEPS:
        pltpu.make_async_remote_copy(
            src_ref=part.at[lax.rem(y + b, SIDE)],
            dst_ref=parts.at[t],
            send_sem=sum_sem.at[0],
            recv_sem=sum_sem.at[1],
            device_id=along(a, b),
            device_id_type=MESH,
        ).start()

    def wait_for(buffer, many, sem):
        some = buffer.at[pl.ds(0, many)]
        pltpu.make_async_copy(some, some, sem).wait()

    parts[t] = part[y]
    pre[own_half] = jnp.dot(cand[...], wr[mp, :width], preferred_element_type=F32)
    wait_for(parts, plane - 1, sum_sem.at[1])
    state = jnp.sum(parts[...], axis=0).astype(BF16).astype(F32)

    own_interest = layer_norm(state).astype(BF16).astype(F32)
    told[...] = own_interest
    pieces[user] = own_interest

    for device in levels:
        pltpu.make_async_remote_copy(
            src_ref=told,
            dst_ref=pieces.at[user],
            send_sem=state_sem.at[0],
            recv_sem=state_sem.at[1],
            device_id=device,
            device_id_type=MESH,
        ).start()

    pltpu.make_async_copy(others, others, spread_sem.at[1]).wait()
    pre[1 - own_half] = jnp.dot(cand[...], wr[across, :width], preferred_element_type=F32)
    wait_for(pieces, height - 1, state_sem.at[1])
    mine = owner * owned + lax.broadcasted_iota(jnp.int32, (owned, line), 0)
    picker = jnp.where(slots[...] == mine, 1.0, 0.0).astype(BF16)
    known = pieces[...].reshape(line, width).astype(BF16)
    own_slots = jnp.dot(picker, known, preferred_element_type=F32)
    chosen[...] = own_slots
    interests[core * SIDE + y] = own_slots
    for b, n in ((2, 0), (2, 1), (1, 0), (3, 0), (1, 1), (3, 1), (0, 1)):
        pltpu.make_async_remote_copy(
            src_ref=chosen,
            dst_ref=interests.at[core * SIDE + y],
            send_sem=pick_sem.at[0],
            recv_sem=pick_sem.at[1],
            device_id=along_y(b, n),
            device_id_type=MESH,
        ).start()

    wait_for(interests, 2 * SIDE - 1, pick_sem.at[1])

    interest = jnp.concatenate(
        [interests[g] + interests[SIDE + g] for g in range(groups)], axis=0
    ).astype(BF16)
    half = (0.5 * width**-0.5) * dot_t(cand[...], interest)
    row = lax.div(lax.broadcasted_iota(jnp.int32, half.shape, 0), count)
    column = lax.rem(lax.broadcasted_iota(jnp.int32, half.shape, 1), owned)
    attn = jnp.where(row == column, silu_of_twice(half), 0.0)
    high = attn.astype(BF16)
    low = (attn - high.astype(F32)).astype(BF16)
    factors = jnp.concatenate([high, low, high], axis=1)
    terms = jnp.zeros_like(pre[0])
    for n in range(2):
        block = core + 2 * n
        mixed_in = jnp.dot(interest, wr[block, width:], preferred_element_type=F32)
        large = mixed_in.astype(BF16)
        small = (mixed_in - large.astype(F32)).astype(BF16)
        more = jnp.dot(
            factors, jnp.concatenate([large, large, small], axis=0), preferred_element_type=F32
        )
        half = 0.5 * (pre[n] + vectors[block, 0:1] + more)
        terms += silu_of_twice(half) * vectors[block, 1:2]
    high = terms.astype(BF16)
    low = (terms - high.astype(F32)).astype(BF16)
    ones = jnp.ones((16, terms.shape[1]), BF16)
    own_share = (dot_t(ones, high) + dot_t(ones, low))[0:1]
    share[...] = own_share
    shares[core] = own_share
    exchange = pltpu.make_async_remote_copy(
        src_ref=share,
        dst_ref=shares.at[core],
        send_sem=twin_sem.at[0],
        recv_sem=twin_sem.at[1],
        device_id={"mp": twin},
        device_id_type=MESH,
    )
    exchange.start()
    exchange.wait_recv()
    total = jnp.sum(shares[...], axis=0)
    for r in range(owned):
        scores[r : r + 1, :] = total[0:1, r * count : (r + 1) * count]

    for copy in kv_copies + q_copies:
        copy.wait_send()
    for n in range(HEADS):
        for m in range(2):
            pass_kv(n, m).wait_send()
        pass_q(n).wait_send()
        back_copy(n, 1).wait_send()
    for n in range(1, HEADS):
        back_copy(n, 0).wait_send()
    wait_for(parts, plane - 1, sum_sem.at[0])
    wait_for(pieces, height - 1, state_sem.at[0])
    wait_for(interests, 2 * SIDE - 1, pick_sem.at[0])
    exchange.wait_send()

    pltpu.make_async_copy(others, others, spread_sem.at[0]).wait()

    @pl.when(near == 0)
    def _():
        for copy in chain_copies(mp, over, over_send):
            copy.wait_send()

    @pl.when(near < ends_at)
    def _():
        for copy in chain_copies(across, onward, chain_send):
            copy.wait_send()


def solution(mesh):
    plane, owners, ranks = mesh.shape["tm"], mesh.shape["users"], mesh.shape["mp"]
    line = owners * ranks

    def shards(
        history,
        ln_gain,
        w_proj,
        w_out,
        pool_query,
        lengths,
        slots,
        cand_ids,
        item_table,
        w_rank,
        b_rank,
        w_score,
    ):
        _, events, width = history.shape
        head_size = width // HEADS
        groups = pool_query.shape[0]
        owned, count = cand_ids.shape
        cands = owned * count
        hidden = w_rank.shape[1]
        vmem = pl.BlockSpec(memory_space=pltpu.VMEM)
        smem = pl.BlockSpec(memory_space=pltpu.SMEM)
        hbm = pl.BlockSpec(memory_space=pltpu.HBM)
        dma = pltpu.SemaphoreType.DMA
        return pl.pallas_call(
            kernel,
            out_shape=(
                jax.ShapeDtypeStruct(history.shape, BF16),
                jax.ShapeDtypeStruct((owned, count), F32),
            ),
            in_specs=[smem] + [hbm] * 11,
            out_specs=(vmem, vmem),
            scratch_shapes=[
                pltpu.VMEM((events, width), BF16),
                pltpu.VMEM((1, width), F32),
                pltpu.VMEM(pool_query.shape, BF16),
                pltpu.VMEM((1, line), jnp.int32),
                pltpu.VMEM((owned, count), jnp.int32),
                pltpu.VMEM((1, hidden), F32),
                pltpu.VMEM((1, hidden), F32),
                pltpu.VMEM((4, width, width), BF16),
                pltpu.VMEM((width, width), BF16),
                pltpu.VMEM(item_table.shape, BF16),
                pltpu.VMEM((ranks, *w_rank.shape), BF16),
                pltpu.VMEM((events, width), BF16),
                pltpu.VMEM((events, width), BF16),
                pltpu.VMEM((HEADS, 3, events, head_size), BF16),
                pltpu.VMEM((2 * HEADS, 2, events, head_size), BF16),
                pltpu.VMEM((2 * HEADS, events, head_size), BF16),
                pltpu.VMEM((2 * HEADS * events, head_size), F32),
                pltpu.VMEM((2, HEADS, events, head_size), BF16),
                pltpu.VMEM((2, HEADS, events, head_size), BF16),
                pltpu.VMEM((3, events, events), F32),
                pltpu.VMEM((cands, width), BF16),
                pltpu.VMEM((2, cands, hidden), F32),
                pltpu.VMEM((groups, 1, width), F32),
                pltpu.VMEM((plane, 1, width), F32),
                pltpu.VMEM((1, width), F32),
                pltpu.VMEM((line, 1, width), F32),
                pltpu.VMEM((owned, width), F32),
                pltpu.VMEM((2 * SIDE, owned, width), F32),
                pltpu.VMEM((ranks, 2, hidden), F32),
                pltpu.VMEM((1, cands), F32),
                pltpu.VMEM((2, 1, cands), F32),
                dma((14,)),
                dma((HEADS, 2)),
                dma((HEADS, 2)),
                dma((HEADS,)),
                dma((HEADS,)),
                dma((3, HEADS)),
                dma((3, HEADS)),
                dma((2, HEADS)),
                dma((2, HEADS)),
                dma((2,)),
                dma((2,)),
                dma((2,)),
                dma((2,)),
                dma((2,)),
                dma((2,)),
                dma((2,)),
                dma((2,)),
            ],
            compiler_params=pltpu.CompilerParams(
                collective_id=0, has_side_effects=True, vmem_limit_bytes=VMEM_BYTES
            ),
            cost_estimate=pl.CostEstimate(
                flops=4_000_000_000, bytes_accessed=6_000_000, transcendentals=5_000_000
            ),
        )(
            lengths,
            history,
            ln_gain.reshape(1, -1),
            w_proj,
            w_out,
            pool_query,
            slots.reshape(1, -1),
            cand_ids,
            item_table,
            w_rank,
            b_rank.reshape(1, -1),
            w_score.reshape(1, -1),
        )

    placed = (
        P(("users", "mp"), "tm", None),
        P(),
        P(),
        P(),
        P(),
        P(("users", "mp")),
        P(),
        P("users", "tm"),
        P("users", None),
        P(None, "mp"),
        P("mp"),
        P("mp"),
    )
    return jax.shard_map(
        shards,
        mesh=mesh,
        in_specs=placed,
        out_specs=(P(("users", "mp"), "tm", None), P("users", "tm")),
        check_vma=False,
    )
```

```python
import jax
import jax.numpy as jnp
from jax import lax
from jax.experimental import pallas as pl
from jax.experimental.pallas import tpu as pltpu
from jax.sharding import PartitionSpec as P

HEADS = 4
SIDE = 4
EPS = 1e-05
VMEM_BYTES = 64 * 1024 * 1024
MESH = pl.DeviceIdType.MESH
STEPS = sorted(
    ((a, b) for a in range(SIDE) for b in range(SIDE) if a or b),
    key=lambda step: -sum(min(n, SIDE - n) for n in step),
)
F32 = jnp.float32
BF16 = jnp.bfloat16
ROWS_BY_ROWS = (((1,), (1,)), ((), ()))


def layer_norm(values):
    mean = jnp.mean(values, axis=-1, keepdims=True)
    centred = values - mean
    var = jnp.mean(centred * centred, axis=-1, keepdims=True)
    return centred * lax.rsqrt(var + EPS)


def silu_of_twice(half):
    return half + half * jnp.tanh(half)


def dot_t(a, b, **kw):
    return lax.dot_general(a, b, ROWS_BY_ROWS, preferred_element_type=F32, **kw)


def kernel(
    lengths,
    history,
    ln_gain_hbm,
    w_proj,
    w_out,
    pool_query_hbm,
    slots_hbm,
    cand_ids_hbm,
    item_table,
    w_rank,
    b_rank_hbm,
    w_score_hbm,
    layer_out,
    scores,
    hist,
    ln_gain,
    pool_query,
    slots,
    cand_ids,
    b_rank,
    w_score,
    wp,
    wo,
    table,
    wr,
    normed,
    gate,
    qkv,
    kv,
    qs,
    acc,
    back,
    att,
    masks,
    cand,
    pre,
    part,
    parts,
    told,
    pieces,
    chosen,
    interests,
    vectors,
    share,
    shares,
    load_sem,
    kv_send,
    kv_recv,
    q_send,
    q_recv,
    pass_send,
    pass_recv,
    back_send,
    back_recv,
    sum_sem,
    state_sem,
    pick_sem,
    over_send,
    chain_send,
    chain_recv,
    spread_sem,
    twin_sem,
):
    events, width = hist.shape
    head_size = width // HEADS
    plane, line, ranks = parts.shape[0], pieces.shape[0], wr.shape[0]
    t = lax.axis_index("tm")
    owner = lax.axis_index("users")
    mp = lax.axis_index("mp")
    user = owner * ranks + mp
    x, y = lax.div(t, SIDE), lax.rem(t, SIDE)
    core = lax.rem(mp, 2)

    def even(v):
        return v + 1 - 2 * lax.rem(v, 2)

    def odd(v):
        return SIDE - 1 - v

    def swap_y(v):
        return even(v) + core * (odd(v) - even(v))

    def ring_y(v):
        return odd(v) + core * (even(v) - odd(v))

    def head_of(a, b):
        first = lax.rem(lax.div(b + 1, 2), 2)
        return 2 * lax.div(a, 2) + first + core * (lax.div(b, 2) - first)

    def moved(a, b, rel):
        first, second = lax.rem(rel, 2), lax.div(rel, 2)
        return a + second * (odd(a) - a), b + first * (swap_y(b) - b)

    def in_plane(a, b):
        return {"tm": a * SIDE + b}

    head = head_of(x, y)

    depth = wr.shape[1] // SIDE
    last = line // ranks - 1
    twin = mp + 1 - 2 * core
    across = lax.rem(mp + 2, ranks)
    near = jnp.minimum(owner, last - owner)
    step_on = jnp.where(owner < near + 1, 1, -1)
    ends_at = last // 2

    def weights_of(whose):
        return wr.at[whose, pl.ds(pl.multiple_of(y * depth, depth), depth)]

    def chain_copies(whose, to, sems):
        return [
            pltpu.make_async_remote_copy(
                src_ref=ref,
                dst_ref=ref,
                send_sem=sems.at[n],
                recv_sem=chain_recv.at[n],
                device_id=to,
                device_id_type=MESH,
            )
            for n, ref in enumerate((weights_of(whose), vectors.at[whose]))
        ]

    over = {"users": last - owner, "mp": across}
    onward = {"users": owner + step_on}

    def relay(j):
        @pl.when(near == j)
        def _():
            for copy in chain_copies(across, onward, chain_send):
                copy.wait_recv()
                if j < ends_at:
                    copy.start()

    loads = [pltpu.make_async_copy(history.at[0], hist, load_sem.at[0])]
    for n, block in enumerate((3, 1, 2, 0)):
        cols = pl.ds(block * width, width)
        loads.append(pltpu.make_async_copy(w_proj.at[:, cols], wp.at[n], load_sem.at[n + 1]))
    rest = (
        (ln_gain_hbm, ln_gain),
        (pool_query_hbm, pool_query),
        (slots_hbm, slots),
        (cand_ids_hbm, cand_ids),
        (b_rank_hbm, b_rank),
        (w_score_hbm, w_score),
        (w_out, wo),
        (item_table, table),
        (w_rank, wr.at[mp]),
    )
    for n, (src, dst) in enumerate(rest):
        loads.append(pltpu.make_async_copy(src, dst, load_sem.at[5 + n]))
    loads[0].start()
    loads[5].start()
    for load in loads[1:5] + loads[6:]:
        load.start()

    pieces[...] = jnp.zeros_like(pieces)

    barrier = pltpu.get_barrier_semaphore()
    height = line // 2
    low = height // 2
    level = lax.div(mp, 2) * low + owner

    levels = []
    for k in range(height - 1):
        chip = lax.rem(level + low + (k + 1) // 2 * (1 - 2 * (k % 2)), height)
        levels.append({"users": lax.rem(chip, low), "mp": 2 * lax.div(chip, low) + core})

    def along(a, b):
        return {"tm": lax.rem(x + a, SIDE) * SIDE + lax.rem(y + b, SIDE)}

    def along_y(b, other):
        return {"tm": x * SIDE + lax.rem(y + b, SIDE), "mp": mp + other * (1 - 2 * core)}

    greeted = [along(a, b) for a, b in STEPS] + [along_y(b, 1) for b in range(SIDE)]
    greeted = levels + greeted
    for device in greeted:
        pl.semaphore_signal(barrier, inc=1, device_id=device, device_id_type=MESH)

    first_pos = t * events
    length = lengths[0]
    pos = first_pos + lax.broadcasted_iota(jnp.int32, (events, 1), 0)
    live = pos < length
    loads[0].wait()
    loads[5].wait()
    normed[...] = (layer_norm(hist[...].astype(F32)) * ln_gain[...]).astype(BF16)

    def project(n):
        loads[n + 1].wait()
        half = 0.5 * jnp.dot(normed[...], wp[n], preferred_element_type=F32)
        return silu_of_twice(half)

    keys = project(0).astype(BF16)
    for h in range(HEADS):
        qkv[h, 0] = keys[:, h * head_size : (h + 1) * head_size]
    values = jnp.where(live, project(1), 0.0).astype(BF16)
    for h in range(HEADS):
        qkv[h, 1] = values[:, h * head_size : (h + 1) * head_size]

    pl.semaphore_wait(barrier, len(greeted))

    kv_copies, q_copies = [], []
    for rel in (3, 2, 1):
        a, b = moved(x, y, rel)
        for n in range(2):
            copy = pltpu.make_async_remote_copy(
                src_ref=qkv.at[head_of(a, b), n],
                dst_ref=kv.at[rel, n],
                send_sem=kv_send.at[rel, n],
                recv_sem=kv_recv.at[rel, n],
                device_id=in_plane(a, b),
                device_id_type=MESH,
            )
            copy.start()
            kv_copies.append(copy)

    query = (project(2) * (0.5 * head_size**-0.5)).astype(BF16)
    for h in range(HEADS):
        qkv[h, 2] = query[:, h * head_size : (h + 1) * head_size]
    for rel in (3, 2, 1):
        a, b = moved(x, y, rel)
        copy = pltpu.make_async_remote_copy(
            src_ref=qkv.at[head_of(a, b), 2],
            dst_ref=qs.at[rel],
            send_sem=q_send.at[rel],
            recv_sem=q_recv.at[rel],
            device_id=in_plane(a, b),
            device_id_type=MESH,
        )
        copy.start()
        q_copies.append(copy)
    for load in loads[9:11] + loads[13:]:
        load.wait()
    vectors[mp, 0:1] = b_rank[...]
    vectors[mp, 1:2] = w_score[...]

    @pl.when(near == 0)
    def _():
        for copy in chain_copies(mp, over, over_send):
            copy.start()

    kv[0] = qkv[head, pl.ds(0, 2)]
    qs[0] = qkv[head, 2]

    x_near, y_near = even(x), ring_y(y)

    def pass_kv(n, m):
        return pltpu.make_async_remote_copy(
            src_ref=kv.at[n, m],
            dst_ref=kv.at[HEADS + n, m],
            send_sem=pass_send.at[m, n],
            recv_sem=pass_recv.at[m, n],
            device_id=in_plane(x_near, y),
            device_id_type=MESH,
        )

    def pass_q(n):
        return pltpu.make_async_remote_copy(
            src_ref=qs.at[n],
            dst_ref=qs.at[HEADS + n],
            send_sem=pass_send.at[2, n],
            recv_sem=pass_recv.at[2, n],
            device_id=in_plane(x, y_near),
            device_id_type=MESH,
        )

    def back_copy(n, which):
        a, b = moved(x, y_near if which else y, n)
        return pltpu.make_async_remote_copy(
            src_ref=back.at[which, n],
            dst_ref=att.at[which, head],
            send_sem=back_send.at[which, n],
            recv_sem=back_recv.at[which, n],
            device_id=in_plane(a, b),
            device_id_type=MESH,
        )

    pass_q(0).start()
    for m in range(2):
        pass_kv(0, m).start()

    gate[...] = project(3).astype(BF16)
    acc[...] = jnp.zeros_like(acc)

    owned, count = cand_ids.shape
    pool = table.shape[0]
    for load in loads[6:9] + loads[11:13]:
        load.wait()

    @pl.loop(0, owned)
    def _(r):
        @pl.when(r > 0)
        def _():
            for m in range(2):
                pltpu.make_async_copy(kv.at[r, m], kv.at[r, m], kv_recv.at[r, m]).wait()
                pass_kv(r, m).start()

        eye = lax.broadcasted_iota(jnp.int32, (count, count), 0) == lax.broadcasted_iota(
            jnp.int32, (count, count), 1
        )
        item = lax.broadcasted_iota(jnp.int32, (count, pool), 1).astype(F32)
        ids = cand_ids[pl.ds(r, 1), :].astype(F32)
        column = jnp.sum(jnp.where(eye, ids, 0.0), axis=1, keepdims=True)
        onehot = jnp.where(item == column, 1.0, 0.0).astype(BF16)
        cand[pl.ds(r * count, count)] = jnp.dot(
            onehot, table[...], preferred_element_type=F32
        ).astype(BF16)

    pairs = 2 * events
    behind = lax.broadcasted_iota(jnp.int32, (events, events), 0) >= lax.broadcasted_iota(
        jnp.int32, (events, events), 1
    )
    masks[0] = jnp.zeros((events, events), F32)
    masks[1] = jnp.where(behind, 1.0, 0.0)
    masks[2] = jnp.ones((events, events), F32)

    def rows_of(which, pair):
        return pl.ds(pl.multiple_of((2 * which + pair) * pairs, pairs), pairs)

    def attend(q_set, q_pair, k_set, k_pair, masked):
        q_first, k_first = HEADS * q_set + 2 * q_pair, HEADS * k_set + 2 * k_pair
        query = qs[pl.ds(q_first, 2)].reshape(pairs, head_size)
        half = jnp.concatenate(
            [dot_t(query, kv[k_first + n, 0]) for n in range(2)], axis=1
        )
        if masked:
            q_y = y_near if q_set else y
            half = jnp.concatenate(
                [
                    jnp.concatenate(
                        [
                            half[a * events : (a + 1) * events, b * events : (b + 1) * events]
                            * masks[1 + jnp.clip(q_row - k_row, -1, 1)]
                            for b, k_row in enumerate((y, swap_y(y)))
                        ],
                        axis=1,
                    )
                    for a, q_row in enumerate((q_y, swap_y(q_y)))
                ],
                axis=0,
            )
        weights = silu_of_twice(half).astype(BF16)
        value = jnp.concatenate([kv[k_first + n, 1] for n in range(2)], axis=0)
        acc[rows_of(q_set, q_pair)] += jnp.dot(weights, value, preferred_element_type=F32)

    late = jnp.where(x < SIDE // 2, 1, 0)
    early = 1 - late
    outer = jnp.logical_or(x == 0, x == SIDE - 1)

    def attend_own(q_set):
        for pair in range(2):
            attend(q_set, pair, 0, pair, True)
        attend(q_set, late, 0, early, False)

    def attend_near(q_set, n):
        q_pair = late if n else jnp.where(outer, late, early)
        k_pair = jnp.where(outer, n, jnp.where(x == 1, 0, 1))
        attend(q_set, q_pair, 1, k_pair, False)

    for n in range(1, HEADS):
        pltpu.make_async_copy(qs.at[n], qs.at[n], q_recv.at[n]).wait()
        pass_q(n).start()
    relay(0)
    attend_own(0)
    for n in range(HEADS):
        pass_q(n).wait_recv()
    attend(1, 0, 0, 0, True)
    attend(1, 1, 0, 1, True)
    attend(1, late, 0, early, False)
    relay(1)
    for n in range(HEADS):
        for m in range(2):
            pass_kv(n, m).wait_recv()
    def send_back(which, pair):
        for m in (1, 0):
            n = 2 * pair + m
            rows = pl.ds(pl.multiple_of((HEADS * which + n) * events, events), events)
            summed = acc[rows].astype(BF16)
            away = n >= 1 - which

            @pl.when(away)
            def _():
                back[which, n] = summed
                back_copy(n, which).start()

            @pl.when(jnp.logical_not(away))
            def _():
                att[which, head] = summed

    attend_near(1, 0)
    send_back(1, early)
    attend_near(1, 1)
    send_back(1, late)
    relay(2)
    attend_near(0, 0)
    send_back(0, early)
    attend_near(0, 1)
    send_back(0, late)
    relay(3)
    for n in range(HEADS):
        back_copy(n, 1).wait_recv()
    for n in range(1, HEADS):
        back_copy(n, 0).wait_recv()

    own_half = lax.div(mp, 2)
    attended = jnp.concatenate(
        [att[0, h].astype(F32) + att[1, h].astype(F32) for h in range(HEADS)], axis=1
    )
    mixed = (layer_norm(attended) * gate[...].astype(F32)).astype(BF16)
    projected = jnp.dot(mixed, wo[...], preferred_element_type=F32)
    out = (hist[...].astype(F32) + projected).astype(BF16)
    layer_out[0] = out
    groups = pool_query.shape[0]
    half = 0.5 * dot_t(pool_query[...], out)
    lane = first_pos + lax.broadcasted_iota(jnp.int32, half.shape, 1)
    pool_w = jnp.where(lane < length, silu_of_twice(half), 0.0).astype(BF16)
    sums = jnp.dot(pool_w, out, preferred_element_type=F32)

    for g in range(groups):
        part[g] = sums[g : g + 1]
    for a, b in STEPS:
        pltpu.make_async_remote_copy(
            src_ref=part.at[lax.rem(y + b, SIDE)],
            dst_ref=parts.at[t],
            send_sem=sum_sem.at[0],
            recv_sem=sum_sem.at[1],
            device_id=along(a, b),
            device_id_type=MESH,
        ).start()

    def wait_for(buffer, many, sem):
        some = buffer.at[pl.ds(0, many)]
        pltpu.make_async_copy(some, some, sem).wait()

    parts[t] = part[y]
    quarter = weights_of(across)
    for b in (2, 1, 3):
        pltpu.make_async_remote_copy(
            src_ref=quarter,
            dst_ref=quarter,
            send_sem=spread_sem.at[0],
            recv_sem=spread_sem.at[1],
            device_id=along(0, b),
            device_id_type=MESH,
        ).start()
    others = wr.at[across, pl.ds(0, (SIDE - 1) * depth)]
    pre[own_half] = jnp.dot(cand[...], wr[mp, :width], preferred_element_type=F32)
    wait_for(parts, plane - 1, sum_sem.at[1])
    state = jnp.sum(parts[...], axis=0).astype(BF16).astype(F32)

    own_interest = layer_norm(state).astype(BF16).astype(F32)
    told[...] = own_interest
    pieces[user] = own_interest

    for device in levels:
        pltpu.make_async_remote_copy(
            src_ref=told,
            dst_ref=pieces.at[user],
            send_sem=state_sem.at[0],
            recv_sem=state_sem.at[1],
            device_id=device,
            device_id_type=MESH,
        ).start()

    wait_for(pieces, height - 1, state_sem.at[1])
    mine = owner * owned + lax.broadcasted_iota(jnp.int32, (owned, line), 0)
    picker = jnp.where(slots[...] == mine, 1.0, 0.0).astype(BF16)
    known = pieces[...].reshape(line, width).astype(BF16)
    own_slots = jnp.dot(picker, known, preferred_element_type=F32)
    chosen[...] = own_slots
    interests[core * SIDE + y] = own_slots
    for b, n in ((2, 0), (2, 1), (1, 0), (3, 0), (1, 1), (3, 1), (0, 1)):
        pltpu.make_async_remote_copy(
            src_ref=chosen,
            dst_ref=interests.at[core * SIDE + y],
            send_sem=pick_sem.at[0],
            recv_sem=pick_sem.at[1],
            device_id=along_y(b, n),
            device_id_type=MESH,
        ).start()

    pltpu.make_async_copy(others, others, spread_sem.at[1]).wait()
    pre[1 - own_half] = jnp.dot(cand[...], wr[across, :width], preferred_element_type=F32)
    wait_for(interests, 2 * SIDE - 1, pick_sem.at[1])

    interest = jnp.concatenate(
        [interests[g] + interests[SIDE + g] for g in range(groups)], axis=0
    ).astype(BF16)
    half = (0.5 * width**-0.5) * dot_t(cand[...], interest)
    row = lax.div(lax.broadcasted_iota(jnp.int32, half.shape, 0), count)
    column = lax.rem(lax.broadcasted_iota(jnp.int32, half.shape, 1), owned)
    attn = jnp.where(row == column, silu_of_twice(half), 0.0)
    high = attn.astype(BF16)
    low = (attn - high.astype(F32)).astype(BF16)
    factors = jnp.concatenate([high, low, high], axis=1)
    terms = jnp.zeros_like(pre[0])
    for n in range(2):
        block = core + 2 * n
        mixed_in = jnp.dot(interest, wr[block, width:], preferred_element_type=F32)
        large = mixed_in.astype(BF16)
        small = (mixed_in - large.astype(F32)).astype(BF16)
        more = jnp.dot(
            factors, jnp.concatenate([large, large, small], axis=0), preferred_element_type=F32
        )
        half = 0.5 * (pre[n] + vectors[block, 0:1] + more)
        terms += silu_of_twice(half) * vectors[block, 1:2]
    high = terms.astype(BF16)
    low = (terms - high.astype(F32)).astype(BF16)
    ones = jnp.ones((16, terms.shape[1]), BF16)
    own_share = (dot_t(ones, high) + dot_t(ones, low))[0:1]
    share[...] = own_share
    shares[core] = own_share
    exchange = pltpu.make_async_remote_copy(
        src_ref=share,
        dst_ref=shares.at[core],
        send_sem=twin_sem.at[0],
        recv_sem=twin_sem.at[1],
        device_id={"mp": twin},
        device_id_type=MESH,
    )
    exchange.start()
    exchange.wait_recv()
    total = jnp.sum(shares[...], axis=0)
    for r in range(owned):
        scores[r : r + 1, :] = total[0:1, r * count : (r + 1) * count]

    for copy in kv_copies + q_copies:
        copy.wait_send()
    for n in range(HEADS):
        for m in range(2):
            pass_kv(n, m).wait_send()
        pass_q(n).wait_send()
        back_copy(n, 1).wait_send()
    for n in range(1, HEADS):
        back_copy(n, 0).wait_send()
    wait_for(parts, plane - 1, sum_sem.at[0])
    wait_for(pieces, height - 1, state_sem.at[0])
    wait_for(interests, 2 * SIDE - 1, pick_sem.at[0])
    exchange.wait_send()

    pltpu.make_async_copy(others, others, spread_sem.at[0]).wait()

    @pl.when(near == 0)
    def _():
        for copy in chain_copies(mp, over, over_send):
            copy.wait_send()

    @pl.when(near < ends_at)
    def _():
        for copy in chain_copies(across, onward, chain_send):
            copy.wait_send()


def solution(mesh):
    plane, owners, ranks = mesh.shape["tm"], mesh.shape["users"], mesh.shape["mp"]
    line = owners * ranks

    def shards(
        history,
        ln_gain,
        w_proj,
        w_out,
        pool_query,
        lengths,
        slots,
        cand_ids,
        item_table,
        w_rank,
        b_rank,
        w_score,
    ):
        _, events, width = history.shape
        head_size = width // HEADS
        groups = pool_query.shape[0]
        owned, count = cand_ids.shape
        cands = owned * count
        hidden = w_rank.shape[1]
        vmem = pl.BlockSpec(memory_space=pltpu.VMEM)
        smem = pl.BlockSpec(memory_space=pltpu.SMEM)
        hbm = pl.BlockSpec(memory_space=pltpu.HBM)
        dma = pltpu.SemaphoreType.DMA
        return pl.pallas_call(
            kernel,
            out_shape=(
                jax.ShapeDtypeStruct(history.shape, BF16),
                jax.ShapeDtypeStruct((owned, count), F32),
            ),
            in_specs=[smem] + [hbm] * 11,
            out_specs=(vmem, vmem),
            scratch_shapes=[
                pltpu.VMEM((events, width), BF16),
                pltpu.VMEM((1, width), F32),
                pltpu.VMEM(pool_query.shape, BF16),
                pltpu.VMEM((1, line), jnp.int32),
                pltpu.VMEM((owned, count), jnp.int32),
                pltpu.VMEM((1, hidden), F32),
                pltpu.VMEM((1, hidden), F32),
                pltpu.VMEM((4, width, width), BF16),
                pltpu.VMEM((width, width), BF16),
                pltpu.VMEM(item_table.shape, BF16),
                pltpu.VMEM((ranks, *w_rank.shape), BF16),
                pltpu.VMEM((events, width), BF16),
                pltpu.VMEM((events, width), BF16),
                pltpu.VMEM((HEADS, 3, events, head_size), BF16),
                pltpu.VMEM((2 * HEADS, 2, events, head_size), BF16),
                pltpu.VMEM((2 * HEADS, events, head_size), BF16),
                pltpu.VMEM((2 * HEADS * events, head_size), F32),
                pltpu.VMEM((2, HEADS, events, head_size), BF16),
                pltpu.VMEM((2, HEADS, events, head_size), BF16),
                pltpu.VMEM((3, events, events), F32),
                pltpu.VMEM((cands, width), BF16),
                pltpu.VMEM((2, cands, hidden), F32),
                pltpu.VMEM((groups, 1, width), F32),
                pltpu.VMEM((plane, 1, width), F32),
                pltpu.VMEM((1, width), F32),
                pltpu.VMEM((line, 1, width), F32),
                pltpu.VMEM((owned, width), F32),
                pltpu.VMEM((2 * SIDE, owned, width), F32),
                pltpu.VMEM((ranks, 2, hidden), F32),
                pltpu.VMEM((1, cands), F32),
                pltpu.VMEM((2, 1, cands), F32),
                dma((14,)),
                dma((HEADS, 2)),
                dma((HEADS, 2)),
                dma((HEADS,)),
                dma((HEADS,)),
                dma((3, HEADS)),
                dma((3, HEADS)),
                dma((2, HEADS)),
                dma((2, HEADS)),
                dma((2,)),
                dma((2,)),
                dma((2,)),
                dma((2,)),
                dma((2,)),
                dma((2,)),
                dma((2,)),
                dma((2,)),
            ],
            compiler_params=pltpu.CompilerParams(
                collective_id=0, has_side_effects=True, vmem_limit_bytes=VMEM_BYTES
            ),
            cost_estimate=pl.CostEstimate(
                flops=4_000_000_000, bytes_accessed=6_000_000, transcendentals=5_000_000
            ),
        )(
            lengths,
            history,
            ln_gain.reshape(1, -1),
            w_proj,
            w_out,
            pool_query,
            slots.reshape(1, -1),
            cand_ids,
            item_table,
            w_rank,
            b_rank.reshape(1, -1),
            w_score.reshape(1, -1),
        )

    placed = (
        P(("users", "mp"), "tm", None),
        P(),
        P(),
        P(),
        P(),
        P(("users", "mp")),
        P(),
        P("users", "tm"),
        P("users", None),
        P(None, "mp"),
        P("mp"),
        P("mp"),
    )
    return jax.shard_map(
        shards,
        mesh=mesh,
        in_specs=placed,
        out_specs=(P(("users", "mp"), "tm", None), P("users", "tm")),
        check_vma=False,
    )
```

```python
import jax
import jax.numpy as jnp
from jax import lax
from jax.experimental import pallas as pl
from jax.experimental.pallas import tpu as pltpu
from jax.sharding import PartitionSpec as P

HEADS = 4
SIDE = 4
EPS = 1e-05
VMEM_BYTES = 64 * 1024 * 1024
MESH = pl.DeviceIdType.MESH
STEPS = sorted(
    ((a, b) for a in range(SIDE) for b in range(SIDE) if a or b),
    key=lambda step: -sum(min(n, SIDE - n) for n in step),
)
F32 = jnp.float32
BF16 = jnp.bfloat16
ROWS_BY_ROWS = (((1,), (1,)), ((), ()))


def layer_norm(values):
    mean = jnp.mean(values, axis=-1, keepdims=True)
    centred = values - mean
    var = jnp.mean(centred * centred, axis=-1, keepdims=True)
    return centred * lax.rsqrt(var + EPS)


def silu_of_twice(half):
    return half + half * jnp.tanh(half)


def dot_t(a, b, **kw):
    return lax.dot_general(a, b, ROWS_BY_ROWS, preferred_element_type=F32, **kw)


def kernel(
    lengths,
    history,
    ln_gain_hbm,
    w_proj,
    w_out,
    pool_query_hbm,
    slots_hbm,
    cand_ids_hbm,
    item_table,
    w_rank,
    b_rank_hbm,
    w_score_hbm,
    layer_out,
    scores,
    hist,
    ln_gain,
    pool_query,
    slots,
    cand_ids,
    b_rank,
    w_score,
    wp,
    wo,
    table,
    wr,
    normed,
    gate,
    qkv,
    kv,
    qs,
    acc,
    back,
    att,
    masks,
    cand,
    pre,
    part,
    parts,
    told,
    pieces,
    chosen,
    interests,
    vectors,
    share,
    shares,
    load_sem,
    kv_send,
    kv_recv,
    q_send,
    q_recv,
    pass_send,
    pass_recv,
    back_send,
    back_recv,
    sum_sem,
    state_sem,
    pick_sem,
    over_send,
    chain_send,
    chain_recv,
    spread_sem,
    twin_sem,
):
    events, width = hist.shape
    head_size = width // HEADS
    plane, line, ranks = parts.shape[0], pieces.shape[0], wr.shape[0]
    t = lax.axis_index("tm")
    owner = lax.axis_index("users")
    mp = lax.axis_index("mp")
    user = owner * ranks + mp
    x, y = lax.div(t, SIDE), lax.rem(t, SIDE)
    core = lax.rem(mp, 2)

    def even(v):
        return v + 1 - 2 * lax.rem(v, 2)

    def odd(v):
        return SIDE - 1 - v

    def swap_y(v):
        return even(v) + core * (odd(v) - even(v))

    def ring_y(v):
        return odd(v) + core * (even(v) - odd(v))

    def head_of(a, b):
        first = lax.rem(lax.div(b + 1, 2), 2)
        return 2 * lax.div(a, 2) + first + core * (lax.div(b, 2) - first)

    def moved(a, b, rel):
        first, second = lax.rem(rel, 2), lax.div(rel, 2)
        return a + second * (odd(a) - a), b + first * (swap_y(b) - b)

    def in_plane(a, b):
        return {"tm": a * SIDE + b}

    head = head_of(x, y)

    depth = wr.shape[1] // SIDE
    last = line // ranks - 1
    twin = mp + 1 - 2 * core
    across = lax.rem(mp + 2, ranks)
    near = jnp.minimum(owner, last - owner)
    step_on = jnp.where(owner < near + 1, 1, -1)
    ends_at = last // 2

    def weights_of(whose):
        return wr.at[whose, pl.ds(pl.multiple_of(y * depth, depth), depth)]

    def chain_copies(whose, to, sems):
        return [
            pltpu.make_async_remote_copy(
                src_ref=ref,
                dst_ref=ref,
                send_sem=sems.at[n],
                recv_sem=chain_recv.at[n],
                device_id=to,
                device_id_type=MESH,
            )
            for n, ref in enumerate((weights_of(whose), vectors.at[whose]))
        ]

    over = {"users": last - owner, "mp": across}
    onward = {"users": owner + step_on}

    def relay(j):
        @pl.when(near == j)
        def _():
            for copy in chain_copies(across, onward, chain_send):
                copy.wait_recv()
                if j < ends_at:
                    copy.start()

    loads = [pltpu.make_async_copy(history.at[0], hist, load_sem.at[0])]
    for n, block in enumerate((3, 1, 2, 0)):
        cols = pl.ds(block * width, width)
        loads.append(pltpu.make_async_copy(w_proj.at[:, cols], wp.at[n], load_sem.at[n + 1]))
    rest = (
        (ln_gain_hbm, ln_gain),
        (pool_query_hbm, pool_query),
        (slots_hbm, slots),
        (cand_ids_hbm, cand_ids),
        (b_rank_hbm, b_rank),
        (w_score_hbm, w_score),
        (w_out, wo),
        (item_table, table),
        (w_rank, wr.at[mp]),
    )
    for n, (src, dst) in enumerate(rest):
        loads.append(pltpu.make_async_copy(src, dst, load_sem.at[5 + n]))
    loads[0].start()
    loads[5].start()
    for load in loads[1:5] + loads[6:]:
        load.start()

    pieces[...] = jnp.zeros_like(pieces)

    barrier = pltpu.get_barrier_semaphore()
    height = line // 2
    low = height // 2
    level = lax.div(mp, 2) * low + owner

    levels = []
    for k in range(height - 1):
        chip = lax.rem(level + low + (k + 1) // 2 * (1 - 2 * (k % 2)), height)
        levels.append({"users": lax.rem(chip, low), "mp": 2 * lax.div(chip, low) + core})

    def along(a, b):
        return {"tm": lax.rem(x + a, SIDE) * SIDE + lax.rem(y + b, SIDE)}

    def along_y(b, other):
        return {"tm": x * SIDE + lax.rem(y + b, SIDE), "mp": mp + other * (1 - 2 * core)}

    greeted = [along(a, b) for a, b in STEPS] + [along_y(b, 1) for b in range(SIDE)]
    greeted = levels + greeted
    for device in greeted:
        pl.semaphore_signal(barrier, inc=1, device_id=device, device_id_type=MESH)

    first_pos = t * events
    length = lengths[0]
    pos = first_pos + lax.broadcasted_iota(jnp.int32, (events, 1), 0)
    live = pos < length
    loads[0].wait()
    loads[5].wait()
    normed[...] = (layer_norm(hist[...].astype(F32)) * ln_gain[...]).astype(BF16)

    def project(n):
        loads[n + 1].wait()
        half = 0.5 * jnp.dot(normed[...], wp[n], preferred_element_type=F32)
        return silu_of_twice(half)

    keys = project(0).astype(BF16)
    for h in range(HEADS):
        qkv[h, 0] = keys[:, h * head_size : (h + 1) * head_size]
    values = jnp.where(live, project(1), 0.0).astype(BF16)
    for h in range(HEADS):
        qkv[h, 1] = values[:, h * head_size : (h + 1) * head_size]

    pl.semaphore_wait(barrier, len(greeted))

    kv_copies, q_copies = [], []
    for rel in (3, 2, 1):
        a, b = moved(x, y, rel)
        for n in range(2):
            copy = pltpu.make_async_remote_copy(
                src_ref=qkv.at[head_of(a, b), n],
                dst_ref=kv.at[rel, n],
                send_sem=kv_send.at[rel, n],
                recv_sem=kv_recv.at[rel, n],
                device_id=in_plane(a, b),
                device_id_type=MESH,
            )
            copy.start()
            kv_copies.append(copy)

    query = (project(2) * (0.5 * head_size**-0.5)).astype(BF16)
    for h in range(HEADS):
        qkv[h, 2] = query[:, h * head_size : (h + 1) * head_size]
    for rel in (3, 2, 1):
        a, b = moved(x, y, rel)
        copy = pltpu.make_async_remote_copy(
            src_ref=qkv.at[head_of(a, b), 2],
            dst_ref=qs.at[rel],
            send_sem=q_send.at[rel],
            recv_sem=q_recv.at[rel],
            device_id=in_plane(a, b),
            device_id_type=MESH,
        )
        copy.start()
        q_copies.append(copy)
    for load in loads[9:11] + loads[13:]:
        load.wait()
    vectors[mp, 0:1] = b_rank[...]
    vectors[mp, 1:2] = w_score[...]

    @pl.when(near == 0)
    def _():
        for copy in chain_copies(mp, over, over_send):
            copy.start()

    kv[0] = qkv[head, pl.ds(0, 2)]
    qs[0] = qkv[head, 2]

    x_near, y_near = even(x), ring_y(y)

    def pass_kv(n, m):
        return pltpu.make_async_remote_copy(
            src_ref=kv.at[n, m],
            dst_ref=kv.at[HEADS + n, m],
            send_sem=pass_send.at[m, n],
            recv_sem=pass_recv.at[m, n],
            device_id=in_plane(x_near, y),
            device_id_type=MESH,
        )

    def pass_q(n):
        return pltpu.make_async_remote_copy(
            src_ref=qs.at[n],
            dst_ref=qs.at[HEADS + n],
            send_sem=pass_send.at[2, n],
            recv_sem=pass_recv.at[2, n],
            device_id=in_plane(x, y_near),
            device_id_type=MESH,
        )

    def back_copy(n, which):
        a, b = moved(x, y_near if which else y, n)
        return pltpu.make_async_remote_copy(
            src_ref=back.at[which, n],
            dst_ref=att.at[which, head],
            send_sem=back_send.at[which, n],
            recv_sem=back_recv.at[which, n],
            device_id=in_plane(a, b),
            device_id_type=MESH,
        )

    pass_q(0).start()
    for m in range(2):
        pass_kv(0, m).start()

    gate[...] = project(3).astype(BF16)
    acc[...] = jnp.zeros_like(acc)

    owned, count = cand_ids.shape
    pool = table.shape[0]
    for load in loads[6:9] + loads[11:13]:
        load.wait()

    @pl.loop(0, owned)
    def _(r):
        @pl.when(r > 0)
        def _():
            for m in range(2):
                pltpu.make_async_copy(kv.at[r, m], kv.at[r, m], kv_recv.at[r, m]).wait()
                pass_kv(r, m).start()

        eye = lax.broadcasted_iota(jnp.int32, (count, count), 0) == lax.broadcasted_iota(
            jnp.int32, (count, count), 1
        )
        item = lax.broadcasted_iota(jnp.int32, (count, pool), 1).astype(F32)
        ids = cand_ids[pl.ds(r, 1), :].astype(F32)
        column = jnp.sum(jnp.where(eye, ids, 0.0), axis=1, keepdims=True)
        onehot = jnp.where(item == column, 1.0, 0.0).astype(BF16)
        cand[pl.ds(r * count, count)] = jnp.dot(
            onehot, table[...], preferred_element_type=F32
        ).astype(BF16)

    pairs = 2 * events
    behind = lax.broadcasted_iota(jnp.int32, (events, events), 0) >= lax.broadcasted_iota(
        jnp.int32, (events, events), 1
    )
    masks[0] = jnp.zeros((events, events), F32)
    masks[1] = jnp.where(behind, 1.0, 0.0)
    masks[2] = jnp.ones((events, events), F32)

    def rows_of(which, pair):
        return pl.ds(pl.multiple_of((2 * which + pair) * pairs, pairs), pairs)

    def attend(q_set, q_pair, k_set, k_pair, masked):
        q_first, k_first = HEADS * q_set + 2 * q_pair, HEADS * k_set + 2 * k_pair
        query = qs[pl.ds(q_first, 2)].reshape(pairs, head_size)
        half = jnp.concatenate(
            [dot_t(query, kv[k_first + n, 0]) for n in range(2)], axis=1
        )
        if masked:
            q_y = y_near if q_set else y
            half = jnp.concatenate(
                [
                    jnp.concatenate(
                        [
                            half[a * events : (a + 1) * events, b * events : (b + 1) * events]
                            * masks[1 + jnp.clip(q_row - k_row, -1, 1)]
                            for b, k_row in enumerate((y, swap_y(y)))
                        ],
                        axis=1,
                    )
                    for a, q_row in enumerate((q_y, swap_y(q_y)))
                ],
                axis=0,
            )
        weights = silu_of_twice(half).astype(BF16)
        value = jnp.concatenate([kv[k_first + n, 1] for n in range(2)], axis=0)
        acc[rows_of(q_set, q_pair)] += jnp.dot(weights, value, preferred_element_type=F32)

    late = jnp.where(x < SIDE // 2, 1, 0)
    early = 1 - late
    outer = jnp.logical_or(x == 0, x == SIDE - 1)

    def attend_own(q_set):
        for pair in range(2):
            attend(q_set, pair, 0, pair, True)
        attend(q_set, late, 0, early, False)

    def attend_near(q_set, n):
        q_pair = late if n else jnp.where(outer, late, early)
        k_pair = jnp.where(outer, n, jnp.where(x == 1, 0, 1))
        attend(q_set, q_pair, 1, k_pair, False)

    for n in range(1, HEADS):
        pltpu.make_async_copy(qs.at[n], qs.at[n], q_recv.at[n]).wait()
        pass_q(n).start()
    attend_own(0)
    relay(0)
    for n in range(HEADS):
        pass_q(n).wait_recv()
    attend(1, 0, 0, 0, True)
    attend(1, 1, 0, 1, True)
    attend(1, late, 0, early, False)
    for n in range(HEADS):
        for m in range(2):
            pass_kv(n, m).wait_recv()
    def send_back(which, pair):
        for m in (1, 0):
            n = 2 * pair + m
            rows = pl.ds(pl.multiple_of((HEADS * which + n) * events, events), events)
            summed = acc[rows].astype(BF16)
            away = n >= 1 - which

            @pl.when(away)
            def _():
                back[which, n] = summed
                back_copy(n, which).start()

            @pl.when(jnp.logical_not(away))
            def _():
                att[which, head] = summed

    attend_near(1, 0)
    send_back(1, early)
    attend_near(1, 1)
    send_back(1, late)
    relay(1)
    attend_near(0, 0)
    send_back(0, early)
    attend_near(0, 1)
    send_back(0, late)
    relay(2)
    for n in range(HEADS):
        back_copy(n, 1).wait_recv()
    for n in range(1, HEADS):
        back_copy(n, 0).wait_recv()

    own_half = lax.div(mp, 2)
    attended = jnp.concatenate(
        [att[0, h].astype(F32) + att[1, h].astype(F32) for h in range(HEADS)], axis=1
    )
    mixed = (layer_norm(attended) * gate[...].astype(F32)).astype(BF16)
    projected = jnp.dot(mixed, wo[...], preferred_element_type=F32)
    out = (hist[...].astype(F32) + projected).astype(BF16)
    layer_out[0] = out
    groups = pool_query.shape[0]
    half = 0.5 * dot_t(pool_query[...], out)
    lane = first_pos + lax.broadcasted_iota(jnp.int32, half.shape, 1)
    pool_w = jnp.where(lane < length, silu_of_twice(half), 0.0).astype(BF16)
    sums = jnp.dot(pool_w, out, preferred_element_type=F32)

    for g in range(groups):
        part[g] = sums[g : g + 1]
    for a, b in STEPS:
        pltpu.make_async_remote_copy(
            src_ref=part.at[lax.rem(y + b, SIDE)],
            dst_ref=parts.at[t],
            send_sem=sum_sem.at[0],
            recv_sem=sum_sem.at[1],
            device_id=along(a, b),
            device_id_type=MESH,
        ).start()

    def wait_for(buffer, many, sem):
        some = buffer.at[pl.ds(0, many)]
        pltpu.make_async_copy(some, some, sem).wait()

    parts[t] = part[y]
    relay(3)
    quarter = weights_of(across)
    for b in (2, 1, 3):
        pltpu.make_async_remote_copy(
            src_ref=quarter,
            dst_ref=quarter,
            send_sem=spread_sem.at[0],
            recv_sem=spread_sem.at[1],
            device_id=along(0, b),
            device_id_type=MESH,
        ).start()
    others = wr.at[across, pl.ds(0, (SIDE - 1) * depth)]
    pre[own_half] = jnp.dot(cand[...], wr[mp, :width], preferred_element_type=F32)
    wait_for(parts, plane - 1, sum_sem.at[1])
    state = jnp.sum(parts[...], axis=0).astype(BF16).astype(F32)

    own_interest = layer_norm(state).astype(BF16).astype(F32)
    told[...] = own_interest
    pieces[user] = own_interest

    for device in levels:
        pltpu.make_async_remote_copy(
            src_ref=told,
            dst_ref=pieces.at[user],
            send_sem=state_sem.at[0],
            recv_sem=state_sem.at[1],
            device_id=device,
            device_id_type=MESH,
        ).start()

    wait_for(pieces, height - 1, state_sem.at[1])
    mine = owner * owned + lax.broadcasted_iota(jnp.int32, (owned, line), 0)
    picker = jnp.where(slots[...] == mine, 1.0, 0.0).astype(BF16)
    known = pieces[...].reshape(line, width).astype(BF16)
    own_slots = jnp.dot(picker, known, preferred_element_type=F32)
    chosen[...] = own_slots
    interests[core * SIDE + y] = own_slots
    for b, n in ((2, 0), (2, 1), (1, 0), (3, 0), (1, 1), (3, 1), (0, 1)):
        pltpu.make_async_remote_copy(
            src_ref=chosen,
            dst_ref=interests.at[core * SIDE + y],
            send_sem=pick_sem.at[0],
            recv_sem=pick_sem.at[1],
            device_id=along_y(b, n),
            device_id_type=MESH,
        ).start()

    pltpu.make_async_copy(others, others, spread_sem.at[1]).wait()
    pre[1 - own_half] = jnp.dot(cand[...], wr[across, :width], preferred_element_type=F32)
    wait_for(interests, 2 * SIDE - 1, pick_sem.at[1])

    interest = jnp.concatenate(
        [interests[g] + interests[SIDE + g] for g in range(groups)], axis=0
    ).astype(BF16)
    half = (0.5 * width**-0.5) * dot_t(cand[...], interest)
    row = lax.div(lax.broadcasted_iota(jnp.int32, half.shape, 0), count)
    column = lax.rem(lax.broadcasted_iota(jnp.int32, half.shape, 1), owned)
    attn = jnp.where(row == column, silu_of_twice(half), 0.0)
    high = attn.astype(BF16)
    low = (attn - high.astype(F32)).astype(BF16)
    factors = jnp.concatenate([high, low, high], axis=1)
    terms = jnp.zeros_like(pre[0])
    for n in range(2):
        block = core + 2 * n
        mixed_in = jnp.dot(interest, wr[block, width:], preferred_element_type=F32)
        large = mixed_in.astype(BF16)
        small = (mixed_in - large.astype(F32)).astype(BF16)
        more = jnp.dot(
            factors, jnp.concatenate([large, large, small], axis=0), preferred_element_type=F32
        )
        half = 0.5 * (pre[n] + vectors[block, 0:1] + more)
        terms += silu_of_twice(half) * vectors[block, 1:2]
    high = terms.astype(BF16)
    low = (terms - high.astype(F32)).astype(BF16)
    ones = jnp.ones((16, terms.shape[1]), BF16)
    own_share = (dot_t(ones, high) + dot_t(ones, low))[0:1]
    share[...] = own_share
    shares[core] = own_share
    exchange = pltpu.make_async_remote_copy(
        src_ref=share,
        dst_ref=shares.at[core],
        send_sem=twin_sem.at[0],
        recv_sem=twin_sem.at[1],
        device_id={"mp": twin},
        device_id_type=MESH,
    )
    exchange.start()
    exchange.wait_recv()
    total = jnp.sum(shares[...], axis=0)
    for r in range(owned):
        scores[r : r + 1, :] = total[0:1, r * count : (r + 1) * count]

    for copy in kv_copies + q_copies:
        copy.wait_send()
    for n in range(HEADS):
        for m in range(2):
            pass_kv(n, m).wait_send()
        pass_q(n).wait_send()
        back_copy(n, 1).wait_send()
    for n in range(1, HEADS):
        back_copy(n, 0).wait_send()
    wait_for(parts, plane - 1, sum_sem.at[0])
    wait_for(pieces, height - 1, state_sem.at[0])
    wait_for(interests, 2 * SIDE - 1, pick_sem.at[0])
    exchange.wait_send()

    pltpu.make_async_copy(others, others, spread_sem.at[0]).wait()

    @pl.when(near == 0)
    def _():
        for copy in chain_copies(mp, over, over_send):
            copy.wait_send()

    @pl.when(near < ends_at)
    def _():
        for copy in chain_copies(across, onward, chain_send):
            copy.wait_send()


def solution(mesh):
    plane, owners, ranks = mesh.shape["tm"], mesh.shape["users"], mesh.shape["mp"]
    line = owners * ranks

    def shards(
        history,
        ln_gain,
        w_proj,
        w_out,
        pool_query,
        lengths,
        slots,
        cand_ids,
        item_table,
        w_rank,
        b_rank,
        w_score,
    ):
        _, events, width = history.shape
        head_size = width // HEADS
        groups = pool_query.shape[0]
        owned, count = cand_ids.shape
        cands = owned * count
        hidden = w_rank.shape[1]
        vmem = pl.BlockSpec(memory_space=pltpu.VMEM)
        smem = pl.BlockSpec(memory_space=pltpu.SMEM)
        hbm = pl.BlockSpec(memory_space=pltpu.HBM)
        dma = pltpu.SemaphoreType.DMA
        return pl.pallas_call(
            kernel,
            out_shape=(
                jax.ShapeDtypeStruct(history.shape, BF16),
                jax.ShapeDtypeStruct((owned, count), F32),
            ),
            in_specs=[smem] + [hbm] * 11,
            out_specs=(vmem, vmem),
            scratch_shapes=[
                pltpu.VMEM((events, width), BF16),
                pltpu.VMEM((1, width), F32),
                pltpu.VMEM(pool_query.shape, BF16),
                pltpu.VMEM((1, line), jnp.int32),
                pltpu.VMEM((owned, count), jnp.int32),
                pltpu.VMEM((1, hidden), F32),
                pltpu.VMEM((1, hidden), F32),
                pltpu.VMEM((4, width, width), BF16),
                pltpu.VMEM((width, width), BF16),
                pltpu.VMEM(item_table.shape, BF16),
                pltpu.VMEM((ranks, *w_rank.shape), BF16),
                pltpu.VMEM((events, width), BF16),
                pltpu.VMEM((events, width), BF16),
                pltpu.VMEM((HEADS, 3, events, head_size), BF16),
                pltpu.VMEM((2 * HEADS, 2, events, head_size), BF16),
                pltpu.VMEM((2 * HEADS, events, head_size), BF16),
                pltpu.VMEM((2 * HEADS * events, head_size), F32),
                pltpu.VMEM((2, HEADS, events, head_size), BF16),
                pltpu.VMEM((2, HEADS, events, head_size), BF16),
                pltpu.VMEM((3, events, events), F32),
                pltpu.VMEM((cands, width), BF16),
                pltpu.VMEM((2, cands, hidden), F32),
                pltpu.VMEM((groups, 1, width), F32),
                pltpu.VMEM((plane, 1, width), F32),
                pltpu.VMEM((1, width), F32),
                pltpu.VMEM((line, 1, width), F32),
                pltpu.VMEM((owned, width), F32),
                pltpu.VMEM((2 * SIDE, owned, width), F32),
                pltpu.VMEM((ranks, 2, hidden), F32),
                pltpu.VMEM((1, cands), F32),
                pltpu.VMEM((2, 1, cands), F32),
                dma((14,)),
                dma((HEADS, 2)),
                dma((HEADS, 2)),
                dma((HEADS,)),
                dma((HEADS,)),
                dma((3, HEADS)),
                dma((3, HEADS)),
                dma((2, HEADS)),
                dma((2, HEADS)),
                dma((2,)),
                dma((2,)),
                dma((2,)),
                dma((2,)),
                dma((2,)),
                dma((2,)),
                dma((2,)),
                dma((2,)),
            ],
            compiler_params=pltpu.CompilerParams(
                collective_id=0, has_side_effects=True, vmem_limit_bytes=VMEM_BYTES
            ),
            cost_estimate=pl.CostEstimate(
                flops=4_000_000_000, bytes_accessed=6_000_000, transcendentals=5_000_000
            ),
        )(
            lengths,
            history,
            ln_gain.reshape(1, -1),
            w_proj,
            w_out,
            pool_query,
            slots.reshape(1, -1),
            cand_ids,
            item_table,
            w_rank,
            b_rank.reshape(1, -1),
            w_score.reshape(1, -1),
        )

    placed = (
        P(("users", "mp"), "tm", None),
        P(),
        P(),
        P(),
        P(),
        P(("users", "mp")),
        P(),
        P("users", "tm"),
        P("users", None),
        P(None, "mp"),
        P("mp"),
        P("mp"),
    )
    return jax.shard_map(
        shards,
        mesh=mesh,
        in_specs=placed,
        out_specs=(P(("users", "mp"), "tm", None), P("users", "tm")),
        check_vma=False,
    )
```

```python
import jax
import jax.numpy as jnp
from jax import lax
from jax.experimental import pallas as pl
from jax.experimental.pallas import tpu as pltpu
from jax.sharding import PartitionSpec as P

HEADS = 4
SIDE = 4
EPS = 1e-05
VMEM_BYTES = 64 * 1024 * 1024
MESH = pl.DeviceIdType.MESH
STEPS = sorted(
    ((a, b) for a in range(SIDE) for b in range(SIDE) if a or b),
    key=lambda step: -sum(min(n, SIDE - n) for n in step),
)
F32 = jnp.float32
BF16 = jnp.bfloat16
ROWS_BY_ROWS = (((1,), (1,)), ((), ()))


def layer_norm(values):
    mean = jnp.mean(values, axis=-1, keepdims=True)
    centred = values - mean
    var = jnp.mean(centred * centred, axis=-1, keepdims=True)
    return centred * lax.rsqrt(var + EPS)


def silu_of_twice(half):
    return half + half * jnp.tanh(half)


def dot_t(a, b, **kw):
    return lax.dot_general(a, b, ROWS_BY_ROWS, preferred_element_type=F32, **kw)


def kernel(
    lengths,
    history,
    ln_gain_hbm,
    w_proj,
    w_out,
    pool_query_hbm,
    slots_hbm,
    cand_ids_hbm,
    item_table,
    w_rank,
    b_rank_hbm,
    w_score_hbm,
    layer_out,
    scores,
    hist,
    ln_gain,
    pool_query,
    slots,
    cand_ids,
    b_rank,
    w_score,
    wp,
    wo,
    table,
    wr,
    normed,
    gate,
    qkv,
    kv,
    qs,
    acc,
    back,
    att,
    masks,
    cand,
    pre,
    part,
    parts,
    told,
    pieces,
    chosen,
    interests,
    vectors,
    share,
    shares,
    load_sem,
    kv_send,
    kv_recv,
    q_send,
    q_recv,
    pass_send,
    pass_recv,
    back_send,
    back_recv,
    sum_sem,
    state_sem,
    pick_sem,
    over_send,
    chain_send,
    chain_recv,
    spread_sem,
    twin_sem,
):
    events, width = hist.shape
    head_size = width // HEADS
    plane, line, ranks = parts.shape[0], pieces.shape[0], wr.shape[0]
    t = lax.axis_index("tm")
    owner = lax.axis_index("users")
    mp = lax.axis_index("mp")
    user = owner * ranks + mp
    x, y = lax.div(t, SIDE), lax.rem(t, SIDE)
    core = lax.rem(mp, 2)

    def even(v):
        return v + 1 - 2 * lax.rem(v, 2)

    def odd(v):
        return SIDE - 1 - v

    def swap_y(v):
        return even(v) + core * (odd(v) - even(v))

    def ring_y(v):
        return odd(v) + core * (even(v) - odd(v))

    def head_of(a, b):
        first = lax.rem(lax.div(b + 1, 2), 2)
        return 2 * lax.div(a, 2) + first + core * (lax.div(b, 2) - first)

    def moved(a, b, rel):
        first, second = lax.rem(rel, 2), lax.div(rel, 2)
        return a + second * (odd(a) - a), b + first * (swap_y(b) - b)

    def in_plane(a, b):
        return {"tm": a * SIDE + b}

    head = head_of(x, y)

    depth = wr.shape[1] // SIDE
    last = line // ranks - 1
    twin = mp + 1 - 2 * core
    across = lax.rem(mp + 2, ranks)
    near = jnp.minimum(owner, last - owner)
    step_on = jnp.where(owner < near + 1, 1, -1)
    ends_at = last // 2

    def weights_of(whose):
        return wr.at[whose, pl.ds(pl.multiple_of(y * depth, depth), depth)]

    def chain_copies(whose, to, sems):
        return [
            pltpu.make_async_remote_copy(
                src_ref=ref,
                dst_ref=ref,
                send_sem=sems.at[n],
                recv_sem=chain_recv.at[n],
                device_id=to,
                device_id_type=MESH,
            )
            for n, ref in enumerate((weights_of(whose), vectors.at[whose]))
        ]

    over = {"users": last - owner, "mp": across}
    onward = {"users": owner + step_on}

    def relay(j):
        @pl.when(near == j)
        def _():
            for copy in chain_copies(across, onward, chain_send):
                copy.wait_recv()
                if j < ends_at:
                    copy.start()

    loads = [pltpu.make_async_copy(history.at[0], hist, load_sem.at[0])]
    for n, block in enumerate((3, 1, 2, 0)):
        cols = pl.ds(block * width, width)
        loads.append(pltpu.make_async_copy(w_proj.at[:, cols], wp.at[n], load_sem.at[n + 1]))
    rest = (
        (ln_gain_hbm, ln_gain),
        (pool_query_hbm, pool_query),
        (slots_hbm, slots),
        (cand_ids_hbm, cand_ids),
        (b_rank_hbm, b_rank),
        (w_score_hbm, w_score),
        (w_out, wo),
        (item_table, table),
        (w_rank, wr.at[mp]),
    )
    for n, (src, dst) in enumerate(rest):
        loads.append(pltpu.make_async_copy(src, dst, load_sem.at[5 + n]))
    loads[0].start()
    loads[5].start()
    for load in loads[1:5] + loads[6:]:
        load.start()

    pieces[...] = jnp.zeros_like(pieces)

    barrier = pltpu.get_barrier_semaphore()
    height = line // 2
    low = height // 2
    level = lax.div(mp, 2) * low + owner

    levels = []
    for k in range(height - 1):
        chip = lax.rem(level + low + (k + 1) // 2 * (1 - 2 * (k % 2)), height)
        levels.append({"users": lax.rem(chip, low), "mp": 2 * lax.div(chip, low) + core})

    def along(a, b):
        return {"tm": lax.rem(x + a, SIDE) * SIDE + lax.rem(y + b, SIDE)}

    def along_y(b, other):
        return {"tm": x * SIDE + lax.rem(y + b, SIDE), "mp": mp + other * (1 - 2 * core)}

    greeted = [along(a, b) for a, b in STEPS] + [along_y(b, 1) for b in range(SIDE)]
    greeted = levels + greeted
    for device in greeted:
        pl.semaphore_signal(barrier, inc=1, device_id=device, device_id_type=MESH)

    first_pos = t * events
    length = lengths[0]
    pos = first_pos + lax.broadcasted_iota(jnp.int32, (events, 1), 0)
    live = pos < length
    loads[0].wait()
    loads[5].wait()
    normed[...] = (layer_norm(hist[...].astype(F32)) * ln_gain[...]).astype(BF16)

    def project(n):
        loads[n + 1].wait()
        half = 0.5 * jnp.dot(normed[...], wp[n], preferred_element_type=F32)
        return silu_of_twice(half)

    keys = project(0).astype(BF16)
    for h in range(HEADS):
        qkv[h, 0] = keys[:, h * head_size : (h + 1) * head_size]
    values = jnp.where(live, project(1), 0.0).astype(BF16)
    for h in range(HEADS):
        qkv[h, 1] = values[:, h * head_size : (h + 1) * head_size]

    pl.semaphore_wait(barrier, len(greeted))

    kv_copies, q_copies = [], []
    for rel in (3, 2, 1):
        a, b = moved(x, y, rel)
        for n in range(2):
            copy = pltpu.make_async_remote_copy(
                src_ref=qkv.at[head_of(a, b), n],
                dst_ref=kv.at[rel, n],
                send_sem=kv_send.at[rel, n],
                recv_sem=kv_recv.at[rel, n],
                device_id=in_plane(a, b),
                device_id_type=MESH,
            )
            copy.start()
            kv_copies.append(copy)

    query = (project(2) * (0.5 * head_size**-0.5)).astype(BF16)
    for h in range(HEADS):
        qkv[h, 2] = query[:, h * head_size : (h + 1) * head_size]
    for rel in (3, 2, 1):
        a, b = moved(x, y, rel)
        copy = pltpu.make_async_remote_copy(
            src_ref=qkv.at[head_of(a, b), 2],
            dst_ref=qs.at[rel],
            send_sem=q_send.at[rel],
            recv_sem=q_recv.at[rel],
            device_id=in_plane(a, b),
            device_id_type=MESH,
        )
        copy.start()
        q_copies.append(copy)
    kv[0] = qkv[head, pl.ds(0, 2)]
    qs[0] = qkv[head, 2]

    x_near, y_near = even(x), ring_y(y)

    def pass_kv(n, m):
        return pltpu.make_async_remote_copy(
            src_ref=kv.at[n, m],
            dst_ref=kv.at[HEADS + n, m],
            send_sem=pass_send.at[m, n],
            recv_sem=pass_recv.at[m, n],
            device_id=in_plane(x_near, y),
            device_id_type=MESH,
        )

    def pass_q(n):
        return pltpu.make_async_remote_copy(
            src_ref=qs.at[n],
            dst_ref=qs.at[HEADS + n],
            send_sem=pass_send.at[2, n],
            recv_sem=pass_recv.at[2, n],
            device_id=in_plane(x, y_near),
            device_id_type=MESH,
        )

    def back_copy(n, which):
        a, b = moved(x, y_near if which else y, n)
        return pltpu.make_async_remote_copy(
            src_ref=back.at[which, n],
            dst_ref=att.at[which, head],
            send_sem=back_send.at[which, n],
            recv_sem=back_recv.at[which, n],
            device_id=in_plane(a, b),
            device_id_type=MESH,
        )

    pass_q(0).start()
    for m in range(2):
        pass_kv(0, m).start()

    for load in loads[9:11] + loads[13:]:
        load.wait()
    vectors[mp, 0:1] = b_rank[...]
    vectors[mp, 1:2] = w_score[...]

    @pl.when(near == 0)
    def _():
        for copy in chain_copies(mp, over, over_send):
            copy.start()

    gate[...] = project(3).astype(BF16)
    acc[...] = jnp.zeros_like(acc)

    owned, count = cand_ids.shape
    pool = table.shape[0]
    for load in loads[6:9] + loads[11:13]:
        load.wait()

    def pass_q_on(n):
        pltpu.make_async_copy(qs.at[n], qs.at[n], q_recv.at[n]).wait()
        pass_q(n).start()

    @pl.loop(0, owned)
    def _(r):
        @pl.when(r > 0)
        def _():
            for m in range(2):
                pltpu.make_async_copy(kv.at[r, m], kv.at[r, m], kv_recv.at[r, m]).wait()
                pass_kv(r, m).start()

        @pl.when(r > 1)
        def _():
            pass_q_on(r - 1)

        eye = lax.broadcasted_iota(jnp.int32, (count, count), 0) == lax.broadcasted_iota(
            jnp.int32, (count, count), 1
        )
        item = lax.broadcasted_iota(jnp.int32, (count, pool), 1).astype(F32)
        ids = cand_ids[pl.ds(r, 1), :].astype(F32)
        column = jnp.sum(jnp.where(eye, ids, 0.0), axis=1, keepdims=True)
        onehot = jnp.where(item == column, 1.0, 0.0).astype(BF16)
        cand[pl.ds(r * count, count)] = jnp.dot(
            onehot, table[...], preferred_element_type=F32
        ).astype(BF16)

    pairs = 2 * events
    behind = lax.broadcasted_iota(jnp.int32, (events, events), 0) >= lax.broadcasted_iota(
        jnp.int32, (events, events), 1
    )
    masks[0] = jnp.zeros((events, events), F32)
    masks[1] = jnp.where(behind, 1.0, 0.0)
    masks[2] = jnp.ones((events, events), F32)

    def rows_of(which, pair):
        return pl.ds(pl.multiple_of((2 * which + pair) * pairs, pairs), pairs)

    def attend(q_set, q_pair, k_set, k_pair, masked):
        q_first, k_first = HEADS * q_set + 2 * q_pair, HEADS * k_set + 2 * k_pair
        query = qs[pl.ds(q_first, 2)].reshape(pairs, head_size)
        half = jnp.concatenate(
            [dot_t(query, kv[k_first + n, 0]) for n in range(2)], axis=1
        )
        if masked:
            q_y = y_near if q_set else y
            half = jnp.concatenate(
                [
                    jnp.concatenate(
                        [
                            half[a * events : (a + 1) * events, b * events : (b + 1) * events]
                            * masks[1 + jnp.clip(q_row - k_row, -1, 1)]
                            for b, k_row in enumerate((y, swap_y(y)))
                        ],
                        axis=1,
                    )
                    for a, q_row in enumerate((q_y, swap_y(q_y)))
                ],
                axis=0,
            )
        weights = silu_of_twice(half).astype(BF16)
        value = jnp.concatenate([kv[k_first + n, 1] for n in range(2)], axis=0)
        acc[rows_of(q_set, q_pair)] += jnp.dot(weights, value, preferred_element_type=F32)

    late = jnp.where(x < SIDE // 2, 1, 0)
    early = 1 - late
    outer = jnp.logical_or(x == 0, x == SIDE - 1)

    def attend_own(q_set):
        for pair in range(2):
            attend(q_set, pair, 0, pair, True)
        attend(q_set, late, 0, early, False)

    def attend_near(q_set, n):
        q_pair = late if n else jnp.where(outer, late, early)
        k_pair = jnp.where(outer, n, jnp.where(x == 1, 0, 1))
        attend(q_set, q_pair, 1, k_pair, False)

    pass_q_on(HEADS - 1)
    attend_own(0)
    relay(0)
    for n in range(HEADS):
        pass_q(n).wait_recv()
    attend(1, 0, 0, 0, True)
    attend(1, 1, 0, 1, True)
    attend(1, late, 0, early, False)
    for n in range(HEADS):
        for m in range(2):
            pass_kv(n, m).wait_recv()
    def send_back(which, pair):
        for m in (1, 0):
            n = 2 * pair + m
            rows = pl.ds(pl.multiple_of((HEADS * which + n) * events, events), events)
            summed = acc[rows].astype(BF16)
            away = n >= 1 - which

            @pl.when(away)
            def _():
                back[which, n] = summed
                back_copy(n, which).start()

            @pl.when(jnp.logical_not(away))
            def _():
                att[which, head] = summed

    attend_near(1, 0)
    send_back(1, early)
    attend_near(1, 1)
    send_back(1, late)
    relay(1)
    attend_near(0, 0)
    send_back(0, early)
    attend_near(0, 1)
    send_back(0, late)
    relay(2)
    for n in range(HEADS):
        back_copy(n, 1).wait_recv()
    for n in range(1, HEADS):
        back_copy(n, 0).wait_recv()

    own_half = lax.div(mp, 2)
    attended = jnp.concatenate(
        [att[0, h].astype(F32) + att[1, h].astype(F32) for h in range(HEADS)], axis=1
    )
    mixed = (layer_norm(attended) * gate[...].astype(F32)).astype(BF16)
    projected = jnp.dot(mixed, wo[...], preferred_element_type=F32)
    out = (hist[...].astype(F32) + projected).astype(BF16)
    layer_out[0] = out
    groups = pool_query.shape[0]
    half = 0.5 * dot_t(pool_query[...], out)
    lane = first_pos + lax.broadcasted_iota(jnp.int32, half.shape, 1)
    pool_w = jnp.where(lane < length, silu_of_twice(half), 0.0).astype(BF16)
    sums = jnp.dot(pool_w, out, preferred_element_type=F32)

    for g in range(groups):
        part[g] = sums[g : g + 1]
    for a, b in STEPS:
        pltpu.make_async_remote_copy(
            src_ref=part.at[lax.rem(y + b, SIDE)],
            dst_ref=parts.at[t],
            send_sem=sum_sem.at[0],
            recv_sem=sum_sem.at[1],
            device_id=along(a, b),
            device_id_type=MESH,
        ).start()

    def wait_for(buffer, many, sem):
        some = buffer.at[pl.ds(0, many)]
        pltpu.make_async_copy(some, some, sem).wait()

    parts[t] = part[y]
    relay(3)
    quarter = weights_of(across)
    for b in (2, 1, 3):
        pltpu.make_async_remote_copy(
            src_ref=quarter,
            dst_ref=quarter,
            send_sem=spread_sem.at[0],
            recv_sem=spread_sem.at[1],
            device_id=along(0, b),
            device_id_type=MESH,
        ).start()
    others = wr.at[across, pl.ds(0, (SIDE - 1) * depth)]
    pre[own_half] = jnp.dot(cand[...], wr[mp, :width], preferred_element_type=F32)
    wait_for(parts, plane - 1, sum_sem.at[1])
    state = jnp.sum(parts[...], axis=0).astype(BF16).astype(F32)

    own_interest = layer_norm(state).astype(BF16).astype(F32)
    told[...] = own_interest
    pieces[user] = own_interest

    for device in levels:
        pltpu.make_async_remote_copy(
            src_ref=told,
            dst_ref=pieces.at[user],
            send_sem=state_sem.at[0],
            recv_sem=state_sem.at[1],
            device_id=device,
            device_id_type=MESH,
        ).start()

    wait_for(pieces, height - 1, state_sem.at[1])
    mine = owner * owned + lax.broadcasted_iota(jnp.int32, (owned, line), 0)
    picker = jnp.where(slots[...] == mine, 1.0, 0.0).astype(BF16)
    known = pieces[...].reshape(line, width).astype(BF16)
    own_slots = jnp.dot(picker, known, preferred_element_type=F32)
    chosen[...] = own_slots
    interests[core * SIDE + y] = own_slots
    for b, n in ((2, 0), (2, 1), (1, 0), (3, 0), (1, 1), (3, 1), (0, 1)):
        pltpu.make_async_remote_copy(
            src_ref=chosen,
            dst_ref=interests.at[core * SIDE + y],
            send_sem=pick_sem.at[0],
            recv_sem=pick_sem.at[1],
            device_id=along_y(b, n),
            device_id_type=MESH,
        ).start()

    pltpu.make_async_copy(others, others, spread_sem.at[1]).wait()
    pre[1 - own_half] = jnp.dot(cand[...], wr[across, :width], preferred_element_type=F32)
    wait_for(interests, 2 * SIDE - 1, pick_sem.at[1])

    interest = jnp.concatenate(
        [interests[g] + interests[SIDE + g] for g in range(groups)], axis=0
    ).astype(BF16)
    half = (0.5 * width**-0.5) * dot_t(cand[...], interest)
    row = lax.div(lax.broadcasted_iota(jnp.int32, half.shape, 0), count)
    column = lax.rem(lax.broadcasted_iota(jnp.int32, half.shape, 1), owned)
    attn = jnp.where(row == column, silu_of_twice(half), 0.0)
    high = attn.astype(BF16)
    low = (attn - high.astype(F32)).astype(BF16)
    factors = jnp.concatenate([high, low, high], axis=1)
    terms = jnp.zeros_like(pre[0])
    for n in range(2):
        block = core + 2 * n
        mixed_in = jnp.dot(interest, wr[block, width:], preferred_element_type=F32)
        large = mixed_in.astype(BF16)
        small = (mixed_in - large.astype(F32)).astype(BF16)
        more = jnp.dot(
            factors, jnp.concatenate([large, large, small], axis=0), preferred_element_type=F32
        )
        half = 0.5 * (pre[n] + vectors[block, 0:1] + more)
        terms += silu_of_twice(half) * vectors[block, 1:2]
    high = terms.astype(BF16)
    low = (terms - high.astype(F32)).astype(BF16)
    ones = jnp.ones((16, terms.shape[1]), BF16)
    own_share = (dot_t(ones, high) + dot_t(ones, low))[0:1]
    share[...] = own_share
    shares[core] = own_share
    exchange = pltpu.make_async_remote_copy(
        src_ref=share,
        dst_ref=shares.at[core],
        send_sem=twin_sem.at[0],
        recv_sem=twin_sem.at[1],
        device_id={"mp": twin},
        device_id_type=MESH,
    )
    exchange.start()
    exchange.wait_recv()
    total = jnp.sum(shares[...], axis=0)
    for r in range(owned):
        scores[r : r + 1, :] = total[0:1, r * count : (r + 1) * count]

    for copy in kv_copies + q_copies:
        copy.wait_send()
    for n in range(HEADS):
        for m in range(2):
            pass_kv(n, m).wait_send()
        pass_q(n).wait_send()
        back_copy(n, 1).wait_send()
    for n in range(1, HEADS):
        back_copy(n, 0).wait_send()
    wait_for(parts, plane - 1, sum_sem.at[0])
    wait_for(pieces, height - 1, state_sem.at[0])
    wait_for(interests, 2 * SIDE - 1, pick_sem.at[0])
    exchange.wait_send()

    pltpu.make_async_copy(others, others, spread_sem.at[0]).wait()

    @pl.when(near == 0)
    def _():
        for copy in chain_copies(mp, over, over_send):
            copy.wait_send()

    @pl.when(near < ends_at)
    def _():
        for copy in chain_copies(across, onward, chain_send):
            copy.wait_send()


def solution(mesh):
    plane, owners, ranks = mesh.shape["tm"], mesh.shape["users"], mesh.shape["mp"]
    line = owners * ranks

    def shards(
        history,
        ln_gain,
        w_proj,
        w_out,
        pool_query,
        lengths,
        slots,
        cand_ids,
        item_table,
        w_rank,
        b_rank,
        w_score,
    ):
        _, events, width = history.shape
        head_size = width // HEADS
        groups = pool_query.shape[0]
        owned, count = cand_ids.shape
        cands = owned * count
        hidden = w_rank.shape[1]
        vmem = pl.BlockSpec(memory_space=pltpu.VMEM)
        smem = pl.BlockSpec(memory_space=pltpu.SMEM)
        hbm = pl.BlockSpec(memory_space=pltpu.HBM)
        dma = pltpu.SemaphoreType.DMA
        return pl.pallas_call(
            kernel,
            out_shape=(
                jax.ShapeDtypeStruct(history.shape, BF16),
                jax.ShapeDtypeStruct((owned, count), F32),
            ),
            in_specs=[smem] + [hbm] * 11,
            out_specs=(vmem, vmem),
            scratch_shapes=[
                pltpu.VMEM((events, width), BF16),
                pltpu.VMEM((1, width), F32),
                pltpu.VMEM(pool_query.shape, BF16),
                pltpu.VMEM((1, line), jnp.int32),
                pltpu.VMEM((owned, count), jnp.int32),
                pltpu.VMEM((1, hidden), F32),
                pltpu.VMEM((1, hidden), F32),
                pltpu.VMEM((4, width, width), BF16),
                pltpu.VMEM((width, width), BF16),
                pltpu.VMEM(item_table.shape, BF16),
                pltpu.VMEM((ranks, *w_rank.shape), BF16),
                pltpu.VMEM((events, width), BF16),
                pltpu.VMEM((events, width), BF16),
                pltpu.VMEM((HEADS, 3, events, head_size), BF16),
                pltpu.VMEM((2 * HEADS, 2, events, head_size), BF16),
                pltpu.VMEM((2 * HEADS, events, head_size), BF16),
                pltpu.VMEM((2 * HEADS * events, head_size), F32),
                pltpu.VMEM((2, HEADS, events, head_size), BF16),
                pltpu.VMEM((2, HEADS, events, head_size), BF16),
                pltpu.VMEM((3, events, events), F32),
                pltpu.VMEM((cands, width), BF16),
                pltpu.VMEM((2, cands, hidden), F32),
                pltpu.VMEM((groups, 1, width), F32),
                pltpu.VMEM((plane, 1, width), F32),
                pltpu.VMEM((1, width), F32),
                pltpu.VMEM((line, 1, width), F32),
                pltpu.VMEM((owned, width), F32),
                pltpu.VMEM((2 * SIDE, owned, width), F32),
                pltpu.VMEM((ranks, 2, hidden), F32),
                pltpu.VMEM((1, cands), F32),
                pltpu.VMEM((2, 1, cands), F32),
                dma((14,)),
                dma((HEADS, 2)),
                dma((HEADS, 2)),
                dma((HEADS,)),
                dma((HEADS,)),
                dma((3, HEADS)),
                dma((3, HEADS)),
                dma((2, HEADS)),
                dma((2, HEADS)),
                dma((2,)),
                dma((2,)),
                dma((2,)),
                dma((2,)),
                dma((2,)),
                dma((2,)),
                dma((2,)),
                dma((2,)),
            ],
            compiler_params=pltpu.CompilerParams(
                collective_id=0, has_side_effects=True, vmem_limit_bytes=VMEM_BYTES
            ),
            cost_estimate=pl.CostEstimate(
                flops=4_000_000_000, bytes_accessed=6_000_000, transcendentals=5_000_000
            ),
        )(
            lengths,
            history,
            ln_gain.reshape(1, -1),
            w_proj,
            w_out,
            pool_query,
            slots.reshape(1, -1),
            cand_ids,
            item_table,
            w_rank,
            b_rank.reshape(1, -1),
            w_score.reshape(1, -1),
        )

    placed = (
        P(("users", "mp"), "tm", None),
        P(),
        P(),
        P(),
        P(),
        P(("users", "mp")),
        P(),
        P("users", "tm"),
        P("users", None),
        P(None, "mp"),
        P("mp"),
        P("mp"),
    )
    return jax.shard_map(
        shards,
        mesh=mesh,
        in_specs=placed,
        out_specs=(P(("users", "mp"), "tm", None), P("users", "tm")),
        check_vma=False,
    )
```

```python
import jax
import jax.numpy as jnp
from jax import lax
from jax.experimental import pallas as pl
from jax.experimental.pallas import tpu as pltpu
from jax.sharding import PartitionSpec as P

HEADS = 4
SIDE = 4
EPS = 1e-05
VMEM_BYTES = 64 * 1024 * 1024
MESH = pl.DeviceIdType.MESH
STEPS = sorted(
    ((a, b) for a in range(SIDE) for b in range(SIDE) if a or b),
    key=lambda step: -sum(min(n, SIDE - n) for n in step),
)
F32 = jnp.float32
BF16 = jnp.bfloat16
ROWS_BY_ROWS = (((1,), (1,)), ((), ()))


def layer_norm(values):
    mean = jnp.mean(values, axis=-1, keepdims=True)
    centred = values - mean
    var = jnp.mean(centred * centred, axis=-1, keepdims=True)
    return centred * lax.rsqrt(var + EPS)


def silu_of_twice(half):
    return half + half * jnp.tanh(half)


def dot_t(a, b, **kw):
    return lax.dot_general(a, b, ROWS_BY_ROWS, preferred_element_type=F32, **kw)


def kernel(
    lengths,
    history,
    ln_gain_hbm,
    w_proj,
    w_out,
    pool_query_hbm,
    slots_hbm,
    cand_ids_hbm,
    item_table,
    w_rank,
    b_rank_hbm,
    w_score_hbm,
    layer_out,
    scores,
    hist,
    ln_gain,
    pool_query,
    slots,
    cand_ids,
    b_rank,
    w_score,
    wp,
    wo,
    table,
    wr,
    normed,
    gate,
    qkv,
    kv,
    qs,
    acc,
    back,
    att,
    masks,
    cand,
    pre,
    part,
    parts,
    told,
    pieces,
    chosen,
    interests,
    vectors,
    share,
    shares,
    load_sem,
    kv_send,
    kv_recv,
    q_send,
    q_recv,
    pass_send,
    pass_recv,
    back_send,
    back_recv,
    sum_sem,
    state_sem,
    pick_sem,
    over_send,
    chain_send,
    chain_recv,
    spread_sem,
    twin_sem,
):
    events, width = hist.shape
    head_size = width // HEADS
    plane, line, ranks = parts.shape[0], pieces.shape[0], wr.shape[0]
    t = lax.axis_index("tm")
    owner = lax.axis_index("users")
    mp = lax.axis_index("mp")
    user = owner * ranks + mp
    x, y = lax.div(t, SIDE), lax.rem(t, SIDE)
    core = lax.rem(mp, 2)

    def even(v):
        return v + 1 - 2 * lax.rem(v, 2)

    def odd(v):
        return SIDE - 1 - v

    def swap_y(v):
        return even(v) + core * (odd(v) - even(v))

    def ring_y(v):
        return odd(v) + core * (even(v) - odd(v))

    def head_of(a, b):
        first = lax.rem(lax.div(b + 1, 2), 2)
        return 2 * lax.div(a, 2) + first + core * (lax.div(b, 2) - first)

    def moved(a, b, rel):
        first, second = lax.rem(rel, 2), lax.div(rel, 2)
        return a + second * (odd(a) - a), b + first * (swap_y(b) - b)

    def in_plane(a, b):
        return {"tm": a * SIDE + b}

    head = head_of(x, y)

    depth = wr.shape[1] // SIDE
    last = line // ranks - 1
    twin = mp + 1 - 2 * core
    across = lax.rem(mp + 2, ranks)
    near = jnp.minimum(owner, last - owner)
    step_on = jnp.where(owner < near + 1, 1, -1)
    ends_at = last // 2

    def weights_of(whose):
        return wr.at[whose, pl.ds(pl.multiple_of(y * depth, depth), depth)]

    def chain_copies(whose, to, sems):
        return [
            pltpu.make_async_remote_copy(
                src_ref=ref,
                dst_ref=ref,
                send_sem=sems.at[n],
                recv_sem=chain_recv.at[n],
                device_id=to,
                device_id_type=MESH,
            )
            for n, ref in enumerate((weights_of(whose), vectors.at[whose]))
        ]

    over = {"users": last - owner, "mp": across}
    onward = {"users": owner + step_on}

    def relay(j):
        @pl.when(near == j)
        def _():
            for copy in chain_copies(across, onward, chain_send):
                copy.wait_recv()
                if j < ends_at:
                    copy.start()

    loads = [pltpu.make_async_copy(history.at[0], hist, load_sem.at[0])]
    for n, block in enumerate((3, 1, 2, 0)):
        cols = pl.ds(block * width, width)
        loads.append(pltpu.make_async_copy(w_proj.at[:, cols], wp.at[n], load_sem.at[n + 1]))
    rest = (
        (ln_gain_hbm, ln_gain),
        (pool_query_hbm, pool_query),
        (slots_hbm, slots),
        (cand_ids_hbm, cand_ids),
        (b_rank_hbm, b_rank),
        (w_score_hbm, w_score),
        (w_out, wo),
        (item_table, table),
        (w_rank, wr.at[mp]),
    )
    for n, (src, dst) in enumerate(rest):
        loads.append(pltpu.make_async_copy(src, dst, load_sem.at[5 + n]))
    loads[0].start()
    loads[5].start()
    for load in loads[1:5] + loads[6:]:
        load.start()

    pieces[...] = jnp.zeros_like(pieces)

    barrier = pltpu.get_barrier_semaphore()
    height = line // 2
    low = height // 2
    level = lax.div(mp, 2) * low + owner

    levels = []
    for k in range(height - 1):
        chip = lax.rem(level + low + (k + 1) // 2 * (1 - 2 * (k % 2)), height)
        levels.append({"users": lax.rem(chip, low), "mp": 2 * lax.div(chip, low) + core})

    def along(a, b):
        return {"tm": lax.rem(x + a, SIDE) * SIDE + lax.rem(y + b, SIDE)}

    def along_y(b, other):
        return {"tm": x * SIDE + lax.rem(y + b, SIDE), "mp": mp + other * (1 - 2 * core)}

    greeted = [along(a, b) for a, b in STEPS] + [along_y(b, 1) for b in range(SIDE)]
    greeted = levels + greeted
    for device in greeted:
        pl.semaphore_signal(barrier, inc=1, device_id=device, device_id_type=MESH)

    first_pos = t * events
    length = lengths[0]
    pos = first_pos + lax.broadcasted_iota(jnp.int32, (events, 1), 0)
    live = pos < length
    loads[0].wait()
    loads[5].wait()
    normed[...] = (layer_norm(hist[...].astype(F32)) * ln_gain[...]).astype(BF16)

    def project(n):
        loads[n + 1].wait()
        half = 0.5 * jnp.dot(normed[...], wp[n], preferred_element_type=F32)
        return silu_of_twice(half)

    keys = project(0).astype(BF16)
    for h in range(HEADS):
        qkv[h, 0] = keys[:, h * head_size : (h + 1) * head_size]
    values = jnp.where(live, project(1), 0.0).astype(BF16)
    for h in range(HEADS):
        qkv[h, 1] = values[:, h * head_size : (h + 1) * head_size]

    pl.semaphore_wait(barrier, len(greeted))

    kv_copies, q_copies = [], []
    for rel in (3, 2, 1):
        a, b = moved(x, y, rel)
        for n in range(2):
            copy = pltpu.make_async_remote_copy(
                src_ref=qkv.at[head_of(a, b), n],
                dst_ref=kv.at[rel, n],
                send_sem=kv_send.at[rel, n],
                recv_sem=kv_recv.at[rel, n],
                device_id=in_plane(a, b),
                device_id_type=MESH,
            )
            copy.start()
            kv_copies.append(copy)

    query = (project(2) * (0.5 * head_size**-0.5)).astype(BF16)
    for h in range(HEADS):
        qkv[h, 2] = query[:, h * head_size : (h + 1) * head_size]
    for rel in (3, 2, 1):
        a, b = moved(x, y, rel)
        copy = pltpu.make_async_remote_copy(
            src_ref=qkv.at[head_of(a, b), 2],
            dst_ref=qs.at[rel],
            send_sem=q_send.at[rel],
            recv_sem=q_recv.at[rel],
            device_id=in_plane(a, b),
            device_id_type=MESH,
        )
        copy.start()
        q_copies.append(copy)
    for load in loads[9:11] + loads[13:]:
        load.wait()
    vectors[mp, 0:1] = b_rank[...]
    vectors[mp, 1:2] = w_score[...]

    @pl.when(near == 0)
    def _():
        for copy in chain_copies(mp, over, over_send):
            copy.start()

    kv[0] = qkv[head, pl.ds(0, 2)]
    qs[0] = qkv[head, 2]

    x_near, y_near = even(x), ring_y(y)

    def pass_kv(n, m):
        return pltpu.make_async_remote_copy(
            src_ref=kv.at[n, m],
            dst_ref=kv.at[HEADS + n, m],
            send_sem=pass_send.at[m, n],
            recv_sem=pass_recv.at[m, n],
            device_id=in_plane(x_near, y),
            device_id_type=MESH,
        )

    def pass_q(n):
        return pltpu.make_async_remote_copy(
            src_ref=qs.at[n],
            dst_ref=qs.at[HEADS + n],
            send_sem=pass_send.at[2, n],
            recv_sem=pass_recv.at[2, n],
            device_id=in_plane(x, y_near),
            device_id_type=MESH,
        )

    def back_copy(n, which):
        a, b = moved(x, y_near if which else y, n)
        return pltpu.make_async_remote_copy(
            src_ref=back.at[which, n],
            dst_ref=att.at[which, head],
            send_sem=back_send.at[which, n],
            recv_sem=back_recv.at[which, n],
            device_id=in_plane(a, b),
            device_id_type=MESH,
        )

    pass_q(0).start()
    for m in range(2):
        pass_kv(0, m).start()

    acc[...] = jnp.zeros_like(acc)

    for r in range(1, HEADS):
        for m in range(2):
            pltpu.make_async_copy(kv.at[r, m], kv.at[r, m], kv_recv.at[r, m]).wait()
            pass_kv(r, m).start()

    pairs = 2 * events
    behind = lax.broadcasted_iota(jnp.int32, (events, events), 0) >= lax.broadcasted_iota(
        jnp.int32, (events, events), 1
    )
    masks[0] = jnp.zeros((events, events), F32)
    masks[1] = jnp.where(behind, 1.0, 0.0)
    masks[2] = jnp.ones((events, events), F32)

    def rows_of(which, pair):
        return pl.ds(pl.multiple_of((2 * which + pair) * pairs, pairs), pairs)

    def attend(q_set, q_pair, k_set, k_pair, masked):
        q_first, k_first = HEADS * q_set + 2 * q_pair, HEADS * k_set + 2 * k_pair
        query = qs[pl.ds(q_first, 2)].reshape(pairs, head_size)
        half = jnp.concatenate(
            [dot_t(query, kv[k_first + n, 0]) for n in range(2)], axis=1
        )
        if masked:
            q_y = y_near if q_set else y
            half = jnp.concatenate(
                [
                    jnp.concatenate(
                        [
                            half[a * events : (a + 1) * events, b * events : (b + 1) * events]
                            * masks[1 + jnp.clip(q_row - k_row, -1, 1)]
                            for b, k_row in enumerate((y, swap_y(y)))
                        ],
                        axis=1,
                    )
                    for a, q_row in enumerate((q_y, swap_y(q_y)))
                ],
                axis=0,
            )
        weights = silu_of_twice(half).astype(BF16)
        value = jnp.concatenate([kv[k_first + n, 1] for n in range(2)], axis=0)
        acc[rows_of(q_set, q_pair)] += jnp.dot(weights, value, preferred_element_type=F32)

    late = jnp.where(x < SIDE // 2, 1, 0)
    early = 1 - late
    outer = jnp.logical_or(x == 0, x == SIDE - 1)

    def attend_own(q_set):
        for pair in range(2):
            attend(q_set, pair, 0, pair, True)
        attend(q_set, late, 0, early, False)

    def attend_near(q_set, n):
        q_pair = late if n else jnp.where(outer, late, early)
        k_pair = jnp.where(outer, n, jnp.where(x == 1, 0, 1))
        attend(q_set, q_pair, 1, k_pair, False)

    for n in range(1, HEADS):
        pltpu.make_async_copy(qs.at[n], qs.at[n], q_recv.at[n]).wait()
        pass_q(n).start()
    attend_own(0)
    relay(0)
    for n in range(HEADS):
        pass_q(n).wait_recv()
    attend(1, 0, 0, 0, True)
    attend(1, 1, 0, 1, True)
    attend(1, late, 0, early, False)
    for n in range(HEADS):
        for m in range(2):
            pass_kv(n, m).wait_recv()
    def send_back(which, pair):
        for m in (1, 0):
            n = 2 * pair + m
            rows = pl.ds(pl.multiple_of((HEADS * which + n) * events, events), events)
            summed = acc[rows].astype(BF16)
            away = n >= 1 - which

            @pl.when(away)
            def _():
                back[which, n] = summed
                back_copy(n, which).start()

            @pl.when(jnp.logical_not(away))
            def _():
                att[which, head] = summed

    attend_near(1, 0)
    send_back(1, early)
    attend_near(1, 1)
    send_back(1, late)
    relay(1)
    attend_near(0, 0)
    send_back(0, early)
    attend_near(0, 1)
    send_back(0, late)
    relay(2)
    gate[...] = project(3).astype(BF16)

    owned, count = cand_ids.shape
    pool = table.shape[0]
    for load in loads[6:9] + loads[11:13]:
        load.wait()

    @pl.loop(0, owned)
    def _(r):
        eye = lax.broadcasted_iota(jnp.int32, (count, count), 0) == lax.broadcasted_iota(
            jnp.int32, (count, count), 1
        )
        item = lax.broadcasted_iota(jnp.int32, (count, pool), 1).astype(F32)
        ids = cand_ids[pl.ds(r, 1), :].astype(F32)
        column = jnp.sum(jnp.where(eye, ids, 0.0), axis=1, keepdims=True)
        onehot = jnp.where(item == column, 1.0, 0.0).astype(BF16)
        cand[pl.ds(r * count, count)] = jnp.dot(
            onehot, table[...], preferred_element_type=F32
        ).astype(BF16)

    for n in range(HEADS):
        back_copy(n, 1).wait_recv()
    for n in range(1, HEADS):
        back_copy(n, 0).wait_recv()

    own_half = lax.div(mp, 2)
    attended = jnp.concatenate(
        [att[0, h].astype(F32) + att[1, h].astype(F32) for h in range(HEADS)], axis=1
    )
    mixed = (layer_norm(attended) * gate[...].astype(F32)).astype(BF16)
    projected = jnp.dot(mixed, wo[...], preferred_element_type=F32)
    out = (hist[...].astype(F32) + projected).astype(BF16)
    layer_out[0] = out
    groups = pool_query.shape[0]
    half = 0.5 * dot_t(pool_query[...], out)
    lane = first_pos + lax.broadcasted_iota(jnp.int32, half.shape, 1)
    pool_w = jnp.where(lane < length, silu_of_twice(half), 0.0).astype(BF16)
    sums = jnp.dot(pool_w, out, preferred_element_type=F32)

    for g in range(groups):
        part[g] = sums[g : g + 1]
    for a, b in STEPS:
        pltpu.make_async_remote_copy(
            src_ref=part.at[lax.rem(y + b, SIDE)],
            dst_ref=parts.at[t],
            send_sem=sum_sem.at[0],
            recv_sem=sum_sem.at[1],
            device_id=along(a, b),
            device_id_type=MESH,
        ).start()

    def wait_for(buffer, many, sem):
        some = buffer.at[pl.ds(0, many)]
        pltpu.make_async_copy(some, some, sem).wait()

    parts[t] = part[y]
    relay(3)
    quarter = weights_of(across)
    for b in (2, 1, 3):
        pltpu.make_async_remote_copy(
            src_ref=quarter,
            dst_ref=quarter,
            send_sem=spread_sem.at[0],
            recv_sem=spread_sem.at[1],
            device_id=along(0, b),
            device_id_type=MESH,
        ).start()
    others = wr.at[across, pl.ds(0, (SIDE - 1) * depth)]
    pre[own_half] = jnp.dot(cand[...], wr[mp, :width], preferred_element_type=F32)
    wait_for(parts, plane - 1, sum_sem.at[1])
    state = jnp.sum(parts[...], axis=0).astype(BF16).astype(F32)

    own_interest = layer_norm(state).astype(BF16).astype(F32)
    told[...] = own_interest
    pieces[user] = own_interest

    for device in levels:
        pltpu.make_async_remote_copy(
            src_ref=told,
            dst_ref=pieces.at[user],
            send_sem=state_sem.at[0],
            recv_sem=state_sem.at[1],
            device_id=device,
            device_id_type=MESH,
        ).start()

    wait_for(pieces, height - 1, state_sem.at[1])
    mine = owner * owned + lax.broadcasted_iota(jnp.int32, (owned, line), 0)
    picker = jnp.where(slots[...] == mine, 1.0, 0.0).astype(BF16)
    known = pieces[...].reshape(line, width).astype(BF16)
    own_slots = jnp.dot(picker, known, preferred_element_type=F32)
    chosen[...] = own_slots
    interests[core * SIDE + y] = own_slots
    for b, n in ((2, 0), (2, 1), (1, 0), (3, 0), (1, 1), (3, 1), (0, 1)):
        pltpu.make_async_remote_copy(
            src_ref=chosen,
            dst_ref=interests.at[core * SIDE + y],
            send_sem=pick_sem.at[0],
            recv_sem=pick_sem.at[1],
            device_id=along_y(b, n),
            device_id_type=MESH,
        ).start()

    pltpu.make_async_copy(others, others, spread_sem.at[1]).wait()
    pre[1 - own_half] = jnp.dot(cand[...], wr[across, :width], preferred_element_type=F32)
    wait_for(interests, 2 * SIDE - 1, pick_sem.at[1])

    interest = jnp.concatenate(
        [interests[g] + interests[SIDE + g] for g in range(groups)], axis=0
    ).astype(BF16)
    half = (0.5 * width**-0.5) * dot_t(cand[...], interest)
    row = lax.div(lax.broadcasted_iota(jnp.int32, half.shape, 0), count)
    column = lax.rem(lax.broadcasted_iota(jnp.int32, half.shape, 1), owned)
    attn = jnp.where(row == column, silu_of_twice(half), 0.0)
    high = attn.astype(BF16)
    low = (attn - high.astype(F32)).astype(BF16)
    factors = jnp.concatenate([high, low, high], axis=1)
    terms = jnp.zeros_like(pre[0])
    for n in range(2):
        block = core + 2 * n
        mixed_in = jnp.dot(interest, wr[block, width:], preferred_element_type=F32)
        large = mixed_in.astype(BF16)
        small = (mixed_in - large.astype(F32)).astype(BF16)
        more = jnp.dot(
            factors, jnp.concatenate([large, large, small], axis=0), preferred_element_type=F32
        )
        half = 0.5 * (pre[n] + vectors[block, 0:1] + more)
        terms += silu_of_twice(half) * vectors[block, 1:2]
    high = terms.astype(BF16)
    low = (terms - high.astype(F32)).astype(BF16)
    ones = jnp.ones((16, terms.shape[1]), BF16)
    own_share = (dot_t(ones, high) + dot_t(ones, low))[0:1]
    share[...] = own_share
    shares[core] = own_share
    exchange = pltpu.make_async_remote_copy(
        src_ref=share,
        dst_ref=shares.at[core],
        send_sem=twin_sem.at[0],
        recv_sem=twin_sem.at[1],
        device_id={"mp": twin},
        device_id_type=MESH,
    )
    exchange.start()
    exchange.wait_recv()
    total = jnp.sum(shares[...], axis=0)
    for r in range(owned):
        scores[r : r + 1, :] = total[0:1, r * count : (r + 1) * count]

    for copy in kv_copies + q_copies:
        copy.wait_send()
    for n in range(HEADS):
        for m in range(2):
            pass_kv(n, m).wait_send()
        pass_q(n).wait_send()
        back_copy(n, 1).wait_send()
    for n in range(1, HEADS):
        back_copy(n, 0).wait_send()
    wait_for(parts, plane - 1, sum_sem.at[0])
    wait_for(pieces, height - 1, state_sem.at[0])
    wait_for(interests, 2 * SIDE - 1, pick_sem.at[0])
    exchange.wait_send()

    pltpu.make_async_copy(others, others, spread_sem.at[0]).wait()

    @pl.when(near == 0)
    def _():
        for copy in chain_copies(mp, over, over_send):
            copy.wait_send()

    @pl.when(near < ends_at)
    def _():
        for copy in chain_copies(across, onward, chain_send):
            copy.wait_send()


def solution(mesh):
    plane, owners, ranks = mesh.shape["tm"], mesh.shape["users"], mesh.shape["mp"]
    line = owners * ranks

    def shards(
        history,
        ln_gain,
        w_proj,
        w_out,
        pool_query,
        lengths,
        slots,
        cand_ids,
        item_table,
        w_rank,
        b_rank,
        w_score,
    ):
        _, events, width = history.shape
        head_size = width // HEADS
        groups = pool_query.shape[0]
        owned, count = cand_ids.shape
        cands = owned * count
        hidden = w_rank.shape[1]
        vmem = pl.BlockSpec(memory_space=pltpu.VMEM)
        smem = pl.BlockSpec(memory_space=pltpu.SMEM)
        hbm = pl.BlockSpec(memory_space=pltpu.HBM)
        dma = pltpu.SemaphoreType.DMA
        return pl.pallas_call(
            kernel,
            out_shape=(
                jax.ShapeDtypeStruct(history.shape, BF16),
                jax.ShapeDtypeStruct((owned, count), F32),
            ),
            in_specs=[smem] + [hbm] * 11,
            out_specs=(vmem, vmem),
            scratch_shapes=[
                pltpu.VMEM((events, width), BF16),
                pltpu.VMEM((1, width), F32),
                pltpu.VMEM(pool_query.shape, BF16),
                pltpu.VMEM((1, line), jnp.int32),
                pltpu.VMEM((owned, count), jnp.int32),
                pltpu.VMEM((1, hidden), F32),
                pltpu.VMEM((1, hidden), F32),
                pltpu.VMEM((4, width, width), BF16),
                pltpu.VMEM((width, width), BF16),
                pltpu.VMEM(item_table.shape, BF16),
                pltpu.VMEM((ranks, *w_rank.shape), BF16),
                pltpu.VMEM((events, width), BF16),
                pltpu.VMEM((events, width), BF16),
                pltpu.VMEM((HEADS, 3, events, head_size), BF16),
                pltpu.VMEM((2 * HEADS, 2, events, head_size), BF16),
                pltpu.VMEM((2 * HEADS, events, head_size), BF16),
                pltpu.VMEM((2 * HEADS * events, head_size), F32),
                pltpu.VMEM((2, HEADS, events, head_size), BF16),
                pltpu.VMEM((2, HEADS, events, head_size), BF16),
                pltpu.VMEM((3, events, events), F32),
                pltpu.VMEM((cands, width), BF16),
                pltpu.VMEM((2, cands, hidden), F32),
                pltpu.VMEM((groups, 1, width), F32),
                pltpu.VMEM((plane, 1, width), F32),
                pltpu.VMEM((1, width), F32),
                pltpu.VMEM((line, 1, width), F32),
                pltpu.VMEM((owned, width), F32),
                pltpu.VMEM((2 * SIDE, owned, width), F32),
                pltpu.VMEM((ranks, 2, hidden), F32),
                pltpu.VMEM((1, cands), F32),
                pltpu.VMEM((2, 1, cands), F32),
                dma((14,)),
                dma((HEADS, 2)),
                dma((HEADS, 2)),
                dma((HEADS,)),
                dma((HEADS,)),
                dma((3, HEADS)),
                dma((3, HEADS)),
                dma((2, HEADS)),
                dma((2, HEADS)),
                dma((2,)),
                dma((2,)),
                dma((2,)),
                dma((2,)),
                dma((2,)),
                dma((2,)),
                dma((2,)),
                dma((2,)),
            ],
            compiler_params=pltpu.CompilerParams(
                collective_id=0, has_side_effects=True, vmem_limit_bytes=VMEM_BYTES
            ),
            cost_estimate=pl.CostEstimate(
                flops=4_000_000_000, bytes_accessed=6_000_000, transcendentals=5_000_000
            ),
        )(
            lengths,
            history,
            ln_gain.reshape(1, -1),
            w_proj,
            w_out,
            pool_query,
            slots.reshape(1, -1),
            cand_ids,
            item_table,
            w_rank,
            b_rank.reshape(1, -1),
            w_score.reshape(1, -1),
        )

    placed = (
        P(("users", "mp"), "tm", None),
        P(),
        P(),
        P(),
        P(),
        P(("users", "mp")),
        P(),
        P("users", "tm"),
        P("users", None),
        P(None, "mp"),
        P("mp"),
        P("mp"),
    )
    return jax.shard_map(
        shards,
        mesh=mesh,
        in_specs=placed,
        out_specs=(P(("users", "mp"), "tm", None), P("users", "tm")),
        check_vma=False,
    )
```

```python
import jax
import jax.numpy as jnp
from jax import lax
from jax.experimental import pallas as pl
from jax.experimental.pallas import tpu as pltpu
from jax.sharding import PartitionSpec as P

HEADS = 4
SIDE = 4
EPS = 1e-05
VMEM_BYTES = 64 * 1024 * 1024
MESH = pl.DeviceIdType.MESH
STEPS = sorted(
    ((a, b) for a in range(SIDE) for b in range(SIDE) if a or b),
    key=lambda step: -sum(min(n, SIDE - n) for n in step),
)
F32 = jnp.float32
BF16 = jnp.bfloat16
ROWS_BY_ROWS = (((1,), (1,)), ((), ()))


def layer_norm(values):
    mean = jnp.mean(values, axis=-1, keepdims=True)
    centred = values - mean
    var = jnp.mean(centred * centred, axis=-1, keepdims=True)
    return centred * lax.rsqrt(var + EPS)


def silu_of_twice(half):
    return half + half * jnp.tanh(half)


def dot_t(a, b, **kw):
    return lax.dot_general(a, b, ROWS_BY_ROWS, preferred_element_type=F32, **kw)


def kernel(
    lengths,
    history,
    ln_gain_hbm,
    w_proj,
    w_out,
    pool_query_hbm,
    slots_hbm,
    cand_ids_hbm,
    item_table,
    w_rank,
    b_rank_hbm,
    w_score_hbm,
    layer_out,
    scores,
    hist,
    ln_gain,
    pool_query,
    slots,
    cand_ids,
    b_rank,
    w_score,
    wp,
    wo,
    table,
    wr,
    normed,
    gate,
    qkv,
    kv,
    qs,
    acc,
    back,
    att,
    masks,
    cand,
    pre,
    part,
    parts,
    told,
    pieces,
    chosen,
    interests,
    vectors,
    share,
    shares,
    load_sem,
    kv_send,
    kv_recv,
    q_send,
    q_recv,
    pass_send,
    pass_recv,
    back_send,
    back_recv,
    sum_sem,
    state_sem,
    pick_sem,
    over_send,
    chain_send,
    chain_recv,
    spread_sem,
    twin_sem,
):
    events, width = hist.shape
    head_size = width // HEADS
    plane, line, ranks = parts.shape[0], pieces.shape[0], wr.shape[0]
    t = lax.axis_index("tm")
    owner = lax.axis_index("users")
    mp = lax.axis_index("mp")
    user = owner * ranks + mp
    x, y = lax.div(t, SIDE), lax.rem(t, SIDE)
    core = lax.rem(mp, 2)

    def even(v):
        return v + 1 - 2 * lax.rem(v, 2)

    def odd(v):
        return SIDE - 1 - v

    def swap_y(v):
        return even(v) + core * (odd(v) - even(v))

    def ring_y(v):
        return odd(v) + core * (even(v) - odd(v))

    def head_of(a, b):
        first = lax.rem(lax.div(b + 1, 2), 2)
        return 2 * lax.div(a, 2) + first + core * (lax.div(b, 2) - first)

    def moved(a, b, rel):
        first, second = lax.rem(rel, 2), lax.div(rel, 2)
        return a + second * (odd(a) - a), b + first * (swap_y(b) - b)

    def in_plane(a, b):
        return {"tm": a * SIDE + b}

    head = head_of(x, y)

    depth = wr.shape[1] // SIDE
    last = line // ranks - 1
    twin = mp + 1 - 2 * core
    across = lax.rem(mp + 2, ranks)
    near = jnp.minimum(owner, last - owner)
    step_on = jnp.where(owner < near + 1, 1, -1)
    ends_at = last // 2

    def weights_of(whose):
        return wr.at[whose, pl.ds(pl.multiple_of(y * depth, depth), depth)]

    def chain_copies(whose, to, sems):
        return [
            pltpu.make_async_remote_copy(
                src_ref=ref,
                dst_ref=ref,
                send_sem=sems.at[n],
                recv_sem=chain_recv.at[n],
                device_id=to,
                device_id_type=MESH,
            )
            for n, ref in enumerate((weights_of(whose), vectors.at[whose]))
        ]

    over = {"users": last - owner, "mp": across}
    onward = {"users": owner + step_on}

    def relay(j):
        @pl.when(near == j)
        def _():
            for copy in chain_copies(across, onward, chain_send):
                copy.wait_recv()
                if j < ends_at:
                    copy.start()

    loads = [pltpu.make_async_copy(history.at[0], hist, load_sem.at[0])]
    for n, block in enumerate((3, 1, 2, 0)):
        cols = pl.ds(block * width, width)
        loads.append(pltpu.make_async_copy(w_proj.at[:, cols], wp.at[n], load_sem.at[n + 1]))
    rest = (
        (ln_gain_hbm, ln_gain),
        (pool_query_hbm, pool_query),
        (slots_hbm, slots),
        (cand_ids_hbm, cand_ids),
        (b_rank_hbm, b_rank),
        (w_score_hbm, w_score),
        (w_out, wo),
        (item_table, table),
        (w_rank, wr.at[mp]),
    )
    for n, (src, dst) in enumerate(rest):
        loads.append(pltpu.make_async_copy(src, dst, load_sem.at[5 + n]))
    loads[0].start()
    loads[5].start()
    for load in loads[1:5] + loads[6:]:
        load.start()

    pieces[...] = jnp.zeros_like(pieces)

    barrier = pltpu.get_barrier_semaphore()
    height = line // 2
    low = height // 2
    level = lax.div(mp, 2) * low + owner

    levels = []
    for k in range(height - 1):
        chip = lax.rem(level + low + (k + 1) // 2 * (1 - 2 * (k % 2)), height)
        levels.append({"users": lax.rem(chip, low), "mp": 2 * lax.div(chip, low) + core})

    def along(a, b):
        return {"tm": lax.rem(x + a, SIDE) * SIDE + lax.rem(y + b, SIDE)}

    def along_y(b, other):
        return {"tm": x * SIDE + lax.rem(y + b, SIDE), "mp": mp + other * (1 - 2 * core)}

    greeted = [along(a, b) for a, b in STEPS] + [along_y(b, 1) for b in range(SIDE)]
    greeted += levels
    for device in greeted:
        pl.semaphore_signal(barrier, inc=1, device_id=device, device_id_type=MESH)

    first_pos = t * events
    length = lengths[0]
    pos = first_pos + lax.broadcasted_iota(jnp.int32, (events, 1), 0)
    live = pos < length
    loads[0].wait()
    loads[5].wait()
    normed[...] = (layer_norm(hist[...].astype(F32)) * ln_gain[...]).astype(BF16)

    def project(n):
        loads[n + 1].wait()
        half = 0.5 * jnp.dot(normed[...], wp[n], preferred_element_type=F32)
        return silu_of_twice(half)

    keys = project(0).astype(BF16)
    for h in range(HEADS):
        qkv[h, 0] = keys[:, h * head_size : (h + 1) * head_size]
    values = jnp.where(live, project(1), 0.0).astype(BF16)
    for h in range(HEADS):
        qkv[h, 1] = values[:, h * head_size : (h + 1) * head_size]

    pl.semaphore_wait(barrier, len(greeted))

    kv_copies, q_copies = [], []
    for rel in (3, 2, 1):
        a, b = moved(x, y, rel)
        for n in range(2):
            copy = pltpu.make_async_remote_copy(
                src_ref=qkv.at[head_of(a, b), n],
                dst_ref=kv.at[rel, n],
                send_sem=kv_send.at[rel, n],
                recv_sem=kv_recv.at[rel, n],
                device_id=in_plane(a, b),
                device_id_type=MESH,
            )
            copy.start()
            kv_copies.append(copy)

    query = (project(2) * (0.5 * head_size**-0.5)).astype(BF16)
    for h in range(HEADS):
        qkv[h, 2] = query[:, h * head_size : (h + 1) * head_size]
    for rel in (3, 2, 1):
        a, b = moved(x, y, rel)
        copy = pltpu.make_async_remote_copy(
            src_ref=qkv.at[head_of(a, b), 2],
            dst_ref=qs.at[rel],
            send_sem=q_send.at[rel],
            recv_sem=q_recv.at[rel],
            device_id=in_plane(a, b),
            device_id_type=MESH,
        )
        copy.start()
        q_copies.append(copy)
    for load in loads[9:11] + loads[13:]:
        load.wait()
    vectors[mp, 0:1] = b_rank[...]
    vectors[mp, 1:2] = w_score[...]

    @pl.when(near == 0)
    def _():
        for copy in chain_copies(mp, over, over_send):
            copy.start()

    kv[0] = qkv[head, pl.ds(0, 2)]
    qs[0] = qkv[head, 2]

    x_near, y_near = even(x), ring_y(y)

    def pass_kv(n, m):
        return pltpu.make_async_remote_copy(
            src_ref=kv.at[n, m],
            dst_ref=kv.at[HEADS + n, m],
            send_sem=pass_send.at[m, n],
            recv_sem=pass_recv.at[m, n],
            device_id=in_plane(x_near, y),
            device_id_type=MESH,
        )

    def pass_q(n):
        return pltpu.make_async_remote_copy(
            src_ref=qs.at[n],
            dst_ref=qs.at[HEADS + n],
            send_sem=pass_send.at[2, n],
            recv_sem=pass_recv.at[2, n],
            device_id=in_plane(x, y_near),
            device_id_type=MESH,
        )

    def back_copy(n, which):
        a, b = moved(x, y_near if which else y, n)
        return pltpu.make_async_remote_copy(
            src_ref=back.at[which, n],
            dst_ref=att.at[which, head],
            send_sem=back_send.at[which, n],
            recv_sem=back_recv.at[which, n],
            device_id=in_plane(a, b),
            device_id_type=MESH,
        )

    pass_q(0).start()
    for m in range(2):
        pass_kv(0, m).start()

    gate[...] = project(3).astype(BF16)
    acc[...] = jnp.zeros_like(acc)

    owned, count = cand_ids.shape
    pool = table.shape[0]
    for load in loads[6:9] + loads[11:13]:
        load.wait()

    @pl.loop(0, owned)
    def _(r):
        @pl.when(r > 0)
        def _():
            for m in range(2):
                pltpu.make_async_copy(kv.at[r, m], kv.at[r, m], kv_recv.at[r, m]).wait()
                pass_kv(r, m).start()

        eye = lax.broadcasted_iota(jnp.int32, (count, count), 0) == lax.broadcasted_iota(
            jnp.int32, (count, count), 1
        )
        item = lax.broadcasted_iota(jnp.int32, (count, pool), 1).astype(F32)
        ids = cand_ids[pl.ds(r, 1), :].astype(F32)
        column = jnp.sum(jnp.where(eye, ids, 0.0), axis=1, keepdims=True)
        onehot = jnp.where(item == column, 1.0, 0.0).astype(BF16)
        cand[pl.ds(r * count, count)] = jnp.dot(
            onehot, table[...], preferred_element_type=F32
        ).astype(BF16)

    pairs = 2 * events
    behind = lax.broadcasted_iota(jnp.int32, (events, events), 0) >= lax.broadcasted_iota(
        jnp.int32, (events, events), 1
    )
    masks[0] = jnp.zeros((events, events), F32)
    masks[1] = jnp.where(behind, 1.0, 0.0)
    masks[2] = jnp.ones((events, events), F32)

    def rows_of(which, pair):
        return pl.ds(pl.multiple_of((2 * which + pair) * pairs, pairs), pairs)

    def attend(q_set, q_pair, k_set, k_pair, masked):
        q_first, k_first = HEADS * q_set + 2 * q_pair, HEADS * k_set + 2 * k_pair
        query = qs[pl.ds(q_first, 2)].reshape(pairs, head_size)
        half = jnp.concatenate(
            [dot_t(query, kv[k_first + n, 0]) for n in range(2)], axis=1
        )
        if masked:
            q_y = y_near if q_set else y
            half = jnp.concatenate(
                [
                    jnp.concatenate(
                        [
                            half[a * events : (a + 1) * events, b * events : (b + 1) * events]
                            * masks[1 + jnp.clip(q_row - k_row, -1, 1)]
                            for b, k_row in enumerate((y, swap_y(y)))
                        ],
                        axis=1,
                    )
                    for a, q_row in enumerate((q_y, swap_y(q_y)))
                ],
                axis=0,
            )
        weights = silu_of_twice(half).astype(BF16)
        value = jnp.concatenate([kv[k_first + n, 1] for n in range(2)], axis=0)
        acc[rows_of(q_set, q_pair)] += jnp.dot(weights, value, preferred_element_type=F32)

    late = jnp.where(x < SIDE // 2, 1, 0)
    early = 1 - late
    outer = jnp.logical_or(x == 0, x == SIDE - 1)

    def attend_own(q_set):
        for pair in range(2):
            attend(q_set, pair, 0, pair, True)
        attend(q_set, late, 0, early, False)

    def attend_near(q_set, n):
        q_pair = late if n else jnp.where(outer, late, early)
        k_pair = jnp.where(outer, n, jnp.where(x == 1, 0, 1))
        attend(q_set, q_pair, 1, k_pair, False)

    for n in range(1, HEADS):
        pltpu.make_async_copy(qs.at[n], qs.at[n], q_recv.at[n]).wait()
        pass_q(n).start()
    attend_own(0)
    relay(0)
    for n in range(HEADS):
        pass_q(n).wait_recv()
    attend(1, 0, 0, 0, True)
    attend(1, 1, 0, 1, True)
    attend(1, late, 0, early, False)
    for n in range(HEADS):
        for m in range(2):
            pass_kv(n, m).wait_recv()
    def send_back(which, pair):
        for m in (1, 0):
            n = 2 * pair + m
            rows = pl.ds(pl.multiple_of((HEADS * which + n) * events, events), events)
            summed = acc[rows].astype(BF16)
            away = n >= 1 - which

            @pl.when(away)
            def _():
                back[which, n] = summed
                back_copy(n, which).start()

            @pl.when(jnp.logical_not(away))
            def _():
                att[which, head] = summed

    attend_near(1, 0)
    send_back(1, early)
    attend_near(1, 1)
    send_back(1, late)
    relay(1)
    attend_near(0, 0)
    send_back(0, early)
    attend_near(0, 1)
    send_back(0, late)
    relay(2)
    for n in range(HEADS):
        back_copy(n, 1).wait_recv()
    for n in range(1, HEADS):
        back_copy(n, 0).wait_recv()

    own_half = lax.div(mp, 2)
    attended = jnp.concatenate(
        [att[0, h].astype(F32) + att[1, h].astype(F32) for h in range(HEADS)], axis=1
    )
    mixed = (layer_norm(attended) * gate[...].astype(F32)).astype(BF16)
    projected = jnp.dot(mixed, wo[...], preferred_element_type=F32)
    out = (hist[...].astype(F32) + projected).astype(BF16)
    layer_out[0] = out
    groups = pool_query.shape[0]
    half = 0.5 * dot_t(pool_query[...], out)
    lane = first_pos + lax.broadcasted_iota(jnp.int32, half.shape, 1)
    pool_w = jnp.where(lane < length, silu_of_twice(half), 0.0).astype(BF16)
    sums = jnp.dot(pool_w, out, preferred_element_type=F32)

    for g in range(groups):
        part[g] = sums[g : g + 1]
    for a, b in STEPS:
        pltpu.make_async_remote_copy(
            src_ref=part.at[lax.rem(y + b, SIDE)],
            dst_ref=parts.at[t],
            send_sem=sum_sem.at[0],
            recv_sem=sum_sem.at[1],
            device_id=along(a, b),
            device_id_type=MESH,
        ).start()

    def wait_for(buffer, many, sem):
        some = buffer.at[pl.ds(0, many)]
        pltpu.make_async_copy(some, some, sem).wait()

    parts[t] = part[y]
    relay(3)
    quarter = weights_of(across)
    for b in (2, 1, 3):
        pltpu.make_async_remote_copy(
            src_ref=quarter,
            dst_ref=quarter,
            send_sem=spread_sem.at[0],
            recv_sem=spread_sem.at[1],
            device_id=along(0, b),
            device_id_type=MESH,
        ).start()
    others = wr.at[across, pl.ds(0, (SIDE - 1) * depth)]
    pre[own_half] = jnp.dot(cand[...], wr[mp, :width], preferred_element_type=F32)
    wait_for(parts, plane - 1, sum_sem.at[1])
    state = jnp.sum(parts[...], axis=0).astype(BF16).astype(F32)

    own_interest = layer_norm(state).astype(BF16).astype(F32)
    told[...] = own_interest
    pieces[user] = own_interest

    for device in levels:
        pltpu.make_async_remote_copy(
            src_ref=told,
            dst_ref=pieces.at[user],
            send_sem=state_sem.at[0],
            recv_sem=state_sem.at[1],
            device_id=device,
            device_id_type=MESH,
        ).start()

    wait_for(pieces, height - 1, state_sem.at[1])
    mine = owner * owned + lax.broadcasted_iota(jnp.int32, (owned, line), 0)
    picker = jnp.where(slots[...] == mine, 1.0, 0.0).astype(BF16)
    known = pieces[...].reshape(line, width).astype(BF16)
    own_slots = jnp.dot(picker, known, preferred_element_type=F32)
    chosen[...] = own_slots
    interests[core * SIDE + y] = own_slots
    for b, n in ((2, 0), (2, 1), (1, 0), (3, 0), (1, 1), (3, 1), (0, 1)):
        pltpu.make_async_remote_copy(
            src_ref=chosen,
            dst_ref=interests.at[core * SIDE + y],
            send_sem=pick_sem.at[0],
            recv_sem=pick_sem.at[1],
            device_id=along_y(b, n),
            device_id_type=MESH,
        ).start()

    pltpu.make_async_copy(others, others, spread_sem.at[1]).wait()
    pre[1 - own_half] = jnp.dot(cand[...], wr[across, :width], preferred_element_type=F32)
    wait_for(interests, 2 * SIDE - 1, pick_sem.at[1])

    interest = jnp.concatenate(
        [interests[g] + interests[SIDE + g] for g in range(groups)], axis=0
    ).astype(BF16)
    half = (0.5 * width**-0.5) * dot_t(cand[...], interest)
    row = lax.div(lax.broadcasted_iota(jnp.int32, half.shape, 0), count)
    column = lax.rem(lax.broadcasted_iota(jnp.int32, half.shape, 1), owned)
    attn = jnp.where(row == column, silu_of_twice(half), 0.0)
    high = attn.astype(BF16)
    low = (attn - high.astype(F32)).astype(BF16)
    factors = jnp.concatenate([high, low, high], axis=1)
    terms = jnp.zeros_like(pre[0])
    for n in range(2):
        block = core + 2 * n
        mixed_in = jnp.dot(interest, wr[block, width:], preferred_element_type=F32)
        large = mixed_in.astype(BF16)
        small = (mixed_in - large.astype(F32)).astype(BF16)
        more = jnp.dot(
            factors, jnp.concatenate([large, large, small], axis=0), preferred_element_type=F32
        )
        half = 0.5 * (pre[n] + vectors[block, 0:1] + more)
        terms += silu_of_twice(half) * vectors[block, 1:2]
    high = terms.astype(BF16)
    low = (terms - high.astype(F32)).astype(BF16)
    ones = jnp.ones((16, terms.shape[1]), BF16)
    own_share = (dot_t(ones, high) + dot_t(ones, low))[0:1]
    share[...] = own_share
    shares[core] = own_share
    exchange = pltpu.make_async_remote_copy(
        src_ref=share,
        dst_ref=shares.at[core],
        send_sem=twin_sem.at[0],
        recv_sem=twin_sem.at[1],
        device_id={"mp": twin},
        device_id_type=MESH,
    )
    exchange.start()
    exchange.wait_recv()
    total = jnp.sum(shares[...], axis=0)
    for r in range(owned):
        scores[r : r + 1, :] = total[0:1, r * count : (r + 1) * count]

    for copy in kv_copies + q_copies:
        copy.wait_send()
    for n in range(HEADS):
        for m in range(2):
            pass_kv(n, m).wait_send()
        pass_q(n).wait_send()
        back_copy(n, 1).wait_send()
    for n in range(1, HEADS):
        back_copy(n, 0).wait_send()
    wait_for(parts, plane - 1, sum_sem.at[0])
    wait_for(pieces, height - 1, state_sem.at[0])
    wait_for(interests, 2 * SIDE - 1, pick_sem.at[0])
    exchange.wait_send()

    pltpu.make_async_copy(others, others, spread_sem.at[0]).wait()

    @pl.when(near == 0)
    def _():
        for copy in chain_copies(mp, over, over_send):
            copy.wait_send()

    @pl.when(near < ends_at)
    def _():
        for copy in chain_copies(across, onward, chain_send):
            copy.wait_send()


def solution(mesh):
    plane, owners, ranks = mesh.shape["tm"], mesh.shape["users"], mesh.shape["mp"]
    line = owners * ranks

    def shards(
        history,
        ln_gain,
        w_proj,
        w_out,
        pool_query,
        lengths,
        slots,
        cand_ids,
        item_table,
        w_rank,
        b_rank,
        w_score,
    ):
        _, events, width = history.shape
        head_size = width // HEADS
        groups = pool_query.shape[0]
        owned, count = cand_ids.shape
        cands = owned * count
        hidden = w_rank.shape[1]
        vmem = pl.BlockSpec(memory_space=pltpu.VMEM)
        smem = pl.BlockSpec(memory_space=pltpu.SMEM)
        hbm = pl.BlockSpec(memory_space=pltpu.HBM)
        dma = pltpu.SemaphoreType.DMA
        return pl.pallas_call(
            kernel,
            out_shape=(
                jax.ShapeDtypeStruct(history.shape, BF16),
                jax.ShapeDtypeStruct((owned, count), F32),
            ),
            in_specs=[smem] + [hbm] * 11,
            out_specs=(vmem, vmem),
            scratch_shapes=[
                pltpu.VMEM((events, width), BF16),
                pltpu.VMEM((1, width), F32),
                pltpu.VMEM(pool_query.shape, BF16),
                pltpu.VMEM((1, line), jnp.int32),
                pltpu.VMEM((owned, count), jnp.int32),
                pltpu.VMEM((1, hidden), F32),
                pltpu.VMEM((1, hidden), F32),
                pltpu.VMEM((4, width, width), BF16),
                pltpu.VMEM((width, width), BF16),
                pltpu.VMEM(item_table.shape, BF16),
                pltpu.VMEM((ranks, *w_rank.shape), BF16),
                pltpu.VMEM((events, width), BF16),
                pltpu.VMEM((events, width), BF16),
                pltpu.VMEM((HEADS, 3, events, head_size), BF16),
                pltpu.VMEM((2 * HEADS, 2, events, head_size), BF16),
                pltpu.VMEM((2 * HEADS, events, head_size), BF16),
                pltpu.VMEM((2 * HEADS * events, head_size), F32),
                pltpu.VMEM((2, HEADS, events, head_size), BF16),
                pltpu.VMEM((2, HEADS, events, head_size), BF16),
                pltpu.VMEM((3, events, events), F32),
                pltpu.VMEM((cands, width), BF16),
                pltpu.VMEM((2, cands, hidden), F32),
                pltpu.VMEM((groups, 1, width), F32),
                pltpu.VMEM((plane, 1, width), F32),
                pltpu.VMEM((1, width), F32),
                pltpu.VMEM((line, 1, width), F32),
                pltpu.VMEM((owned, width), F32),
                pltpu.VMEM((2 * SIDE, owned, width), F32),
                pltpu.VMEM((ranks, 2, hidden), F32),
                pltpu.VMEM((1, cands), F32),
                pltpu.VMEM((2, 1, cands), F32),
                dma((14,)),
                dma((HEADS, 2)),
                dma((HEADS, 2)),
                dma((HEADS,)),
                dma((HEADS,)),
                dma((3, HEADS)),
                dma((3, HEADS)),
                dma((2, HEADS)),
                dma((2, HEADS)),
                dma((2,)),
                dma((2,)),
                dma((2,)),
                dma((2,)),
                dma((2,)),
                dma((2,)),
                dma((2,)),
                dma((2,)),
            ],
            compiler_params=pltpu.CompilerParams(
                collective_id=0, has_side_effects=True, vmem_limit_bytes=VMEM_BYTES
            ),
            cost_estimate=pl.CostEstimate(
                flops=4_000_000_000, bytes_accessed=6_000_000, transcendentals=5_000_000
            ),
        )(
            lengths,
            history,
            ln_gain.reshape(1, -1),
            w_proj,
            w_out,
            pool_query,
            slots.reshape(1, -1),
            cand_ids,
            item_table,
            w_rank,
            b_rank.reshape(1, -1),
            w_score.reshape(1, -1),
        )

    placed = (
        P(("users", "mp"), "tm", None),
        P(),
        P(),
        P(),
        P(),
        P(("users", "mp")),
        P(),
        P("users", "tm"),
        P("users", None),
        P(None, "mp"),
        P("mp"),
        P("mp"),
    )
    return jax.shard_map(
        shards,
        mesh=mesh,
        in_specs=placed,
        out_specs=(P(("users", "mp"), "tm", None), P("users", "tm")),
        check_vma=False,
    )
```

```python
import jax
import jax.numpy as jnp
from jax import lax
from jax.experimental import pallas as pl
from jax.experimental.pallas import tpu as pltpu
from jax.sharding import PartitionSpec as P

HEADS = 4
SIDE = 4
EPS = 1e-05
VMEM_BYTES = 64 * 1024 * 1024
MESH = pl.DeviceIdType.MESH
STEPS = sorted(
    ((a, b) for a in range(SIDE) for b in range(SIDE) if a or b),
    key=lambda step: -sum(min(n, SIDE - n) for n in step),
)
F32 = jnp.float32
BF16 = jnp.bfloat16
ROWS_BY_ROWS = (((1,), (1,)), ((), ()))


def layer_norm(values):
    mean = jnp.mean(values, axis=-1, keepdims=True)
    centred = values - mean
    var = jnp.mean(centred * centred, axis=-1, keepdims=True)
    return centred * lax.rsqrt(var + EPS)


def silu_of_twice(half):
    return half + half * jnp.tanh(half)


def dot_t(a, b, **kw):
    return lax.dot_general(a, b, ROWS_BY_ROWS, preferred_element_type=F32, **kw)


def kernel(
    lengths,
    history,
    ln_gain_hbm,
    w_proj,
    w_out,
    pool_query_hbm,
    slots_hbm,
    cand_ids_hbm,
    item_table,
    w_rank,
    b_rank_hbm,
    w_score_hbm,
    layer_out,
    scores,
    hist,
    ln_gain,
    pool_query,
    slots,
    cand_ids,
    b_rank,
    w_score,
    wp,
    wo,
    table,
    wr,
    normed,
    gate,
    qkv,
    kv,
    qs,
    acc,
    back,
    att,
    masks,
    cand,
    pre,
    part,
    parts,
    told,
    pieces,
    chosen,
    interests,
    vectors,
    share,
    shares,
    load_sem,
    kv_send,
    kv_recv,
    q_send,
    q_recv,
    pass_send,
    pass_recv,
    back_send,
    back_recv,
    sum_sem,
    state_sem,
    pick_sem,
    over_send,
    chain_send,
    chain_recv,
    spread_sem,
    twin_sem,
):
    events, width = hist.shape
    head_size = width // HEADS
    plane, line, ranks = parts.shape[0], pieces.shape[0], wr.shape[0]
    t = lax.axis_index("tm")
    owner = lax.axis_index("users")
    mp = lax.axis_index("mp")
    user = owner * ranks + mp
    x, y = lax.div(t, SIDE), lax.rem(t, SIDE)
    core = lax.rem(mp, 2)

    def even(v):
        return v + 1 - 2 * lax.rem(v, 2)

    def odd(v):
        return SIDE - 1 - v

    def swap_y(v):
        return even(v) + core * (odd(v) - even(v))

    def ring_y(v):
        return odd(v) + core * (even(v) - odd(v))

    def head_of(a, b):
        first = lax.rem(lax.div(b + 1, 2), 2)
        return 2 * lax.div(a, 2) + first + core * (lax.div(b, 2) - first)

    def moved(a, b, rel):
        first, second = lax.rem(rel, 2), lax.div(rel, 2)
        return a + second * (odd(a) - a), b + first * (swap_y(b) - b)

    def in_plane(a, b):
        return {"tm": a * SIDE + b}

    head = head_of(x, y)

    depth = wr.shape[1] // SIDE
    last = line // ranks - 1
    twin = mp + 1 - 2 * core
    across = lax.rem(mp + 2, ranks)
    near = jnp.minimum(owner, last - owner)
    step_on = jnp.where(owner < near + 1, 1, -1)
    ends_at = last // 2

    def weights_of(whose):
        return wr.at[whose, pl.ds(pl.multiple_of(y * depth, depth), depth)]

    def chain_copies(whose, to, sems):
        return [
            pltpu.make_async_remote_copy(
                src_ref=ref,
                dst_ref=ref,
                send_sem=sems.at[n],
                recv_sem=chain_recv.at[n],
                device_id=to,
                device_id_type=MESH,
            )
            for n, ref in enumerate((weights_of(whose), vectors.at[whose]))
        ]

    over = {"users": last - owner, "mp": across}
    onward = {"users": owner + step_on}

    def relay(j):
        @pl.when(near == j)
        def _():
            for copy in chain_copies(across, onward, chain_send):
                copy.wait_recv()
                if j < ends_at:
                    copy.start()

    loads = [pltpu.make_async_copy(history.at[0], hist, load_sem.at[0])]
    for n, block in enumerate((3, 1, 2, 0)):
        cols = pl.ds(block * width, width)
        loads.append(pltpu.make_async_copy(w_proj.at[:, cols], wp.at[n], load_sem.at[n + 1]))
    rest = (
        (ln_gain_hbm, ln_gain),
        (pool_query_hbm, pool_query),
        (slots_hbm, slots),
        (cand_ids_hbm, cand_ids),
        (b_rank_hbm, b_rank),
        (w_score_hbm, w_score),
        (w_out, wo),
        (item_table, table),
        (w_rank, wr.at[mp]),
    )
    for n, (src, dst) in enumerate(rest):
        loads.append(pltpu.make_async_copy(src, dst, load_sem.at[5 + n]))
    loads[0].start()
    loads[5].start()
    for load in loads[1:5] + loads[6:]:
        load.start()

    pieces[...] = jnp.zeros_like(pieces)

    barrier = pltpu.get_barrier_semaphore()
    height = line // 2
    low = height // 2
    level = lax.div(mp, 2) * low + owner

    levels = []
    for k in range(height - 1):
        chip = lax.rem(level + low + (k + 1) // 2 * (1 - 2 * (k % 2)), height)
        levels.append({"users": lax.rem(chip, low), "mp": 2 * lax.div(chip, low) + core})

    def along(a, b):
        return {"tm": lax.rem(x + a, SIDE) * SIDE + lax.rem(y + b, SIDE)}

    def along_y(b, other):
        return {"tm": x * SIDE + lax.rem(y + b, SIDE), "mp": mp + other * (1 - 2 * core)}

    greeted = [along(a, b) for a, b in STEPS] + [along_y(b, 1) for b in range(SIDE)]
    greeted = levels + greeted
    for device in greeted:
        pl.semaphore_signal(barrier, inc=1, device_id=device, device_id_type=MESH)

    first_pos = t * events
    length = lengths[0]
    pos = first_pos + lax.broadcasted_iota(jnp.int32, (events, 1), 0)
    live = pos < length
    loads[0].wait()
    loads[5].wait()
    normed[...] = (layer_norm(hist[...].astype(F32)) * ln_gain[...]).astype(BF16)

    def project(n):
        loads[n + 1].wait()
        half = 0.5 * jnp.dot(normed[...], wp[n], preferred_element_type=F32)
        return silu_of_twice(half)

    keys = project(0).astype(BF16)
    for h in range(HEADS):
        qkv[h, 0] = keys[:, h * head_size : (h + 1) * head_size]
    values = jnp.where(live, project(1), 0.0).astype(BF16)
    for h in range(HEADS):
        qkv[h, 1] = values[:, h * head_size : (h + 1) * head_size]

    pl.semaphore_wait(barrier, len(greeted))

    kv_copies, q_copies = [], []
    for rel in (3, 2, 1):
        a, b = moved(x, y, rel)
        for n in range(2):
            copy = pltpu.make_async_remote_copy(
                src_ref=qkv.at[head_of(a, b), n],
                dst_ref=kv.at[rel, n],
                send_sem=kv_send.at[rel, n],
                recv_sem=kv_recv.at[rel, n],
                device_id=in_plane(a, b),
                device_id_type=MESH,
            )
            copy.start()
            kv_copies.append(copy)

    query = (project(2) * (0.5 * head_size**-0.5)).astype(BF16)
    for h in range(HEADS):
        qkv[h, 2] = query[:, h * head_size : (h + 1) * head_size]
    for rel in (3, 2, 1):
        a, b = moved(x, y, rel)
        copy = pltpu.make_async_remote_copy(
            src_ref=qkv.at[head_of(a, b), 2],
            dst_ref=qs.at[rel],
            send_sem=q_send.at[rel],
            recv_sem=q_recv.at[rel],
            device_id=in_plane(a, b),
            device_id_type=MESH,
        )
        copy.start()
        q_copies.append(copy)
    for load in loads[9:11] + loads[13:]:
        load.wait()
    vectors[mp, 0:1] = b_rank[...]
    vectors[mp, 1:2] = w_score[...]

    @pl.when(near == 0)
    def _():
        for copy in chain_copies(mp, over, over_send):
            copy.start()

    kv[0] = qkv[head, pl.ds(0, 2)]
    qs[0] = qkv[head, 2]

    x_near, y_near = even(x), ring_y(y)

    def pass_kv(n, m):
        return pltpu.make_async_remote_copy(
            src_ref=kv.at[n, m],
            dst_ref=kv.at[HEADS + n, m],
            send_sem=pass_send.at[m, n],
            recv_sem=pass_recv.at[m, n],
            device_id=in_plane(x_near, y),
            device_id_type=MESH,
        )

    def pass_q(n):
        return pltpu.make_async_remote_copy(
            src_ref=qs.at[n],
            dst_ref=qs.at[HEADS + n],
            send_sem=pass_send.at[2, n],
            recv_sem=pass_recv.at[2, n],
            device_id=in_plane(x, y_near),
            device_id_type=MESH,
        )

    def back_copy(n, which):
        a, b = moved(x, y_near if which else y, n)
        return pltpu.make_async_remote_copy(
            src_ref=back.at[which, n],
            dst_ref=att.at[which, head],
            send_sem=back_send.at[which, n],
            recv_sem=back_recv.at[which, n],
            device_id=in_plane(a, b),
            device_id_type=MESH,
        )

    pass_q(0).start()
    for m in range(2):
        pass_kv(0, m).start()

    gate[...] = project(3).astype(BF16)
    acc[...] = jnp.zeros_like(acc)

    owned, count = cand_ids.shape
    pool = table.shape[0]
    for load in loads[6:9] + loads[11:13]:
        load.wait()

    @pl.loop(0, owned)
    def _(r):
        @pl.when(r > 0)
        def _():
            for m in range(2):
                pltpu.make_async_copy(kv.at[r, m], kv.at[r, m], kv_recv.at[r, m]).wait()
                pass_kv(r, m).start()

        eye = lax.broadcasted_iota(jnp.int32, (count, count), 0) == lax.broadcasted_iota(
            jnp.int32, (count, count), 1
        )
        item = lax.broadcasted_iota(jnp.int32, (count, pool), 1).astype(F32)
        ids = cand_ids[pl.ds(r, 1), :].astype(F32)
        column = jnp.sum(jnp.where(eye, ids, 0.0), axis=1, keepdims=True)
        onehot = jnp.where(item == column, 1.0, 0.0).astype(BF16)
        cand[pl.ds(r * count, count)] = jnp.dot(
            onehot, table[...], preferred_element_type=F32
        ).astype(BF16)

    pairs = 2 * events
    behind = lax.broadcasted_iota(jnp.int32, (events, events), 0) >= lax.broadcasted_iota(
        jnp.int32, (events, events), 1
    )
    masks[0] = jnp.zeros((events, events), F32)
    masks[1] = jnp.where(behind, 1.0, 0.0)
    masks[2] = jnp.ones((events, events), F32)

    def rows_of(which, pair):
        return pl.ds(pl.multiple_of((2 * which + pair) * pairs, pairs), pairs)

    def attend(q_set, q_pair, k_set, k_pair, masked):
        q_first, k_first = HEADS * q_set + 2 * q_pair, HEADS * k_set + 2 * k_pair
        query = qs[pl.ds(q_first, 2)].reshape(pairs, head_size)
        half = jnp.concatenate(
            [dot_t(query, kv[k_first + n, 0]) for n in range(2)], axis=1
        )
        if masked:
            q_y = y_near if q_set else y
            half = jnp.concatenate(
                [
                    jnp.concatenate(
                        [
                            half[a * events : (a + 1) * events, b * events : (b + 1) * events]
                            * masks[1 + jnp.clip(q_row - k_row, -1, 1)]
                            for b, k_row in enumerate((y, swap_y(y)))
                        ],
                        axis=1,
                    )
                    for a, q_row in enumerate((q_y, swap_y(q_y)))
                ],
                axis=0,
            )
        weights = silu_of_twice(half).astype(BF16)
        value = jnp.concatenate([kv[k_first + n, 1] for n in range(2)], axis=0)
        acc[rows_of(q_set, q_pair)] += jnp.dot(weights, value, preferred_element_type=F32)

    late = jnp.where(x < SIDE // 2, 1, 0)
    early = 1 - late
    outer = jnp.logical_or(x == 0, x == SIDE - 1)

    def attend_own(q_set):
        for pair in range(2):
            attend(q_set, pair, 0, pair, True)
        attend(q_set, late, 0, early, False)

    def attend_near(q_set, n):
        q_pair = late if n else jnp.where(outer, late, early)
        k_pair = jnp.where(outer, n, jnp.where(x == 1, 0, 1))
        attend(q_set, q_pair, 1, k_pair, False)

    for n in range(1, HEADS):
        pltpu.make_async_copy(qs.at[n], qs.at[n], q_recv.at[n]).wait()
        pass_q(n).start()
    attend_own(0)
    relay(0)
    for n in range(HEADS):
        pass_q(n).wait_recv()
    attend(1, 0, 0, 0, True)
    attend(1, 1, 0, 1, True)
    attend(1, late, 0, early, False)
    for n in range(HEADS):
        for m in range(2):
            pass_kv(n, m).wait_recv()
    def send_back(which, pair):
        for m in (1, 0):
            n = 2 * pair + m
            rows = pl.ds(pl.multiple_of((HEADS * which + n) * events, events), events)
            summed = acc[rows].astype(BF16)
            away = n >= 1 - which

            @pl.when(away)
            def _():
                back[which, n] = summed
                back_copy(n, which).start()

            @pl.when(jnp.logical_not(away))
            def _():
                att[which, head] = summed

    attend_near(1, 0)
    send_back(1, early)
    attend_near(1, 1)
    send_back(1, late)
    relay(1)
    attend_near(0, 0)
    send_back(0, early)
    attend_near(0, 1)
    send_back(0, late)
    relay(2)
    for n in range(HEADS):
        back_copy(n, 1).wait_recv()
    for n in range(1, HEADS):
        back_copy(n, 0).wait_recv()

    own_half = lax.div(mp, 2)
    attended = jnp.concatenate(
        [att[0, h].astype(F32) + att[1, h].astype(F32) for h in range(HEADS)], axis=1
    )
    mixed = (layer_norm(attended) * gate[...].astype(F32)).astype(BF16)
    projected = jnp.dot(mixed, wo[...], preferred_element_type=F32)
    out = (hist[...].astype(F32) + projected).astype(BF16)
    layer_out[0] = out
    groups = pool_query.shape[0]
    half = 0.5 * dot_t(pool_query[...], out)
    lane = first_pos + lax.broadcasted_iota(jnp.int32, half.shape, 1)
    pool_w = jnp.where(lane < length, silu_of_twice(half), 0.0).astype(BF16)
    sums = jnp.dot(pool_w, out, preferred_element_type=F32)

    for g in range(groups):
        part[g] = sums[g : g + 1]
    for a, b in STEPS:
        pltpu.make_async_remote_copy(
            src_ref=part.at[lax.rem(y + b, SIDE)],
            dst_ref=parts.at[t],
            send_sem=sum_sem.at[0],
            recv_sem=sum_sem.at[1],
            device_id=along(a, b),
            device_id_type=MESH,
        ).start()

    def wait_for(buffer, many, sem):
        some = buffer.at[pl.ds(0, many)]
        pltpu.make_async_copy(some, some, sem).wait()

    parts[t] = part[y]
    others = wr.at[across, pl.ds(0, (SIDE - 1) * depth)]
    pre[own_half] = jnp.dot(cand[...], wr[mp, :width], preferred_element_type=F32)
    wait_for(parts, plane - 1, sum_sem.at[1])
    state = jnp.sum(parts[...], axis=0).astype(BF16).astype(F32)

    own_interest = layer_norm(state).astype(BF16).astype(F32)
    told[...] = own_interest
    pieces[user] = own_interest

    for device in levels:
        pltpu.make_async_remote_copy(
            src_ref=told,
            dst_ref=pieces.at[user],
            send_sem=state_sem.at[0],
            recv_sem=state_sem.at[1],
            device_id=device,
            device_id_type=MESH,
        ).start()

    relay(3)
    quarter = weights_of(across)
    for b in (2, 1, 3):
        pltpu.make_async_remote_copy(
            src_ref=quarter,
            dst_ref=quarter,
            send_sem=spread_sem.at[0],
            recv_sem=spread_sem.at[1],
            device_id=along(0, b),
            device_id_type=MESH,
        ).start()
    wait_for(pieces, height - 1, state_sem.at[1])
    mine = owner * owned + lax.broadcasted_iota(jnp.int32, (owned, line), 0)
    picker = jnp.where(slots[...] == mine, 1.0, 0.0).astype(BF16)
    known = pieces[...].reshape(line, width).astype(BF16)
    own_slots = jnp.dot(picker, known, preferred_element_type=F32)
    chosen[...] = own_slots
    interests[core * SIDE + y] = own_slots
    for b, n in ((2, 0), (2, 1), (1, 0), (3, 0), (1, 1), (3, 1), (0, 1)):
        pltpu.make_async_remote_copy(
            src_ref=chosen,
            dst_ref=interests.at[core * SIDE + y],
            send_sem=pick_sem.at[0],
            recv_sem=pick_sem.at[1],
            device_id=along_y(b, n),
            device_id_type=MESH,
        ).start()

    pltpu.make_async_copy(others, others, spread_sem.at[1]).wait()
    pre[1 - own_half] = jnp.dot(cand[...], wr[across, :width], preferred_element_type=F32)
    wait_for(interests, 2 * SIDE - 1, pick_sem.at[1])

    interest = jnp.concatenate(
        [interests[g] + interests[SIDE + g] for g in range(groups)], axis=0
    ).astype(BF16)
    half = (0.5 * width**-0.5) * dot_t(cand[...], interest)
    row = lax.div(lax.broadcasted_iota(jnp.int32, half.shape, 0), count)
    column = lax.rem(lax.broadcasted_iota(jnp.int32, half.shape, 1), owned)
    attn = jnp.where(row == column, silu_of_twice(half), 0.0)
    high = attn.astype(BF16)
    low = (attn - high.astype(F32)).astype(BF16)
    factors = jnp.concatenate([high, low, high], axis=1)
    terms = jnp.zeros_like(pre[0])
    for n in range(2):
        block = core + 2 * n
        mixed_in = jnp.dot(interest, wr[block, width:], preferred_element_type=F32)
        large = mixed_in.astype(BF16)
        small = (mixed_in - large.astype(F32)).astype(BF16)
        more = jnp.dot(
            factors, jnp.concatenate([large, large, small], axis=0), preferred_element_type=F32
        )
        half = 0.5 * (pre[n] + vectors[block, 0:1] + more)
        terms += silu_of_twice(half) * vectors[block, 1:2]
    high = terms.astype(BF16)
    low = (terms - high.astype(F32)).astype(BF16)
    ones = jnp.ones((16, terms.shape[1]), BF16)
    own_share = (dot_t(ones, high) + dot_t(ones, low))[0:1]
    share[...] = own_share
    shares[core] = own_share
    exchange = pltpu.make_async_remote_copy(
        src_ref=share,
        dst_ref=shares.at[core],
        send_sem=twin_sem.at[0],
        recv_sem=twin_sem.at[1],
        device_id={"mp": twin},
        device_id_type=MESH,
    )
    exchange.start()
    exchange.wait_recv()
    total = jnp.sum(shares[...], axis=0)
    for r in range(owned):
        scores[r : r + 1, :] = total[0:1, r * count : (r + 1) * count]

    for copy in kv_copies + q_copies:
        copy.wait_send()
    for n in range(HEADS):
        for m in range(2):
            pass_kv(n, m).wait_send()
        pass_q(n).wait_send()
        back_copy(n, 1).wait_send()
    for n in range(1, HEADS):
        back_copy(n, 0).wait_send()
    wait_for(parts, plane - 1, sum_sem.at[0])
    wait_for(pieces, height - 1, state_sem.at[0])
    wait_for(interests, 2 * SIDE - 1, pick_sem.at[0])
    exchange.wait_send()

    pltpu.make_async_copy(others, others, spread_sem.at[0]).wait()

    @pl.when(near == 0)
    def _():
        for copy in chain_copies(mp, over, over_send):
            copy.wait_send()

    @pl.when(near < ends_at)
    def _():
        for copy in chain_copies(across, onward, chain_send):
            copy.wait_send()


def solution(mesh):
    plane, owners, ranks = mesh.shape["tm"], mesh.shape["users"], mesh.shape["mp"]
    line = owners * ranks

    def shards(
        history,
        ln_gain,
        w_proj,
        w_out,
        pool_query,
        lengths,
        slots,
        cand_ids,
        item_table,
        w_rank,
        b_rank,
        w_score,
    ):
        _, events, width = history.shape
        head_size = width // HEADS
        groups = pool_query.shape[0]
        owned, count = cand_ids.shape
        cands = owned * count
        hidden = w_rank.shape[1]
        vmem = pl.BlockSpec(memory_space=pltpu.VMEM)
        smem = pl.BlockSpec(memory_space=pltpu.SMEM)
        hbm = pl.BlockSpec(memory_space=pltpu.HBM)
        dma = pltpu.SemaphoreType.DMA
        return pl.pallas_call(
            kernel,
            out_shape=(
                jax.ShapeDtypeStruct(history.shape, BF16),
                jax.ShapeDtypeStruct((owned, count), F32),
            ),
            in_specs=[smem] + [hbm] * 11,
            out_specs=(vmem, vmem),
            scratch_shapes=[
                pltpu.VMEM((events, width), BF16),
                pltpu.VMEM((1, width), F32),
                pltpu.VMEM(pool_query.shape, BF16),
                pltpu.VMEM((1, line), jnp.int32),
                pltpu.VMEM((owned, count), jnp.int32),
                pltpu.VMEM((1, hidden), F32),
                pltpu.VMEM((1, hidden), F32),
                pltpu.VMEM((4, width, width), BF16),
                pltpu.VMEM((width, width), BF16),
                pltpu.VMEM(item_table.shape, BF16),
                pltpu.VMEM((ranks, *w_rank.shape), BF16),
                pltpu.VMEM((events, width), BF16),
                pltpu.VMEM((events, width), BF16),
                pltpu.VMEM((HEADS, 3, events, head_size), BF16),
                pltpu.VMEM((2 * HEADS, 2, events, head_size), BF16),
                pltpu.VMEM((2 * HEADS, events, head_size), BF16),
                pltpu.VMEM((2 * HEADS * events, head_size), F32),
                pltpu.VMEM((2, HEADS, events, head_size), BF16),
                pltpu.VMEM((2, HEADS, events, head_size), BF16),
                pltpu.VMEM((3, events, events), F32),
                pltpu.VMEM((cands, width), BF16),
                pltpu.VMEM((2, cands, hidden), F32),
                pltpu.VMEM((groups, 1, width), F32),
                pltpu.VMEM((plane, 1, width), F32),
                pltpu.VMEM((1, width), F32),
                pltpu.VMEM((line, 1, width), F32),
                pltpu.VMEM((owned, width), F32),
                pltpu.VMEM((2 * SIDE, owned, width), F32),
                pltpu.VMEM((ranks, 2, hidden), F32),
                pltpu.VMEM((1, cands), F32),
                pltpu.VMEM((2, 1, cands), F32),
                dma((14,)),
                dma((HEADS, 2)),
                dma((HEADS, 2)),
                dma((HEADS,)),
                dma((HEADS,)),
                dma((3, HEADS)),
                dma((3, HEADS)),
                dma((2, HEADS)),
                dma((2, HEADS)),
                dma((2,)),
                dma((2,)),
                dma((2,)),
                dma((2,)),
                dma((2,)),
                dma((2,)),
                dma((2,)),
                dma((2,)),
            ],
            compiler_params=pltpu.CompilerParams(
                collective_id=0, has_side_effects=True, vmem_limit_bytes=VMEM_BYTES
            ),
            cost_estimate=pl.CostEstimate(
                flops=4_000_000_000, bytes_accessed=6_000_000, transcendentals=5_000_000
            ),
        )(
            lengths,
            history,
            ln_gain.reshape(1, -1),
            w_proj,
            w_out,
            pool_query,
            slots.reshape(1, -1),
            cand_ids,
            item_table,
            w_rank,
            b_rank.reshape(1, -1),
            w_score.reshape(1, -1),
        )

    placed = (
        P(("users", "mp"), "tm", None),
        P(),
        P(),
        P(),
        P(),
        P(("users", "mp")),
        P(),
        P("users", "tm"),
        P("users", None),
        P(None, "mp"),
        P("mp"),
        P("mp"),
    )
    return jax.shard_map(
        shards,
        mesh=mesh,
        in_specs=placed,
        out_specs=(P(("users", "mp"), "tm", None), P("users", "tm")),
        check_vma=False,
    )
```
